32 devices in a mesh: ctx: 8 (over z, y), head: 4 (over x, core).
Axes of the slice: x: 2, y: 2, z: 4, core: 2. Of those that a mesh axis runs over, the one named last changes fastest.
Arguments:
- queries: bfloat16 [8192, 12288], P('ctx', 'head'), may hold values from -24 to 24
- key_rows: bfloat16 [8192, 768], P('ctx'), may hold values from -6 to 6
- value_rows: bfloat16 [8192, 512], P('ctx'), may hold values from -6 to 6
- comp_key_weight: float32 [32, 768], replicated, may hold values from 0.35355338 to 0.70710677
- comp_value_weight: float32 [32, 512], replicated, may hold values from 0.17677669 to 0.53033006
- block_picks: int32 [32, 4, 16], P('ctx'), may hold values from 0 to 124, as said below
- gate_logits: float32 [8192, 3, 64], P('ctx', None, 'head'), may hold values from -6 to 6
- out_weight: bfloat16 [8192, 2560], P('head'), may hold values from -0.25 to 0.25
Outputs:
- layer_out: bfloat16 [8192, 2560], P(('ctx', 'head'))
The draws below stay inside these ranges and needn't reach their ends.
Inputs may be any that keep to these rules, and one draw needn't show every extreme that they name: `block_picks`: for each group, the lists of the 256-position query blocks held by one ctx shard name exactly 1024 / 256 distinct blocks of each earlier shard and of their own shard, and none of later shards; the own-shard blocks named are the first blocks of those query blocks. Every list names the first block of its own query block. Names may repeat within a list.
All inputs are finite; a program needn't handle non-finite values.
Results may differ from the reference program's by a relative error of at most 0.03.
Values may be sent and summed in bfloat16 or wider, within the bound.
No kernel may reach another device: no remote copies, remote signals or barrier semaphores. Data moves between devices by JAX's collectives and lax.ppermute only.
A program may use at most 192 MiB of HBM per device.

```python
import jax
import jax.numpy as jnp
from jax import lax

HEADS = 64
GROUPS = 4
QUERY_KEY_WIDTH = 192
DV = 128
D = 2560
CBLK = 32
KBLK = 64
PICKS = 16
WINDOW = 512
QBLK = 256
TOK_DEV = 1024
TOKENS = 8192
N_HEAD = 4


def draw_queries(key, part):
    base_key = jax.random.fold_in(key, 1)
    bulk = jnp.clip(jax.random.normal(base_key, (TOKENS, HEADS * QUERY_KEY_WIDTH)), -6.0, 6.0)
    return bulk.astype(jnp.bfloat16)


def draw_key_rows(key, part):
    base_key = jax.random.fold_in(key, 2)
    bulk = jnp.clip(jax.random.normal(base_key, (TOKENS, GROUPS * QUERY_KEY_WIDTH)), -6.0, 6.0)
    return bulk.astype(jnp.bfloat16)


def draw_block_picks(key, part):
    shards = TOKENS // TOK_DEV
    lists_here = TOK_DEV // QBLK
    per_owner = TOK_DEV // KBLK
    spread = QBLK // KBLK
    filled = lists_here * (PICKS - 1)
    pool_size = shards * lists_here

    def one_list_set(pair_index):
        shard_index = pair_index // GROUPS
        pair_key = jax.random.fold_in(key, pair_index)
        first_draw = jax.random.randint(jax.random.fold_in(pair_key, 1), (shards, per_owner), 0, 2 ** 20)
        chosen = jnp.argsort(first_draw * per_owner + jnp.arange(per_owner, dtype=jnp.int32)[None, :], axis=1)[:, :lists_here]
        owners = jnp.arange(shards, dtype=jnp.int32)[:, None]
        pool_blocks = (owners * per_owner + chosen).reshape(pool_size)
        earlier = jnp.repeat(jnp.arange(shards, dtype=jnp.int32) < shard_index, lists_here)
        second_sample = jax.random.randint(jax.random.fold_in(pair_key, 2), (pool_size,), 0, 2 ** 20)
        ranking = second_sample * pool_size + jnp.arange(pool_size, dtype=jnp.int32) + jnp.where(earlier, 0, 2 ** 29)
        pool_blocks = pool_blocks[jnp.argsort(ranking)]
        firsts = (shard_index * lists_here + jnp.arange(lists_here, dtype=jnp.int32)) * spread
        pool_count = lists_here * shard_index
        slot_range = jnp.arange(filled, dtype=jnp.int32)
        others = jnp.where(pool_count > 0, pool_blocks[slot_range % jnp.maximum(pool_count, 1)], firsts[slot_range % lists_here])
        pick_lists = jnp.concatenate([firsts[:, None], others.reshape(lists_here, PICKS - 1)], axis=1)
        third_draw = jax.random.randint(jax.random.fold_in(pair_key, 3), (lists_here, PICKS), 0, 2 ** 20)
        mixing = jnp.argsort(third_draw * PICKS + jnp.arange(PICKS, dtype=jnp.int32)[None, :], axis=1)
        return jnp.take_along_axis(pick_lists, mixing, axis=1)
    all_lists = jax.vmap(one_list_set)(jnp.arange(shards * GROUPS, dtype=jnp.int32))
    return all_lists.reshape(shards, GROUPS, lists_here, PICKS).transpose(0, 2, 1, 3).reshape(TOKENS // QBLK, GROUPS, PICKS).astype(jnp.int32)


def levels(stream_key, shape, cuts, low, top_value):
    def one(axis_at, shards_of):
        heights = jax.random.uniform(jax.random.fold_in(jax.random.fold_in(stream_key, 6), axis_at), (shards_of,), jnp.float32, low / len(cuts), top_value / len(cuts))
        return jnp.repeat(jnp.exp(heights), shape[axis_at] // shards_of).reshape((-1,) + (1,) * (len(shape) - axis_at - 1))

    gain = one(*cuts[0])
    for cut in cuts[1:]:
        gain = gain * one(*cut)
    return gain


def normal_values(rng, extent, deviation, limit, split=(), kind=jnp.bfloat16):
    loudness = levels(rng, extent, split, -0.22, 0.18) if split else 1.0
    result = jax.random.normal(rng, extent, jnp.float32) * deviation * loudness
    return jnp.minimum(jnp.maximum(result, -limit), limit).astype(kind)


def setup_inputs(seed: int = 0) -> dict:
    arg_keys = jax.random.split(jax.random.key(seed), 9)
    return {
        "queries": draw_queries(jax.random.fold_in(arg_keys[8], 71), 0),
        "key_rows": draw_key_rows(jax.random.fold_in(arg_keys[8], 71), 0),
        "value_rows": normal_values(arg_keys[2], (TOKENS, GROUPS * DV), 1.0, 6.0, ((0, 8),)),
        "comp_key_weight": jnp.clip(jax.random.uniform(arg_keys[3], (CBLK, GROUPS * QUERY_KEY_WIDTH), jnp.float32, 0.35355338, 0.70710677), 0.35355338, 0.70710677),
        "comp_value_weight": jnp.clip(jax.random.uniform(arg_keys[4], (CBLK, GROUPS * DV), jnp.float32, 0.17677669, 0.53033006), 0.17677669, 0.53033006),
        "block_picks": draw_block_picks(jax.random.fold_in(arg_keys[8], 71), 0),
        "gate_logits": normal_values(arg_keys[6], (TOKENS, 3, HEADS), 1.5, 6.0, ((0, 8), (2, 4)), jnp.float32),
        "out_weight": normal_values(arg_keys[7], (HEADS * DV, D), (HEADS * DV // 16) ** -0.5, 0.25, ((0, 4),)),
    }


NEG_FILL = -1e30


def softmax_parts(scores, keep_mask):
    row_top = jnp.max(jnp.where(keep_mask, scores, NEG_FILL), axis=-1, keepdims=True)
    weights = jnp.where(keep_mask, jnp.exp(scores - row_top), 0.0)
    weight_sum = jnp.sum(weights, axis=-1)
    rounded = lax.optimization_barrier(weights.astype(jnp.bfloat16)).astype(jnp.float32)
    return rounded, weight_sum


def reference(queries, key_rows, value_rows, comp_key_weight, comp_value_weight, block_picks, gate_logits, out_weight):
    per_group = HEADS // GROUPS
    score_scale = QUERY_KEY_WIDTH ** -0.5
    key_groups = key_rows.reshape(TOKENS, GROUPS, QUERY_KEY_WIDTH)
    value_groups = value_rows.reshape(TOKENS, GROUPS, DV)
    comp_keys = jnp.sum(key_rows.reshape(TOKENS // CBLK, CBLK, GROUPS * QUERY_KEY_WIDTH).astype(jnp.float32) * comp_key_weight[None], axis=1).astype(jnp.bfloat16).reshape(TOKENS // CBLK, GROUPS, QUERY_KEY_WIDTH)
    comp_values = jnp.sum(value_rows.reshape(TOKENS // CBLK, CBLK, GROUPS * DV).astype(jnp.float32) * comp_value_weight[None], axis=1).astype(jnp.bfloat16).reshape(TOKENS // CBLK, GROUPS, DV)
    comp_ends = (jnp.arange(TOKENS // CBLK, dtype=jnp.int32) + 1) * CBLK - 1
    key_pad = jnp.concatenate([jnp.zeros((WINDOW, GROUPS, QUERY_KEY_WIDTH), jnp.bfloat16), key_groups], axis=0)
    value_pad = jnp.concatenate([jnp.zeros((WINDOW, GROUPS, DV), jnp.bfloat16), value_groups], axis=0)
    key_tiles = key_groups.reshape(TOKENS // KBLK, KBLK, GROUPS, QUERY_KEY_WIDTH).transpose(2, 0, 1, 3)
    value_tiles = value_groups.reshape(TOKENS // KBLK, KBLK, GROUPS, DV).transpose(2, 0, 1, 3)
    gates = jax.nn.sigmoid(gate_logits)
    group_column = jnp.arange(GROUPS, dtype=jnp.int32)[:, None]
    pick_order = jnp.arange(PICKS, dtype=jnp.int32)

    def one_block(block_index):
        block_start = (block_index * QBLK).astype(jnp.int32)
        query_pos = block_start + jnp.arange(QBLK, dtype=jnp.int32)
        block_q = lax.dynamic_slice_in_dim(queries, block_start, QBLK, 0).reshape(QBLK, GROUPS, per_group, QUERY_KEY_WIDTH).astype(jnp.float32)

        comp_scores = jnp.einsum("qghc,ngc->qghn", block_q, comp_keys.astype(jnp.float32)) * score_scale
        keep_mask = (comp_ends[None, :] <= query_pos[:, None])[:, None, None, :]
        weights, weight_sum = softmax_parts(comp_scores, keep_mask)
        comp_out = jnp.einsum("qghn,ngd->qghd", weights, comp_values.astype(jnp.float32)) / jnp.maximum(weight_sum, 1.0)[..., None]

        win_keys = lax.dynamic_slice_in_dim(key_pad, block_start, WINDOW + QBLK, 0).astype(jnp.float32)
        win_values = lax.dynamic_slice_in_dim(value_pad, block_start, WINDOW + QBLK, 0).astype(jnp.float32)
        key_pos = block_start - WINDOW + jnp.arange(WINDOW + QBLK, dtype=jnp.int32)
        keep_mask = ((key_pos[None, :] >= 0) & (key_pos[None, :] <= query_pos[:, None]) & (key_pos[None, :] >= query_pos[:, None] - WINDOW))[:, None, None, :]
        win_scores = jnp.einsum("qghc,kgc->qghk", block_q, win_keys) * score_scale
        weights, weight_sum = softmax_parts(win_scores, keep_mask)
        win_out = jnp.einsum("qghk,kgd->qghd", weights, win_values) / weight_sum[..., None]

        chosen = lax.dynamic_index_in_dim(block_picks, block_index.astype(jnp.int32), 0, keepdims=False)
        sel_keys = key_tiles[group_column, chosen].reshape(GROUPS, PICKS * KBLK, QUERY_KEY_WIDTH).astype(jnp.float32)
        sel_values = value_tiles[group_column, chosen].reshape(GROUPS, PICKS * KBLK, DV).astype(jnp.float32)
        repeated = jnp.any((chosen[:, :, None] == chosen[:, None, :]) & (pick_order[None, None, :] < pick_order[None, :, None]), axis=-1)
        pick_pos = (chosen[:, :, None] * KBLK + jnp.arange(KBLK, dtype=jnp.int32)).reshape(GROUPS, PICKS * KBLK)
        live_mask = jnp.repeat(jnp.logical_not(repeated), KBLK, axis=1)
        keep_mask = ((pick_pos[None, :, :] <= query_pos[:, None, None]) & live_mask[None])[:, :, None, :]
        sel_scores = jnp.einsum("qghc,gkc->qghk", block_q, sel_keys) * score_scale
        weights, weight_sum = softmax_parts(sel_scores, keep_mask)
        sel_out = jnp.einsum("qghk,gkd->qghd", weights, sel_values) / weight_sum[..., None]

        block_gates = lax.dynamic_slice_in_dim(gates, block_start, QBLK, 0).reshape(QBLK, 3, GROUPS, per_group)
        mixed = block_gates[:, 0, :, :, None] * comp_out + block_gates[:, 1, :, :, None] * sel_out + block_gates[:, 2, :, :, None] * win_out
        return mixed.astype(jnp.bfloat16).reshape(QBLK, HEADS * DV)

    attended = lax.map(one_block, jnp.arange(TOKENS // QBLK, dtype=jnp.int32)).reshape(TOKENS, HEADS * DV)
    per_device = (HEADS // N_HEAD) * DV
    summed = jnp.zeros((TOKENS, D), jnp.float32)
    for head_portion in range(N_HEAD):
        partial_rows = jnp.dot(attended[:, head_portion * per_device:(head_portion + 1) * per_device], out_weight[head_portion * per_device:(head_portion + 1) * per_device], preferred_element_type=jnp.float32)
        summed = summed + lax.optimization_barrier(partial_rows.astype(jnp.bfloat16)).astype(jnp.float32)
    return summed.astype(jnp.bfloat16)
```

```python
import functools

import jax
import jax.numpy as jnp
from jax import lax
from jax.experimental import pallas as pl
from jax.experimental.pallas import tpu as pltpu
from jax.sharding import PartitionSpec as P

HEADS = 64
GROUPS = 4
QK = 192
DV = 128
CBLK = 32
KBLK = 64
PICKS = 16
WINDOW = 512
QBLK = 256
PAIR = 2 * QK
BROWS = KBLK + KBLK // 2 + KBLK
VMEM_LIMIT = 50 * 1024 * 1024
NEG = -1e30
SCALE = QK ** (-0.5) * 1.4426950408889634
NT = (((1,), (1,)), ((), ()))
F32 = jnp.float32
BF16 = jnp.bfloat16


def half_lanes(rows):
    return lax.broadcasted_iota(jnp.int32, (rows, 128), 1) < 64


def swap_halves(x):
    return pltpu.roll(x, 64, 1)


def prep_kernel(group_ref, keys_ref, values_ref, kw_ref, vw_ref, picks_ref, blocks_ref, comp_ref):
    group = group_ref[0]
    odd = lax.rem(group, 2) == 1
    first = pl.multiple_of(lax.div(group, 2) * PAIR, 128)
    vfirst = pl.multiple_of(group * DV, 128)

    def own_columns(ref):
        t0 = ref[:, pl.ds(first, 128)].astype(F32)
        t1 = ref[:, pl.ds(first + 128, 128)].astype(F32)
        t2 = ref[:, pl.ds(first + 256, 128)].astype(F32)
        r1, r2 = swap_halves(t1), swap_halves(t2)
        left = half_lanes(t0.shape[0])
        low = jnp.where(odd, jnp.where(left, r1, r2), t0)
        high = jnp.where(left, jnp.where(odd, r2, t1), 0.0)
        return low, high

    low, high = own_columns(keys_ref)
    values = values_ref[:, pl.ds(vfirst, DV)]
    count = low.shape[0] // KBLK
    high3 = high.reshape(count, KBLK, 128)
    packed_high = high3[:, : KBLK // 2] + swap_halves(
        high3[:, KBLK // 2 :].reshape(count * KBLK // 2, 128)
    ).reshape(count, KBLK // 2, 128)
    blocks_ref[:, :KBLK] = low.astype(BF16).reshape(count, KBLK, 128)
    blocks_ref[:, KBLK : KBLK + KBLK // 2] = packed_high.astype(BF16)
    blocks_ref[:, KBLK + KBLK // 2 :] = values.reshape(count, KBLK, DV)

    wlow, whigh = own_columns(kw_ref)
    wval = vw_ref[:, pl.ds(vfirst, DV)]
    folds = low.shape[0] // CBLK

    def fold(x, w):
        return jnp.sum(x.reshape(folds, CBLK, 128) * w[None], axis=1).astype(BF16)

    comp_ref[:folds, :128] = fold(low, wlow)
    comp_ref[:folds, 128:256] = fold(high, whigh)
    comp_ref[:folds, 256:] = fold(values.astype(F32), wval)
    comp_ref[folds:, :] = jnp.zeros((16, 3 * 128), BF16)
    comp_ref[folds:, :128] = picks_ref[...]


def pack_kernel(n_ctx, lists, me_ref, picks_ref, blocks_ref, *outs):
    per_owner = blocks_ref.shape[0]
    me = me_ref[0]
    for distance in range(1, n_ctx):
        out = outs[distance - 1]
        dest = me + distance

        @pl.when(dest < n_ctx)
        def _():
            named = jnp.int32(0)
            for entry in range(lists * PICKS):
                block = picks_ref[dest * (lists * PICKS) + entry] - me * per_owner
                here = (block >= 0) & (block < per_owner)
                named = named | jnp.where(here, jnp.int32(1) << jnp.where(here, block, 0), 0)
            rank = jnp.int32(0)
            for block in range(per_owner):
                bit = (named >> block) & 1

                @pl.when((bit == 1) & (rank < lists))
                def _():
                    out[jnp.minimum(rank, lists - 1)] = blocks_ref[block]

                rank = rank + bit


def unpack(block):
    low = block[:KBLK].astype(F32)
    packed_high = block[KBLK : KBLK + KBLK // 2].astype(F32)
    value = block[KBLK + KBLK // 2 :].astype(F32)
    swapped = swap_halves(packed_high)
    left = half_lanes(KBLK)
    high_left = jnp.concatenate([packed_high, swapped], axis=0)
    high_right = jnp.concatenate([swapped, packed_high], axis=0)
    low_swapped = swap_halves(low)
    even = (low, jnp.where(left, high_left, 0.0))
    odd = (jnp.where(left, 0.0, low_swapped), jnp.where(left, low_swapped, high_right))
    return even, odd, value


def put_block(slot, block, dead, safe, key_even, key_odd, val):
    even, odd, value = unpack(block)
    rows = pl.ds(slot * KBLK, KBLK)
    for part in range(2):
        cols = slice(part * 128, part * 128 + 128)
        key_even[rows, cols] = jnp.where(dead, safe[0][part], even[part]).astype(BF16)
        key_odd[rows, cols] = jnp.where(dead, safe[1][part], odd[part]).astype(BF16)
    val[rows, :DV] = jnp.where(dead, 0.0, value).astype(BF16)
    val[rows, DV:] = jnp.where(dead, 0.0, jnp.ones((KBLK, DV), F32)).astype(BF16)


def safe_rows(block):
    even, odd, _ = unpack(block)
    return [[x[:1] for x in even], [x[:1] for x in odd]]


def attend(q, keys, values, mask, floor=None):
    scores = lax.dot_general(q, keys, NT, preferred_element_type=F32)
    scores = mask(scores)
    top = jnp.max(scores, axis=1, keepdims=True)
    if floor is not None:
        top = jnp.maximum(top, floor)
    weights = jnp.exp2(scores * SCALE - top * SCALE).astype(BF16)
    out = jnp.dot(weights, values, preferred_element_type=F32)
    return out[:, :DV], out[:, DV:]


def iota(rows, cols, axis):
    return lax.broadcasted_iota(jnp.int32, (rows, cols), axis)


def window_mask(scores):
    rows = scores.shape[0]
    row, col = iota(rows, QBLK, 0), iota(rows, QBLK, 1)
    old = jnp.where(col >= row, scores[:, :QBLK], NEG)
    new = jnp.where(col <= row, scores[:, WINDOW:], NEG)
    return jnp.concatenate([old, scores[:, QBLK:WINDOW], new], axis=1)


def near_kernel(first_block, window, comp, prior, heads, meta_ref, *refs):
    refs = list(refs)
    q_ref, gate_ref = refs.pop(0), refs.pop(0)
    rim_ref, own_ref = (refs.pop(0), refs.pop(0)) if window else (None, None)
    comp_in = refs.pop(0) if comp else None
    prior_ref = refs.pop(0) if prior == "add" else None
    if prior == "alias":
        refs.pop(0)
    out_ref, gates = refs.pop(0), refs.pop(0)
    if window:
        key_even, key_odd, val = refs.pop(0), refs.pop(0), refs.pop(0)
    if comp:
        ck_even, ck_odd, cval = refs.pop(0), refs.pop(0), refs.pop(0)
    shard = meta_ref[0]
    query_block = pl.program_id(0) + first_block
    pair = pl.program_id(1)
    used = ([2] if window else []) + ([0] if comp else [])

    @pl.when(pair == 0)
    def _():
        for place, branch in enumerate(used):
            columns = jax.nn.sigmoid(gate_ref[:, branch, :])
            for head in range(heads):
                gates[place * heads + head] = jnp.broadcast_to(
                    columns[:, head : head + 1], (QBLK, DV)
                )
        if window:
            safe = safe_rows(own_ref[0])
            rim_blocks = WINDOW // KBLK
            for slot in range((WINDOW + QBLK) // KBLK):
                at = query_block * (QBLK // KBLK) + slot - rim_blocks
                in_rim = at < 0
                block = jnp.where(
                    in_rim,
                    rim_ref[jnp.clip(at + rim_blocks, 0, rim_ref.shape[0] - 1)],
                    own_ref[jnp.maximum(at, 0)],
                )
                put_block(slot, block, in_rim & (shard == 0), safe, key_even, key_odd, val)

    if comp:

        @pl.when((pair == 0) & (pl.program_id(0) == 0))
        def _():
            shards = comp_in.shape[0]
            for owner in range(shards):
                rows = slice(owner * CBLK, owner * CBLK + CBLK)
                low = comp_in[owner, :CBLK, :128].astype(F32)
                high = comp_in[owner, :CBLK, 128:256].astype(F32)
                low_swapped, high_swapped = swap_halves(low), swap_halves(high)
                left = half_lanes(CBLK)
                ck_even[rows, :128] = low.astype(BF16)
                ck_even[rows, 128:] = high.astype(BF16)
                ck_odd[rows, :128] = jnp.where(left, 0.0, low_swapped).astype(BF16)
                ck_odd[rows, 128:] = jnp.where(left, low_swapped, high_swapped).astype(BF16)
                cval[rows, :DV] = comp_in[owner, :CBLK, 256:]
                cval[rows, DV:] = jnp.ones((CBLK, DV), BF16)

    position = meta_ref[1] + query_block * QBLK

    def comp_mask(scores):
        rows, cols = scores.shape
        ends = (iota(rows, cols, 1) + 1) * CBLK - 1
        return jnp.where(ends <= position + iota(rows, cols, 0), scores, NEG)

    for side in range(2):
        q = q_ref[:, side * 128 : side * 128 + 256]
        head = pair * 2 + side
        total = None
        if window:
            num, den = attend(q, (key_even, key_odd)[side][...], val[...], window_mask)
            total = gates[head] * (num / den)
        if comp:
            num, den = attend(q, (ck_even, ck_odd)[side][...], cval[...], comp_mask, -1e29)
            term = gates[(heads if window else 0) + head] * (num / jnp.maximum(den, 1.0))
            total = term if total is None else total + term
        cols = slice(side * DV, side * DV + DV)
        if prior == "add":
            total = total + prior_ref[:, cols]
        out_ref[:, cols] = total


def near_branches(
    first_block, block_count, meta, queries, gate_logits, rim, own, comp_all, prior, add_prior
):
    tokens, width = queries.shape
    heads = width // QK
    pairs = heads // 2
    window, comp = own is not None, comp_all is not None
    mode = None if prior is None else ("add" if add_prior else "alias")
    row_block = lambda i, p, *_: (i + first_block, p)
    whole = lambda x: pl.BlockSpec(x.shape, lambda i, p, *_: (0,) * x.ndim)
    operands = [queries, gate_logits]
    specs = [
        pl.BlockSpec((QBLK, PAIR), row_block),
        pl.BlockSpec((QBLK, 3, heads), lambda i, p, *_: (i + first_block, 0, 0)),
    ]
    scratch = [pltpu.VMEM(((window + comp) * heads, QBLK, DV), F32)]
    columns = 0
    if window:
        operands += [rim, own]
        specs += [whole(rim), whole(own)]
        scratch += [pltpu.VMEM((WINDOW + QBLK, 256), BF16)] * 3
        columns += WINDOW + QBLK
    if comp:
        operands += [comp_all]
        specs += [whole(comp_all)]
        count = comp_all.shape[0] * CBLK
        scratch += [pltpu.VMEM((count, 256), BF16)] * 3
        columns += count
    alias = {}
    if mode is not None:
        operands.append(prior)
        specs.append(
            pl.BlockSpec((QBLK, 2 * DV), row_block)
            if mode == "add"
            else pl.BlockSpec(memory_space=pl.ANY)
        )
        alias = {len(operands): 0}
    rows = block_count * QBLK * heads
    return pl.pallas_call(
        functools.partial(near_kernel, first_block, window, comp, mode, heads),
        grid_spec=pltpu.PrefetchScalarGridSpec(
            num_scalar_prefetch=1,
            grid=(block_count, pairs),
            in_specs=specs,
            out_specs=pl.BlockSpec((QBLK, 2 * DV), row_block),
            scratch_shapes=scratch,
        ),
        out_shape=jax.ShapeDtypeStruct((tokens, heads * DV), F32),
        input_output_aliases=alias,
        compiler_params=pltpu.CompilerParams(vmem_limit_bytes=VMEM_LIMIT),
        cost_estimate=pl.CostEstimate(
            flops=rows * columns * 1024, bytes_accessed=rows * (2 * QK + 4 * DV), transcendentals=0
        ),
        name="near_branches",
    )(meta, *operands)


def chosen_kernel(
    heads,
    meta_ref,
    slots_ref,
    dead_ref,
    q_ref,
    gate_ref,
    near_ref,
    pool_ref,
    weight_ref,
    out_ref,
    gates,
    key_even,
    key_odd,
    val,
    attended,
    weight,
    weight_sem,
):
    pair = pl.program_id(0)
    last = pl.num_programs(0) - 1
    rows = q_ref.shape[0]
    list_at = meta_ref[1] * PICKS
    first_row = meta_ref[2]
    copy = pltpu.make_async_copy(weight_ref, weight, weight_sem)

    @pl.when(pair == 0)
    def _():
        copy.start()
        columns = jax.nn.sigmoid(gate_ref[:, 1, :])
        for head in range(heads):
            gates[head] = jnp.broadcast_to(columns[:, head : head + 1], (rows, DV))
        safe = safe_rows(pool_ref[slots_ref[list_at]])
        for slot in range(PICKS):
            put_block(
                slot,
                pool_ref[slots_ref[list_at + slot]],
                dead_ref[list_at + slot] == 1,
                safe,
                key_even,
                key_odd,
                val,
            )

    def mask(scores):
        row, col = iota(rows, 128, 0) + first_row, iota(rows, 128, 1)
        own = jnp.where((col >= KBLK) | (col <= row), scores[:, :128], NEG)
        return jnp.concatenate([own, scores[:, 128:]], axis=1)

    for side in range(2):
        q = q_ref[:, side * 128 : side * 128 + 256]
        num, den = attend(q, (key_even, key_odd)[side][...], val[...], mask)
        cols = slice(side * DV, side * DV + DV)
        mixed = near_ref[:, cols] + gates[pair * 2 + side] * (num / den)
        attended[pair, :, cols] = mixed.astype(BF16)

    @pl.when(pair == last)
    def _():
        copy.wait()
        rows_in = jnp.concatenate([attended[p] for p in range(heads // 2)], axis=1)
        for at in range(0, out_ref.shape[1], 256):
            out_ref[:, at : at + 256] = jnp.dot(
                rows_in, weight[:, at : at + 256], preferred_element_type=F32
            ).astype(out_ref.dtype)


def chosen_and_project(chunk, rows, slots, dead, queries, gate_logits, near, pool, out_weight):
    tokens, width = queries.shape
    heads = width // QK
    pairs = heads // 2
    model = out_weight.shape[1]
    meta = jnp.stack([chunk, chunk * rows // QBLK, lax.rem(chunk * rows, QBLK)]).astype(jnp.int32)
    return pl.pallas_call(
        functools.partial(chosen_kernel, heads),
        grid_spec=pltpu.PrefetchScalarGridSpec(
            num_scalar_prefetch=3,
            grid=(pairs,),
            in_specs=[
                pl.BlockSpec((rows, PAIR), lambda p, m, *_: (m[0], p)),
                pl.BlockSpec((rows, 3, heads), lambda p, m, *_: (m[0], 0, 0)),
                pl.BlockSpec((rows, 2 * DV), lambda p, m, *_: (m[0], p)),
                pl.BlockSpec(pool.shape, lambda p, *_: (0, 0, 0)),
                pl.BlockSpec(memory_space=pl.ANY),
            ],
            out_specs=pl.BlockSpec((rows, model), lambda p, *_: (0, 0)),
            scratch_shapes=[
                pltpu.VMEM((heads, rows, DV), F32),
                pltpu.VMEM((PICKS * KBLK, 256), BF16),
                pltpu.VMEM((PICKS * KBLK, 256), BF16),
                pltpu.VMEM((PICKS * KBLK, 256), BF16),
                pltpu.VMEM((pairs, rows, 2 * DV), BF16),
                pltpu.VMEM(out_weight.shape, BF16),
                pltpu.SemaphoreType.DMA,
            ],
        ),
        out_shape=jax.ShapeDtypeStruct((rows, model), BF16),
        compiler_params=pltpu.CompilerParams(vmem_limit_bytes=VMEM_LIMIT),
        cost_estimate=pl.CostEstimate(
            flops=rows * heads * (PICKS * KBLK * 1024 + 2 * DV * model),
            bytes_accessed=out_weight.size * 2 + rows * width * 2,
            transcendentals=0,
        ),
        name="chosen_and_project",
    )(meta, slots, dead, queries, gate_logits, near, pool, out_weight)


def plan_picks(my_picks, shard, per_owner, n_ctx):
    lists = my_picks.shape[0]
    first = shard * per_owner + jnp.arange(lists, dtype=jnp.int32) * (QBLK // KBLK)
    place = jnp.arange(PICKS, dtype=jnp.int32)[None, :]
    found = jnp.min(jnp.where(my_picks == first[:, None], place, PICKS), axis=1, keepdims=True)
    ordered = jnp.where(place == found, my_picks[:, :1], my_picks)
    ordered = jnp.where(place == 0, first[:, None], ordered)
    repeated = jnp.any(
        (ordered[:, :, None] == ordered[:, None, :]) & (place[0][None, :] < place[0][:, None]),
        axis=-1,
    )
    dead = repeated | (ordered > first[:, None])
    named = jnp.any(
        my_picks.reshape(-1)[None, :] == jnp.arange(n_ctx * per_owner, dtype=jnp.int32)[:, None],
        axis=1,
    ).astype(jnp.int32)
    owner_start = (ordered // per_owner) * per_owner
    block = jnp.arange(n_ctx * per_owner, dtype=jnp.int32)
    before = (block >= owner_start[..., None]) & (block < ordered[..., None])
    rank = jnp.sum(jnp.where(before, named, 0), axis=-1)
    slot = (shard - ordered // per_owner) * lists + jnp.minimum(rank, lists - 1)
    slot = jnp.clip(slot, 0, n_ctx * lists - 1)
    return slot.reshape(-1).astype(jnp.int32), dead.reshape(-1).astype(jnp.int32)


def local(
    queries,
    key_rows,
    value_rows,
    comp_key_weight,
    comp_value_weight,
    block_picks,
    gate_logits,
    out_weight,
):
    tokens = queries.shape[0]
    heads = queries.shape[1] // QK
    n_ctx, n_head = lax.axis_size("ctx"), lax.axis_size("head")
    shard, head_at = lax.axis_index("ctx"), lax.axis_index("head")
    group = head_at * heads // (HEADS // GROUPS)
    per_owner = tokens // KBLK
    lists = tokens // QBLK
    folds = tokens // CBLK
    rim_blocks = WINDOW // KBLK
    params = pltpu.CompilerParams(vmem_limit_bytes=VMEM_LIMIT)

    my_picks = lax.dynamic_index_in_dim(block_picks, group, 1, keepdims=False)
    picks_rows = jnp.pad(my_picks.astype(BF16), ((0, 16 - lists), (0, 128 - PICKS)))
    smem = pl.BlockSpec(memory_space=pltpu.SMEM)
    vmem = pl.BlockSpec(memory_space=pltpu.VMEM)
    blocks, comp_part = pl.pallas_call(
        prep_kernel,
        in_specs=[smem] + [vmem] * 5,
        out_specs=[vmem] * 2,
        out_shape=[
            jax.ShapeDtypeStruct((per_owner, BROWS, 128), BF16),
            jax.ShapeDtypeStruct((folds + 16, 3 * 128), BF16),
        ],
        compiler_params=params,
        name="prep",
    )(group.reshape(1), key_rows, value_rows, comp_key_weight, comp_value_weight, picks_rows)

    comp_all = lax.all_gather(comp_part, "ctx", axis=0)
    rim = lax.ppermute(
        blocks[per_owner - rim_blocks :], "ctx", [(i, i + 1) for i in range(n_ctx - 1)]
    )

    meta = jnp.stack([shard, shard * tokens]).astype(jnp.int32)
    near = functools.partial(near_branches, meta=meta, queries=queries, gate_logits=gate_logits)
    reach = WINDOW // QBLK
    mixed = near(
        reach, lists - reach, rim=blocks, own=blocks, comp_all=None, prior=None, add_prior=False
    )

    all_picks = comp_all[:, folds : folds + lists, :PICKS].astype(jnp.int32).reshape(-1)
    sends = pl.pallas_call(
        functools.partial(pack_kernel, n_ctx, lists),
        in_specs=[smem, smem, vmem],
        out_specs=[vmem] * (n_ctx - 1),
        out_shape=[jax.ShapeDtypeStruct((lists, BROWS, 128), BF16)] * (n_ctx - 1),
        compiler_params=params,
        name="pack",
    )(shard.reshape(1), all_picks, blocks)
    received = [
        lax.ppermute(send, "ctx", [(i, i + d) for i in range(n_ctx - d)])
        for d, send in enumerate(sends, 1)
    ]

    mixed = near(0, reach, rim=rim, own=blocks, comp_all=comp_all, prior=mixed, add_prior=False)
    mixed = near(
        reach, lists - reach, rim=None, own=None, comp_all=comp_all, prior=mixed, add_prior=True
    )

    slots, dead = plan_picks(my_picks, shard, per_owner, n_ctx)
    pool = jnp.concatenate([blocks[:: QBLK // KBLK]] + received, axis=0)
    rows = tokens // n_head
    project = lambda chunk: chosen_and_project(
        chunk, rows, slots, dead, queries, gate_logits, mixed, pool, out_weight
    )
    chips = n_head // 2
    chip, core = head_at // 2, lax.rem(head_at, 2)
    across = [(i, i ^ 1) for i in range(n_head)]
    arrived = []
    for step in range(1, chips):
        target = lax.rem(chip + step, chips) * 2
        other = lax.ppermute(project(target + 1 - core), "head", across)
        mine = project(target + core)
        summed = (mine.astype(F32) + other.astype(F32)).astype(BF16)
        route = [(i, (i + 2 * step) % n_head) for i in range(n_head)]
        arrived.append(lax.ppermute(summed, "head", route))
    arrived.append(lax.ppermute(project(chip * 2 + 1 - core), "head", across))
    total = project(head_at).astype(F32)
    for part in arrived:
        total = total + part.astype(F32)
    return total.astype(BF16)


def solution(mesh):
    placed = (
        P("ctx", "head"),
        P("ctx", None),
        P("ctx", None),
        P(),
        P(),
        P("ctx", None, None),
        P("ctx", None, "head"),
        P("head", None),
    )
    return jax.shard_map(
        local, mesh=mesh, in_specs=placed, out_specs=P(("ctx", "head"), None), check_vma=False
    )
```

```python
import functools

import jax
import jax.numpy as jnp
from jax import lax
from jax.experimental import pallas as pl
from jax.experimental.pallas import tpu as pltpu
from jax.sharding import PartitionSpec as P

HEADS = 64
GROUPS = 4
QK = 192
DV = 128
CBLK = 32
KBLK = 64
PICKS = 16
WINDOW = 512
QBLK = 256
PAIR = 2 * QK
BROWS = KBLK + KBLK // 2 + KBLK
VMEM_LIMIT = 50 * 1024 * 1024
NEG = -1e30
SCALE = QK ** (-0.5) * 1.4426950408889634
NT = (((1,), (1,)), ((), ()))
F32 = jnp.float32
BF16 = jnp.bfloat16


def half_lanes(rows):
    return lax.broadcasted_iota(jnp.int32, (rows, 128), 1) < 64


def swap_halves(x):
    return pltpu.roll(x, 64, 1)


def shift_matrix():
    return jnp.where(iota(256, 256, 1) == iota(256, 256, 0) + 64, 1.0, 0.0).astype(BF16)


def shifted_keys(even):
    return jnp.dot(even, shift_matrix(), preferred_element_type=F32).astype(BF16)


def with_ones(values):
    return jnp.concatenate([values, jnp.ones_like(values)], axis=1)


def prep_kernel(group_ref, keys_ref, values_ref, kw_ref, vw_ref, packed_ref, even_ref, odd_ref, val_ref):
    group = group_ref[0]
    odd = lax.rem(group, 2) == 1
    first = pl.multiple_of(lax.div(group, 2) * PAIR, 128)
    vfirst = pl.multiple_of(group * DV, 128)

    def own_columns(ref):
        t0 = ref[:, pl.ds(first, 128)].astype(F32)
        t1 = ref[:, pl.ds(first + 128, 128)].astype(F32)
        t2 = ref[:, pl.ds(first + 256, 128)].astype(F32)
        r1, r2 = swap_halves(t1), swap_halves(t2)
        left = half_lanes(t0.shape[0])
        low = jnp.where(odd, jnp.where(left, r1, r2), t0)
        high = jnp.where(left, jnp.where(odd, r2, t1), 0.0)
        return low, high

    low, high = own_columns(keys_ref)
    values = values_ref[:, pl.ds(vfirst, DV)]
    rows = low.shape[0]
    count = rows // KBLK
    high3 = high.reshape(count, KBLK, 128)
    packed_high = high3[:, : KBLK // 2] + swap_halves(
        high3[:, KBLK // 2 :].reshape(count * KBLK // 2, 128)
    ).reshape(count, KBLK // 2, 128)
    even = jnp.concatenate([low.astype(BF16), high.astype(BF16)], axis=1)
    even_ref[...] = even
    odd_ref[...] = shifted_keys(even)
    val_ref[...] = with_ones(values)
    for block in range(count):
        at = block * BROWS
        token = slice(block * KBLK, block * KBLK + KBLK)
        packed_ref[at : at + KBLK] = low[token].astype(BF16)
        packed_ref[at + KBLK : at + KBLK + KBLK // 2] = packed_high[block].astype(BF16)
        packed_ref[at + KBLK + KBLK // 2 : at + BROWS] = values[token]

    wlow, whigh = own_columns(kw_ref)
    wval = vw_ref[:, pl.ds(vfirst, DV)]
    folds = rows // CBLK

    def fold(x, w):
        return jnp.sum(x.reshape(folds, CBLK, 128) * w[None], axis=1).astype(BF16)

    at = count * BROWS
    packed_ref[at : at + folds] = fold(low, wlow)
    packed_ref[at + folds : at + 2 * folds] = fold(high, whigh)
    packed_ref[at + 2 * folds :] = fold(values.astype(F32), wval)


def pack_kernel(groups, lists, per_owner, me_ref, *refs):
    picks, (own_ref, other_ref), outs = refs[:groups], refs[groups : groups + 2], refs[groups + 2 :]
    me = me_ref[0]
    parity = lax.rem(me, 2)
    base = me - parity
    data = per_owner * BROWS
    folded = own_ref.shape[0] - data
    for distance in range(groups):
        out = outs[distance]

        @pl.when(base + 2 * distance < 2 * groups)
        def _():
            named = [jnp.int32(0), jnp.int32(0)]
            for row in range(lists):
                for col in range(PICKS):
                    entry = picks[distance][row, col]
                    for side in range(2):
                        block = entry - (base + side) * per_owner
                        here = (block >= 0) & (block < per_owner)
                        bit = jnp.int32(1) << jnp.where(here, block, 0)
                        named[side] = named[side] | jnp.where(here, bit, 0)
            for mine, ref in ((True, own_ref), (False, other_ref)):
                side = parity if mine else 1 - parity
                bits = jnp.where(side == 0, named[0], named[1])
                rank = jnp.int32(0)
                for block in range(per_owner):
                    bit = (bits >> block) & 1

                    @pl.when((bit == 1) & (rank < lists))
                    def _():
                        at = pl.multiple_of(
                            (side * lists + jnp.minimum(rank, lists - 1)) * BROWS, 16
                        )
                        out[pl.ds(at, BROWS)] = ref[block * BROWS : (block + 1) * BROWS]

                    rank = rank + bit
                at = pl.multiple_of(2 * lists * BROWS + side * folded, 16)
                out[pl.ds(at, folded)] = ref[data:]


def unpack(ref, at, count):
    lows, packed, values = [], [], []
    for block in range(count):
        first = at + block * BROWS
        lows.append(ref[first : first + KBLK])
        packed.append(ref[first + KBLK : first + KBLK + KBLK // 2])
        values.append(ref[first + KBLK + KBLK // 2 : first + BROWS])
    packed = jnp.concatenate(packed, axis=0)
    row, col = iota(128, 256, 0), iota(128, 256, 1)
    take = (row == jnp.where(col < 128, col, col - 64)) & (lax.rem(col, 128) < 64)
    both = jnp.dot(packed, take.astype(BF16), preferred_element_type=F32).astype(BF16)
    half = KBLK // 2
    highs = []
    for block in range(count):
        rows = slice(block * half, block * half + half)
        highs += [both[rows, :128], both[rows, 128:]]
    even = jnp.concatenate(
        [jnp.concatenate(lows, axis=0), jnp.concatenate(highs, axis=0)], axis=1
    )
    return even, jnp.concatenate(values, axis=0)


def rim_kernel(rim_at, shard_ref, near_ref, far_ref, even_in, odd_in, val_in, even_ref, odd_ref, val_ref):
    shard = shard_ref[0]
    rim_blocks = WINDOW // KBLK
    even_ref[WINDOW:] = even_in[:WINDOW]
    odd_ref[WINDOW:] = odd_in[:WINDOW]
    val_ref[WINDOW:] = val_in[:WINDOW]

    def fill(ref, at):
        even, values = unpack(ref, at, rim_blocks)
        even_ref[:WINDOW] = even
        odd_ref[:WINDOW] = shifted_keys(even)
        val_ref[:WINDOW] = with_ones(values)

    @pl.when(lax.rem(shard, 2) == 1)
    def _():
        fill(near_ref, rim_at)

    @pl.when((lax.rem(shard, 2) == 0) & (shard > 0))
    def _():
        fill(far_ref, 0)

    @pl.when(shard == 0)
    def _():
        even_ref[:WINDOW] = jnp.broadcast_to(even_in[:1], (WINDOW, 256))
        odd_ref[:WINDOW] = jnp.broadcast_to(odd_in[:1], (WINDOW, 256))
        val_ref[:WINDOW] = jnp.zeros((WINDOW, 256), BF16)


def pool_kernel(groups, lists, shard_ref, *refs):
    ins, (even_ref, odd_ref, val_ref, ceven_ref, codd_ref, cval_ref) = refs[:groups], refs[groups:]
    shard = shard_ref[0]
    base = shard - lax.rem(shard, 2)
    blocks = 2 * lists
    rows = blocks * KBLK
    folds = (ins[0].shape[0] - blocks * BROWS) // 6
    ceven_ref[...] = jnp.zeros_like(ceven_ref)
    codd_ref[...] = jnp.zeros_like(codd_ref)
    cval_ref[...] = jnp.zeros_like(cval_ref)
    for distance in range(groups):
        ref = ins[distance]

        @pl.when(base >= 2 * distance)
        def _():
            even, values = unpack(ref, 0, blocks)
            at = slice(distance * rows, distance * rows + rows)
            even_ref[at] = even
            odd_ref[at] = shifted_keys(even)
            val_ref[at] = with_ones(values)
            for side in range(2):
                first = blocks * BROWS + side * 3 * folds
                low = ref[first : first + folds]
                high = ref[first + folds : first + 2 * folds]
                folded = jnp.concatenate([low, high], axis=1)
                place = pl.ds(pl.multiple_of((base - 2 * distance + side) * folds, 32), folds)
                ceven_ref[place] = folded
                codd_ref[place] = shifted_keys(folded)
                cval_ref[place] = with_ones(ref[first + 2 * folds : first + 3 * folds])


def iota(rows, cols, axis):
    return lax.broadcasted_iota(jnp.int32, (rows, cols), axis)


def attend(q, keys, values, mask, floor=None):
    scores = lax.dot_general(q, keys, NT, preferred_element_type=F32)
    scores = mask(scores)
    top = jnp.max(scores, axis=1, keepdims=True)
    if floor is not None:
        top = jnp.maximum(top, floor)
    weights = jnp.exp2(scores * SCALE - top * SCALE).astype(BF16)
    out = jnp.dot(weights, values, preferred_element_type=F32)
    return out[:, :DV], out[:, DV:]


def stacked(x, times):
    return jnp.concatenate([x] * times, axis=0) if times > 1 else x


def stacked_queries(q_ref, side):
    pairs = q_ref.shape[1] // PAIR
    return jnp.concatenate(
        [q_ref[:, p * PAIR + side * 128 : p * PAIR + side * 128 + 256] for p in range(pairs)],
        axis=0,
    )


def gate_columns(gate_ref, first, branch, heads, side, count):
    turned = pltpu.roll(gate_ref[...], lax.rem(128 - first, 128), 1)
    at = branch * heads + side
    rows = turned.shape[0]
    return jnp.concatenate(
        [
            jnp.broadcast_to(turned[:, at + 2 * p : at + 2 * p + 1], (rows, DV))
            for p in range(count)
        ],
        axis=0,
    )


def near_kernel(heads, q_ref, gate_ref, even_ref, odd_ref, val_ref, *refs):
    out_ref = refs[-1]
    rows = pl.ds(pl.multiple_of(pl.program_id(0) * QBLK, QBLK), WINDOW + QBLK)
    pairs = q_ref.shape[1] // PAIR
    first = pl.program_id(1) * 2 * pairs

    def mask(scores):
        row, col = iota(QBLK, QBLK, 0), iota(QBLK, QBLK, 1)
        old = jnp.where(stacked(col >= row, pairs), scores[:, :QBLK], NEG)
        new = jnp.where(stacked(col <= row, pairs), scores[:, WINDOW:], NEG)
        return jnp.concatenate([old, scores[:, QBLK:WINDOW], new], axis=1)

    for side in range(2):
        keys = (even_ref, odd_ref)[side][rows]
        num, den = attend(stacked_queries(q_ref, side), keys, val_ref[rows], mask)
        total = gate_columns(gate_ref, first, 2, heads, side, pairs) * (num / den)
        for p in range(pairs):
            at = (2 * p + side) * DV
            out_ref[:, at : at + DV] = total[p * QBLK : (p + 1) * QBLK]


def near_branch(first_block, block_count, queries, gates, even, odd, val, prior):
    tokens, width = queries.shape
    heads = width // QK
    steps = heads // 4
    row_block = lambda i, p: (i + first_block, p)
    whole = lambda x: pl.BlockSpec(x.shape, lambda i, p: (0,) * x.ndim)
    operands = [queries, gates, even, odd, val]
    specs = [
        pl.BlockSpec((QBLK, 2 * PAIR), row_block),
        pl.BlockSpec((QBLK, 128), lambda i, p: (i + first_block, 0)),
        whole(even),
        whole(odd),
        whole(val),
    ]
    alias = {}
    if prior is not None:
        alias = {len(operands): 0}
        operands.append(prior)
        specs.append(pl.BlockSpec(memory_space=pl.ANY))
    rows = block_count * QBLK * heads
    return pl.pallas_call(
        functools.partial(near_kernel, heads),
        grid=(block_count, steps),
        in_specs=specs,
        out_specs=pl.BlockSpec((QBLK, 4 * DV), row_block),
        out_shape=jax.ShapeDtypeStruct((tokens, heads * DV), F32),
        input_output_aliases=alias,
        compiler_params=pltpu.CompilerParams(vmem_limit_bytes=VMEM_LIMIT),
        cost_estimate=pl.CostEstimate(
            flops=rows * (WINDOW + QBLK) * 1024,
            bytes_accessed=rows * (2 * QK + 4 * DV),
            transcendentals=0,
        ),
        name="near_branch",
    )(*operands)


def chosen_kernel(heads, *refs):
    meta_ref, slots_ref, dead_ref, q_ref, gate_ref, near_ref = refs[:6]
    pools, cfold, (weight_ref, out_ref) = refs[6:9], refs[9:12], refs[12:14]
    keys, (attended, weight, weight_sem) = refs[14:17], refs[17:]
    step = pl.program_id(0)
    last = pl.num_programs(0) - 1
    rows = q_ref.shape[0]
    pairs = q_ref.shape[1] // PAIR
    first = step * 2 * pairs
    list_at = meta_ref[1] * PICKS
    first_row = meta_ref[2]
    position = meta_ref[3]
    copy = pltpu.make_async_copy(weight_ref, weight, weight_sem)

    @pl.when(step == 0)
    def _():
        for slot in range(PICKS):
            source = pl.multiple_of(slots_ref[list_at + slot] * KBLK, KBLK)
            for pool, key in zip(pools, keys):
                key[slot * KBLK : (slot + 1) * KBLK] = pool[pl.ds(source, KBLK)]
        for slot in range(1, PICKS):

            @pl.when(dead_ref[list_at + slot] == 1)
            def _():
                at = slice(slot * KBLK, (slot + 1) * KBLK)
                for key in keys[:2]:
                    key[at] = jnp.broadcast_to(key[:1], (KBLK, 256))
                keys[2][at] = jnp.zeros((KBLK, 256), BF16)

        copy.start()

    def own_mask(scores):
        row, col = iota(rows, 128, 0) + first_row, iota(rows, 128, 1)
        keep = stacked((col >= KBLK) | (col <= row), pairs)
        own = jnp.where(keep, scores[:, :128], NEG)
        return jnp.concatenate([own, scores[:, 128:]], axis=1)

    def comp_mask(scores):
        cols = scores.shape[1]
        ends = (iota(rows, cols, 1) + 1) * CBLK - 1
        return jnp.where(stacked(ends <= position + iota(rows, cols, 0), pairs), scores, NEG)

    for side in range(2):
        q = stacked_queries(q_ref, side)
        num, den = attend(q, keys[side][...], keys[2][...], own_mask)
        total = gate_columns(gate_ref, first, 1, heads, side, pairs) * (num / den)
        num, den = attend(q, cfold[side][...], cfold[2][...], comp_mask, -1e29)
        gate = gate_columns(gate_ref, first, 0, heads, side, pairs)
        total = total + gate * (num / jnp.maximum(den, 1.0))
        for p in range(pairs):
            at = (2 * p + side) * DV
            mixed = near_ref[:, at : at + DV] + total[p * rows : (p + 1) * rows]
            attended[step, :, at : at + DV] = mixed.astype(BF16)

    @pl.when(step == last)
    def _():
        copy.wait()
        rows_in = jnp.concatenate([attended[s] for s in range(heads // 4)], axis=1)
        for at in range(0, out_ref.shape[1], 256):
            out_ref[:, at : at + 256] = jnp.dot(
                rows_in, weight[:, at : at + 256], preferred_element_type=F32
            ).astype(out_ref.dtype)


def chosen_and_project(chunk, rows, shard, slots, dead, queries, gates, near, pools, out_weight):
    tokens, width = queries.shape
    heads = width // QK
    steps = heads // 4
    model = out_weight.shape[1]
    start = chunk * rows
    meta = jnp.stack([chunk, start // QBLK, lax.rem(start, QBLK), shard * tokens + start])
    whole = lambda x: pl.BlockSpec(x.shape, lambda p, *_: (0,) * x.ndim)
    return pl.pallas_call(
        functools.partial(chosen_kernel, heads),
        grid_spec=pltpu.PrefetchScalarGridSpec(
            num_scalar_prefetch=3,
            grid=(steps,),
            in_specs=[
                pl.BlockSpec((rows, 2 * PAIR), lambda p, m, *_: (m[0], p)),
                pl.BlockSpec((rows, 128), lambda p, m, *_: (m[0], 0)),
                pl.BlockSpec((rows, 4 * DV), lambda p, m, *_: (m[0], p)),
            ]
            + [whole(x) for x in pools]
            + [pl.BlockSpec(memory_space=pl.ANY)],
            out_specs=pl.BlockSpec((rows, model), lambda p, *_: (0, 0)),
            scratch_shapes=[pltpu.VMEM((PICKS * KBLK, 256), BF16)] * 3
            + [
                pltpu.VMEM((steps, rows, 4 * DV), BF16),
                pltpu.VMEM(out_weight.shape, BF16),
                pltpu.SemaphoreType.DMA,
            ],
        ),
        out_shape=jax.ShapeDtypeStruct((rows, model), BF16),
        compiler_params=pltpu.CompilerParams(vmem_limit_bytes=VMEM_LIMIT),
        cost_estimate=pl.CostEstimate(
            flops=rows * heads * (PICKS * KBLK * 1280 + 2 * DV * model),
            bytes_accessed=out_weight.size * 2 + rows * width * 2,
            transcendentals=0,
        ),
        name="chosen_and_project",
    )(meta.astype(jnp.int32), slots, dead, queries, gates, near, *pools, out_weight)


def plan_picks(my_picks, shard, per_owner, n_ctx):
    lists = my_picks.shape[0]
    first = shard * per_owner + jnp.arange(lists, dtype=jnp.int32) * (QBLK // KBLK)
    place = jnp.arange(PICKS, dtype=jnp.int32)[None, :]
    found = jnp.min(jnp.where(my_picks == first[:, None], place, PICKS), axis=1, keepdims=True)
    ordered = jnp.where(place == found, my_picks[:, :1], my_picks)
    ordered = jnp.where(place == 0, first[:, None], ordered)
    repeated = jnp.any(
        (ordered[:, :, None] == ordered[:, None, :]) & (place[0][None, :] < place[0][:, None]),
        axis=-1,
    )
    dead = repeated | (ordered > first[:, None])
    named = jnp.any(
        my_picks.reshape(-1)[None, :] == jnp.arange(n_ctx * per_owner, dtype=jnp.int32)[:, None],
        axis=1,
    ).astype(jnp.int32)
    owner_start = (ordered // per_owner) * per_owner
    block = jnp.arange(n_ctx * per_owner, dtype=jnp.int32)
    before = (block >= owner_start[..., None]) & (block < ordered[..., None])
    rank = jnp.sum(jnp.where(before, named, 0), axis=-1)
    owner = ordered // per_owner
    slot = (shard // 2 - owner // 2) * 2 * lists + lax.rem(owner, 2) * lists
    slot = slot + jnp.minimum(rank, lists - 1)
    slot = jnp.clip(slot, 0, n_ctx * lists - 1)
    return slot.reshape(-1).astype(jnp.int32), dead.reshape(-1).astype(jnp.int32)


def local(
    queries,
    key_rows,
    value_rows,
    comp_key_weight,
    comp_value_weight,
    block_picks,
    gate_logits,
    out_weight,
):
    tokens = queries.shape[0]
    heads = queries.shape[1] // QK
    n_ctx, n_head = lax.axis_size("ctx"), lax.axis_size("head")
    shard, head_at = lax.axis_index("ctx"), lax.axis_index("head")
    group = head_at * heads // (HEADS // GROUPS)
    per_owner = tokens // KBLK
    lists = tokens // QBLK
    folds = tokens // CBLK
    groups = n_ctx // 2
    rim_blocks = WINDOW // KBLK
    packed_rows = per_owner * BROWS
    params = pltpu.CompilerParams(vmem_limit_bytes=VMEM_LIMIT)
    smem = pl.BlockSpec(memory_space=pltpu.SMEM)
    vmem = pl.BlockSpec(memory_space=pltpu.VMEM)
    bf16 = lambda *shape: jax.ShapeDtypeStruct(shape, BF16)

    my_picks = lax.dynamic_index_in_dim(block_picks, group, 1, keepdims=False)
    picks = [my_picks] + [
        lax.ppermute(my_picks, "ctx", [(i, i - 2 * d) for i in range(2 * d, n_ctx)])
        for d in range(1, groups)
    ]
    packed, even, odd, val = pl.pallas_call(
        prep_kernel,
        in_specs=[smem] + [vmem] * 4,
        out_specs=[vmem] * 4,
        out_shape=[bf16(packed_rows + 3 * folds, 128)] + [bf16(tokens, 256)] * 3,
        compiler_params=params,
        name="prep",
    )(group.reshape(1), key_rows, value_rows, comp_key_weight, comp_value_weight)
    other = lax.ppermute(packed, "ctx", [(i, i ^ 1) for i in range(n_ctx)])
    rim_at = (per_owner - rim_blocks) * BROWS
    far_rim = lax.ppermute(
        packed[rim_at:packed_rows], "ctx", [(i, i + 1) for i in range(1, n_ctx - 1, 2)]
    )

    gates = jax.nn.sigmoid(gate_logits).reshape(tokens, 3 * heads)
    gates = jnp.pad(gates, ((0, 0), (0, 128 - 3 * heads)))
    reach = WINDOW // QBLK
    mixed = near_branch(reach, lists - reach, queries, gates, even, odd, val, None)

    sent_rows = 2 * lists * BROWS + 6 * folds
    sends = pl.pallas_call(
        functools.partial(pack_kernel, groups, lists, per_owner),
        in_specs=[smem] * (1 + groups) + [vmem] * 2,
        out_specs=[vmem] * groups,
        out_shape=[bf16(sent_rows, 128)] * groups,
        compiler_params=params,
        name="pack",
    )(shard.reshape(1), *picks, packed, other)
    received = [sends[0]] + [
        lax.ppermute(sends[d], "ctx", [(i, i + 2 * d) for i in range(n_ctx - 2 * d)])
        for d in range(1, groups)
    ]

    ext = pl.pallas_call(
        functools.partial(rim_kernel, rim_at),
        in_specs=[smem] + [vmem] * 5,
        out_specs=[vmem] * 3,
        out_shape=[bf16(2 * WINDOW, 256)] * 3,
        compiler_params=params,
        name="rim",
    )(shard.reshape(1), other, far_rim, even, odd, val)
    mixed = near_branch(0, reach, queries, gates, *ext, mixed)

    slots, dead = plan_picks(my_picks, shard, per_owner, n_ctx)
    pools = pl.pallas_call(
        functools.partial(pool_kernel, groups, lists),
        in_specs=[smem] + [vmem] * groups,
        out_specs=[vmem] * 6,
        out_shape=[bf16(n_ctx * lists * KBLK, 256)] * 3 + [bf16(n_ctx * folds, 256)] * 3,
        compiler_params=params,
        name="pool",
    )(shard.reshape(1), *received)
    rows = tokens // n_head
    project = lambda chunk: chosen_and_project(
        chunk, rows, shard, slots, dead, queries, gates, mixed, pools, out_weight
    )
    chips = n_head // 2
    chip, core = head_at // 2, lax.rem(head_at, 2)
    across = [(i, i ^ 1) for i in range(n_head)]
    arrived = []
    for step in range(1, chips):
        target = lax.rem(chip + step, chips) * 2
        other = lax.ppermute(project(target + 1 - core), "head", across)
        mine = project(target + core)
        summed = (mine.astype(F32) + other.astype(F32)).astype(BF16)
        route = [(i, (i + 2 * step) % n_head) for i in range(n_head)]
        arrived.append(lax.ppermute(summed, "head", route))
    arrived.append(lax.ppermute(project(chip * 2 + 1 - core), "head", across))
    total = project(head_at).astype(F32)
    for part in arrived:
        total = total + part.astype(F32)
    return total.astype(BF16)


def solution(mesh):
    placed = (
        P("ctx", "head"),
        P("ctx", None),
        P("ctx", None),
        P(),
        P(),
        P("ctx", None, None),
        P("ctx", None, "head"),
        P("head", None),
    )
    return jax.shard_map(
        local, mesh=mesh, in_specs=placed, out_specs=P(("ctx", "head"), None), check_vma=False
    )
```

```python
import functools

import jax
import jax.numpy as jnp
from jax import lax
from jax.experimental import pallas as pl
from jax.experimental.pallas import tpu as pltpu
from jax.sharding import PartitionSpec as P

HEADS = 64
GROUPS = 4
QK = 192
DV = 128
CBLK = 32
KBLK = 64
PICKS = 16
WINDOW = 512
QBLK = 256
PAIR = 2 * QK
BROWS = KBLK + KBLK // 2 + KBLK
VMEM_LIMIT = 60 * 1024 * 1024
NEG = -1e30
SCALE = QK ** (-0.5) * 1.4426950408889634
LOW_TOTAL, HIGH_TOTAL = 2.0**-60, 2.0**100
NT = (((1,), (1,)), ((), ()))
F32 = jnp.float32
BF16 = jnp.bfloat16


def half_lanes(rows):
    return lax.broadcasted_iota(jnp.int32, (rows, 128), 1) < 64


def swap_halves(x):
    return pltpu.roll(x, 64, 1)


def shift_matrix():
    return jnp.where(iota(256, 256, 1) == iota(256, 256, 0) + 64, 1.0, 0.0).astype(BF16)


def shifted_keys(even):
    return jnp.dot(even, shift_matrix(), preferred_element_type=F32).astype(BF16)


def with_ones(values):
    return jnp.concatenate([values, jnp.ones_like(values)], axis=1)


def prep_kernel(
    group_ref,
    keys_ref,
    values_ref,
    kw_ref,
    vw_ref,
    packed_ref,
    rim_ref,
    even_ref,
    odd_ref,
    val_ref,
):
    odd = lax.rem(group_ref[0], 2) == 1

    def own_columns(ref):
        t0 = ref[:, :128].astype(F32)
        t1 = ref[:, 128:256].astype(F32)
        t2 = ref[:, 256:].astype(F32)
        r1, r2 = swap_halves(t1), swap_halves(t2)
        left = half_lanes(t0.shape[0])
        low = jnp.where(odd, jnp.where(left, r1, r2), t0)
        high = jnp.where(left, jnp.where(odd, r2, t1), 0.0)
        return low, high

    low, high = own_columns(keys_ref)
    values = values_ref[...]
    rows = low.shape[0]
    count = rows // KBLK
    high3 = high.reshape(count, KBLK, 128)
    packed_high = high3[:, : KBLK // 2] + swap_halves(
        high3[:, KBLK // 2 :].reshape(count * KBLK // 2, 128)
    ).reshape(count, KBLK // 2, 128)
    even = jnp.concatenate([low.astype(BF16), high.astype(BF16)], axis=1)
    even_ref[...] = even
    odd_ref[...] = shifted_keys(even)
    val_ref[...] = with_ones(values)
    for block in range(count):
        at = block * BROWS
        token = slice(block * KBLK, block * KBLK + KBLK)
        packed_ref[at : at + KBLK] = low[token].astype(BF16)
        packed_ref[at + KBLK : at + KBLK + KBLK // 2] = packed_high[block].astype(BF16)
        packed_ref[at + KBLK + KBLK // 2 : at + BROWS] = values[token]
    rim_rows = rim_ref.shape[0]
    rim_ref[...] = packed_ref[count * BROWS - rim_rows : count * BROWS]

    wlow, whigh = own_columns(kw_ref)
    folds = rows // CBLK

    def fold(x, w):
        return jnp.sum(x.reshape(folds, CBLK, 128) * w[None], axis=1).astype(BF16)

    at = count * BROWS
    packed_ref[at : at + folds] = fold(low, wlow)
    packed_ref[at + folds : at + 2 * folds] = fold(high, whigh)
    packed_ref[at + 2 * folds :] = fold(values.astype(F32), vw_ref[...])


def pack_kernel(groups, lists, per_owner, me_ref, *refs):
    picks, (own_ref, other_ref), outs = refs[:groups], refs[groups : groups + 2], refs[groups + 2 :]
    me = me_ref[0]
    parity = lax.rem(me, 2)
    base = me - parity
    data = per_owner * BROWS
    folded = own_ref.shape[0] - data
    for distance in range(groups):
        out = outs[distance]

        @pl.when(base + 2 * distance < 2 * groups)
        def _():
            named = [jnp.int32(0), jnp.int32(0)]
            for row in range(lists):
                for col in range(PICKS):
                    entry = picks[distance][row, col]
                    for side in range(2):
                        block = entry - (base + side) * per_owner
                        here = (block >= 0) & (block < per_owner)
                        bit = jnp.int32(1) << jnp.where(here, block, 0)
                        named[side] = named[side] | jnp.where(here, bit, 0)
            for mine, ref in ((True, own_ref), (False, other_ref)):
                side = parity if mine else 1 - parity
                bits = jnp.where(side == 0, named[0], named[1])
                rank = jnp.int32(0)
                for block in range(per_owner):
                    bit = (bits >> block) & 1

                    @pl.when((bit == 1) & (rank < lists))
                    def _():
                        at = pl.multiple_of(
                            (side * lists + jnp.minimum(rank, lists - 1)) * BROWS, 16
                        )
                        out[pl.ds(at, BROWS)] = ref[block * BROWS : (block + 1) * BROWS]

                    rank = rank + bit
                at = pl.multiple_of(2 * lists * BROWS + side * folded, 16)
                out[pl.ds(at, folded)] = ref[data:]


def unpack(ref, at, count):
    lows, packed, values = [], [], []
    for block in range(count):
        first = at + block * BROWS
        lows.append(ref[first : first + KBLK])
        packed.append(ref[first + KBLK : first + KBLK + KBLK // 2])
        values.append(ref[first + KBLK + KBLK // 2 : first + BROWS])
    packed = jnp.concatenate(packed, axis=0)
    row, col = iota(128, 256, 0), iota(128, 256, 1)
    take = (row == jnp.where(col < 128, col, col - 64)) & (lax.rem(col, 128) < 64)
    both = jnp.dot(packed, take.astype(BF16), preferred_element_type=F32).astype(BF16)
    half = KBLK // 2
    highs = []
    for block in range(count):
        rows = slice(block * half, block * half + half)
        highs += [both[rows, :128], both[rows, 128:]]
    even = jnp.concatenate(
        [jnp.concatenate(lows, axis=0), jnp.concatenate(highs, axis=0)], axis=1
    )
    return even, jnp.concatenate(values, axis=0)


def rim_kernel(rim_at, shard_ref, near_ref, far_ref, even_in, odd_in, val_in, even_ref, odd_ref, val_ref):
    shard = shard_ref[0]
    rim_blocks = WINDOW // KBLK
    even_ref[WINDOW:] = even_in[:WINDOW]
    odd_ref[WINDOW:] = odd_in[:WINDOW]
    val_ref[WINDOW:] = val_in[:WINDOW]

    def fill(ref, at):
        even, values = unpack(ref, at, rim_blocks)
        even_ref[:WINDOW] = even
        odd_ref[:WINDOW] = shifted_keys(even)
        val_ref[:WINDOW] = with_ones(values)

    @pl.when(lax.rem(shard, 2) == 1)
    def _():
        fill(near_ref, rim_at)

    @pl.when((lax.rem(shard, 2) == 0) & (shard > 0))
    def _():
        fill(far_ref, 0)

    @pl.when(shard == 0)
    def _():
        even_ref[:WINDOW] = jnp.broadcast_to(even_in[:1], (WINDOW, 256))
        odd_ref[:WINDOW] = jnp.broadcast_to(odd_in[:1], (WINDOW, 256))
        val_ref[:WINDOW] = jnp.zeros((WINDOW, 256), BF16)


def pool_kernel(groups, lists, shard_ref, *refs):
    ins, (even_ref, odd_ref, val_ref, ceven_ref, codd_ref, cval_ref) = refs[:groups], refs[groups:]
    shard = shard_ref[0]
    base = shard - lax.rem(shard, 2)
    blocks = 2 * lists
    rows = blocks * KBLK
    folds = (ins[0].shape[0] - blocks * BROWS) // 6
    ceven_ref[...] = jnp.zeros_like(ceven_ref)
    codd_ref[...] = jnp.zeros_like(codd_ref)
    cval_ref[...] = jnp.zeros_like(cval_ref)
    for distance in range(groups):
        ref = ins[distance]

        @pl.when(base >= 2 * distance)
        def _():
            even, values = unpack(ref, 0, blocks)
            at = slice(distance * rows, distance * rows + rows)
            even_ref[at] = even
            odd_ref[at] = shifted_keys(even)
            val_ref[at] = with_ones(values)
            for side in range(2):
                first = blocks * BROWS + side * 3 * folds
                low = ref[first : first + folds]
                high = ref[first + folds : first + 2 * folds]
                folded = jnp.concatenate([low, high], axis=1)
                place = pl.ds(pl.multiple_of((base - 2 * distance + side) * folds, 32), folds)
                ceven_ref[place] = folded
                codd_ref[place] = shifted_keys(folded)
                cval_ref[place] = with_ones(ref[first + 2 * folds : first + 3 * folds])


def iota(rows, cols, axis):
    return lax.broadcasted_iota(jnp.int32, (rows, cols), axis)


def attend(q, keys, values, mask, exact):
    scores = mask(lax.dot_general(q, keys, NT, preferred_element_type=F32)) * SCALE
    if exact:
        scores = scores - jnp.maximum(jnp.max(scores, axis=1, keepdims=True), -1e28)
    weights = jnp.exp2(scores).astype(BF16)
    out = jnp.dot(weights, values, preferred_element_type=F32)
    return out[:, :DV], out[:, DV:]


def in_range(total):
    return jnp.where((total >= LOW_TOTAL) & (total <= HIGH_TOTAL), 1.0, 0.0)


def with_fallback(run):
    good = run(False)
    worst = functools.reduce(jnp.minimum, good)

    @pl.when(jnp.min(worst) < 0.5)
    def _():
        run(True)


def stacked(x, times):
    return jnp.concatenate([x] * times, axis=0) if times > 1 else x


def stacked_queries(q_ref, side):
    pairs = q_ref.shape[1] // PAIR
    return jnp.concatenate(
        [q_ref[:, p * PAIR + side * 128 : p * PAIR + side * 128 + 256] for p in range(pairs)],
        axis=0,
    )


def gate_columns(gate_ref, first, branch, heads, side, count):
    turned = pltpu.roll(gate_ref[...], lax.rem(128 - first, 128), 1)
    at = branch * heads + side
    rows = turned.shape[0]
    return jnp.concatenate(
        [
            jnp.broadcast_to(turned[:, at + 2 * p : at + 2 * p + 1], (rows, DV))
            for p in range(count)
        ],
        axis=0,
    )


def near_kernel(heads, q_ref, gate_ref, even_ref, odd_ref, val_ref, *refs):
    out_ref = refs[-1]
    rows = pl.ds(pl.multiple_of(pl.program_id(0) * QBLK, QBLK), WINDOW + QBLK)
    pairs = q_ref.shape[1] // PAIR
    first = pl.program_id(1) * 2 * pairs

    def mask(scores):
        row, col = iota(QBLK, QBLK, 0), iota(QBLK, QBLK, 1)
        old = jnp.where(stacked(col >= row, pairs), scores[:, :QBLK], NEG)
        new = jnp.where(stacked(col <= row, pairs), scores[:, WINDOW:], NEG)
        return jnp.concatenate([old, scores[:, QBLK:WINDOW], new], axis=1)

    def run(exact):
        good = []
        for side in range(2):
            keys = (even_ref, odd_ref)[side][rows]
            num, den = attend(stacked_queries(q_ref, side), keys, val_ref[rows], mask, exact)
            good.append(in_range(den))
            total = gate_columns(gate_ref, first, 2, heads, side, pairs) * (num / den)
            for p in range(pairs):
                at = (2 * p + side) * DV
                out_ref[:, at : at + DV] = total[p * QBLK : (p + 1) * QBLK]
        return good

    with_fallback(run)


def near_branch(first_block, block_count, queries, gates, even, odd, val, prior):
    tokens, width = queries.shape
    heads = width // QK
    steps = heads // 4
    row_block = lambda i, p: (i + first_block, p)
    whole = lambda x: pl.BlockSpec(x.shape, lambda i, p: (0,) * x.ndim)
    operands = [queries, gates, even, odd, val]
    specs = [
        pl.BlockSpec((QBLK, 2 * PAIR), row_block),
        pl.BlockSpec((QBLK, 128), lambda i, p: (i + first_block, 0)),
        whole(even),
        whole(odd),
        whole(val),
    ]
    alias = {}
    if prior is not None:
        alias = {len(operands): 0}
        operands.append(prior)
        specs.append(pl.BlockSpec(memory_space=pl.ANY))
    rows = block_count * QBLK * heads
    return pl.pallas_call(
        functools.partial(near_kernel, heads),
        grid=(block_count, steps),
        in_specs=specs,
        out_specs=pl.BlockSpec((QBLK, 4 * DV), row_block),
        out_shape=jax.ShapeDtypeStruct((tokens, heads * DV), F32),
        input_output_aliases=alias,
        compiler_params=pltpu.CompilerParams(vmem_limit_bytes=VMEM_LIMIT),
        cost_estimate=pl.CostEstimate(
            flops=rows * (WINDOW + QBLK) * 64,
            bytes_accessed=rows * (2 * QK + 4 * DV),
            transcendentals=0,
        ),
        name="near_branch",
    )(*operands)


def chosen_kernel(heads, chunks, *refs):
    meta_ref, slots_ref, dead_ref, q_ref, gate_ref, near_ref = refs[:6]
    pools, cfold, weight_ref = refs[6:9], refs[9:12], refs[12]
    outs, keys = refs[13 : 13 + chunks], refs[13 + chunks : 16 + chunks]
    attended, weight, weight_sem = refs[16 + chunks :]
    turn, step = pl.program_id(0), pl.program_id(1)
    last = pl.num_programs(1) - 1
    rows = q_ref.shape[0]
    pairs = q_ref.shape[1] // PAIR
    first = step * 2 * pairs
    chunk_start = meta_ref[1 + turn] * rows
    list_at = lax.div(chunk_start, QBLK) * PICKS
    first_row = lax.rem(chunk_start, QBLK)
    position = meta_ref[0] + chunk_start
    copy = pltpu.make_async_copy(weight_ref, weight, weight_sem)

    @pl.when(step == 0)
    def _():
        for slot in range(PICKS):
            source = pl.multiple_of(slots_ref[list_at + slot] * KBLK, KBLK)
            for pool, key in zip(pools, keys):
                key[slot * KBLK : (slot + 1) * KBLK] = pool[pl.ds(source, KBLK)]
        for slot in range(1, PICKS):

            @pl.when(dead_ref[list_at + slot] == 1)
            def _():
                at = slice(slot * KBLK, (slot + 1) * KBLK)
                for key in keys[:2]:
                    key[at] = jnp.broadcast_to(key[:1], (KBLK, 256))
                keys[2][at] = jnp.zeros((KBLK, 256), BF16)

    @pl.when((turn == 0) & (step == 0))
    def _():
        copy.start()

    def own_mask(scores):
        row, col = iota(rows, 128, 0) + first_row, iota(rows, 128, 1)
        keep = stacked((col >= KBLK) | (col <= row), pairs)
        own = jnp.where(keep, scores[:, :128], NEG)
        return jnp.concatenate([own, scores[:, 128:]], axis=1)

    def comp_mask(scores):
        cols = scores.shape[1]
        ends = (iota(rows, cols, 1) + 1) * CBLK - 1
        return jnp.where(stacked(ends <= position + iota(rows, cols, 0), pairs), scores, NEG)

    def run(exact):
        good = []
        empty = stacked(position + iota(rows, DV, 0) < CBLK - 1, pairs)
        for side in range(2):
            q = stacked_queries(q_ref, side)
            num, den = attend(q, keys[side][...], keys[2][...], own_mask, exact)
            good.append(in_range(den))
            total = gate_columns(gate_ref, first, 1, heads, side, pairs) * (num / den)
            num, den = attend(q, cfold[side][...], cfold[2][...], comp_mask, exact)
            den = jnp.where(empty, 1.0, den)
            good.append(in_range(den))
            total = total + gate_columns(gate_ref, first, 0, heads, side, pairs) * (num / den)
            for p in range(pairs):
                at = (2 * p + side) * DV
                mixed = near_ref[:, at : at + DV] + total[p * rows : (p + 1) * rows]
                attended[step, :, at : at + DV] = mixed.astype(BF16)
        return good

    with_fallback(run)

    @pl.when((turn == 0) & (step == last))
    def _():
        copy.wait()

    for place, out_ref in enumerate(outs):

        @pl.when((turn == place) & (step == last))
        def _():
            rows_in = jnp.concatenate([attended[s] for s in range(heads // 4)], axis=1)
            for at in range(0, out_ref.shape[1], 256):
                out_ref[:, at : at + 256] = jnp.dot(
                    rows_in, weight[:, at : at + 256], preferred_element_type=F32
                ).astype(out_ref.dtype)


def chosen_and_project(chunks, rows, shard, slots, dead, queries, gates, near, pools, out_weight):
    tokens, width = queries.shape
    heads = width // QK
    steps = heads // 4
    model = out_weight.shape[1]
    meta = jnp.stack([shard * tokens] + chunks)
    whole = lambda x: pl.BlockSpec(x.shape, lambda i, p, *_: (0,) * x.ndim)
    out = jax.ShapeDtypeStruct((rows, model), BF16)
    return pl.pallas_call(
        functools.partial(chosen_kernel, heads, len(chunks)),
        grid_spec=pltpu.PrefetchScalarGridSpec(
            num_scalar_prefetch=3,
            grid=(len(chunks), steps),
            in_specs=[
                pl.BlockSpec((rows, 2 * PAIR), lambda i, p, m, *_: (m[1 + i], p)),
                pl.BlockSpec((rows, 128), lambda i, p, m, *_: (m[1 + i], 0)),
                pl.BlockSpec((rows, 4 * DV), lambda i, p, m, *_: (m[1 + i], p)),
            ]
            + [whole(x) for x in pools]
            + [pl.BlockSpec(memory_space=pl.ANY)],
            out_specs=[whole(out)] * len(chunks),
            scratch_shapes=[pltpu.VMEM((PICKS * KBLK, 256), BF16)] * 3
            + [
                pltpu.VMEM((steps, rows, 4 * DV), BF16),
                pltpu.VMEM(out_weight.shape, BF16),
                pltpu.SemaphoreType.DMA,
            ],
        ),
        out_shape=[out] * len(chunks),
        compiler_params=pltpu.CompilerParams(vmem_limit_bytes=VMEM_LIMIT),
        cost_estimate=pl.CostEstimate(
            flops=rows * heads * PICKS * KBLK * 64,
            bytes_accessed=out_weight.size,
            transcendentals=0,
        ),
        name="chosen_and_project",
    )(meta.astype(jnp.int32), slots, dead, queries, gates, near, *pools, out_weight)


def plan_picks(my_picks, shard, per_owner, n_ctx):
    lists = my_picks.shape[0]
    first = shard * per_owner + jnp.arange(lists, dtype=jnp.int32) * (QBLK // KBLK)
    place = jnp.arange(PICKS, dtype=jnp.int32)[None, :]
    found = jnp.min(jnp.where(my_picks == first[:, None], place, PICKS), axis=1, keepdims=True)
    ordered = jnp.where(place == found, my_picks[:, :1], my_picks)
    ordered = jnp.where(place == 0, first[:, None], ordered)
    repeated = jnp.any(
        (ordered[:, :, None] == ordered[:, None, :]) & (place[0][None, :] < place[0][:, None]),
        axis=-1,
    )
    dead = repeated | (ordered > first[:, None])
    named = jnp.any(
        my_picks.reshape(-1)[None, :] == jnp.arange(n_ctx * per_owner, dtype=jnp.int32)[:, None],
        axis=1,
    ).astype(jnp.int32)
    owner_start = (ordered // per_owner) * per_owner
    block = jnp.arange(n_ctx * per_owner, dtype=jnp.int32)
    before = (block >= owner_start[..., None]) & (block < ordered[..., None])
    rank = jnp.sum(jnp.where(before, named, 0), axis=-1)
    owner = ordered // per_owner
    slot = (shard // 2 - owner // 2) * 2 * lists + lax.rem(owner, 2) * lists
    slot = slot + jnp.minimum(rank, lists - 1)
    slot = jnp.clip(slot, 0, n_ctx * lists - 1)
    return slot.reshape(-1).astype(jnp.int32), dead.reshape(-1).astype(jnp.int32)


def local(
    queries,
    key_rows,
    value_rows,
    comp_key_weight,
    comp_value_weight,
    block_picks,
    gate_logits,
    out_weight,
):
    tokens = queries.shape[0]
    heads = queries.shape[1] // QK
    n_ctx, n_head = lax.axis_size("ctx"), lax.axis_size("head")
    shard, head_at = lax.axis_index("ctx"), lax.axis_index("head")
    group = head_at * heads // (HEADS // GROUPS)
    per_owner = tokens // KBLK
    lists = tokens // QBLK
    folds = tokens // CBLK
    groups = n_ctx // 2
    rim_blocks = WINDOW // KBLK
    packed_rows = per_owner * BROWS
    params = pltpu.CompilerParams(vmem_limit_bytes=24 * 1024 * 1024)
    smem = pl.BlockSpec(memory_space=pltpu.SMEM)
    vmem = pl.BlockSpec(memory_space=pltpu.VMEM)
    bf16 = lambda *shape: jax.ShapeDtypeStruct(shape, BF16)

    rim_rows = rim_blocks * BROWS
    prep_out = [bf16(packed_rows + 3 * folds, 128), bf16(rim_rows, 128)] + [bf16(tokens, 256)] * 3
    packed, rim, even, odd, val = pl.pallas_call(
        prep_kernel,
        grid_spec=pltpu.PrefetchScalarGridSpec(
            num_scalar_prefetch=1,
            grid=(1,),
            in_specs=[
                pl.BlockSpec((tokens, PAIR), lambda i, g: (0, g[0] // 2)),
                pl.BlockSpec((tokens, DV), lambda i, g: (0, g[0])),
                pl.BlockSpec((CBLK, PAIR), lambda i, g: (0, g[0] // 2)),
                pl.BlockSpec((CBLK, DV), lambda i, g: (0, g[0])),
            ],
            out_specs=[pl.BlockSpec(x.shape, lambda i, g: (0, 0)) for x in prep_out],
        ),
        out_shape=prep_out,
        compiler_params=pltpu.CompilerParams(vmem_limit_bytes=VMEM_LIMIT),
        name="prep",
    )(group.reshape(1), key_rows, value_rows, comp_key_weight, comp_value_weight)
    other = lax.ppermute(packed, "ctx", [(i, i ^ 1) for i in range(n_ctx)])
    far_rim = lax.ppermute(rim, "ctx", [(i, i + 1) for i in range(1, n_ctx - 1, 2)])
    packed, block_picks = lax.optimization_barrier((packed, block_picks))
    my_picks = lax.dynamic_index_in_dim(block_picks, group, 1, keepdims=False)
    picks = [my_picks] + [
        lax.ppermute(my_picks, "ctx", [(i, i - 2 * d) for i in range(2 * d, n_ctx)])
        for d in range(1, groups)
    ]
    gates = jax.nn.sigmoid(gate_logits).reshape(tokens, 3 * heads)
    gates = jnp.pad(gates, ((0, 0), (0, 128 - 3 * heads)))
    reach = WINDOW // QBLK
    mixed = near_branch(reach, lists - reach, queries, gates, even, odd, val, None)

    sent_rows = 2 * lists * BROWS + 6 * folds
    sends = pl.pallas_call(
        functools.partial(pack_kernel, groups, lists, per_owner),
        in_specs=[smem] * (1 + groups) + [vmem] * 2,
        out_specs=[vmem] * groups,
        out_shape=[bf16(sent_rows, 128)] * groups,
        compiler_params=params,
        name="pack",
    )(shard.reshape(1), *picks, packed, other)
    received = [sends[0]] + [
        lax.ppermute(sends[d], "ctx", [(i, i + 2 * d) for i in range(n_ctx - 2 * d)])
        for d in range(1, groups)
    ]

    ext = pl.pallas_call(
        functools.partial(rim_kernel, packed_rows - rim_rows),
        in_specs=[smem] + [vmem] * 5,
        out_specs=[vmem] * 3,
        out_shape=[bf16(2 * WINDOW, 256)] * 3,
        compiler_params=params,
        name="rim",
    )(shard.reshape(1), other, far_rim, even, odd, val)
    mixed = near_branch(0, reach, queries, gates, *ext, mixed)

    slots, dead = plan_picks(my_picks, shard, per_owner, n_ctx)
    pools = pl.pallas_call(
        functools.partial(pool_kernel, groups, lists),
        in_specs=[smem] + [vmem] * groups,
        out_specs=[vmem] * 6,
        out_shape=[bf16(n_ctx * lists * KBLK, 256)] * 3 + [bf16(n_ctx * folds, 256)] * 3,
        compiler_params=params,
        name="pool",
    )(shard.reshape(1), *received)
    rows = tokens // n_head
    project = lambda *chunks: chosen_and_project(
        list(chunks), rows, shard, slots, dead, queries, gates, mixed, pools, out_weight
    )
    chips = n_head // 2
    chip, core = head_at // 2, lax.rem(head_at, 2)
    across = [(i, i ^ 1) for i in range(n_head)]
    sums = []
    for step in range(1, chips):
        target = lax.rem(chip + step, chips) * 2
        other = lax.ppermute(project(target + 1 - core)[0], "head", across)
        mine = project(target + core)[0]
        summed = (mine.astype(F32) + other.astype(F32)).astype(BF16)
        summed, chip = lax.optimization_barrier((summed, chip))
        sums.append(summed)
    passed, kept = project(chip * 2 + 1 - core, chip * 2 + core)
    arrived = [lax.ppermute(passed, "head", across)]
    for step, summed in enumerate(sums, 1):
        route = [(i, (i + 2 * step) % n_head) for i in range(n_head)]
        arrived.append(lax.ppermute(summed, "head", route))
    total = kept.astype(F32)
    for part in arrived:
        total = total + part.astype(F32)
    return total.astype(BF16)


def solution(mesh):
    placed = (
        P("ctx", "head"),
        P("ctx", None),
        P("ctx", None),
        P(),
        P(),
        P("ctx", None, None),
        P("ctx", None, "head"),
        P("head", None),
    )
    return jax.shard_map(
        local, mesh=mesh, in_specs=placed, out_specs=P(("ctx", "head"), None), check_vma=False
    )
```

```python
import functools

import jax
import jax.numpy as jnp
from jax import lax
from jax.experimental import pallas as pl
from jax.experimental.pallas import tpu as pltpu
from jax.sharding import PartitionSpec as P

HEADS = 64
GROUPS = 4
QK = 192
DV = 128
CBLK = 32
KBLK = 64
PICKS = 16
WINDOW = 512
QBLK = 256
PAIR = 2 * QK
BROWS = KBLK + KBLK // 2 + KBLK
VMEM_LIMIT = 60 * 1024 * 1024
NEG = -1e30
SCALE = QK ** (-0.5) * 1.4426950408889634
LOW_TOTAL, HIGH_TOTAL = 2.0**-60, 2.0**100
NT = (((1,), (1,)), ((), ()))
F32 = jnp.float32
BF16 = jnp.bfloat16


def half_lanes(rows):
    return lax.broadcasted_iota(jnp.int32, (rows, 128), 1) < 64


def swap_halves(x):
    return pltpu.roll(x, 64, 1)


def turned(keys):
    row, col = iota(256, 256, 0), iota(256, 256, 1)
    unit = (row == col).astype(BF16)
    even = lax.dot_general(unit, keys, NT, preferred_element_type=F32).astype(BF16)
    return even, lower(even)


def lower(even):
    return jnp.concatenate([jnp.zeros((64, even.shape[1]), BF16), even[:QK]], axis=0)


def with_ones(values):
    return jnp.concatenate([values, jnp.ones_like(values)], axis=1)


def prep_kernel(
    group_ref,
    keys_ref,
    values_ref,
    kw_ref,
    vw_ref,
    packed_ref,
    rim_ref,
    even_ref,
    odd_ref,
    val_ref,
):
    odd = lax.rem(group_ref[0], 2) == 1

    def own_columns(ref):
        t0 = ref[:, :128].astype(F32)
        t1 = ref[:, 128:256].astype(F32)
        t2 = ref[:, 256:].astype(F32)
        r1, r2 = swap_halves(t1), swap_halves(t2)
        left = half_lanes(t0.shape[0])
        low = jnp.where(odd, jnp.where(left, r1, r2), t0)
        high = jnp.where(left, jnp.where(odd, r2, t1), 0.0)
        return low, high

    low, high = own_columns(keys_ref)
    values = values_ref[...]
    rows = low.shape[0]
    count = rows // KBLK
    high3 = high.reshape(count, KBLK, 128)
    packed_high = high3[:, : KBLK // 2] + swap_halves(
        high3[:, KBLK // 2 :].reshape(count * KBLK // 2, 128)
    ).reshape(count, KBLK // 2, 128)
    even = jnp.concatenate([low.astype(BF16), high.astype(BF16)], axis=1)
    even_ref[...], odd_ref[...] = turned(even)
    val_ref[...] = with_ones(values)
    for block in range(count):
        at = block * BROWS
        token = slice(block * KBLK, block * KBLK + KBLK)
        packed_ref[at : at + KBLK] = low[token].astype(BF16)
        packed_ref[at + KBLK : at + KBLK + KBLK // 2] = packed_high[block].astype(BF16)
        packed_ref[at + KBLK + KBLK // 2 : at + BROWS] = values[token]
    rim_rows = rim_ref.shape[0]
    rim_ref[...] = packed_ref[count * BROWS - rim_rows : count * BROWS]

    wlow, whigh = own_columns(kw_ref)
    folds = rows // CBLK

    def fold(x, w):
        return jnp.sum(x.reshape(folds, CBLK, 128) * w[None], axis=1).astype(BF16)

    at = count * BROWS
    packed_ref[at : at + folds] = fold(low, wlow)
    packed_ref[at + folds : at + 2 * folds] = fold(high, whigh)
    packed_ref[at + 2 * folds :] = fold(values.astype(F32), vw_ref[...])


def pack_kernel(distances, lists, per_owner, limit, where_ref, picks_ref, ref, *outs):
    owner, base = where_ref[0], where_ref[1]
    data = per_owner * BROWS
    for distance, out in zip(distances, outs):

        @pl.when(base + 2 * distance < limit)
        def _():
            named = jnp.int32(0)
            for entry in range(lists * PICKS):
                block = picks_ref[distance * lists * PICKS + entry] - owner * per_owner
                here = (block >= 0) & (block < per_owner)
                named = named | jnp.where(here, jnp.int32(1) << jnp.where(here, block, 0), 0)
            rank = jnp.int32(0)
            for block in range(per_owner):
                bit = (named >> block) & 1

                @pl.when((bit == 1) & (rank < lists))
                def _():
                    at = pl.multiple_of(jnp.minimum(rank, lists - 1) * BROWS, BROWS)
                    out[pl.ds(at, BROWS)] = ref[block * BROWS : (block + 1) * BROWS]

                rank = rank + bit
            out[lists * BROWS :] = ref[data:]


def unpack(ref, at, count, step=1):
    lows, packed, values = [], [], []
    for block in range(count):
        first = at + block * step * BROWS
        lows.append(ref[first : first + KBLK])
        packed.append(ref[first + KBLK : first + KBLK + KBLK // 2])
        values.append(ref[first + KBLK + KBLK // 2 : first + BROWS])
    packed = jnp.concatenate(packed, axis=0)
    row, col = iota(128, 256, 0), iota(128, 256, 1)
    take = (row == jnp.where(col < 128, col, col - 64)) & (lax.rem(col, 128) < 64)
    both = jnp.dot(packed, take.astype(BF16), preferred_element_type=F32).astype(BF16)
    half = KBLK // 2
    highs = []
    for block in range(count):
        rows = slice(block * half, block * half + half)
        highs += [both[rows, :128], both[rows, 128:]]
    even = jnp.concatenate(
        [jnp.concatenate(lows, axis=0), jnp.concatenate(highs, axis=0)], axis=1
    )
    return even, jnp.concatenate(values, axis=0)


def rim_kernel(
    rim_at, shard_ref, near_ref, far_ref, even_in, odd_in, val_in, even_ref, odd_ref, val_ref
):
    shard = shard_ref[0]
    rim_blocks = WINDOW // KBLK
    even_ref[:, WINDOW:] = even_in[:, :WINDOW]
    odd_ref[:, WINDOW:] = odd_in[:, :WINDOW]
    val_ref[WINDOW:] = val_in[:WINDOW]

    def fill(ref, at):
        keys, values = unpack(ref, at, rim_blocks)
        even_ref[:, :WINDOW], odd_ref[:, :WINDOW] = turned(keys)
        val_ref[:WINDOW] = with_ones(values)

    @pl.when(lax.rem(shard, 2) == 1)
    def _():
        fill(near_ref, rim_at)

    @pl.when((lax.rem(shard, 2) == 0) & (shard > 0))
    def _():
        fill(far_ref, 0)

    @pl.when(shard == 0)
    def _():
        even = jnp.broadcast_to(even_in[:, :1].astype(F32), (256, WINDOW)).astype(BF16)
        even_ref[:, :WINDOW], odd_ref[:, :WINDOW] = even, lower(even)
        val_ref[:WINDOW] = jnp.zeros((WINDOW, 256), BF16)


def pool_kernel(groups, lists, shard_ref, own_ref, *refs):
    sent = 2 * groups - 1
    ins, (key_ref, val_ref, ceven_ref, codd_ref, cval_ref, folded) = refs[:sent], refs[sent:]
    shard = shard_ref[0]
    parity = lax.rem(shard, 2)
    base = shard - parity
    rows = lists * KBLK
    folds = (ins[0].shape[0] - lists * BROWS) // 3
    folded[...] = jnp.zeros_like(folded)
    cval_ref[...] = jnp.zeros_like(cval_ref)

    def fill(place, owner, ref, step, fold_at):
        keys, values = unpack(ref, 0, lists, step)
        at = slice(place * rows, place * rows + rows)
        key_ref[at] = keys
        val_ref[at] = with_ones(values)
        low = ref[fold_at : fold_at + folds]
        high = ref[fold_at + folds : fold_at + 2 * folds]
        owned = pl.ds(pl.multiple_of(owner * folds, 32), folds)
        folded[owned] = jnp.concatenate([low, high], axis=1)
        cval_ref[owned] = with_ones(ref[fold_at + 2 * folds : fold_at + 3 * folds])

    fill(0, shard, own_ref, QBLK // KBLK, own_ref.shape[0] - 3 * folds)
    fill(1, base + 1 - parity, ins[0], 1, lists * BROWS)
    for distance in range(1, groups):

        @pl.when(base >= 2 * distance)
        def _():
            for side in range(2):
                owner = base - 2 * distance + (parity if side == 0 else 1 - parity)
                fill(2 * distance + side, owner, ins[2 * distance - 1 + side], 1, lists * BROWS)

    ceven_ref[...], codd_ref[...] = turned(folded[...])


def iota(rows, cols, axis):
    return lax.broadcasted_iota(jnp.int32, (rows, cols), axis)


def attend(q, keys, values, mask, exact):
    scores = mask(jnp.dot(q, keys, preferred_element_type=F32)) * SCALE
    if exact:
        scores = scores - jnp.maximum(jnp.max(scores, axis=1, keepdims=True), -1e28)
    weights = jnp.exp2(scores).astype(BF16)
    out = jnp.dot(weights, values, preferred_element_type=F32)
    return out[:, :DV], out[:, DV:]


def in_range(total):
    return jnp.where((total >= LOW_TOTAL) & (total <= HIGH_TOTAL), 1.0, 0.0)


def with_fallback(run):
    good = run(False)
    worst = functools.reduce(jnp.minimum, good)

    @pl.when(jnp.min(worst) < 0.5)
    def _():
        run(True)


def stacked(x, times):
    return jnp.concatenate([x] * times, axis=0) if times > 1 else x


def stacked_queries(q_ref, side):
    pairs = q_ref.shape[1] // PAIR
    return jnp.concatenate(
        [q_ref[:, p * PAIR + side * 128 : p * PAIR + side * 128 + 256] for p in range(pairs)],
        axis=0,
    )


def gate_columns(gate_ref, first, branch, heads, side, count):
    turned = pltpu.roll(gate_ref[...], lax.rem(128 - first, 128), 1)
    at = branch * heads + side
    rows = turned.shape[0]
    return jnp.concatenate(
        [
            jnp.broadcast_to(turned[:, at + 2 * p : at + 2 * p + 1], (rows, DV))
            for p in range(count)
        ],
        axis=0,
    )


def near_kernel(heads, q_ref, gate_ref, even_ref, odd_ref, val_ref, *refs):
    out_ref = refs[-1]
    rows = pl.ds(pl.multiple_of(pl.program_id(0) * QBLK, QBLK), WINDOW + QBLK)
    pairs = q_ref.shape[1] // PAIR
    first = pl.program_id(1) * 2 * pairs

    def mask(scores):
        row, col = iota(QBLK, QBLK, 0), iota(QBLK, QBLK, 1)
        old = jnp.where(stacked(col >= row, pairs), scores[:, :QBLK], NEG)
        new = jnp.where(stacked(col <= row, pairs), scores[:, WINDOW:], NEG)
        return jnp.concatenate([old, scores[:, QBLK:WINDOW], new], axis=1)

    def run(exact):
        good = []
        for side in range(2):
            keys = (even_ref, odd_ref)[side][:, rows]
            num, den = attend(stacked_queries(q_ref, side), keys, val_ref[rows], mask, exact)
            good.append(in_range(den))
            total = gate_columns(gate_ref, first, 2, heads, side, pairs) * (num / den)
            for p in range(pairs):
                at = (2 * p + side) * DV
                out_ref[:, at : at + DV] = total[p * QBLK : (p + 1) * QBLK]
        return good

    with_fallback(run)


def near_branch(first_block, block_count, queries, gates, even, odd, val, prior):
    tokens, width = queries.shape
    heads = width // QK
    steps = heads // 4
    row_block = lambda i, p: (i + first_block, p)
    whole = lambda x: pl.BlockSpec(x.shape, lambda i, p: (0,) * x.ndim)
    operands = [queries, gates, even, odd, val]
    specs = [
        pl.BlockSpec((QBLK, 2 * PAIR), row_block),
        pl.BlockSpec((QBLK, 128), lambda i, p: (i + first_block, 0)),
        whole(even),
        whole(odd),
        whole(val),
    ]
    alias = {}
    if prior is not None:
        alias = {len(operands): 0}
        operands.append(prior)
        specs.append(pl.BlockSpec(memory_space=pl.ANY))
    rows = block_count * QBLK * heads
    return pl.pallas_call(
        functools.partial(near_kernel, heads),
        grid=(block_count, steps),
        in_specs=specs,
        out_specs=pl.BlockSpec((QBLK, 4 * DV), row_block),
        out_shape=jax.ShapeDtypeStruct((tokens, heads * DV), F32),
        input_output_aliases=alias,
        compiler_params=pltpu.CompilerParams(vmem_limit_bytes=VMEM_LIMIT),
        cost_estimate=pl.CostEstimate(
            flops=rows * (WINDOW + QBLK) * 64,
            bytes_accessed=rows * (2 * QK + 4 * DV),
            transcendentals=0,
        ),
        name="near_branch",
    )(*operands)


def chosen_kernel(heads, span, *refs):
    first_chunk, widths = span
    count = sum(len(w) for w in widths)
    meta_ref, slots_ref, dead_ref, q_ref, gate_ref, near_ref = refs[:6]
    (key_pool, val_pool), cfold, weight_ref = refs[6:8], refs[8:11], refs[11]
    outs = list(refs[12 : 12 + count])
    gathered, even, odd, val, attended, weight, weight_sem = refs[12 + count :]
    keys = (even, odd)
    turn, step = pl.program_id(0), pl.program_id(1)
    last = pl.num_programs(1) - 1
    rows = q_ref.shape[0]
    pairs = q_ref.shape[1] // PAIR
    first = step * 2 * pairs
    chunk_start = meta_ref[first_chunk + turn] * rows
    list_at = lax.div(chunk_start, QBLK) * PICKS
    first_row = lax.rem(chunk_start, QBLK)
    position = meta_ref[0] + chunk_start
    copy = pltpu.make_async_copy(weight_ref, weight, weight_sem)

    @pl.when(step == 0)
    def _():
        for slot in range(PICKS):
            source = pl.multiple_of(slots_ref[list_at + slot] * KBLK, KBLK)
            gathered[slot * KBLK : (slot + 1) * KBLK] = key_pool[pl.ds(source, KBLK)]
            val[slot * KBLK : (slot + 1) * KBLK] = val_pool[pl.ds(source, KBLK)]
        for slot in range(1, PICKS):

            @pl.when(dead_ref[list_at + slot] == 1)
            def _():
                at = slice(slot * KBLK, (slot + 1) * KBLK)
                gathered[at] = jnp.broadcast_to(gathered[:1], (KBLK, 256))
                val[at] = jnp.zeros((KBLK, 256), BF16)

        even[...], odd[...] = turned(gathered[...])

    @pl.when((turn == 0) & (step == 0))
    def _():
        copy.start()

    def own_mask(scores):
        row, col = iota(rows, 128, 0) + first_row, iota(rows, 128, 1)
        keep = stacked((col >= KBLK) | (col <= row), pairs)
        own = jnp.where(keep, scores[:, :128], NEG)
        return jnp.concatenate([own, scores[:, 128:]], axis=1)

    def comp_mask(scores):
        cols = scores.shape[1]
        ends = (iota(rows, cols, 1) + 1) * CBLK - 1
        return jnp.where(stacked(ends <= position + iota(rows, cols, 0), pairs), scores, NEG)

    def run(exact):
        good = []
        empty = stacked(position + iota(rows, DV, 0) < CBLK - 1, pairs)
        for side in range(2):
            q = stacked_queries(q_ref, side)
            num, den = attend(q, keys[side][...], val[...], own_mask, exact)
            good.append(in_range(den))
            total = gate_columns(gate_ref, first, 1, heads, side, pairs) * (num / den)
            num, den = attend(q, cfold[side][...], cfold[2][...], comp_mask, exact)
            den = jnp.where(empty, 1.0, den)
            good.append(in_range(den))
            total = total + gate_columns(gate_ref, first, 0, heads, side, pairs) * (num / den)
            for p in range(pairs):
                at = (2 * p + side) * DV
                mixed = near_ref[:, at : at + DV] + total[p * rows : (p + 1) * rows]
                attended[step, :, at : at + DV] = mixed.astype(BF16)
        return good

    with_fallback(run)

    @pl.when((turn == 0) & (step == last))
    def _():
        copy.wait()

    for place, parts in enumerate(widths):
        chunk_outs = [outs.pop(0) for _ in parts]

        @pl.when((turn == place) & (step == last))
        def _():
            rows_in = jnp.concatenate([attended[s] for s in range(heads // 4)], axis=1)
            first_col = 0
            for out_ref in chunk_outs:
                for at in range(0, out_ref.shape[1], 256):
                    cols = weight[:, first_col + at : first_col + at + 256]
                    part = jnp.dot(rows_in, cols, preferred_element_type=F32)
                    out_ref[:, at : at + 256] = part.astype(out_ref.dtype)
                first_col += out_ref.shape[1]


def chosen_and_project(first_chunk, widths, rows, meta, slots, dead, queries, gates, near, pools, out_weight):
    tokens, width = queries.shape
    heads = width // QK
    steps = heads // 4
    whole = lambda x: pl.BlockSpec(x.shape, lambda i, p, *_: (0,) * x.ndim)
    outs = [jax.ShapeDtypeStruct((rows, width), BF16) for chunk in widths for width in chunk]
    return pl.pallas_call(
        functools.partial(chosen_kernel, heads, (first_chunk, widths)),
        grid_spec=pltpu.PrefetchScalarGridSpec(
            num_scalar_prefetch=3,
            grid=(len(widths), steps),
            in_specs=[
                pl.BlockSpec((rows, 2 * PAIR), lambda i, p, m, *_: (m[first_chunk + i], p)),
                pl.BlockSpec((rows, 128), lambda i, p, m, *_: (m[first_chunk + i], 0)),
                pl.BlockSpec((rows, 4 * DV), lambda i, p, m, *_: (m[first_chunk + i], p)),
            ]
            + [whole(x) for x in pools]
            + [pl.BlockSpec(memory_space=pl.ANY)],
            out_specs=[whole(out) for out in outs],
            scratch_shapes=[
                pltpu.VMEM((PICKS * KBLK, 256), BF16),
                pltpu.VMEM((256, PICKS * KBLK), BF16),
                pltpu.VMEM((256, PICKS * KBLK), BF16),
                pltpu.VMEM((PICKS * KBLK, 256), BF16),
                pltpu.VMEM((steps, rows, 4 * DV), BF16),
                pltpu.VMEM(out_weight.shape, BF16),
                pltpu.SemaphoreType.DMA,
            ],
        ),
        out_shape=outs,
        compiler_params=pltpu.CompilerParams(vmem_limit_bytes=VMEM_LIMIT),
        cost_estimate=pl.CostEstimate(
            flops=rows * heads * PICKS * KBLK * 64,
            bytes_accessed=out_weight.size,
            transcendentals=0,
        ),
        name="chosen_and_project",
    )(meta, slots, dead, queries, gates, near, *pools, out_weight)


def plan_picks(my_picks, shard, per_owner, n_ctx):
    lists = my_picks.shape[0]
    first = shard * per_owner + jnp.arange(lists, dtype=jnp.int32) * (QBLK // KBLK)
    place = jnp.arange(PICKS, dtype=jnp.int32)[None, :]
    found = jnp.min(jnp.where(my_picks == first[:, None], place, PICKS), axis=1, keepdims=True)
    ordered = jnp.where(place == found, my_picks[:, :1], my_picks)
    ordered = jnp.where(place == 0, first[:, None], ordered)
    repeated = jnp.any(
        (ordered[:, :, None] == ordered[:, None, :]) & (place[0][None, :] < place[0][:, None]),
        axis=-1,
    )
    dead = repeated | (ordered > first[:, None])
    named = jnp.any(
        my_picks.reshape(-1)[None, :] == jnp.arange(n_ctx * per_owner, dtype=jnp.int32)[:, None],
        axis=1,
    ).astype(jnp.int32)
    owner_start = (ordered // per_owner) * per_owner
    block = jnp.arange(n_ctx * per_owner, dtype=jnp.int32)
    before = (block >= owner_start[..., None]) & (block < ordered[..., None])
    rank = jnp.sum(jnp.where(before, named, 0), axis=-1)
    owner = ordered // per_owner
    slot = (shard // 2 - owner // 2) * 2 * lists + lax.rem(owner + shard, 2) * lists
    slot = slot + jnp.minimum(rank, lists - 1)
    slot = jnp.clip(slot, 0, n_ctx * lists - 1)
    return slot.reshape(-1).astype(jnp.int32), dead.reshape(-1).astype(jnp.int32)


def single_step(kernel, name, scalars, arrays, outs, scratch=()):
    whole = lambda x: pl.BlockSpec(x.shape, lambda i, *_: (0,) * len(x.shape))
    return pl.pallas_call(
        kernel,
        grid_spec=pltpu.PrefetchScalarGridSpec(
            num_scalar_prefetch=len(scalars),
            grid=(1,),
            in_specs=[whole(x) for x in arrays],
            out_specs=[whole(x) for x in outs],
            scratch_shapes=list(scratch),
        ),
        out_shape=outs,
        compiler_params=pltpu.CompilerParams(vmem_limit_bytes=VMEM_LIMIT),
        name=name,
    )(*scalars, *arrays)


def local(
    queries,
    key_rows,
    value_rows,
    comp_key_weight,
    comp_value_weight,
    block_picks,
    gate_logits,
    out_weight,
):
    tokens = queries.shape[0]
    heads = queries.shape[1] // QK
    n_ctx, n_head = lax.axis_size("ctx"), lax.axis_size("head")
    shard, head_at = lax.axis_index("ctx"), lax.axis_index("head")
    group = head_at * heads // (HEADS // GROUPS)
    per_owner = tokens // KBLK
    lists = tokens // QBLK
    folds = tokens // CBLK
    groups = n_ctx // 2
    rim_blocks = WINDOW // KBLK
    packed_rows = per_owner * BROWS
    bf16 = lambda *shape: jax.ShapeDtypeStruct(shape, BF16)

    rim_rows = rim_blocks * BROWS
    prep_out = [bf16(packed_rows + 3 * folds, 128), bf16(rim_rows, 128)]
    prep_out += [bf16(256, tokens)] * 2 + [bf16(tokens, 256)]
    packed, rim, even, odd, val = pl.pallas_call(
        prep_kernel,
        grid_spec=pltpu.PrefetchScalarGridSpec(
            num_scalar_prefetch=1,
            grid=(1,),
            in_specs=[
                pl.BlockSpec((tokens, PAIR), lambda i, g: (0, g[0] // 2)),
                pl.BlockSpec((tokens, DV), lambda i, g: (0, g[0])),
                pl.BlockSpec((CBLK, PAIR), lambda i, g: (0, g[0] // 2)),
                pl.BlockSpec((CBLK, DV), lambda i, g: (0, g[0])),
            ],
            out_specs=[pl.BlockSpec(x.shape, lambda i, g: (0, 0)) for x in prep_out],
        ),
        out_shape=prep_out,
        compiler_params=pltpu.CompilerParams(vmem_limit_bytes=VMEM_LIMIT),
        name="prep",
    )(group.reshape(1), key_rows, value_rows, comp_key_weight, comp_value_weight)
    other = lax.ppermute(packed, "ctx", [(i, i ^ 1) for i in range(n_ctx)])
    slots, dead = plan_picks(
        lax.dynamic_index_in_dim(block_picks, group, 1, keepdims=False), shard, per_owner, n_ctx
    )
    packed, block_picks = lax.optimization_barrier((packed, block_picks))
    my_picks = lax.dynamic_index_in_dim(block_picks, group, 1, keepdims=False)
    picks = [my_picks] + [
        lax.ppermute(my_picks, "ctx", [(i, i - 2 * d) for i in range(2 * d, n_ctx)])
        for d in range(1, groups)
    ]
    far_rim = lax.ppermute(rim, "ctx", [(i, i + 1) for i in range(1, n_ctx - 1, 2)])

    gates = jax.nn.sigmoid(gate_logits).reshape(tokens, 3 * heads)
    gates = jnp.pad(gates, ((0, 0), (0, 128 - 3 * heads)))
    sent = bf16(lists * BROWS + 3 * folds, 128)
    picks = jnp.stack(picks).reshape(-1)

    def pack(owner, distances, rows):
        return single_step(
            functools.partial(pack_kernel, distances, lists, per_owner, n_ctx),
            "pack",
            [jnp.stack([owner, shard - lax.rem(shard, 2)]), picks],
            [rows],
            [sent] * len(distances),
        )

    def ahead(send, distance):
        return lax.ppermute(send, "ctx", [(i, i + 2 * distance) for i in range(n_ctx - 2 * distance)])

    own_sends = pack(shard, range(1, groups), packed)
    own_sends, even = lax.optimization_barrier((own_sends, even))
    from_same = [ahead(send, d) for d, send in enumerate(own_sends, 1)]

    reach = WINDOW // QBLK
    mixed = near_branch(reach, lists - reach, queries, gates, even, odd, val, None)

    other, mixed = lax.optimization_barrier((other, mixed))
    beside, *other_sends = pack(shard + 1 - 2 * lax.rem(shard, 2), range(groups), other)
    from_other = [ahead(send, d) for d, send in enumerate(other_sends, 1)]

    ext = single_step(
        functools.partial(rim_kernel, packed_rows - rim_rows),
        "rim",
        [shard.reshape(1)],
        [other, far_rim, even, odd, val],
        [bf16(256, 2 * WINDOW)] * 2 + [bf16(2 * WINDOW, 256)],
    )
    mixed = near_branch(0, reach, queries, gates, *ext, mixed)

    received = [beside] + [x for both in zip(from_same, from_other) for x in both]
    pools = single_step(
        functools.partial(pool_kernel, groups, lists),
        "pool",
        [shard.reshape(1)],
        [packed] + received,
        [bf16(n_ctx * lists * KBLK, 256)] * 2
        + [bf16(256, n_ctx * folds)] * 2
        + [bf16(n_ctx * folds, 256)],
        [pltpu.VMEM((n_ctx * folds, 256), BF16)],
    )
    rows = tokens // n_head
    chips = n_head // 2
    chip, core = head_at // 2, lax.rem(head_at, 2)
    order = []
    for step in list(range(1, chips)) + [0]:
        target = lax.rem(chip + step, chips) * 2
        order += [target + 1 - core, target + core]
    meta = jnp.stack([shard * tokens] + order).astype(jnp.int32)
    across = [(i, i ^ 1) for i in range(n_head)]

    model = out_weight.shape[1]

    def project(first_chunk, widths):
        return chosen_and_project(
            first_chunk, widths, rows, meta, slots, dead, queries, gates, mixed, pools, out_weight
        )

    sums = []
    for step in range(chips - 1):
        other = lax.ppermute(project(1 + 2 * step, [[model]])[0], "head", across)
        mine = project(2 + 2 * step, [[model]])[0]
        summed = (mine.astype(F32) + other.astype(F32)).astype(BF16)
        summed, meta = lax.optimization_barrier((summed, meta))
        sums.append(summed)
    *passed, kept = project(n_head - 1, [[model // 2] * 2, [model]])
    arrived = [jnp.concatenate([lax.ppermute(x, "head", across) for x in passed], axis=1)]
    for step, summed in enumerate(sums, 1):
        route = [(i, (i + 2 * step) % n_head) for i in range(n_head)]
        arrived.append(lax.ppermute(summed, "head", route))
    total = kept.astype(F32)
    for part in arrived:
        total = total + part.astype(F32)
    return total.astype(BF16)


def solution(mesh):
    placed = (
        P("ctx", "head"),
        P("ctx", None),
        P("ctx", None),
        P(),
        P(),
        P("ctx", None, None),
        P("ctx", None, "head"),
        P("head", None),
    )
    return jax.shard_map(
        local, mesh=mesh, in_specs=placed, out_specs=P(("ctx", "head"), None), check_vma=False
    )
```

```python
import functools

import jax
import jax.numpy as jnp
from jax import lax
from jax.experimental import pallas as pl
from jax.experimental.pallas import tpu as pltpu
from jax.sharding import PartitionSpec as P

HEADS = 64
GROUPS = 4
QK = 192
DV = 128
CBLK = 32
KBLK = 64
PICKS = 16
WINDOW = 512
QBLK = 256
PAIR = 2 * QK
BROWS = KBLK + KBLK // 2 + KBLK
VMEM_LIMIT = 60 * 1024 * 1024
NEG = -1e30
SCALE = QK ** (-0.5) * 1.4426950408889634
LOW_TOTAL, HIGH_TOTAL = 2.0**-60, 2.0**100
NT = (((1,), (1,)), ((), ()))
F32 = jnp.float32
BF16 = jnp.bfloat16


def half_lanes(rows):
    return lax.broadcasted_iota(jnp.int32, (rows, 128), 1) < 64


def swap_halves(x):
    return pltpu.roll(x, 64, 1)


def turned(keys):
    row, col = iota(256, 256, 0), iota(256, 256, 1)
    unit = (row == col).astype(BF16)
    even = lax.dot_general(unit, keys, NT, preferred_element_type=F32).astype(BF16)
    return even, lower(even)


def lower(even):
    return jnp.concatenate([jnp.zeros((64, even.shape[1]), BF16), even[:QK]], axis=0)


def with_ones(values):
    return jnp.concatenate([values, jnp.ones_like(values)], axis=1)


def prep_kernel(
    group_ref,
    keys_ref,
    values_ref,
    kw_ref,
    vw_ref,
    packed_ref,
    rim_ref,
    even_ref,
    odd_ref,
    val_ref,
):
    odd = lax.rem(group_ref[0], 2) == 1

    def own_columns(ref):
        t0 = ref[:, :128].astype(F32)
        t1 = ref[:, 128:256].astype(F32)
        t2 = ref[:, 256:].astype(F32)
        r1, r2 = swap_halves(t1), swap_halves(t2)
        left = half_lanes(t0.shape[0])
        low = jnp.where(odd, jnp.where(left, r1, r2), t0)
        high = jnp.where(left, jnp.where(odd, r2, t1), 0.0)
        return low, high

    low, high = own_columns(keys_ref)
    values = values_ref[...]
    rows = low.shape[0]
    count = rows // KBLK
    high3 = high.reshape(count, KBLK, 128)
    packed_high = high3[:, : KBLK // 2] + swap_halves(
        high3[:, KBLK // 2 :].reshape(count * KBLK // 2, 128)
    ).reshape(count, KBLK // 2, 128)
    even = jnp.concatenate([low.astype(BF16), high.astype(BF16)], axis=1)
    even_ref[...], odd_ref[...] = turned(even)
    val_ref[...] = with_ones(values)
    for block in range(count):
        at = block * BROWS
        token = slice(block * KBLK, block * KBLK + KBLK)
        packed_ref[at : at + KBLK] = low[token].astype(BF16)
        packed_ref[at + KBLK : at + KBLK + KBLK // 2] = packed_high[block].astype(BF16)
        packed_ref[at + KBLK + KBLK // 2 : at + BROWS] = values[token]
    rim_rows = rim_ref.shape[0]
    rim_ref[...] = packed_ref[count * BROWS - rim_rows : count * BROWS]

    wlow, whigh = own_columns(kw_ref)
    folds = rows // CBLK

    def fold(x, w):
        return jnp.sum(x.reshape(folds, CBLK, 128) * w[None], axis=1).astype(BF16)

    at = count * BROWS
    packed_ref[at : at + folds] = fold(low, wlow)
    packed_ref[at + folds : at + 2 * folds] = fold(high, whigh)
    packed_ref[at + 2 * folds :] = fold(values.astype(F32), vw_ref[...])


def plan_kernel(shape, where_ref, picks_ref, lists_ref, slots_ref, dead_ref, named, rank, seen):
    n_ctx, lists, per_owner = shape
    group, shard = where_ref[0], where_ref[1]
    for owner in range(n_ctx):
        named[owner] = 0
    for entry in range(n_ctx * lists + 1):
        lists_ref[entry] = 0

    def mark(query_block, _):
        for entry in range(PICKS):
            block = picks_ref[query_block, group, entry]
            owner = lax.div(block, per_owner)
            named[owner] = named[owner] | (jnp.int32(1) << lax.rem(block, per_owner))
        return 0

    lax.fori_loop(0, lists, mark, 0)

    def enlist(owner, _):
        bits = named[owner]
        count = jnp.int32(0)
        for block in range(per_owner):
            bit = (bits >> block) & 1
            rank[owner * per_owner + block] = jnp.minimum(count, lists - 1)
            taken = (bit == 1) & (count < lists)
            lists_ref[jnp.where(taken, owner * lists + count, n_ctx * lists)] = block
            count = count + bit
        return 0

    lax.fori_loop(0, n_ctx, enlist, 0)

    def place(block):
        owner = lax.div(block, per_owner)
        turn = (lax.div(shard, 2) - lax.div(owner, 2)) * 2 + ((owner ^ shard) & 1)
        return jnp.clip(turn * lists + rank[block], 0, n_ctx * lists - 1)

    def one_list(query_block, _):
        first = shard * per_owner + query_block * (QBLK // KBLK)
        at = query_block * PICKS
        for owner in range(n_ctx):
            seen[owner] = 0
        seen[shard] = jnp.int32(1) << lax.rem(first, per_owner)
        slots_ref[at] = place(first)
        dead_ref[at] = 0
        at = at + 1
        met = jnp.int32(0)
        for entry in range(PICKS):
            block = picks_ref[query_block, group, entry]
            owner = lax.div(block, per_owner)
            inside = lax.rem(block, per_owner)
            before = (seen[owner] >> inside) & 1
            own = jnp.where(block == first, 1, 0)
            slots_ref[at] = place(block)
            dead_ref[at] = before | jnp.where(block > first, 1, 0)
            seen[owner] = seen[owner] | (jnp.int32(1) << inside)
            at = at + 1 - (own & (1 - met))
            met = met | own
        return 0

    lax.fori_loop(0, lists, one_list, 0)


def pack_kernel(lists, beside, where_ref, *refs):
    count = (len(refs) - 2) // 2
    named, ref, outs, sems = refs[:count], refs[count], refs[count + 1 : -1], refs[-1]
    shard = where_ref[1]
    owner = shard + 1 - 2 * lax.rem(shard, 2) if beside else shard
    data = ref.shape[0] - (outs[0].shape[0] - lists * BROWS)
    copies = []
    for blocks, out in zip(named, outs):
        for place in range(lists):
            at = pl.multiple_of(blocks[owner * lists + place] * BROWS, 16)
            to = out.at[place * BROWS : (place + 1) * BROWS]
            copies.append((ref.at[pl.ds(at, BROWS)], to))
        copies.append((ref.at[data:], out.at[lists * BROWS :]))
    copies = [pltpu.make_async_copy(*pair, sems.at[i]) for i, pair in enumerate(copies)]
    for copy in copies:
        copy.start()
    for copy in copies:
        copy.wait()


def unpack(ref, at, count, step=1):
    lows, packed, values = [], [], []
    for block in range(count):
        first = at + block * step * BROWS
        lows.append(ref[first : first + KBLK])
        packed.append(ref[first + KBLK : first + KBLK + KBLK // 2])
        values.append(ref[first + KBLK + KBLK // 2 : first + BROWS])
    packed = jnp.concatenate(packed, axis=0)
    row, col = iota(128, 256, 0), iota(128, 256, 1)
    take = (row == jnp.where(col < 128, col, col - 64)) & (lax.rem(col, 128) < 64)
    both = jnp.dot(packed, take.astype(BF16), preferred_element_type=F32).astype(BF16)
    half = KBLK // 2
    highs = []
    for block in range(count):
        rows = slice(block * half, block * half + half)
        highs += [both[rows, :128], both[rows, 128:]]
    even = jnp.concatenate(
        [jnp.concatenate(lows, axis=0), jnp.concatenate(highs, axis=0)], axis=1
    )
    return even, jnp.concatenate(values, axis=0)


def fill_rim(shard, near_ref, far_ref, own, ext):
    rim_blocks = WINDOW // KBLK
    even_in, odd_in, val_in = own
    even_ref, odd_ref, val_ref = ext
    even_ref[:, WINDOW:] = even_in[:, :WINDOW]
    odd_ref[:, WINDOW:] = odd_in[:, :WINDOW]
    val_ref[WINDOW:] = val_in[:WINDOW]
    use_near = lax.rem(shard, 2) == 1

    @pl.when(shard > 0)
    def _():
        keys, values = unpack(jnp.where(use_near, near_ref[...], far_ref[...]), 0, rim_blocks)
        even_ref[:, :WINDOW], odd_ref[:, :WINDOW] = turned(keys)
        val_ref[:WINDOW] = with_ones(values)

    @pl.when(shard == 0)
    def _():
        even = jnp.broadcast_to(even_in[:, :1].astype(F32), (256, WINDOW)).astype(BF16)
        even_ref[:, :WINDOW], odd_ref[:, :WINDOW] = even, lower(even)
        val_ref[:WINDOW] = jnp.zeros((WINDOW, 256), BF16)


def pool_kernel(groups, lists, shard_ref, own_ref, *refs):
    sent = 2 * groups - 1
    ins, (key_ref, val_ref, ceven_ref, codd_ref, cval_ref, folded) = refs[:sent], refs[sent:]
    shard = shard_ref[0]
    parity = lax.rem(shard, 2)
    base = shard - parity
    rows = lists * KBLK
    folds = (ins[0].shape[0] - lists * BROWS) // 3
    folded[...] = jnp.zeros_like(folded)
    cval_ref[...] = jnp.zeros_like(cval_ref)

    def fill(place, owner, ref, step, fold_at):
        keys, values = unpack(ref, 0, lists, step)
        at = slice(place * rows, place * rows + rows)
        key_ref[at] = keys
        val_ref[at] = with_ones(values)
        low = ref[fold_at : fold_at + folds]
        high = ref[fold_at + folds : fold_at + 2 * folds]
        owned = pl.ds(pl.multiple_of(owner * folds, 32), folds)
        folded[owned] = jnp.concatenate([low, high], axis=1)
        cval_ref[owned] = with_ones(ref[fold_at + 2 * folds : fold_at + 3 * folds])

    fill(0, shard, own_ref, QBLK // KBLK, own_ref.shape[0] - 3 * folds)
    fill(1, base + 1 - parity, ins[0], 1, lists * BROWS)
    for distance in range(1, groups):

        @pl.when(base >= 2 * distance)
        def _():
            for side in range(2):
                owner = base - 2 * distance + (parity if side == 0 else 1 - parity)
                fill(2 * distance + side, owner, ins[2 * distance - 1 + side], 1, lists * BROWS)

    ceven_ref[...], codd_ref[...] = turned(folded[...])


def iota(rows, cols, axis):
    return lax.broadcasted_iota(jnp.int32, (rows, cols), axis)


def attend(q, keys, values, mask, exact):
    scores = mask(jnp.dot(q, keys, preferred_element_type=F32)) * SCALE
    if exact:
        scores = scores - jnp.maximum(jnp.max(scores, axis=1, keepdims=True), -1e28)
    weights = jnp.exp2(scores).astype(BF16)
    out = jnp.dot(weights, values, preferred_element_type=F32)
    return out[:, :DV], out[:, DV:]


def in_range(total):
    good = jnp.where((total >= LOW_TOTAL) & (total <= HIGH_TOTAL), 1.0, 0.0)
    return jnp.min(good.reshape(-1, 8, DV), axis=0)


def over_heads(run, pairs):
    at_once = 2 if pairs % 2 == 0 else 1

    def quick(turn, worst):
        return jnp.minimum(worst, run(turn * at_once, at_once, False))

    def exact(turn, _):
        run(turn, 1, True)
        return 0

    worst = lax.fori_loop(0, pairs // at_once, quick, jnp.ones((8, DV), F32))

    @pl.when(jnp.min(worst) < 0.5)
    def _():
        lax.fori_loop(0, pairs, exact, 0)


def stacked(x, times):
    return jnp.concatenate([x] * times, axis=0) if times > 1 else x


def stacked_queries(q_ref, first, pairs, side):
    at = [pl.multiple_of((first + p) * PAIR + side * 128, 128) for p in range(pairs)]
    return jnp.concatenate([q_ref[:, pl.ds(x, 256)] for x in at], axis=0)


def head_columns(first, pair, side):
    return pl.ds(pl.multiple_of((first + pair) * 2 * DV + side * DV, DV), DV)


def gate_columns(gate_ref, first, branch, heads, side, count):
    turned = pltpu.roll(gate_ref[...], lax.rem(128 - first, 128), 1)
    at = branch * heads + side
    rows = turned.shape[0]
    return jnp.concatenate(
        [
            jnp.broadcast_to(turned[:, at + 2 * p : at + 2 * p + 1], (rows, DV))
            for p in range(count)
        ],
        axis=0,
    )


def near_kernel(heads, rim, where_ref, q_ref, gate_ref, *refs):
    keys = refs[:3]
    if rim:
        out_ref, ext = refs[6], refs[7:]

        @pl.when(pl.program_id(0) == 0)
        def _():
            fill_rim(where_ref[1], refs[3], refs[4], keys, ext)

        keys = ext
    else:
        out_ref = refs[3]
    rows = pl.ds(pl.multiple_of(pl.program_id(0) * QBLK, QBLK), WINDOW + QBLK)

    def run(first, pairs, exact):
        def mask(scores):
            row, col = iota(QBLK, QBLK, 0), iota(QBLK, QBLK, 1)
            old = jnp.where(stacked(col >= row, pairs), scores[:, :QBLK], NEG)
            new = jnp.where(stacked(col <= row, pairs), scores[:, WINDOW:], NEG)
            return jnp.concatenate([old, scores[:, QBLK:WINDOW], new], axis=1)

        good = []
        for side in range(2):
            q = stacked_queries(q_ref, first, pairs, side)
            num, den = attend(q, keys[side][:, rows], keys[2][rows], mask, exact)
            good.append(in_range(den))
            total = gate_columns(gate_ref, 2 * first, 2, heads, side, pairs) * (num / den)
            for p in range(pairs):
                out_ref[:, head_columns(first, p, side)] = total[p * QBLK : (p + 1) * QBLK]
        return jnp.minimum(*good)

    over_heads(run, heads // 2)


def near_branch(first_block, block_count, where, queries, gates, keys, rims, prior):
    tokens, width = queries.shape
    heads = width // QK
    row_block = lambda i, *_: (i + first_block, 0)
    whole = lambda x: pl.BlockSpec(x.shape, lambda i, *_: (0,) * x.ndim)
    operands = [queries, gates, *keys]
    specs = [pl.BlockSpec((QBLK, width), row_block), pl.BlockSpec((QBLK, 128), row_block)]
    specs += [whole(x) for x in keys]
    alias, scratch = {}, []
    if rims is not None:
        other, far = rims
        rim_rows = far.shape[0]
        last_rim = tokens // KBLK * BROWS // rim_rows - 1
        operands += [other, far, prior]
        specs += [
            pl.BlockSpec(far.shape, lambda i, *_: (last_rim, 0)),
            whole(far),
            pl.BlockSpec(memory_space=pl.ANY),
        ]
        alias = {len(operands): 0}
        scratch = [pltpu.VMEM((256, 2 * WINDOW), BF16)] * 2 + [pltpu.VMEM((2 * WINDOW, 256), BF16)]
    rows = block_count * QBLK * heads
    return pl.pallas_call(
        functools.partial(near_kernel, heads, rims is not None),
        grid_spec=pltpu.PrefetchScalarGridSpec(
            num_scalar_prefetch=1,
            grid=(block_count,),
            in_specs=specs,
            out_specs=pl.BlockSpec((QBLK, heads * DV), row_block),
            scratch_shapes=scratch,
        ),
        out_shape=jax.ShapeDtypeStruct((tokens, heads * DV), F32),
        input_output_aliases=alias,
        compiler_params=pltpu.CompilerParams(vmem_limit_bytes=VMEM_LIMIT),
        cost_estimate=pl.CostEstimate(
            flops=rows * (WINDOW + QBLK) * 64,
            bytes_accessed=rows * (2 * QK + 4 * DV),
            transcendentals=0,
        ),
        name="near_branch",
    )(where, *operands)


def chosen_kernel(heads, span, *refs):
    first_chunk, widths = span
    count = sum(len(w) for w in widths)
    meta_ref, slots_ref, dead_ref, q_ref, gate_ref, near_ref = refs[:6]
    (key_pool, val_pool), cfold, weight_ref = refs[6:8], refs[8:11], refs[11]
    outs = list(refs[12 : 12 + count])
    gathered, even, odd, val, attended, weight, weight_sem = refs[12 + count :]
    keys = (even, odd)
    turn = pl.program_id(0)
    rows = q_ref.shape[0]
    chunk_start = meta_ref[first_chunk + turn] * rows
    list_at = lax.div(chunk_start, QBLK) * PICKS
    first_row = lax.rem(chunk_start, QBLK)
    position = meta_ref[0] + chunk_start
    copy = pltpu.make_async_copy(weight_ref, weight, weight_sem)

    @pl.when(turn == 0)
    def _():
        copy.start()

    for slot in range(PICKS):
        source = pl.multiple_of(slots_ref[list_at + slot] * KBLK, KBLK)
        gathered[slot * KBLK : (slot + 1) * KBLK] = key_pool[pl.ds(source, KBLK)]
        val[slot * KBLK : (slot + 1) * KBLK] = val_pool[pl.ds(source, KBLK)]

    def clear(slot, _):
        @pl.when(dead_ref[list_at + slot] == 1)
        def _():
            at = pl.ds(pl.multiple_of(slot * KBLK, KBLK), KBLK)
            gathered[at] = jnp.broadcast_to(gathered[:1], (KBLK, 256))
            val[at] = jnp.zeros((KBLK, 256), BF16)

        return 0

    lax.fori_loop(1, PICKS, clear, 0)
    even[...], odd[...] = turned(gathered[...])

    def run(first, pairs, exact):
        def own_mask(scores):
            row, col = iota(rows, 128, 0) + first_row, iota(rows, 128, 1)
            keep = stacked((col >= KBLK) | (col <= row), pairs)
            own = jnp.where(keep, scores[:, :128], NEG)
            return jnp.concatenate([own, scores[:, 128:]], axis=1)

        def comp_mask(scores):
            cols = scores.shape[1]
            ends = (iota(rows, cols, 1) + 1) * CBLK - 1
            keep = stacked(ends <= position + iota(rows, cols, 0), pairs)
            return jnp.where(keep, scores, NEG)

        good = []
        empty = stacked(position + iota(rows, DV, 0) < CBLK - 1, pairs)
        for side in range(2):
            q = stacked_queries(q_ref, first, pairs, side)
            num, den = attend(q, keys[side][...], val[...], own_mask, exact)
            good.append(in_range(den))
            total = gate_columns(gate_ref, 2 * first, 1, heads, side, pairs) * (num / den)
            num, den = attend(q, cfold[side][...], cfold[2][...], comp_mask, exact)
            den = jnp.where(empty, 1.0, den)
            good.append(in_range(den))
            total = total + gate_columns(gate_ref, 2 * first, 0, heads, side, pairs) * (num / den)
            for p in range(pairs):
                cols = head_columns(first, p, side)
                mixed = near_ref[:, cols] + total[p * rows : (p + 1) * rows]
                attended[:, cols] = mixed.astype(BF16)
        return functools.reduce(jnp.minimum, good)

    over_heads(run, heads // 2)

    @pl.when(turn == 0)
    def _():
        copy.wait()

    for place, parts in enumerate(widths):
        chunk_outs = [outs.pop(0) for _ in parts]

        @pl.when(turn == place)
        def _():
            first_col = 0
            for out_ref in chunk_outs:

                def columns(tile, _, out_ref=out_ref, first_col=first_col):
                    at = pl.multiple_of(tile * 256, 256)
                    cols = weight[:, pl.ds(first_col + at, 256)]
                    part = jnp.dot(attended[...], cols, preferred_element_type=F32)
                    out_ref[:, pl.ds(at, 256)] = part.astype(out_ref.dtype)
                    return 0

                lax.fori_loop(0, out_ref.shape[1] // 256, columns, 0)
                first_col += out_ref.shape[1]


def chosen_and_project(first_chunk, widths, rows, meta, slots, dead, queries, gates, near, pools, out_weight):
    tokens, width = queries.shape
    heads = width // QK
    whole = lambda x: pl.BlockSpec(x.shape, lambda i, *_: (0,) * x.ndim)
    outs = [jax.ShapeDtypeStruct((rows, width), BF16) for chunk in widths for width in chunk]
    return pl.pallas_call(
        functools.partial(chosen_kernel, heads, (first_chunk, widths)),
        grid_spec=pltpu.PrefetchScalarGridSpec(
            num_scalar_prefetch=3,
            grid=(len(widths),),
            in_specs=[
                pl.BlockSpec((rows, width), lambda i, m, *_: (m[first_chunk + i], 0)),
                pl.BlockSpec((rows, 128), lambda i, m, *_: (m[first_chunk + i], 0)),
                pl.BlockSpec((rows, heads * DV), lambda i, m, *_: (m[first_chunk + i], 0)),
            ]
            + [whole(x) for x in pools]
            + [pl.BlockSpec(memory_space=pl.ANY)],
            out_specs=[whole(out) for out in outs],
            scratch_shapes=[
                pltpu.VMEM((PICKS * KBLK, 256), BF16),
                pltpu.VMEM((256, PICKS * KBLK), BF16),
                pltpu.VMEM((256, PICKS * KBLK), BF16),
                pltpu.VMEM((PICKS * KBLK, 256), BF16),
                pltpu.VMEM((rows, heads * DV), BF16),
                pltpu.VMEM(out_weight.shape, BF16),
                pltpu.SemaphoreType.DMA,
            ],
        ),
        out_shape=outs,
        compiler_params=pltpu.CompilerParams(vmem_limit_bytes=VMEM_LIMIT),
        cost_estimate=pl.CostEstimate(
            flops=rows * heads * PICKS * KBLK * 64,
            bytes_accessed=out_weight.size,
            transcendentals=0,
        ),
        name="chosen_and_project",
    )(meta, slots, dead, queries, gates, near, *pools, out_weight)


def single_step(kernel, name, scalars, arrays, outs, scratch=()):
    whole = lambda x: pl.BlockSpec(x.shape, lambda i, *_: (0,) * len(x.shape))
    return pl.pallas_call(
        kernel,
        grid_spec=pltpu.PrefetchScalarGridSpec(
            num_scalar_prefetch=len(scalars),
            grid=(1,),
            in_specs=[whole(x) for x in arrays],
            out_specs=[whole(x) for x in outs],
            scratch_shapes=list(scratch),
        ),
        out_shape=outs,
        compiler_params=pltpu.CompilerParams(vmem_limit_bytes=VMEM_LIMIT),
        name=name,
    )(*scalars, *arrays)


def local(
    queries,
    key_rows,
    value_rows,
    comp_key_weight,
    comp_value_weight,
    block_picks,
    gate_logits,
    out_weight,
):
    tokens = queries.shape[0]
    heads = queries.shape[1] // QK
    n_ctx, n_head = lax.axis_size("ctx"), lax.axis_size("head")
    shard, head_at = lax.axis_index("ctx"), lax.axis_index("head")
    group = head_at * heads // (HEADS // GROUPS)
    per_owner = tokens // KBLK
    lists = tokens // QBLK
    folds = tokens // CBLK
    groups = n_ctx // 2
    rim_blocks = WINDOW // KBLK
    packed_rows = per_owner * BROWS
    bf16 = lambda *shape: jax.ShapeDtypeStruct(shape, BF16)

    rim_rows = rim_blocks * BROWS
    where = jnp.stack([group, shard]).astype(jnp.int32)
    prep_out = [bf16(packed_rows + 3 * folds, 128), bf16(rim_rows, 128)]
    prep_out += [bf16(256, tokens)] * 2 + [bf16(tokens, 256)]
    packed, rim, even, odd, val = pl.pallas_call(
        prep_kernel,
        grid_spec=pltpu.PrefetchScalarGridSpec(
            num_scalar_prefetch=1,
            grid=(1,),
            in_specs=[
                pl.BlockSpec((tokens, PAIR), lambda i, g: (0, g[0] // 2)),
                pl.BlockSpec((tokens, DV), lambda i, g: (0, g[0])),
                pl.BlockSpec((CBLK, PAIR), lambda i, g: (0, g[0] // 2)),
                pl.BlockSpec((CBLK, DV), lambda i, g: (0, g[0])),
            ],
            out_specs=[pl.BlockSpec(x.shape, lambda i, g: (0, 0)) for x in prep_out],
        ),
        out_shape=prep_out,
        compiler_params=pltpu.CompilerParams(vmem_limit_bytes=VMEM_LIMIT),
        name="prep",
    )(where, key_rows, value_rows, comp_key_weight, comp_value_weight)
    other = lax.ppermute(packed, "ctx", [(i, i ^ 1) for i in range(n_ctx)])
    packed, block_picks = lax.optimization_barrier((packed, block_picks))
    smem = pl.BlockSpec(memory_space=pltpu.SMEM)
    plan_out = [jax.ShapeDtypeStruct((n_ctx * lists + 1,), jnp.int32)]
    plan_out += [jax.ShapeDtypeStruct((lists * PICKS + 1,), jnp.int32)] * 2
    named, slots, dead = pl.pallas_call(
        functools.partial(plan_kernel, (n_ctx, lists, per_owner)),
        in_specs=[smem] * 2,
        out_specs=[smem] * 3,
        out_shape=plan_out,
        scratch_shapes=[
            pltpu.SMEM((n_ctx,), jnp.int32),
            pltpu.SMEM((n_ctx * per_owner,), jnp.int32),
            pltpu.SMEM((n_ctx,), jnp.int32),
        ],
        name="plan",
    )(where, block_picks)
    named = [named] + [
        lax.ppermute(named, "ctx", [(i, i - 2 * d) for i in range(2 * d, n_ctx)])
        for d in range(1, groups)
    ]
    far_rim = lax.ppermute(rim, "ctx", [(i, i + 1) for i in range(1, n_ctx - 1, 2)])

    gates = jax.nn.sigmoid(gate_logits).reshape(tokens, 3 * heads)
    gates = jnp.pad(gates, ((0, 0), (0, 128 - 3 * heads)))
    sent = bf16(lists * BROWS + 3 * folds, 128)

    def pack(beside, lists_in, rows):
        any_space = pl.BlockSpec(memory_space=pl.ANY)
        return pl.pallas_call(
            functools.partial(pack_kernel, lists, beside),
            grid_spec=pltpu.PrefetchScalarGridSpec(
                num_scalar_prefetch=1 + len(lists_in),
                grid=(1,),
                in_specs=[any_space],
                out_specs=[any_space] * len(lists_in),
                scratch_shapes=[pltpu.SemaphoreType.DMA((len(lists_in) * (lists + 1),))],
            ),
            out_shape=[sent] * len(lists_in),
            compiler_params=pltpu.CompilerParams(vmem_limit_bytes=VMEM_LIMIT),
            name="pack",
        )(where, *lists_in, rows)

    def ahead(send, distance):
        return lax.ppermute(send, "ctx", [(i, i + 2 * distance) for i in range(n_ctx - 2 * distance)])

    own_sends = pack(False, named[1:], packed)
    own_sends, even = lax.optimization_barrier((own_sends, even))
    from_same = [ahead(send, d) for d, send in enumerate(own_sends, 1)]

    reach = WINDOW // QBLK
    near = functools.partial(near_branch, where=where, queries=queries, gates=gates)
    mixed = near(reach, lists - reach, keys=(even, odd, val), rims=None, prior=None)

    other, mixed = lax.optimization_barrier((other, mixed))
    beside, *other_sends = pack(True, named, other)
    from_other = [ahead(send, d) for d, send in enumerate(other_sends, 1)]

    mixed = near(0, reach, keys=(even, odd, val), rims=(other, far_rim), prior=mixed)

    received = [beside] + [x for both in zip(from_same, from_other) for x in both]
    pools = single_step(
        functools.partial(pool_kernel, groups, lists),
        "pool",
        [shard.reshape(1)],
        [packed] + received,
        [bf16(n_ctx * lists * KBLK, 256)] * 2
        + [bf16(256, n_ctx * folds)] * 2
        + [bf16(n_ctx * folds, 256)],
        [pltpu.VMEM((n_ctx * folds, 256), BF16)],
    )
    rows = tokens // n_head
    chips = n_head // 2
    chip, core = head_at // 2, lax.rem(head_at, 2)
    order = []
    for step in list(range(1, chips)) + [0]:
        target = lax.rem(chip + step, chips) * 2
        order += [target + 1 - core, target + core]
    meta = jnp.stack([shard * tokens] + order).astype(jnp.int32)
    across = [(i, i ^ 1) for i in range(n_head)]

    model = out_weight.shape[1]

    def project(first_chunk, widths):
        return chosen_and_project(
            first_chunk, widths, rows, meta, slots, dead, queries, gates, mixed, pools, out_weight
        )

    sums = []
    for step in range(chips - 1):
        other = lax.ppermute(project(1 + 2 * step, [[model]])[0], "head", across)
        mine = project(2 + 2 * step, [[model]])[0]
        summed = (mine.astype(F32) + other.astype(F32)).astype(BF16)
        summed, meta = lax.optimization_barrier((summed, meta))
        sums.append(summed)
    *passed, kept = project(n_head - 1, [[model // 2] * 2, [model]])
    arrived = [jnp.concatenate([lax.ppermute(x, "head", across) for x in passed], axis=1)]
    for step, summed in enumerate(sums, 1):
        route = [(i, (i + 2 * step) % n_head) for i in range(n_head)]
        arrived.append(lax.ppermute(summed, "head", route))
    total = kept.astype(F32)
    for part in arrived:
        total = total + part.astype(F32)
    return total.astype(BF16)


def solution(mesh):
    placed = (
        P("ctx", "head"),
        P("ctx", None),
        P("ctx", None),
        P(),
        P(),
        P("ctx", None, None),
        P("ctx", None, "head"),
        P("head", None),
    )
    return jax.shard_map(
        local, mesh=mesh, in_specs=placed, out_specs=P(("ctx", "head"), None), check_vma=False
    )
```

```python
import functools

import jax
import jax.numpy as jnp
from jax import lax
from jax.experimental import pallas as pl
from jax.experimental.pallas import tpu as pltpu
from jax.sharding import PartitionSpec as P

HEADS = 64
GROUPS = 4
QK = 192
DV = 128
CBLK = 32
KBLK = 64
PICKS = 16
WINDOW = 512
QBLK = 256
PAIR = 2 * QK
BROWS = KBLK + KBLK // 2 + KBLK
VMEM_LIMIT = 60 * 1024 * 1024
NEG = -1e30
SCALE = QK ** (-0.5) * 1.4426950408889634
TOP = 3.0
NT = (((1,), (1,)), ((), ()))
F32 = jnp.float32
BF16 = jnp.bfloat16


def half_lanes(rows):
    return lax.broadcasted_iota(jnp.int32, (rows, 128), 1) < 64


def swap_halves(x):
    return pltpu.roll(x, 64, 1)


def turned(keys):
    row, col = iota(256, 256, 0), iota(256, 256, 1)
    unit = (row == col).astype(BF16)
    even = lax.dot_general(unit, keys, NT, preferred_element_type=F32).astype(BF16)
    return even, lower(even)


def lower(even):
    return jnp.concatenate([jnp.zeros((64, even.shape[1]), BF16), even[:QK]], axis=0)


def with_ones(values):
    return jnp.concatenate([values, jnp.ones_like(values)], axis=1)


def prep_kernel(
    group_ref,
    keys_ref,
    values_ref,
    kw_ref,
    vw_ref,
    packed_ref,
    rim_ref,
    even_ref,
    odd_ref,
    val_ref,
):
    odd = lax.rem(group_ref[0], 2) == 1

    def own_columns(ref):
        t0 = ref[:, :128].astype(F32)
        t1 = ref[:, 128:256].astype(F32)
        t2 = ref[:, 256:].astype(F32)
        r1, r2 = swap_halves(t1), swap_halves(t2)
        left = half_lanes(t0.shape[0])
        low = jnp.where(odd, jnp.where(left, r1, r2), t0)
        high = jnp.where(left, jnp.where(odd, r2, t1), 0.0)
        return low, high

    low, high = own_columns(keys_ref)
    values = values_ref[...]
    rows = low.shape[0]
    count = rows // KBLK
    high3 = high.reshape(count, KBLK, 128)
    packed_high = high3[:, : KBLK // 2] + swap_halves(
        high3[:, KBLK // 2 :].reshape(count * KBLK // 2, 128)
    ).reshape(count, KBLK // 2, 128)
    even = jnp.concatenate([low.astype(BF16), high.astype(BF16)], axis=1)
    even_ref[...], odd_ref[...] = turned(even)
    val_ref[...] = with_ones(values)
    for block in range(count):
        at = block * BROWS
        token = slice(block * KBLK, block * KBLK + KBLK)
        packed_ref[at : at + KBLK] = low[token].astype(BF16)
        packed_ref[at + KBLK : at + KBLK + KBLK // 2] = packed_high[block].astype(BF16)
        packed_ref[at + KBLK + KBLK // 2 : at + BROWS] = values[token]
    rim_rows = rim_ref.shape[0]
    rim_ref[...] = packed_ref[count * BROWS - rim_rows : count * BROWS]

    wlow, whigh = own_columns(kw_ref)
    folds = rows // CBLK

    def fold(x, w):
        return jnp.sum(x.reshape(folds, CBLK, 128) * w[None], axis=1).astype(BF16)

    at = count * BROWS
    packed_ref[at : at + folds] = fold(low, wlow)
    packed_ref[at + folds : at + 2 * folds] = fold(high, whigh)
    packed_ref[at + 2 * folds :] = fold(values.astype(F32), vw_ref[...])


def plan_kernel(shape, where_ref, picks_ref, lists_ref, slots_ref, dead_ref, named, rank, seen):
    n_ctx, lists, per_owner = shape
    group, shard = where_ref[0], where_ref[1]
    for owner in range(n_ctx):
        named[owner] = 0
    for entry in range(n_ctx * lists + 1):
        lists_ref[entry] = 0

    def mark(query_block, _):
        for entry in range(PICKS):
            block = picks_ref[query_block, group, entry]
            owner = lax.div(block, per_owner)
            named[owner] = named[owner] | (jnp.int32(1) << lax.rem(block, per_owner))
        return 0

    lax.fori_loop(0, lists, mark, 0)

    def enlist(owner, _):
        bits = named[owner]
        count = jnp.int32(0)
        for block in range(per_owner):
            bit = (bits >> block) & 1
            rank[owner * per_owner + block] = jnp.minimum(count, lists - 1)
            taken = (bit == 1) & (count < lists)
            lists_ref[jnp.where(taken, owner * lists + count, n_ctx * lists)] = block
            count = count + bit
        return 0

    lax.fori_loop(0, n_ctx, enlist, 0)

    def place(block):
        owner = lax.div(block, per_owner)
        turn = (lax.div(shard, 2) - lax.div(owner, 2)) * 2 + ((owner ^ shard) & 1)
        return jnp.clip(turn * lists + rank[block], 0, n_ctx * lists - 1)

    def one_list(query_block, _):
        first = shard * per_owner + query_block * (QBLK // KBLK)
        at = query_block * PICKS
        for owner in range(n_ctx):
            seen[owner] = 0
        seen[shard] = jnp.int32(1) << lax.rem(first, per_owner)
        slots_ref[at] = place(first)
        dead_ref[at] = 0
        at = at + 1
        met = jnp.int32(0)
        for entry in range(PICKS):
            block = picks_ref[query_block, group, entry]
            owner = lax.div(block, per_owner)
            inside = lax.rem(block, per_owner)
            before = (seen[owner] >> inside) & 1
            own = jnp.where(block == first, 1, 0)
            slots_ref[at] = place(block)
            dead_ref[at] = before | jnp.where(block > first, 1, 0)
            seen[owner] = seen[owner] | (jnp.int32(1) << inside)
            at = at + 1 - (own & (1 - met))
            met = met | own
        return 0

    lax.fori_loop(0, lists, one_list, 0)


def pack_kernel(lists, beside, where_ref, *refs):
    count = len(refs) // 2
    named, ref, outs = refs[:count], refs[count], refs[count + 1 :]
    shard = where_ref[1]
    owner = shard + 1 - 2 * lax.rem(shard, 2) if beside else shard
    data = ref.shape[0] - (outs[0].shape[0] - lists * BROWS)
    for blocks, out in zip(named, outs):
        for place in range(lists):
            at = pl.multiple_of(blocks[owner * lists + place] * BROWS, 16)
            out[place * BROWS : (place + 1) * BROWS] = ref[pl.ds(at, BROWS)]
        out[lists * BROWS :] = ref[data:]


def unpack(ref, at, count, step=1):
    lows, packed, values = [], [], []
    for block in range(count):
        first = at + block * step * BROWS
        lows.append(ref[first : first + KBLK])
        packed.append(ref[first + KBLK : first + KBLK + KBLK // 2])
        values.append(ref[first + KBLK + KBLK // 2 : first + BROWS])
    packed = jnp.concatenate(packed, axis=0)
    row, col = iota(128, 256, 0), iota(128, 256, 1)
    take = (row == jnp.where(col < 128, col, col - 64)) & (lax.rem(col, 128) < 64)
    both = jnp.dot(packed, take.astype(BF16), preferred_element_type=F32).astype(BF16)
    half = KBLK // 2
    highs = []
    for block in range(count):
        rows = slice(block * half, block * half + half)
        highs += [both[rows, :128], both[rows, 128:]]
    even = jnp.concatenate(
        [jnp.concatenate(lows, axis=0), jnp.concatenate(highs, axis=0)], axis=1
    )
    return even, jnp.concatenate(values, axis=0)


def fill_rim(shard, near_ref, far_ref, own, ext):
    rim_blocks = WINDOW // KBLK
    even_in, odd_in, val_in = own
    even_ref, odd_ref, val_ref = ext
    even_ref[:, WINDOW:] = even_in[:, :WINDOW]
    odd_ref[:, WINDOW:] = odd_in[:, :WINDOW]
    val_ref[WINDOW:] = val_in[:WINDOW]
    use_near = lax.rem(shard, 2) == 1

    @pl.when(shard > 0)
    def _():
        keys, values = unpack(jnp.where(use_near, near_ref[...], far_ref[...]), 0, rim_blocks)
        even_ref[:, :WINDOW], odd_ref[:, :WINDOW] = turned(keys)
        val_ref[:WINDOW] = with_ones(values)

    @pl.when(shard == 0)
    def _():
        even = jnp.broadcast_to(even_in[:, :1].astype(F32), (256, WINDOW)).astype(BF16)
        even_ref[:, :WINDOW], odd_ref[:, :WINDOW] = even, lower(even)
        val_ref[:WINDOW] = jnp.zeros((WINDOW, 256), BF16)


def pool_kernel(groups, lists, shard_ref, own_ref, *refs):
    sent = 2 * groups - 1
    ins, (key_ref, val_ref, ceven_ref, codd_ref, cval_ref, folded) = refs[:sent], refs[sent:]
    shard = shard_ref[0]
    parity = lax.rem(shard, 2)
    base = shard - parity
    rows = lists * KBLK
    folds = (ins[0].shape[0] - lists * BROWS) // 3
    folded[...] = jnp.zeros_like(folded)
    cval_ref[...] = jnp.zeros_like(cval_ref)

    def fill(place, owner, ref, step, fold_at):
        keys, values = unpack(ref, 0, lists, step)
        at = slice(place * rows, place * rows + rows)
        key_ref[at] = keys
        val_ref[at] = with_ones(values)
        low = ref[fold_at : fold_at + folds]
        high = ref[fold_at + folds : fold_at + 2 * folds]
        owned = pl.ds(pl.multiple_of(owner * folds, 32), folds)
        folded[owned] = jnp.concatenate([low, high], axis=1)
        cval_ref[owned] = with_ones(ref[fold_at + 2 * folds : fold_at + 3 * folds])

    fill(0, shard, own_ref, QBLK // KBLK, own_ref.shape[0] - 3 * folds)
    fill(1, base + 1 - parity, ins[0], 1, lists * BROWS)
    for distance in range(1, groups):

        @pl.when(base >= 2 * distance)
        def _():
            for side in range(2):
                owner = base - 2 * distance + (parity if side == 0 else 1 - parity)
                fill(2 * distance + side, owner, ins[2 * distance - 1 + side], 1, lists * BROWS)

    ceven_ref[...], codd_ref[...] = turned(folded[...])


def iota(rows, cols, axis):
    return lax.broadcasted_iota(jnp.int32, (rows, cols), axis)


def attend(q, keys, values, mask):
    scores = mask(jnp.dot(q, keys, preferred_element_type=F32))
    top = jnp.maximum(jnp.max(scores, axis=1, keepdims=True), -1e28) * SCALE - TOP
    weights = jnp.exp2((scores * SCALE - top).astype(BF16))
    out = jnp.dot(weights, values, preferred_element_type=F32)
    return out[:, :DV], out[:, DV:]


def stacked(x, times):
    return jnp.concatenate([x] * times, axis=0) if times > 1 else x


def stacked_queries(q_ref, side):
    pairs = q_ref.shape[1] // PAIR
    return jnp.concatenate(
        [q_ref[:, p * PAIR + side * 128 : p * PAIR + side * 128 + 256] for p in range(pairs)],
        axis=0,
    )


def gate_columns(gate_ref, first, branch, heads, side, count):
    turned = pltpu.roll(gate_ref[...], lax.rem(128 - first, 128), 1)
    at = branch * heads + side
    rows = turned.shape[0]
    return jnp.concatenate(
        [
            jnp.broadcast_to(turned[:, at + 2 * p : at + 2 * p + 1], (rows, DV))
            for p in range(count)
        ],
        axis=0,
    )


def near_kernel(heads, rim, where_ref, q_ref, gate_ref, *refs):
    keys = refs[:3]
    if rim:
        out_ref, ext = refs[6], refs[7:]

        @pl.when((pl.program_id(0) == 0) & (pl.program_id(1) == 0))
        def _():
            fill_rim(where_ref[1], refs[3], refs[4], keys, ext)

        keys = ext
    else:
        out_ref = refs[3]
    rows = pl.ds(pl.multiple_of(pl.program_id(0) * QBLK, QBLK), WINDOW + QBLK)

    pairs = q_ref.shape[1] // PAIR
    first = pl.program_id(1) * 2 * pairs

    def mask(scores):
        row, col = iota(QBLK, QBLK, 0), iota(QBLK, QBLK, 1)
        old = jnp.where(stacked(col >= row, pairs), scores[:, :QBLK], NEG)
        new = jnp.where(stacked(col <= row, pairs), scores[:, WINDOW:], NEG)
        return jnp.concatenate([old, scores[:, QBLK:WINDOW], new], axis=1)

    for side in range(2):
        num, den = attend(stacked_queries(q_ref, side), keys[side][:, rows], keys[2][rows], mask)
        total = gate_columns(gate_ref, first, 2, heads, side, pairs) * (num / den)
        for p in range(pairs):
            at = (2 * p + side) * DV
            out_ref[:, at : at + DV] = total[p * QBLK : (p + 1) * QBLK]


def near_branch(first_block, block_count, where, queries, gates, keys, rims, prior):
    tokens, width = queries.shape
    heads = width // QK
    row_block = lambda i, p, *_: (i + first_block, p)
    whole = lambda x: pl.BlockSpec(x.shape, lambda i, p, *_: (0,) * x.ndim)
    operands = [queries, gates, *keys]
    specs = [
        pl.BlockSpec((QBLK, 2 * PAIR), row_block),
        pl.BlockSpec((QBLK, 128), lambda i, p, *_: (i + first_block, 0)),
    ]
    specs += [whole(x) for x in keys]
    alias, scratch = {}, []
    if rims is not None:
        other, far = rims
        rim_rows = far.shape[0]
        last_rim = tokens // KBLK * BROWS // rim_rows - 1
        operands += [other, far, prior]
        specs += [
            pl.BlockSpec(far.shape, lambda i, p, *_: (last_rim, 0)),
            whole(far),
            pl.BlockSpec(memory_space=pl.ANY),
        ]
        alias = {len(operands): 0}
        scratch = [pltpu.VMEM((256, 2 * WINDOW), BF16)] * 2 + [pltpu.VMEM((2 * WINDOW, 256), BF16)]
    rows = block_count * QBLK * heads
    return pl.pallas_call(
        functools.partial(near_kernel, heads, rims is not None),
        grid_spec=pltpu.PrefetchScalarGridSpec(
            num_scalar_prefetch=1,
            grid=(block_count, heads // 4),
            in_specs=specs,
            out_specs=pl.BlockSpec((QBLK, 4 * DV), row_block),
            scratch_shapes=scratch,
        ),
        out_shape=jax.ShapeDtypeStruct((tokens, heads * DV), F32),
        input_output_aliases=alias,
        compiler_params=pltpu.CompilerParams(vmem_limit_bytes=VMEM_LIMIT),
        cost_estimate=pl.CostEstimate(
            flops=rows * (WINDOW + QBLK) * 64,
            bytes_accessed=rows * (2 * QK + 4 * DV),
            transcendentals=0,
        ),
        name="near_branch",
    )(where, *operands)


def chosen_kernel(heads, span, *refs):
    first_chunk, widths = span
    count = sum(len(w) for w in widths)
    meta_ref, slots_ref, dead_ref, q_ref, gate_ref, near_ref = refs[:6]
    (key_pool, val_pool), cfold, weight_ref = refs[6:8], refs[8:11], refs[11]
    outs = list(refs[12 : 12 + count])
    gathered, even, odd, val, attended, weight, weight_sem = refs[12 + count :]
    keys = (even, odd)
    turn, step = pl.program_id(0), pl.program_id(1)
    last = pl.num_programs(1) - 1
    rows = q_ref.shape[0]
    pairs = q_ref.shape[1] // PAIR
    first = step * 2 * pairs
    chunk_start = meta_ref[first_chunk + turn] * rows
    list_at = lax.div(chunk_start, QBLK) * PICKS
    first_row = lax.rem(chunk_start, QBLK)
    position = meta_ref[0] + chunk_start
    copy = pltpu.make_async_copy(weight_ref, weight, weight_sem)

    @pl.when(step == 0)
    def _():
        for slot in range(PICKS):
            source = pl.multiple_of(slots_ref[list_at + slot] * KBLK, KBLK)
            gathered[slot * KBLK : (slot + 1) * KBLK] = key_pool[pl.ds(source, KBLK)]
            val[slot * KBLK : (slot + 1) * KBLK] = val_pool[pl.ds(source, KBLK)]
        for slot in range(1, PICKS):

            @pl.when(dead_ref[list_at + slot] == 1)
            def _():
                at = slice(slot * KBLK, (slot + 1) * KBLK)
                gathered[at] = jnp.broadcast_to(gathered[:1], (KBLK, 256))
                val[at] = jnp.zeros((KBLK, 256), BF16)

        even[...], odd[...] = turned(gathered[...])

    @pl.when((turn == 0) & (step == 0))
    def _():
        copy.start()

    def own_mask(scores):
        row, col = iota(rows, 128, 0) + first_row, iota(rows, 128, 1)
        keep = stacked((col >= KBLK) | (col <= row), pairs)
        own = jnp.where(keep, scores[:, :128], NEG)
        return jnp.concatenate([own, scores[:, 128:]], axis=1)

    def comp_mask(scores):
        cols = scores.shape[1]
        ends = (iota(rows, cols, 1) + 1) * CBLK - 1
        return jnp.where(stacked(ends <= position + iota(rows, cols, 0), pairs), scores, NEG)

    empty = stacked(position + iota(rows, DV, 0) < CBLK - 1, pairs)
    for side in range(2):
        q = stacked_queries(q_ref, side)
        num, den = attend(q, keys[side][...], val[...], own_mask)
        total = gate_columns(gate_ref, first, 1, heads, side, pairs) * (num / den)
        num, den = attend(q, cfold[side][...], cfold[2][...], comp_mask)
        den = jnp.where(empty, 1.0, den)
        total = total + gate_columns(gate_ref, first, 0, heads, side, pairs) * (num / den)
        for p in range(pairs):
            at = (2 * p + side) * DV
            mixed = near_ref[:, at : at + DV] + total[p * rows : (p + 1) * rows]
            attended[step, :, at : at + DV] = mixed.astype(BF16)

    @pl.when((turn == 0) & (step == last))
    def _():
        copy.wait()

    for place, parts in enumerate(widths):
        chunk_outs = [outs.pop(0) for _ in parts]

        @pl.when((turn == place) & (step == last))
        def _():
            rows_in = jnp.concatenate([attended[s] for s in range(heads // 4)], axis=1)
            first_col = 0
            for out_ref in chunk_outs:
                for at in range(0, out_ref.shape[1], 256):
                    cols = weight[:, first_col + at : first_col + at + 256]
                    part = jnp.dot(rows_in, cols, preferred_element_type=F32)
                    out_ref[:, at : at + 256] = part.astype(out_ref.dtype)
                first_col += out_ref.shape[1]


def chosen_and_project(first_chunk, widths, rows, meta, slots, dead, queries, gates, near, pools, out_weight):
    tokens, width = queries.shape
    heads = width // QK
    steps = heads // 4
    whole = lambda x: pl.BlockSpec(x.shape, lambda i, p, *_: (0,) * x.ndim)
    outs = [jax.ShapeDtypeStruct((rows, width), BF16) for chunk in widths for width in chunk]
    return pl.pallas_call(
        functools.partial(chosen_kernel, heads, (first_chunk, widths)),
        grid_spec=pltpu.PrefetchScalarGridSpec(
            num_scalar_prefetch=3,
            grid=(len(widths), steps),
            in_specs=[
                pl.BlockSpec((rows, 2 * PAIR), lambda i, p, m, *_: (m[first_chunk + i], p)),
                pl.BlockSpec((rows, 128), lambda i, p, m, *_: (m[first_chunk + i], 0)),
                pl.BlockSpec((rows, 4 * DV), lambda i, p, m, *_: (m[first_chunk + i], p)),
            ]
            + [whole(x) for x in pools]
            + [pl.BlockSpec(memory_space=pl.ANY)],
            out_specs=[whole(out) for out in outs],
            scratch_shapes=[
                pltpu.VMEM((PICKS * KBLK, 256), BF16),
                pltpu.VMEM((256, PICKS * KBLK), BF16),
                pltpu.VMEM((256, PICKS * KBLK), BF16),
                pltpu.VMEM((PICKS * KBLK, 256), BF16),
                pltpu.VMEM((steps, rows, 4 * DV), BF16),
                pltpu.VMEM(out_weight.shape, BF16),
                pltpu.SemaphoreType.DMA,
            ],
        ),
        out_shape=outs,
        compiler_params=pltpu.CompilerParams(vmem_limit_bytes=VMEM_LIMIT),
        cost_estimate=pl.CostEstimate(
            flops=rows * heads * PICKS * KBLK * 64,
            bytes_accessed=out_weight.size,
            transcendentals=0,
        ),
        name="chosen_and_project",
    )(meta, slots, dead, queries, gates, near, *pools, out_weight)


def single_step(kernel, name, scalars, arrays, outs, scratch=()):
    whole = lambda x: pl.BlockSpec(x.shape, lambda i, *_: (0,) * len(x.shape))
    return pl.pallas_call(
        kernel,
        grid_spec=pltpu.PrefetchScalarGridSpec(
            num_scalar_prefetch=len(scalars),
            grid=(1,),
            in_specs=[whole(x) for x in arrays],
            out_specs=[whole(x) for x in outs],
            scratch_shapes=list(scratch),
        ),
        out_shape=outs,
        compiler_params=pltpu.CompilerParams(vmem_limit_bytes=VMEM_LIMIT),
        name=name,
    )(*scalars, *arrays)


def local(
    queries,
    key_rows,
    value_rows,
    comp_key_weight,
    comp_value_weight,
    block_picks,
    gate_logits,
    out_weight,
):
    tokens = queries.shape[0]
    heads = queries.shape[1] // QK
    n_ctx, n_head = lax.axis_size("ctx"), lax.axis_size("head")
    shard, head_at = lax.axis_index("ctx"), lax.axis_index("head")
    group = head_at * heads // (HEADS // GROUPS)
    per_owner = tokens // KBLK
    lists = tokens // QBLK
    folds = tokens // CBLK
    groups = n_ctx // 2
    rim_blocks = WINDOW // KBLK
    packed_rows = per_owner * BROWS
    bf16 = lambda *shape: jax.ShapeDtypeStruct(shape, BF16)

    rim_rows = rim_blocks * BROWS
    where = jnp.stack([group, shard]).astype(jnp.int32)
    prep_out = [bf16(packed_rows + 3 * folds, 128), bf16(rim_rows, 128)]
    prep_out += [bf16(256, tokens)] * 2 + [bf16(tokens, 256)]
    packed, rim, even, odd, val = pl.pallas_call(
        prep_kernel,
        grid_spec=pltpu.PrefetchScalarGridSpec(
            num_scalar_prefetch=1,
            grid=(1,),
            in_specs=[
                pl.BlockSpec((tokens, PAIR), lambda i, g: (0, g[0] // 2)),
                pl.BlockSpec((tokens, DV), lambda i, g: (0, g[0])),
                pl.BlockSpec((CBLK, PAIR), lambda i, g: (0, g[0] // 2)),
                pl.BlockSpec((CBLK, DV), lambda i, g: (0, g[0])),
            ],
            out_specs=[pl.BlockSpec(x.shape, lambda i, g: (0, 0)) for x in prep_out],
        ),
        out_shape=prep_out,
        compiler_params=pltpu.CompilerParams(vmem_limit_bytes=VMEM_LIMIT),
        name="prep",
    )(where, key_rows, value_rows, comp_key_weight, comp_value_weight)
    other = lax.ppermute(packed, "ctx", [(i, i ^ 1) for i in range(n_ctx)])
    packed, block_picks = lax.optimization_barrier((packed, block_picks))
    smem = pl.BlockSpec(memory_space=pltpu.SMEM)
    plan_out = [jax.ShapeDtypeStruct((n_ctx * lists + 1,), jnp.int32)]
    plan_out += [jax.ShapeDtypeStruct((lists * PICKS + 1,), jnp.int32)] * 2
    named, slots, dead = pl.pallas_call(
        functools.partial(plan_kernel, (n_ctx, lists, per_owner)),
        in_specs=[smem] * 2,
        out_specs=[smem] * 3,
        out_shape=plan_out,
        scratch_shapes=[
            pltpu.SMEM((n_ctx,), jnp.int32),
            pltpu.SMEM((n_ctx * per_owner,), jnp.int32),
            pltpu.SMEM((n_ctx,), jnp.int32),
        ],
        name="plan",
    )(where, block_picks)
    named = [named] + [
        lax.ppermute(named, "ctx", [(i, i - 2 * d) for i in range(2 * d, n_ctx)])
        for d in range(1, groups)
    ]
    far_rim = lax.ppermute(rim, "ctx", [(i, i + 1) for i in range(1, n_ctx - 1, 2)])

    gates = jax.nn.sigmoid(gate_logits).reshape(tokens, 3 * heads)
    gates = jnp.pad(gates, ((0, 0), (0, 128 - 3 * heads)))
    sent = bf16(lists * BROWS + 3 * folds, 128)

    def pack(beside, lists_in, rows):
        return single_step(
            functools.partial(pack_kernel, lists, beside),
            "pack",
            [where, *lists_in],
            [rows],
            [sent] * len(lists_in),
        )

    def ahead(send, distance):
        return lax.ppermute(send, "ctx", [(i, i + 2 * distance) for i in range(n_ctx - 2 * distance)])

    own_sends = pack(False, named[1:], packed)
    own_sends, even = lax.optimization_barrier((own_sends, even))
    from_same = [ahead(send, d) for d, send in enumerate(own_sends, 1)]

    reach = WINDOW // QBLK
    near = functools.partial(near_branch, where=where, queries=queries, gates=gates)
    mixed = near(reach, lists - reach, keys=(even, odd, val), rims=None, prior=None)

    other, mixed = lax.optimization_barrier((other, mixed))
    beside, *other_sends = pack(True, named, other)
    from_other = [ahead(send, d) for d, send in enumerate(other_sends, 1)]

    mixed = near(0, reach, keys=(even, odd, val), rims=(other, far_rim), prior=mixed)

    received = [beside] + [x for both in zip(from_same, from_other) for x in both]
    pools = single_step(
        functools.partial(pool_kernel, groups, lists),
        "pool",
        [shard.reshape(1)],
        [packed] + received,
        [bf16(n_ctx * lists * KBLK, 256)] * 2
        + [bf16(256, n_ctx * folds)] * 2
        + [bf16(n_ctx * folds, 256)],
        [pltpu.VMEM((n_ctx * folds, 256), BF16)],
    )
    rows = tokens // n_head
    chips = n_head // 2
    chip, core = head_at // 2, lax.rem(head_at, 2)
    order = []
    for step in list(range(1, chips)) + [0]:
        target = lax.rem(chip + step, chips) * 2
        order += [target + 1 - core, target + core]
    meta = jnp.stack([shard * tokens] + order).astype(jnp.int32)
    across = [(i, i ^ 1) for i in range(n_head)]

    model = out_weight.shape[1]

    def project(first_chunk, widths):
        return chosen_and_project(
            first_chunk, widths, rows, meta, slots, dead, queries, gates, mixed, pools, out_weight
        )

    sums = []
    for step in range(chips - 1):
        other = lax.ppermute(project(1 + 2 * step, [[model]])[0], "head", across)
        mine = project(2 + 2 * step, [[model]])[0]
        summed = (mine.astype(F32) + other.astype(F32)).astype(BF16)
        summed, meta = lax.optimization_barrier((summed, meta))
        sums.append(summed)
    *passed, kept = project(n_head - 1, [[model // 2] * 2, [model]])
    arrived = [jnp.concatenate([lax.ppermute(x, "head", across) for x in passed], axis=1)]
    for step, summed in enumerate(sums, 1):
        route = [(i, (i + 2 * step) % n_head) for i in range(n_head)]
        arrived.append(lax.ppermute(summed, "head", route))
    total = kept.astype(F32)
    for part in arrived:
        total = total + part.astype(F32)
    return total.astype(BF16)


def solution(mesh):
    placed = (
        P("ctx", "head"),
        P("ctx", None),
        P("ctx", None),
        P(),
        P(),
        P("ctx", None, None),
        P("ctx", None, "head"),
        P("head", None),
    )
    return jax.shard_map(
        local, mesh=mesh, in_specs=placed, out_specs=P(("ctx", "head"), None), check_vma=False
    )
```

```python
import functools

import jax
import jax.numpy as jnp
from jax import lax
from jax.experimental import pallas as pl
from jax.experimental.pallas import tpu as pltpu
from jax.sharding import PartitionSpec as P

HEADS = 64
GROUPS = 4
QK = 192
DV = 128
CBLK = 32
KBLK = 64
PICKS = 16
WINDOW = 512
QBLK = 256
PAIR = 2 * QK
BROWS = KBLK + KBLK // 2 + KBLK
VMEM_LIMIT = 60 * 1024 * 1024
NEG = -1e30
SCALE = QK ** (-0.5) * 1.4426950408889634
LOW_TOTAL, HIGH_TOTAL = 2.0**-60, 2.0**100
TILE = 256
NT = (((1,), (1,)), ((), ()))
F32 = jnp.float32
BF16 = jnp.bfloat16


def half_lanes(rows):
    return lax.broadcasted_iota(jnp.int32, (rows, 128), 1) < 64


def swap_halves(x):
    return pltpu.roll(x, 64, 1)


def turned(keys):
    row, col = iota(256, 256, 0), iota(256, 256, 1)
    unit = (row == col).astype(BF16)
    even = lax.dot_general(unit, keys, NT, preferred_element_type=F32).astype(BF16)
    return even, lower(even)


def lower(even):
    return jnp.concatenate([jnp.zeros((64, even.shape[1]), BF16), even[:QK]], axis=0)


def with_ones(values):
    return jnp.concatenate([values, jnp.ones_like(values)], axis=1)


def prep_kernel(
    group_ref,
    keys_ref,
    values_ref,
    kw_ref,
    vw_ref,
    packed_ref,
    rim_ref,
    even_ref,
    odd_ref,
    val_ref,
):
    odd = lax.rem(group_ref[0], 2) == 1

    def own_columns(ref):
        t0 = ref[:, :128].astype(F32)
        t1 = ref[:, 128:256].astype(F32)
        t2 = ref[:, 256:].astype(F32)
        r1, r2 = swap_halves(t1), swap_halves(t2)
        left = half_lanes(t0.shape[0])
        low = jnp.where(odd, jnp.where(left, r1, r2), t0)
        high = jnp.where(left, jnp.where(odd, r2, t1), 0.0)
        return low, high

    low, high = own_columns(keys_ref)
    values = values_ref[...]
    rows = low.shape[0]
    count = rows // KBLK
    high3 = high.reshape(count, KBLK, 128)
    packed_high = high3[:, : KBLK // 2] + swap_halves(
        high3[:, KBLK // 2 :].reshape(count * KBLK // 2, 128)
    ).reshape(count, KBLK // 2, 128)
    even = jnp.concatenate([low.astype(BF16), high.astype(BF16)], axis=1)
    even_ref[...], odd_ref[...] = turned(even)
    val_ref[...] = with_ones(values)
    for block in range(count):
        at = block * BROWS
        token = slice(block * KBLK, block * KBLK + KBLK)
        packed_ref[at : at + KBLK] = low[token].astype(BF16)
        packed_ref[at + KBLK : at + KBLK + KBLK // 2] = packed_high[block].astype(BF16)
        packed_ref[at + KBLK + KBLK // 2 : at + BROWS] = values[token]
    rim_rows = rim_ref.shape[0]
    rim_ref[...] = packed_ref[count * BROWS - rim_rows : count * BROWS]

    wlow, whigh = own_columns(kw_ref)
    folds = rows // CBLK

    def fold(x, w):
        return jnp.sum(x.reshape(folds, CBLK, 128) * w[None], axis=1).astype(BF16)

    at = count * BROWS
    packed_ref[at : at + folds] = fold(low, wlow)
    packed_ref[at + folds : at + 2 * folds] = fold(high, whigh)
    packed_ref[at + 2 * folds :] = fold(values.astype(F32), vw_ref[...])


def plan_kernel(shape, where_ref, picks_ref, lists_ref, slots_ref, dead_ref, named, rank, seen):
    n_ctx, lists, per_owner = shape
    group, shard = where_ref[0], where_ref[1]
    for owner in range(n_ctx):
        named[owner] = 0
    for entry in range(n_ctx * lists + 1):
        lists_ref[entry] = 0

    def mark(query_block, _):
        for entry in range(PICKS):
            block = picks_ref[query_block, group, entry]
            owner = lax.div(block, per_owner)
            named[owner] = named[owner] | (jnp.int32(1) << lax.rem(block, per_owner))
        return 0

    lax.fori_loop(0, lists, mark, 0)

    def enlist(owner, _):
        bits = named[owner]
        count = jnp.int32(0)
        for block in range(per_owner):
            bit = (bits >> block) & 1
            rank[owner * per_owner + block] = jnp.minimum(count, lists - 1)
            taken = (bit == 1) & (count < lists)
            lists_ref[jnp.where(taken, owner * lists + count, n_ctx * lists)] = block
            count = count + bit
        return 0

    lax.fori_loop(0, n_ctx, enlist, 0)

    def place(block):
        owner = lax.div(block, per_owner)
        turn = (lax.div(shard, 2) - lax.div(owner, 2)) * 2 + ((owner ^ shard) & 1)
        return jnp.clip(turn * lists + rank[block], 0, n_ctx * lists - 1)

    def one_list(query_block, _):
        first = shard * per_owner + query_block * (QBLK // KBLK)
        at = query_block * PICKS
        for owner in range(n_ctx):
            seen[owner] = 0
        seen[shard] = jnp.int32(1) << lax.rem(first, per_owner)
        slots_ref[at] = place(first)
        dead_ref[at] = 0
        at = at + 1
        met = jnp.int32(0)
        for entry in range(PICKS):
            block = picks_ref[query_block, group, entry]
            owner = lax.div(block, per_owner)
            inside = lax.rem(block, per_owner)
            before = (seen[owner] >> inside) & 1
            own = jnp.where(block == first, 1, 0)
            slots_ref[at] = place(block)
            dead_ref[at] = before | jnp.where(block > first, 1, 0)
            seen[owner] = seen[owner] | (jnp.int32(1) << inside)
            at = at + 1 - (own & (1 - met))
            met = met | own
        return 0

    lax.fori_loop(0, lists, one_list, 0)


def pack_kernel(lists, beside, where_ref, *refs):
    count = len(refs) // 2
    named, ref, outs = refs[:count], refs[count], refs[count + 1 :]
    shard = where_ref[1]
    owner = shard + 1 - 2 * lax.rem(shard, 2) if beside else shard
    data = ref.shape[0] - (outs[0].shape[0] - lists * BROWS)
    for blocks, out in zip(named, outs):
        for place in range(lists):
            at = pl.multiple_of(blocks[owner * lists + place] * BROWS, 16)
            out[place * BROWS : (place + 1) * BROWS] = ref[pl.ds(at, BROWS)]
        out[lists * BROWS :] = ref[data:]


def unpack(ref, at, count, step=1):
    lows, packed, values = [], [], []
    for block in range(count):
        first = at + block * step * BROWS
        lows.append(ref[first : first + KBLK])
        packed.append(ref[first + KBLK : first + KBLK + KBLK // 2])
        values.append(ref[first + KBLK + KBLK // 2 : first + BROWS])
    packed = jnp.concatenate(packed, axis=0)
    row, col = iota(128, 256, 0), iota(128, 256, 1)
    take = (row == jnp.where(col < 128, col, col - 64)) & (lax.rem(col, 128) < 64)
    both = jnp.dot(packed, take.astype(BF16), preferred_element_type=F32).astype(BF16)
    half = KBLK // 2
    highs = []
    for block in range(count):
        rows = slice(block * half, block * half + half)
        highs += [both[rows, :128], both[rows, 128:]]
    even = jnp.concatenate(
        [jnp.concatenate(lows, axis=0), jnp.concatenate(highs, axis=0)], axis=1
    )
    return even, jnp.concatenate(values, axis=0)


def fill_rim(shard, near_ref, far_ref, own, ext):
    rim_blocks = WINDOW // KBLK
    even_in, odd_in, val_in = own
    even_ref, odd_ref, val_ref = ext
    even_ref[:, WINDOW:] = even_in[:, :WINDOW]
    odd_ref[:, WINDOW:] = odd_in[:, :WINDOW]
    val_ref[WINDOW:] = val_in[:WINDOW]
    use_near = lax.rem(shard, 2) == 1

    @pl.when(shard > 0)
    def _():
        keys, values = unpack(jnp.where(use_near, near_ref[...], far_ref[...]), 0, rim_blocks)
        even_ref[:, :WINDOW], odd_ref[:, :WINDOW] = turned(keys)
        val_ref[:WINDOW] = with_ones(values)

    @pl.when(shard == 0)
    def _():
        even = jnp.broadcast_to(even_in[:, :1].astype(F32), (256, WINDOW)).astype(BF16)
        even_ref[:, :WINDOW], odd_ref[:, :WINDOW] = even, lower(even)
        val_ref[:WINDOW] = jnp.zeros((WINDOW, 256), BF16)


def pool_kernel(groups, lists, shard_ref, own_ref, *refs):
    sent = 2 * groups - 1
    ins, (key_ref, val_ref, ceven_ref, codd_ref, cval_ref, folded) = refs[:sent], refs[sent:]
    shard = shard_ref[0]
    parity = lax.rem(shard, 2)
    base = shard - parity
    rows = lists * KBLK
    folds = (ins[0].shape[0] - lists * BROWS) // 3
    folded[...] = jnp.zeros_like(folded)
    cval_ref[...] = jnp.zeros_like(cval_ref)

    def fill(place, owner, ref, step, fold_at):
        keys, values = unpack(ref, 0, lists, step)
        at = slice(place * rows, place * rows + rows)
        key_ref[at] = keys
        val_ref[at] = with_ones(values)
        low = ref[fold_at : fold_at + folds]
        high = ref[fold_at + folds : fold_at + 2 * folds]
        owned = pl.ds(pl.multiple_of(owner * folds, 32), folds)
        folded[owned] = jnp.concatenate([low, high], axis=1)
        cval_ref[owned] = with_ones(ref[fold_at + 2 * folds : fold_at + 3 * folds])

    fill(0, shard, own_ref, QBLK // KBLK, own_ref.shape[0] - 3 * folds)
    fill(1, base + 1 - parity, ins[0], 1, lists * BROWS)
    for distance in range(1, groups):

        @pl.when(base >= 2 * distance)
        def _():
            for side in range(2):
                owner = base - 2 * distance + (parity if side == 0 else 1 - parity)
                fill(2 * distance + side, owner, ins[2 * distance - 1 + side], 1, lists * BROWS)

    ceven_ref[...], codd_ref[...] = turned(folded[...])


def iota(rows, cols, axis):
    return lax.broadcasted_iota(jnp.int32, (rows, cols), axis)


def scores_of(q, keys, mask):
    scores = jnp.dot(q, keys, preferred_element_type=F32)
    return scores if mask is None else mask(scores)


def in_range(total):
    good = jnp.where((total >= LOW_TOTAL) & (total <= HIGH_TOTAL), 1.0, 0.0)
    return jnp.min(good.reshape(-1, 8, DV), axis=0)


def over_heads(count, load, branches, finish):
    def sums(weights, values):
        out = jnp.dot(weights, values(), preferred_element_type=F32)
        return out[:, :DV], out[:, DV:]

    worst, held = [], None
    for head in range(count + 1):
        side = head % 2
        q = load(head // 2, side) if head < count else None
        fresh, parts = [], []
        for at, (tiles, values) in enumerate(branches):
            weights, ahead = [], []
            for place, (keys, mask) in enumerate(tiles):
                if q is not None:
                    ahead.append(scores_of(q, keys(side), mask))
                if held is not None:
                    weights.append(jnp.exp2(held[at][place] * SCALE).astype(BF16))
            fresh.append(ahead)
            if held is not None:
                parts.append((weights, values))
        if held is not None:
            parts = [sums(jnp.concatenate(w, axis=1), values) for w, values in parts]
            worst += [in_range(x) for x in finish((head - 1) // 2, (head - 1) % 2, parts)]
        held = fresh if q is not None else None

    @pl.when(jnp.min(functools.reduce(jnp.minimum, worst)) < 0.5)
    def _():
        def exact(pair, _):
            for side in range(2):
                q = load(pair, side)
                parts = []
                for tiles, values in branches:
                    scores = [scores_of(q, keys(side), mask) for keys, mask in tiles]
                    scores = jnp.concatenate(scores, axis=1)
                    top = jnp.max(scores, axis=1, keepdims=True)
                    shifted = (scores - jnp.maximum(top, -1e28)) * SCALE
                    parts.append(sums(jnp.exp2(shifted).astype(BF16), values))
                finish(pair, side, parts)
            return 0

        lax.fori_loop(0, count // 2, exact, 0)


def query_loader(q_ref):
    def load(pair, side):
        at = pair * PAIR + side * 128
        return q_ref[:, pl.ds(at if isinstance(at, int) else pl.multiple_of(at, 128), 256)]

    return load


def head_columns(pair, side):
    at = pair * 2 * DV + side * DV
    return pl.ds(at if isinstance(at, int) else pl.multiple_of(at, DV), DV)


def gate_loader(gate_ref, first, heads):
    turned = pltpu.roll(gate_ref[...], lax.rem(128 - first, 128), 1)

    def load(pair, side, branch):
        at = branch * heads + side
        if isinstance(pair, int):
            column = turned[:, at + 2 * pair : at + 2 * pair + 1]
        else:
            column = pltpu.roll(turned, lax.rem(128 - 2 * pair, 128), 1)[:, at : at + 1]
        return jnp.broadcast_to(column, (turned.shape[0], DV))

    return load


def near_kernel(heads, rim, where_ref, q_ref, gate_ref, *refs):
    keys = refs[:3]
    if rim:
        out_ref, ext = refs[6], refs[7:]

        @pl.when((pl.program_id(0) == 0) & (pl.program_id(1) == 0))
        def _():
            fill_rim(where_ref[1], refs[3], refs[4], keys, ext)

        keys = ext
    else:
        out_ref = refs[3]
    count = q_ref.shape[1] // QK
    gate = gate_loader(gate_ref, pl.program_id(1) * count, heads)
    base = pl.multiple_of(pl.program_id(0) * QBLK, QBLK)
    row, col = iota(QBLK, QBLK, 0), iota(QBLK, QBLK, 1)

    def tile(place, mask):
        return (lambda side: keys[side][:, pl.ds(base + place * QBLK, QBLK)]), mask

    def finish(pair, side, parts):
        ((num, den),) = parts
        out_ref[:, head_columns(pair, side)] = gate(pair, side, 2) * (num / den)
        return [den]

    tiles = [
        tile(0, lambda scores: jnp.where(col >= row, scores, NEG)),
        tile(1, None),
        tile(2, lambda scores: jnp.where(col <= row, scores, NEG)),
    ]
    values = lambda: keys[2][pl.ds(base, WINDOW + QBLK)]
    over_heads(count, query_loader(q_ref), [(tiles, values)], finish)


def near_branch(first_block, block_count, where, queries, gates, keys, rims, prior):
    tokens, width = queries.shape
    heads = width // QK
    at_once = 8 if heads % 8 == 0 else 2
    row_block = lambda i, p, *_: (i + first_block, p)
    whole = lambda x: pl.BlockSpec(x.shape, lambda i, p, *_: (0,) * x.ndim)
    operands = [queries, gates, *keys]
    specs = [
        pl.BlockSpec((QBLK, at_once * QK), row_block),
        pl.BlockSpec((QBLK, 128), lambda i, p, *_: (i + first_block, 0)),
    ]
    specs += [whole(x) for x in keys]
    alias, scratch = {}, []
    if rims is not None:
        other, far = rims
        rim_rows = far.shape[0]
        last_rim = tokens // KBLK * BROWS // rim_rows - 1
        operands += [other, far, prior]
        specs += [
            pl.BlockSpec(far.shape, lambda i, p, *_: (last_rim, 0)),
            whole(far),
            pl.BlockSpec(memory_space=pl.ANY),
        ]
        alias = {len(operands): 0}
        scratch = [pltpu.VMEM((256, 2 * WINDOW), BF16)] * 2 + [pltpu.VMEM((2 * WINDOW, 256), BF16)]
    rows = block_count * QBLK * heads
    return pl.pallas_call(
        functools.partial(near_kernel, heads, rims is not None),
        grid_spec=pltpu.PrefetchScalarGridSpec(
            num_scalar_prefetch=1,
            grid=(block_count, heads // at_once),
            in_specs=specs,
            out_specs=pl.BlockSpec((QBLK, at_once * DV), row_block),
            scratch_shapes=scratch,
        ),
        out_shape=jax.ShapeDtypeStruct((tokens, heads * DV), F32),
        input_output_aliases=alias,
        compiler_params=pltpu.CompilerParams(vmem_limit_bytes=VMEM_LIMIT),
        cost_estimate=pl.CostEstimate(
            flops=rows * (WINDOW + QBLK) * 64,
            bytes_accessed=rows * (2 * QK + 4 * DV),
            transcendentals=0,
        ),
        name="near_branch",
    )(where, *operands)


def chosen_kernel(heads, span, *refs):
    first_chunk, widths = span
    out_count = sum(len(w) for w in widths)
    meta_ref, slots_ref, dead_ref, q_ref, gate_ref, near_ref = refs[:6]
    (key_pool, val_pool), cfold, weight_ref = refs[6:8], refs[8:11], refs[11]
    outs = list(refs[12 : 12 + out_count])
    gathered, even, odd, val, attended, weight, weight_sem = refs[12 + out_count :]
    keys = (even, odd)
    turn, step = pl.program_id(0), pl.program_id(1)
    last = pl.num_programs(1) - 1
    rows = q_ref.shape[0]
    count = q_ref.shape[1] // QK
    chunk_start = meta_ref[first_chunk + turn] * rows
    list_at = lax.div(chunk_start, QBLK) * PICKS
    first_row = lax.rem(chunk_start, QBLK)
    position = meta_ref[0] + chunk_start
    copy = pltpu.make_async_copy(weight_ref, weight, weight_sem)

    @pl.when(step == 0)
    def _():
        for slot in range(PICKS):
            source = pl.multiple_of(slots_ref[list_at + slot] * KBLK, KBLK)
            gathered[slot * KBLK : (slot + 1) * KBLK] = key_pool[pl.ds(source, KBLK)]
            val[slot * KBLK : (slot + 1) * KBLK] = val_pool[pl.ds(source, KBLK)]
        for slot in range(1, PICKS):

            @pl.when(dead_ref[list_at + slot] == 1)
            def _():
                at = slice(slot * KBLK, (slot + 1) * KBLK)
                gathered[at] = jnp.broadcast_to(gathered[:1], (KBLK, 256))
                val[at] = jnp.zeros((KBLK, 256), BF16)

        even[...], odd[...] = turned(gathered[...])

    @pl.when((turn == 0) & (step == 0))
    def _():
        copy.start()

    gate = gate_loader(gate_ref, step * count, heads)
    row = iota(rows, TILE, 0)
    col = iota(rows, TILE, 1)
    own_keep = (col >= KBLK) | (col <= row + first_row)

    def own_mask(scores):
        own = jnp.where(own_keep[:, :128], scores[:, :128], NEG)
        return jnp.concatenate([own, scores[:, 128:]], axis=1)

    def comp_mask(place):
        ends = (col + place * TILE + 1) * CBLK - 1
        return lambda scores: jnp.where(ends <= row + position, scores, NEG)

    def tile(refs, place, mask):
        return (lambda side: refs[side][:, place * TILE : (place + 1) * TILE]), mask

    chosen = [tile(keys, p, own_mask if p == 0 else None) for p in range(PICKS * KBLK // TILE)]
    folded = [tile(cfold, p, comp_mask(p)) for p in range(cfold[2].shape[0] // TILE)]
    empty = row[:, :DV] + position < CBLK - 1

    def finish(pair, side, parts):
        (num, den), (folded_num, folded_den) = parts
        folded_den = jnp.where(empty, 1.0, folded_den)
        cols = head_columns(pair, side)
        mixed = near_ref[:, cols] + gate(pair, side, 1) * (num / den)
        mixed = mixed + gate(pair, side, 0) * (folded_num / folded_den)
        attended[step, :, cols] = mixed.astype(BF16)
        return [den, folded_den]

    branches = [(chosen, lambda: val[...]), (folded, lambda: cfold[2][...])]
    over_heads(count, query_loader(q_ref), branches, finish)

    @pl.when((turn == 0) & (step == last))
    def _():
        copy.wait()

    for place, parts in enumerate(widths):
        chunk_outs = [outs.pop(0) for _ in parts]

        @pl.when((turn == place) & (step == last))
        def _():
            rows_in = jnp.concatenate([attended[s] for s in range(attended.shape[0])], axis=1)
            first_col = 0
            for out_ref in chunk_outs:
                for at in range(0, out_ref.shape[1], 256):
                    cols = weight[:, first_col + at : first_col + at + 256]
                    part = jnp.dot(rows_in, cols, preferred_element_type=F32)
                    out_ref[:, at : at + 256] = part.astype(out_ref.dtype)
                first_col += out_ref.shape[1]


def chosen_and_project(first_chunk, widths, rows, meta, slots, dead, queries, gates, near, pools, out_weight):
    tokens, width = queries.shape
    heads = width // QK
    at_once = 8 if heads % 8 == 0 else 2
    steps = heads // at_once
    whole = lambda x: pl.BlockSpec(x.shape, lambda i, p, *_: (0,) * x.ndim)
    outs = [jax.ShapeDtypeStruct((rows, width), BF16) for chunk in widths for width in chunk]
    return pl.pallas_call(
        functools.partial(chosen_kernel, heads, (first_chunk, widths)),
        grid_spec=pltpu.PrefetchScalarGridSpec(
            num_scalar_prefetch=3,
            grid=(len(widths), steps),
            in_specs=[
                pl.BlockSpec((rows, at_once * QK), lambda i, p, m, *_: (m[first_chunk + i], p)),
                pl.BlockSpec((rows, 128), lambda i, p, m, *_: (m[first_chunk + i], 0)),
                pl.BlockSpec((rows, at_once * DV), lambda i, p, m, *_: (m[first_chunk + i], p)),
            ]
            + [whole(x) for x in pools]
            + [pl.BlockSpec(memory_space=pl.ANY)],
            out_specs=[whole(out) for out in outs],
            scratch_shapes=[
                pltpu.VMEM((PICKS * KBLK, 256), BF16),
                pltpu.VMEM((256, PICKS * KBLK), BF16),
                pltpu.VMEM((256, PICKS * KBLK), BF16),
                pltpu.VMEM((PICKS * KBLK, 256), BF16),
                pltpu.VMEM((steps, rows, at_once * DV), BF16),
                pltpu.VMEM(out_weight.shape, BF16),
                pltpu.SemaphoreType.DMA,
            ],
        ),
        out_shape=outs,
        compiler_params=pltpu.CompilerParams(vmem_limit_bytes=VMEM_LIMIT),
        cost_estimate=pl.CostEstimate(
            flops=rows * heads * PICKS * KBLK * 64,
            bytes_accessed=out_weight.size,
            transcendentals=0,
        ),
        name="chosen_and_project",
    )(meta, slots, dead, queries, gates, near, *pools, out_weight)


def single_step(kernel, name, scalars, arrays, outs, scratch=()):
    whole = lambda x: pl.BlockSpec(x.shape, lambda i, *_: (0,) * len(x.shape))
    return pl.pallas_call(
        kernel,
        grid_spec=pltpu.PrefetchScalarGridSpec(
            num_scalar_prefetch=len(scalars),
            grid=(1,),
            in_specs=[whole(x) for x in arrays],
            out_specs=[whole(x) for x in outs],
            scratch_shapes=list(scratch),
        ),
        out_shape=outs,
        compiler_params=pltpu.CompilerParams(vmem_limit_bytes=VMEM_LIMIT),
        name=name,
    )(*scalars, *arrays)


def local(
    queries,
    key_rows,
    value_rows,
    comp_key_weight,
    comp_value_weight,
    block_picks,
    gate_logits,
    out_weight,
):
    tokens = queries.shape[0]
    heads = queries.shape[1] // QK
    n_ctx, n_head = lax.axis_size("ctx"), lax.axis_size("head")
    shard, head_at = lax.axis_index("ctx"), lax.axis_index("head")
    group = head_at * heads // (HEADS // GROUPS)
    per_owner = tokens // KBLK
    lists = tokens // QBLK
    folds = tokens // CBLK
    groups = n_ctx // 2
    rim_blocks = WINDOW // KBLK
    packed_rows = per_owner * BROWS
    bf16 = lambda *shape: jax.ShapeDtypeStruct(shape, BF16)

    rim_rows = rim_blocks * BROWS
    where = jnp.stack([group, shard]).astype(jnp.int32)
    prep_out = [bf16(packed_rows + 3 * folds, 128), bf16(rim_rows, 128)]
    prep_out += [bf16(256, tokens)] * 2 + [bf16(tokens, 256)]
    packed, rim, even, odd, val = pl.pallas_call(
        prep_kernel,
        grid_spec=pltpu.PrefetchScalarGridSpec(
            num_scalar_prefetch=1,
            grid=(1,),
            in_specs=[
                pl.BlockSpec((tokens, PAIR), lambda i, g: (0, g[0] // 2)),
                pl.BlockSpec((tokens, DV), lambda i, g: (0, g[0])),
                pl.BlockSpec((CBLK, PAIR), lambda i, g: (0, g[0] // 2)),
                pl.BlockSpec((CBLK, DV), lambda i, g: (0, g[0])),
            ],
            out_specs=[pl.BlockSpec(x.shape, lambda i, g: (0, 0)) for x in prep_out],
        ),
        out_shape=prep_out,
        compiler_params=pltpu.CompilerParams(vmem_limit_bytes=VMEM_LIMIT),
        name="prep",
    )(where, key_rows, value_rows, comp_key_weight, comp_value_weight)
    other = lax.ppermute(packed, "ctx", [(i, i ^ 1) for i in range(n_ctx)])
    packed, block_picks = lax.optimization_barrier((packed, block_picks))
    smem = pl.BlockSpec(memory_space=pltpu.SMEM)
    plan_out = [jax.ShapeDtypeStruct((n_ctx * lists + 1,), jnp.int32)]
    plan_out += [jax.ShapeDtypeStruct((lists * PICKS + 1,), jnp.int32)] * 2
    named, slots, dead = pl.pallas_call(
        functools.partial(plan_kernel, (n_ctx, lists, per_owner)),
        in_specs=[smem] * 2,
        out_specs=[smem] * 3,
        out_shape=plan_out,
        scratch_shapes=[
            pltpu.SMEM((n_ctx,), jnp.int32),
            pltpu.SMEM((n_ctx * per_owner,), jnp.int32),
            pltpu.SMEM((n_ctx,), jnp.int32),
        ],
        name="plan",
    )(where, block_picks)
    named = [named] + [
        lax.ppermute(named, "ctx", [(i, i - 2 * d) for i in range(2 * d, n_ctx)])
        for d in range(1, groups)
    ]
    far_rim = lax.ppermute(rim, "ctx", [(i, i + 1) for i in range(1, n_ctx - 1, 2)])

    gates = jax.nn.sigmoid(gate_logits).reshape(tokens, 3 * heads)
    gates = jnp.pad(gates, ((0, 0), (0, 128 - 3 * heads)))
    sent = bf16(lists * BROWS + 3 * folds, 128)

    def pack(beside, lists_in, rows):
        return single_step(
            functools.partial(pack_kernel, lists, beside),
            "pack",
            [where, *lists_in],
            [rows],
            [sent] * len(lists_in),
        )

    def ahead(send, distance):
        return lax.ppermute(send, "ctx", [(i, i + 2 * distance) for i in range(n_ctx - 2 * distance)])

    own_sends = pack(False, named[1:], packed)
    own_sends, even = lax.optimization_barrier((own_sends, even))
    from_same = [ahead(send, d) for d, send in enumerate(own_sends, 1)]

    reach = WINDOW // QBLK
    near = functools.partial(near_branch, where=where, queries=queries, gates=gates)
    mixed = near(reach, lists - reach, keys=(even, odd, val), rims=None, prior=None)

    other, mixed = lax.optimization_barrier((other, mixed))
    beside, *other_sends = pack(True, named, other)
    from_other = [ahead(send, d) for d, send in enumerate(other_sends, 1)]

    mixed = near(0, reach, keys=(even, odd, val), rims=(other, far_rim), prior=mixed)

    received = [beside] + [x for both in zip(from_same, from_other) for x in both]
    pools = single_step(
        functools.partial(pool_kernel, groups, lists),
        "pool",
        [shard.reshape(1)],
        [packed] + received,
        [bf16(n_ctx * lists * KBLK, 256)] * 2
        + [bf16(256, n_ctx * folds)] * 2
        + [bf16(n_ctx * folds, 256)],
        [pltpu.VMEM((n_ctx * folds, 256), BF16)],
    )
    rows = tokens // n_head
    chips = n_head // 2
    chip, core = head_at // 2, lax.rem(head_at, 2)
    order = []
    for step in list(range(1, chips)) + [0]:
        target = lax.rem(chip + step, chips) * 2
        order += [target + 1 - core, target + core]
    meta = jnp.stack([shard * tokens] + order).astype(jnp.int32)
    across = [(i, i ^ 1) for i in range(n_head)]

    model = out_weight.shape[1]

    def project(first_chunk, widths):
        return chosen_and_project(
            first_chunk, widths, rows, meta, slots, dead, queries, gates, mixed, pools, out_weight
        )

    sums = []
    for step in range(chips - 1):
        other = lax.ppermute(project(1 + 2 * step, [[model]])[0], "head", across)
        mine = project(2 + 2 * step, [[model]])[0]
        summed = (mine.astype(F32) + other.astype(F32)).astype(BF16)
        summed, meta = lax.optimization_barrier((summed, meta))
        sums.append(summed)
    *passed, kept = project(n_head - 1, [[model // 2] * 2, [model]])
    arrived = [jnp.concatenate([lax.ppermute(x, "head", across) for x in passed], axis=1)]
    for step, summed in enumerate(sums, 1):
        route = [(i, (i + 2 * step) % n_head) for i in range(n_head)]
        arrived.append(lax.ppermute(summed, "head", route))
    total = kept.astype(F32)
    for part in arrived:
        total = total + part.astype(F32)
    return total.astype(BF16)


def solution(mesh):
    placed = (
        P("ctx", "head"),
        P("ctx", None),
        P("ctx", None),
        P(),
        P(),
        P("ctx", None, None),
        P("ctx", None, "head"),
        P("head", None),
    )
    return jax.shard_map(
        local, mesh=mesh, in_specs=placed, out_specs=P(("ctx", "head"), None), check_vma=False
    )
```

```python
import functools

import jax
import jax.numpy as jnp
from jax import lax
from jax.experimental import pallas as pl
from jax.experimental.pallas import tpu as pltpu
from jax.sharding import PartitionSpec as P

HEADS = 64
GROUPS = 4
QK = 192
DV = 128
CBLK = 32
KBLK = 64
PICKS = 16
WINDOW = 512
QBLK = 256
PAIR = 2 * QK
BROWS = KBLK + KBLK // 2 + KBLK
VMEM_LIMIT = 60 * 1024 * 1024
NEG = -1e30
SCALE = QK ** (-0.5) * 1.4426950408889634
LOW_TOTAL, HIGH_TOTAL = 2.0**-60, 2.0**100
TILE = 256
NT = (((1,), (1,)), ((), ()))
F32 = jnp.float32
BF16 = jnp.bfloat16


def half_lanes(rows):
    return lax.broadcasted_iota(jnp.int32, (rows, 128), 1) < 64


def swap_halves(x):
    return pltpu.roll(x, 64, 1)


def turned(keys):
    row, col = iota(256, 256, 0), iota(256, 256, 1)
    unit = (row == col).astype(BF16)
    even = lax.dot_general(unit, keys, NT, preferred_element_type=F32).astype(BF16)
    return even, lower(even)


def lower(even):
    return jnp.concatenate([jnp.zeros((64, even.shape[1]), BF16), even[:QK]], axis=0)


def with_ones(values):
    return jnp.concatenate([values, jnp.ones_like(values)], axis=1)


def prep_kernel(
    group_ref,
    keys_ref,
    values_ref,
    kw_ref,
    vw_ref,
    packed_ref,
    rim_ref,
    even_ref,
    odd_ref,
    val_ref,
):
    odd = lax.rem(group_ref[0], 2) == 1

    def own_columns(ref):
        t0 = ref[:, :128].astype(F32)
        t1 = ref[:, 128:256].astype(F32)
        t2 = ref[:, 256:].astype(F32)
        r1, r2 = swap_halves(t1), swap_halves(t2)
        left = half_lanes(t0.shape[0])
        low = jnp.where(odd, jnp.where(left, r1, r2), t0)
        high = jnp.where(left, jnp.where(odd, r2, t1), 0.0)
        return low, high

    low, high = own_columns(keys_ref)
    values = values_ref[...]
    rows = low.shape[0]
    count = rows // KBLK
    high3 = high.reshape(count, KBLK, 128)
    packed_high = high3[:, : KBLK // 2] + swap_halves(
        high3[:, KBLK // 2 :].reshape(count * KBLK // 2, 128)
    ).reshape(count, KBLK // 2, 128)
    even = jnp.concatenate([low.astype(BF16), high.astype(BF16)], axis=1)
    even_ref[...], odd_ref[...] = turned(even)
    val_ref[...] = with_ones(values)
    for block in range(count):
        at = block * BROWS
        token = slice(block * KBLK, block * KBLK + KBLK)
        packed_ref[at : at + KBLK] = low[token].astype(BF16)
        packed_ref[at + KBLK : at + KBLK + KBLK // 2] = packed_high[block].astype(BF16)
        packed_ref[at + KBLK + KBLK // 2 : at + BROWS] = values[token]
    rim_rows = rim_ref.shape[0]
    rim_ref[...] = packed_ref[count * BROWS - rim_rows : count * BROWS]

    wlow, whigh = own_columns(kw_ref)
    folds = rows // CBLK

    def fold(x, w):
        return jnp.sum(x.reshape(folds, CBLK, 128) * w[None], axis=1).astype(BF16)

    at = count * BROWS
    packed_ref[at : at + folds] = fold(low, wlow)
    packed_ref[at + folds : at + 2 * folds] = fold(high, whigh)
    packed_ref[at + 2 * folds :] = fold(values.astype(F32), vw_ref[...])


def plan_kernel(shape, where_ref, picks_ref, lists_ref, slots_ref, dead_ref, named, rank, seen):
    n_ctx, lists, per_owner = shape
    group, shard = where_ref[0], where_ref[1]
    for owner in range(n_ctx):
        named[owner] = 0
    for entry in range(n_ctx * lists + 1):
        lists_ref[entry] = 0

    def mark(query_block, _):
        for entry in range(PICKS):
            block = picks_ref[query_block, group, entry]
            owner = lax.div(block, per_owner)
            named[owner] = named[owner] | (jnp.int32(1) << lax.rem(block, per_owner))
        return 0

    lax.fori_loop(0, lists, mark, 0)

    def enlist(owner, _):
        bits = named[owner]
        count = jnp.int32(0)
        for block in range(per_owner):
            bit = (bits >> block) & 1
            rank[owner * per_owner + block] = jnp.minimum(count, lists - 1)
            taken = (bit == 1) & (count < lists)
            lists_ref[jnp.where(taken, owner * lists + count, n_ctx * lists)] = block
            count = count + bit
        return 0

    lax.fori_loop(0, n_ctx, enlist, 0)

    def place(block):
        owner = lax.div(block, per_owner)
        turn = (lax.div(shard, 2) - lax.div(owner, 2)) * 2 + ((owner ^ shard) & 1)
        return jnp.clip(turn * lists + rank[block], 0, n_ctx * lists - 1)

    def one_list(query_block, _):
        first = shard * per_owner + query_block * (QBLK // KBLK)
        at = query_block * PICKS
        for owner in range(n_ctx):
            seen[owner] = 0
        seen[shard] = jnp.int32(1) << lax.rem(first, per_owner)
        slots_ref[at] = place(first)
        dead_ref[at] = 0
        at = at + 1
        met = jnp.int32(0)
        for entry in range(PICKS):
            block = picks_ref[query_block, group, entry]
            owner = lax.div(block, per_owner)
            inside = lax.rem(block, per_owner)
            before = (seen[owner] >> inside) & 1
            own = jnp.where(block == first, 1, 0)
            slots_ref[at] = place(block)
            dead_ref[at] = before | jnp.where(block > first, 1, 0)
            seen[owner] = seen[owner] | (jnp.int32(1) << inside)
            at = at + 1 - (own & (1 - met))
            met = met | own
        return 0

    lax.fori_loop(0, lists, one_list, 0)


def pack_kernel(lists, beside, where_ref, *refs):
    count = len(refs) // 2
    named, ref, outs = refs[:count], refs[count], refs[count + 1 :]
    shard = where_ref[1]
    owner = shard + 1 - 2 * lax.rem(shard, 2) if beside else shard
    data = ref.shape[0] - (outs[0].shape[0] - lists * BROWS)
    for blocks, out in zip(named, outs):
        for place in range(lists):
            at = pl.multiple_of(blocks[owner * lists + place] * BROWS, 16)
            out[place * BROWS : (place + 1) * BROWS] = ref[pl.ds(at, BROWS)]
        out[lists * BROWS :] = ref[data:]


def unpack(ref, at, count, step=1):
    lows, packed, values = [], [], []
    for block in range(count):
        first = at + block * step * BROWS
        lows.append(ref[first : first + KBLK])
        packed.append(ref[first + KBLK : first + KBLK + KBLK // 2])
        values.append(ref[first + KBLK + KBLK // 2 : first + BROWS])
    packed = jnp.concatenate(packed, axis=0)
    row, col = iota(128, 256, 0), iota(128, 256, 1)
    take = (row == jnp.where(col < 128, col, col - 64)) & (lax.rem(col, 128) < 64)
    both = jnp.dot(packed, take.astype(BF16), preferred_element_type=F32).astype(BF16)
    half = KBLK // 2
    highs = []
    for block in range(count):
        rows = slice(block * half, block * half + half)
        highs += [both[rows, :128], both[rows, 128:]]
    even = jnp.concatenate(
        [jnp.concatenate(lows, axis=0), jnp.concatenate(highs, axis=0)], axis=1
    )
    return even, jnp.concatenate(values, axis=0)


def fill_rim(shard, near_ref, far_ref, own, ext):
    rim_blocks = WINDOW // KBLK
    even_in, odd_in, val_in = own
    even_ref, odd_ref, val_ref = ext
    even_ref[:, WINDOW:] = even_in[:, :WINDOW]
    odd_ref[:, WINDOW:] = odd_in[:, :WINDOW]
    val_ref[WINDOW:] = val_in[:WINDOW]
    use_near = lax.rem(shard, 2) == 1

    @pl.when(shard > 0)
    def _():
        keys, values = unpack(jnp.where(use_near, near_ref[...], far_ref[...]), 0, rim_blocks)
        even_ref[:, :WINDOW], odd_ref[:, :WINDOW] = turned(keys)
        val_ref[:WINDOW] = with_ones(values)

    @pl.when(shard == 0)
    def _():
        even = jnp.broadcast_to(even_in[:, :1].astype(F32), (256, WINDOW)).astype(BF16)
        even_ref[:, :WINDOW], odd_ref[:, :WINDOW] = even, lower(even)
        val_ref[:WINDOW] = jnp.zeros((WINDOW, 256), BF16)


def pool_kernel(groups, lists, where_ref, own_ref, *refs):
    sent = 2 * groups - 1
    ins, (key_ref, val_ref, ceven_ref, codd_ref, cval_ref, folded) = refs[:sent], refs[sent:]
    shard = where_ref[1]
    parity = lax.rem(shard, 2)
    base = shard - parity
    rows = lists * KBLK
    folds = (ins[0].shape[0] - lists * BROWS) // 3
    folded[...] = jnp.zeros_like(folded)
    cval_ref[...] = jnp.zeros_like(cval_ref)

    def fill(place, owner, ref, step, fold_at):
        keys, values = unpack(ref, 0, lists, step)
        at = slice(place * rows, place * rows + rows)
        key_ref[at] = keys
        val_ref[at] = values
        low = ref[fold_at : fold_at + folds]
        high = ref[fold_at + folds : fold_at + 2 * folds]
        owned = pl.ds(pl.multiple_of(owner * folds, 32), folds)
        folded[owned] = jnp.concatenate([low, high], axis=1)
        cval_ref[owned] = with_ones(ref[fold_at + 2 * folds : fold_at + 3 * folds])

    fill(0, shard, own_ref, QBLK // KBLK, own_ref.shape[0] - 3 * folds)
    fill(1, base + 1 - parity, ins[0], 1, lists * BROWS)
    for distance in range(1, groups):

        @pl.when(base >= 2 * distance)
        def _():
            for side in range(2):
                owner = base - 2 * distance + (parity if side == 0 else 1 - parity)
                fill(2 * distance + side, owner, ins[2 * distance - 1 + side], 1, lists * BROWS)

    ceven_ref[...], codd_ref[...] = turned(folded[...])


def iota(rows, cols, axis):
    return lax.broadcasted_iota(jnp.int32, (rows, cols), axis)


def scores_of(q, keys, mask):
    scores = jnp.dot(q, keys, preferred_element_type=F32)
    return scores if mask is None else mask(scores)


def in_range(total):
    good = jnp.where((total >= LOW_TOTAL) & (total <= HIGH_TOTAL), 1.0, 0.0)
    return jnp.min(good.reshape(-1, 8, DV), axis=0)


def over_heads(pairs, load, branches, finish):
    def sums(weights, values):
        out = jnp.dot(weights, values(), preferred_element_type=F32)
        return out[:, :DV], out[:, DV:]

    at_once = 2 if pairs % 2 == 0 else 1
    units = [(pair, side) for pair in range(0, pairs, at_once) for side in range(2)]
    worst, held = [], None
    for now, unit in zip([None] + units, units + [None]):
        q = None if unit is None else load(*unit, at_once)
        fresh, parts = [], []
        for at, (tiles, values) in enumerate(branches):
            weights, ahead = [], []
            for place, (keys, mask) in enumerate(tiles):
                if q is not None:
                    ahead.append(scores_of(q, keys(unit[1]), mask))
                if held is not None:
                    weights.append(jnp.exp2(held[at][place] * SCALE).astype(BF16))
            fresh.append(ahead)
            parts.append((weights, values))
        if held is not None:
            parts = [sums(jnp.concatenate(w, axis=1), values) for w, values in parts]
            worst += [in_range(x) for x in finish(*now, at_once, parts)]
        held = fresh

    @pl.when(jnp.min(functools.reduce(jnp.minimum, worst)) < 0.5)
    def _():
        def exact(pair, _):
            for side in range(2):
                q = load(pair, side, 1)
                parts = []
                for tiles, values in branches:
                    scores = [scores_of(q, keys(side), mask) for keys, mask in tiles]
                    scores = jnp.concatenate(scores, axis=1)
                    top = jnp.max(scores, axis=1, keepdims=True)
                    shifted = (scores - jnp.maximum(top, -1e28)) * SCALE
                    parts.append(sums(jnp.exp2(shifted).astype(BF16), values))
                finish(pair, side, 1, parts)
            return 0

        lax.fori_loop(0, pairs, exact, 0)


def aligned(at):
    return at if isinstance(at, int) else pl.multiple_of(at, 128)


def query_loader(q_ref):
    def load(pair, side, n):
        at = [aligned((pair + p) * PAIR + side * 128) for p in range(n)]
        return jnp.concatenate([q_ref[:, pl.ds(x, 256)] for x in at], axis=0)

    return load


def head_columns(pair, side):
    return pl.ds(aligned(pair * 2 * DV + side * DV), DV)


def gate_loader(gate_ref, first, heads):
    turned = pltpu.roll(gate_ref[...], lax.rem(128 - first, 128), 1)

    def load(pair, side, n, branch):
        if isinstance(pair, int):
            local, at = turned, branch * heads + side + 2 * pair
        else:
            local, at = pltpu.roll(turned, lax.rem(128 - 2 * pair, 128), 1), branch * heads + side
        columns = [local[:, at + 2 * p : at + 2 * p + 1] for p in range(n)]
        shape = (turned.shape[0], DV)
        return jnp.concatenate([jnp.broadcast_to(x, shape) for x in columns], axis=0)

    return load


def stacked(x, times):
    return jnp.concatenate([x] * times, axis=0) if times > 1 else x


def repeated(keep, rows):
    return stacked(keep, rows // keep.shape[0])


def near_kernel(heads, rim, where_ref, q_ref, gate_ref, *refs):
    keys = refs[:3]
    if rim:
        out_ref, ext = refs[6], refs[7:]

        @pl.when((pl.program_id(0) == 0) & (pl.program_id(1) == 0))
        def _():
            fill_rim(where_ref[1], refs[3], refs[4], keys, ext)

        keys = ext
    else:
        out_ref = refs[3]
    count = q_ref.shape[1] // QK
    gate = gate_loader(gate_ref, pl.program_id(1) * count, heads)
    base = pl.multiple_of(pl.program_id(0) * QBLK, QBLK)
    row, col = iota(QBLK, QBLK, 0), iota(QBLK, QBLK, 1)

    def tile(place, mask):
        return (lambda side: keys[side][:, pl.ds(base + place * QBLK, QBLK)]), mask

    def finish(pair, side, n, parts):
        ((num, den),) = parts
        total = gate(pair, side, n, 2) * (num / den)
        for p in range(n):
            out_ref[:, head_columns(pair + p, side)] = total[p * QBLK : (p + 1) * QBLK]
        return [den]

    tiles = [
        tile(0, lambda x: jnp.where(repeated(col >= row, x.shape[0]), x, NEG)),
        tile(1, None),
        tile(2, lambda x: jnp.where(repeated(col <= row, x.shape[0]), x, NEG)),
    ]
    values = lambda: keys[2][pl.ds(base, WINDOW + QBLK)]
    over_heads(count // 2, query_loader(q_ref), [(tiles, values)], finish)


def near_branch(first_block, block_count, where, queries, gates, keys, rims, prior):
    tokens, width = queries.shape
    heads = width // QK
    at_once = 8 if heads % 8 == 0 else 2
    row_block = lambda i, p, *_: (i + first_block, p)
    whole = lambda x: pl.BlockSpec(x.shape, lambda i, p, *_: (0,) * x.ndim)
    operands = [queries, gates, *keys]
    specs = [
        pl.BlockSpec((QBLK, at_once * QK), row_block),
        pl.BlockSpec((QBLK, 128), lambda i, p, *_: (i + first_block, 0)),
    ]
    specs += [whole(x) for x in keys]
    alias, scratch = {}, []
    if rims is not None:
        other, far = rims
        rim_rows = far.shape[0]
        last_rim = tokens // KBLK * BROWS // rim_rows - 1
        operands += [other, far, prior]
        specs += [
            pl.BlockSpec(far.shape, lambda i, p, *_: (last_rim, 0)),
            whole(far),
            pl.BlockSpec(memory_space=pl.ANY),
        ]
        alias = {len(operands): 0}
        scratch = [pltpu.VMEM((256, 2 * WINDOW), BF16)] * 2 + [pltpu.VMEM((2 * WINDOW, 256), BF16)]
    rows = block_count * QBLK * heads
    return pl.pallas_call(
        functools.partial(near_kernel, heads, rims is not None),
        grid_spec=pltpu.PrefetchScalarGridSpec(
            num_scalar_prefetch=1,
            grid=(block_count, heads // at_once),
            in_specs=specs,
            out_specs=pl.BlockSpec((QBLK, at_once * DV), row_block),
            scratch_shapes=scratch,
        ),
        out_shape=jax.ShapeDtypeStruct((tokens, heads * DV), F32),
        input_output_aliases=alias,
        compiler_params=pltpu.CompilerParams(vmem_limit_bytes=VMEM_LIMIT),
        cost_estimate=pl.CostEstimate(
            flops=rows * (WINDOW + QBLK) * 64,
            bytes_accessed=rows * (2 * QK + 4 * DV),
            transcendentals=0,
        ),
        name="near_branch",
    )(where, *operands)


def chosen_kernel(heads, span, *refs):
    first_chunk, widths = span
    out_count = sum(len(w) for w in widths)
    meta_ref, slots_ref, dead_ref, q_ref, gate_ref, near_ref = refs[:6]
    (key_pool, val_pool), cfold, weight_ref = refs[6:8], refs[8:11], refs[11]
    outs = list(refs[12 : 12 + out_count])
    gathered, even, odd, val, attended, weight, weight_sem = refs[12 + out_count :]
    keys = (even, odd)
    turn, step = pl.program_id(0), pl.program_id(1)
    last = pl.num_programs(1) - 1
    rows = q_ref.shape[0]
    count = q_ref.shape[1] // QK
    chunk_start = meta_ref[2 + first_chunk + turn] * rows
    list_at = lax.div(chunk_start, QBLK) * PICKS
    first_row = lax.rem(chunk_start, QBLK)
    position = meta_ref[2] + chunk_start
    copy = pltpu.make_async_copy(weight_ref, weight, weight_sem)

    @pl.when(step == 0)
    def _():
        for slot in range(PICKS):
            source = pl.multiple_of(slots_ref[list_at + slot] * KBLK, KBLK)
            gathered[slot * KBLK : (slot + 1) * KBLK] = key_pool[pl.ds(source, KBLK)]
            val[slot * KBLK : (slot + 1) * KBLK] = with_ones(val_pool[pl.ds(source, KBLK)])
        for slot in range(1, PICKS):

            @pl.when(dead_ref[list_at + slot] == 1)
            def _():
                at = slice(slot * KBLK, (slot + 1) * KBLK)
                gathered[at] = jnp.broadcast_to(gathered[:1], (KBLK, 256))
                val[at] = jnp.zeros((KBLK, 256), BF16)

        even[...], odd[...] = turned(gathered[...])

    @pl.when((turn == 0) & (step == 0))
    def _():
        copy.start()

    gate = gate_loader(gate_ref, step * count, heads)
    row = iota(rows, TILE, 0)
    col = iota(rows, TILE, 1)
    own_keep = (col >= KBLK) | (col <= row + first_row)

    def own_mask(scores):
        own = jnp.where(repeated(own_keep[:, :128], scores.shape[0]), scores[:, :128], NEG)
        return jnp.concatenate([own, scores[:, 128:]], axis=1)

    def comp_mask(place):
        ends = (col + place * TILE + 1) * CBLK - 1
        return lambda x: jnp.where(repeated(ends <= row + position, x.shape[0]), x, NEG)

    def tile(refs, place, mask):
        return (lambda side: refs[side][:, place * TILE : (place + 1) * TILE]), mask

    chosen = [tile(keys, p, own_mask if p == 0 else None) for p in range(PICKS * KBLK // TILE)]
    folded = [tile(cfold, p, comp_mask(p)) for p in range(cfold[2].shape[0] // TILE)]
    empty = row[:, :DV] + position < CBLK - 1

    def finish(pair, side, n, parts):
        (num, den), (folded_num, folded_den) = parts
        folded_den = jnp.where(stacked(empty, n), 1.0, folded_den)
        total = gate(pair, side, n, 1) * (num / den)
        total = total + gate(pair, side, n, 0) * (folded_num / folded_den)
        for p in range(n):
            cols = head_columns(pair + p, side)
            mixed = near_ref[:, cols] + total[p * rows : (p + 1) * rows]
            attended[step, :, cols] = mixed.astype(BF16)
        return [den, folded_den]

    branches = [(chosen, lambda: val[...]), (folded, lambda: cfold[2][...])]
    over_heads(count // 2, query_loader(q_ref), branches, finish)

    @pl.when((turn == 0) & (step == last))
    def _():
        copy.wait()

    for place, parts in enumerate(widths):
        chunk_outs = [outs.pop(0) for _ in parts]

        @pl.when((turn == place) & (step == last))
        def _():
            rows_in = jnp.concatenate([attended[s] for s in range(attended.shape[0])], axis=1)
            first_col = 0
            for out_ref in chunk_outs:
                for at in range(0, out_ref.shape[1], 256):
                    cols = weight[:, first_col + at : first_col + at + 256]
                    part = jnp.dot(rows_in, cols, preferred_element_type=F32)
                    out_ref[:, at : at + 256] = part.astype(out_ref.dtype)
                first_col += out_ref.shape[1]


def chosen_and_project(first_chunk, widths, rows, meta, slots, dead, queries, gates, near, pools, out_weight):
    tokens, width = queries.shape
    heads = width // QK
    at_once = 8 if heads % 8 == 0 else 2
    steps = heads // at_once
    whole = lambda x: pl.BlockSpec(x.shape, lambda i, p, *_: (0,) * x.ndim)
    outs = [jax.ShapeDtypeStruct((rows, width), BF16) for chunk in widths for width in chunk]
    return pl.pallas_call(
        functools.partial(chosen_kernel, heads, (first_chunk, widths)),
        grid_spec=pltpu.PrefetchScalarGridSpec(
            num_scalar_prefetch=3,
            grid=(len(widths), steps),
            in_specs=[
                pl.BlockSpec((rows, at_once * QK), lambda i, p, m, *_: (m[2 + first_chunk + i], p)),
                pl.BlockSpec((rows, 128), lambda i, p, m, *_: (m[2 + first_chunk + i], 0)),
                pl.BlockSpec((rows, at_once * DV), lambda i, p, m, *_: (m[2 + first_chunk + i], p)),
            ]
            + [whole(x) for x in pools]
            + [pl.BlockSpec(memory_space=pl.ANY)],
            out_specs=[whole(out) for out in outs],
            scratch_shapes=[
                pltpu.VMEM((PICKS * KBLK, 256), BF16),
                pltpu.VMEM((256, PICKS * KBLK), BF16),
                pltpu.VMEM((256, PICKS * KBLK), BF16),
                pltpu.VMEM((PICKS * KBLK, 256), BF16),
                pltpu.VMEM((steps, rows, at_once * DV), BF16),
                pltpu.VMEM(out_weight.shape, BF16),
                pltpu.SemaphoreType.DMA,
            ],
        ),
        out_shape=outs,
        compiler_params=pltpu.CompilerParams(vmem_limit_bytes=VMEM_LIMIT),
        cost_estimate=pl.CostEstimate(
            flops=rows * heads * PICKS * KBLK * 64,
            bytes_accessed=out_weight.size,
            transcendentals=0,
        ),
        name="chosen_and_project",
    )(meta, slots, dead, queries, gates, near, *pools, out_weight)


def single_step(kernel, name, scalars, arrays, outs, scratch=()):
    whole = lambda x: pl.BlockSpec(x.shape, lambda i, *_: (0,) * len(x.shape))
    return pl.pallas_call(
        kernel,
        grid_spec=pltpu.PrefetchScalarGridSpec(
            num_scalar_prefetch=len(scalars),
            grid=(1,),
            in_specs=[whole(x) for x in arrays],
            out_specs=[whole(x) for x in outs],
            scratch_shapes=list(scratch),
        ),
        out_shape=outs,
        compiler_params=pltpu.CompilerParams(vmem_limit_bytes=VMEM_LIMIT),
        name=name,
    )(*scalars, *arrays)


def local(
    queries,
    key_rows,
    value_rows,
    comp_key_weight,
    comp_value_weight,
    block_picks,
    gate_logits,
    out_weight,
):
    tokens = queries.shape[0]
    heads = queries.shape[1] // QK
    n_ctx, n_head = lax.axis_size("ctx"), lax.axis_size("head")
    shard, head_at = lax.axis_index("ctx"), lax.axis_index("head")
    group = head_at * heads // (HEADS // GROUPS)
    per_owner = tokens // KBLK
    lists = tokens // QBLK
    folds = tokens // CBLK
    groups = n_ctx // 2
    rim_blocks = WINDOW // KBLK
    packed_rows = per_owner * BROWS
    bf16 = lambda *shape: jax.ShapeDtypeStruct(shape, BF16)

    chips = n_head // 2
    chip, core = head_at // 2, lax.rem(head_at, 2)
    order = []
    for step in list(range(1, chips)) + [0]:
        target = lax.rem(chip + step, chips) * 2
        order += [target + 1 - core, target + core]
    where = jnp.stack([group, shard, shard * tokens] + order).astype(jnp.int32)
    rim_rows = rim_blocks * BROWS
    prep_out = [bf16(packed_rows + 3 * folds, 128), bf16(rim_rows, 128)]
    prep_out += [bf16(256, tokens)] * 2 + [bf16(tokens, 256)]
    packed, rim, even, odd, val = pl.pallas_call(
        prep_kernel,
        grid_spec=pltpu.PrefetchScalarGridSpec(
            num_scalar_prefetch=1,
            grid=(1,),
            in_specs=[
                pl.BlockSpec((tokens, PAIR), lambda i, g: (0, g[0] // 2)),
                pl.BlockSpec((tokens, DV), lambda i, g: (0, g[0])),
                pl.BlockSpec((CBLK, PAIR), lambda i, g: (0, g[0] // 2)),
                pl.BlockSpec((CBLK, DV), lambda i, g: (0, g[0])),
            ],
            out_specs=[pl.BlockSpec(x.shape, lambda i, g: (0, 0)) for x in prep_out],
        ),
        out_shape=prep_out,
        compiler_params=pltpu.CompilerParams(vmem_limit_bytes=VMEM_LIMIT),
        name="prep",
    )(where, key_rows, value_rows, comp_key_weight, comp_value_weight)
    other = lax.ppermute(packed, "ctx", [(i, i ^ 1) for i in range(n_ctx)])
    packed, block_picks = lax.optimization_barrier((packed, block_picks))
    smem = pl.BlockSpec(memory_space=pltpu.SMEM)
    plan_out = [jax.ShapeDtypeStruct((n_ctx * lists + 1,), jnp.int32)]
    plan_out += [jax.ShapeDtypeStruct((lists * PICKS + 1,), jnp.int32)] * 2
    named, slots, dead = pl.pallas_call(
        functools.partial(plan_kernel, (n_ctx, lists, per_owner)),
        in_specs=[smem] * 2,
        out_specs=[smem] * 3,
        out_shape=plan_out,
        scratch_shapes=[
            pltpu.SMEM((n_ctx,), jnp.int32),
            pltpu.SMEM((n_ctx * per_owner,), jnp.int32),
            pltpu.SMEM((n_ctx,), jnp.int32),
        ],
        name="plan",
    )(where, block_picks)
    named = [named] + [
        lax.ppermute(named, "ctx", [(i, i - 2 * d) for i in range(2 * d, n_ctx)])
        for d in range(1, groups)
    ]
    far_rim = lax.ppermute(rim, "ctx", [(i, i + 1) for i in range(1, n_ctx - 1, 2)])

    gates = jax.nn.sigmoid(gate_logits).reshape(tokens, 3 * heads)
    gates = jnp.pad(gates, ((0, 0), (0, 128 - 3 * heads)))
    sent = bf16(lists * BROWS + 3 * folds, 128)

    def pack(beside, lists_in, rows):
        return single_step(
            functools.partial(pack_kernel, lists, beside),
            "pack",
            [where, *lists_in],
            [rows],
            [sent] * len(lists_in),
        )

    def ahead(send, distance):
        return lax.ppermute(send, "ctx", [(i, i + 2 * distance) for i in range(n_ctx - 2 * distance)])

    own_sends = pack(False, named[1:], packed)
    own_sends, even = lax.optimization_barrier((own_sends, even))
    from_same = [ahead(send, d) for d, send in enumerate(own_sends, 1)]

    reach = WINDOW // QBLK
    near = functools.partial(near_branch, where=where, queries=queries, gates=gates)
    mixed = near(reach, lists - reach, keys=(even, odd, val), rims=None, prior=None)

    other, mixed = lax.optimization_barrier((other, mixed))
    beside, *other_sends = pack(True, named, other)
    from_other = [ahead(send, d) for d, send in enumerate(other_sends, 1)]

    mixed = near(0, reach, keys=(even, odd, val), rims=(other, far_rim), prior=mixed)

    received = [beside] + [x for both in zip(from_same, from_other) for x in both]
    pools = single_step(
        functools.partial(pool_kernel, groups, lists),
        "pool",
        [where],
        [packed] + received,
        [bf16(n_ctx * lists * KBLK, 256), bf16(n_ctx * lists * KBLK, DV)]
        + [bf16(256, n_ctx * folds)] * 2
        + [bf16(n_ctx * folds, 256)],
        [pltpu.VMEM((n_ctx * folds, 256), BF16)],
    )
    rows = tokens // n_head
    across = [(i, i ^ 1) for i in range(n_head)]

    model = out_weight.shape[1]

    def project(first_chunk, widths):
        return chosen_and_project(
            first_chunk, widths, rows, where, slots, dead, queries, gates, mixed, pools, out_weight
        )

    sums = []
    for step in range(chips - 1):
        other = lax.ppermute(project(1 + 2 * step, [[model]])[0], "head", across)
        mine = project(2 + 2 * step, [[model]])[0]
        summed = (mine.astype(F32) + other.astype(F32)).astype(BF16)
        summed, where = lax.optimization_barrier((summed, where))
        sums.append(summed)
    *passed, kept = project(n_head - 1, [[model // 2] * 2, [model]])
    arrived = [jnp.concatenate([lax.ppermute(x, "head", across) for x in passed], axis=1)]
    for step, summed in enumerate(sums, 1):
        route = [(i, (i + 2 * step) % n_head) for i in range(n_head)]
        arrived.append(lax.ppermute(summed, "head", route))
    total = kept.astype(F32)
    for part in arrived:
        total = total + part.astype(F32)
    return total.astype(BF16)


def solution(mesh):
    placed = (
        P("ctx", "head"),
        P("ctx", None),
        P("ctx", None),
        P(),
        P(),
        P("ctx", None, None),
        P("ctx", None, "head"),
        P("head", None),
    )
    return jax.shard_map(
        local, mesh=mesh, in_specs=placed, out_specs=P(("ctx", "head"), None), check_vma=False
    )
```

```python
import functools

import jax
import jax.numpy as jnp
from jax import lax
from jax.experimental import pallas as pl
from jax.experimental.pallas import tpu as pltpu
from jax.sharding import PartitionSpec as P

HEADS = 64
GROUPS = 4
QK = 192
DV = 128
CBLK = 32
KBLK = 64
PICKS = 16
WINDOW = 512
QBLK = 256
PAIR = 2 * QK
BROWS = KBLK + KBLK // 2 + KBLK
VMEM_LIMIT = 58 * 1024 * 1024
NEG = -1e30
SCALE = QK ** (-0.5) * 1.4426950408889634
LOW_TOTAL, HIGH_TOTAL = 2.0**-60, 2.0**100
TILE = 256
NT = (((1,), (1,)), ((), ()))
F32 = jnp.float32
BF16 = jnp.bfloat16


def half_lanes(rows):
    return lax.broadcasted_iota(jnp.int32, (rows, 128), 1) < 64


def swap_halves(x):
    return pltpu.roll(x, 64, 1)


def turned(keys):
    row, col = iota(256, 256, 0), iota(256, 256, 1)
    unit = (row == col).astype(BF16)
    even = lax.dot_general(unit, keys, NT, preferred_element_type=F32).astype(BF16)
    return even, lower(even)


def lower(even):
    return jnp.concatenate([jnp.zeros((64, even.shape[1]), BF16), even[:QK]], axis=0)


def with_ones(values):
    return jnp.concatenate([values, jnp.ones_like(values)], axis=1)


def plan(group, shard, per_owner, picks_ref, lists_ref, slots_ref, dead_ref):
    lists = picks_ref.shape[0]
    total = lists_ref.shape[1] // lists * per_owner
    width = slots_ref.shape[1]
    picks = jnp.zeros((lists, PICKS), jnp.int32)
    for each in range(picks_ref.shape[1]):
        picks = jnp.where(group == each, picks_ref[:, each, :], picks)
    block = iota(lists, total, 1)
    hits = [block == picks[:, entry : entry + 1] for entry in range(PICKS)]
    named = functools.reduce(jnp.logical_or, hits).astype(F32)
    named = jnp.broadcast_to(jnp.max(named, axis=0, keepdims=True), (8, total))
    row, col = iota(total, total, 0), iota(total, total, 1)
    before = (lax.div(row, per_owner) == lax.div(col, per_owner)) & (row < col)
    rank = jnp.dot(named, before.astype(F32), preferred_element_type=F32)
    rank = jnp.minimum(rank, float(lists - 1))
    inside = lax.rem(iota(8, total, 1), per_owner).astype(F32)
    found = jnp.zeros((8, lists_ref.shape[1]), F32)
    row, col = iota(total, lists_ref.shape[1], 0), iota(total, lists_ref.shape[1], 1)
    for place in range(lists):
        to = (col == lax.div(row, per_owner) * lists + place).astype(F32)
        value = jnp.where(rank == float(place), named * inside, 0.0)
        found = found + jnp.dot(value, to, preferred_element_type=F32)
    lists_ref[...] = found[:1].astype(jnp.int32)

    owner = lax.div(block, per_owner)
    turn = (lax.div(shard, 2) - lax.div(owner, 2)) * 2 + ((owner ^ shard) & 1)
    slot = jnp.clip(turn * lists + rank[:lists].astype(jnp.int32), 0, lists_ref.shape[1] - 1)
    slot = slot.astype(F32)
    first = shard * per_owner + iota(lists, 1, 0) * (QBLK // KBLK)
    own = block == first

    def pick_out(hit, values):
        return jnp.sum(jnp.where(hit, values, 0.0), axis=1, keepdims=True)

    lane = iota(lists, width, 1)
    slots = jnp.where(lane == 0, pick_out(own, slot), 0.0)
    dead = jnp.zeros((lists, width), F32)
    seen = own.astype(F32)
    at = jnp.ones((lists, 1), jnp.int32)
    met = jnp.zeros((lists, 1), jnp.int32)
    for entry, hit in enumerate(hits):
        pick = picks[:, entry : entry + 1]
        is_own = (pick == first).astype(jnp.int32)
        gone = jnp.maximum(pick_out(hit, seen), (pick > first).astype(F32))
        slots = jnp.where(lane == at, pick_out(hit, slot), slots)
        dead = jnp.where(lane == at, gone, dead)
        seen = jnp.maximum(seen, hit.astype(F32))
        at = at + 1 - is_own * (1 - met)
        met = jnp.maximum(met, is_own)
    slots_ref[...] = slots.astype(jnp.int32)
    dead_ref[...] = dead.astype(jnp.int32)


def prep_kernel(
    where_ref,
    picks_ref,
    keys_ref,
    values_ref,
    kw_ref,
    vw_ref,
    packed_ref,
    rim_ref,
    lists_ref,
    slots_ref,
    dead_ref,
    even_ref,
    odd_ref,
    val_ref,
):
    group, shard = where_ref[0], where_ref[1]
    plan(group, shard, keys_ref.shape[0] // KBLK, picks_ref, lists_ref, slots_ref, dead_ref)
    odd = lax.rem(group, 2) == 1

    def own_columns(ref):
        t0 = ref[:, :128].astype(F32)
        t1 = ref[:, 128:256].astype(F32)
        t2 = ref[:, 256:].astype(F32)
        r1, r2 = swap_halves(t1), swap_halves(t2)
        left = half_lanes(t0.shape[0])
        low = jnp.where(odd, jnp.where(left, r1, r2), t0)
        high = jnp.where(left, jnp.where(odd, r2, t1), 0.0)
        return low, high

    low, high = own_columns(keys_ref)
    values = values_ref[...]
    rows = low.shape[0]
    count = rows // KBLK
    high3 = high.reshape(count, KBLK, 128)
    packed_high = high3[:, : KBLK // 2] + swap_halves(
        high3[:, KBLK // 2 :].reshape(count * KBLK // 2, 128)
    ).reshape(count, KBLK // 2, 128)
    even = jnp.concatenate([low.astype(BF16), high.astype(BF16)], axis=1)
    even_ref[...], odd_ref[...] = turned(even)
    val_ref[...] = with_ones(values)
    for block in range(count):
        at = block * BROWS
        token = slice(block * KBLK, block * KBLK + KBLK)
        packed_ref[at : at + KBLK] = low[token].astype(BF16)
        packed_ref[at + KBLK : at + KBLK + KBLK // 2] = packed_high[block].astype(BF16)
        packed_ref[at + KBLK + KBLK // 2 : at + BROWS] = values[token]
    rim_rows = rim_ref.shape[0]
    rim_ref[...] = packed_ref[count * BROWS - rim_rows : count * BROWS]

    wlow, whigh = own_columns(kw_ref)
    folds = rows // CBLK

    def fold(x, w):
        return jnp.sum(x.reshape(folds, CBLK, 128) * w[None], axis=1).astype(BF16)

    at = count * BROWS
    packed_ref[at : at + folds] = fold(low, wlow)
    packed_ref[at + folds : at + 2 * folds] = fold(high, whigh)
    packed_ref[at + 2 * folds :] = fold(values.astype(F32), vw_ref[...])


def pack_kernel(lists, beside, where_ref, *refs):
    count = (len(refs) - 2) // 2
    named, ref, outs, sems = refs[:count], refs[count], refs[count + 1 : -1], refs[-1]
    shard = where_ref[1]
    owner = shard + 1 - 2 * lax.rem(shard, 2) if beside else shard
    data = ref.shape[0] - (outs[0].shape[0] - lists * BROWS)
    copies = []
    for blocks, out in zip(named, outs):
        for place in range(lists):
            at = pl.multiple_of(blocks[0, owner * lists + place] * BROWS, 16)
            copies.append((ref.at[pl.ds(at, BROWS)], out.at[place * BROWS : (place + 1) * BROWS]))
        copies.append((ref.at[data:], out.at[lists * BROWS :]))
    copies = [pltpu.make_async_copy(*pair, sems.at[i]) for i, pair in enumerate(copies)]
    for copy in copies:
        copy.start()
    for copy in copies:
        copy.wait()


def unpack(ref, at, count, step=1):
    lows, packed, values = [], [], []
    for block in range(count):
        first = at + block * step * BROWS
        lows.append(ref[first : first + KBLK])
        packed.append(ref[first + KBLK : first + KBLK + KBLK // 2])
        values.append(ref[first + KBLK + KBLK // 2 : first + BROWS])
    packed = jnp.concatenate(packed, axis=0)
    row, col = iota(128, 256, 0), iota(128, 256, 1)
    take = (row == jnp.where(col < 128, col, col - 64)) & (lax.rem(col, 128) < 64)
    both = jnp.dot(packed, take.astype(BF16), preferred_element_type=F32).astype(BF16)
    half = KBLK // 2
    highs = []
    for block in range(count):
        rows = slice(block * half, block * half + half)
        highs += [both[rows, :128], both[rows, 128:]]
    even = jnp.concatenate(
        [jnp.concatenate(lows, axis=0), jnp.concatenate(highs, axis=0)], axis=1
    )
    return even, jnp.concatenate(values, axis=0)


def fill_rim(shard, near_ref, far_ref, own, ext):
    rim_blocks = WINDOW // KBLK
    even_in, odd_in, val_in = own
    even_ref, odd_ref, val_ref = ext
    even_ref[:, WINDOW:] = even_in[:, :WINDOW]
    odd_ref[:, WINDOW:] = odd_in[:, :WINDOW]
    val_ref[WINDOW:] = val_in[:WINDOW]
    use_near = lax.rem(shard, 2) == 1

    @pl.when(shard > 0)
    def _():
        keys, values = unpack(jnp.where(use_near, near_ref[...], far_ref[...]), 0, rim_blocks)
        even_ref[:, :WINDOW], odd_ref[:, :WINDOW] = turned(keys)
        val_ref[:WINDOW] = with_ones(values)

    @pl.when(shard == 0)
    def _():
        even = jnp.broadcast_to(even_in[:, :1].astype(F32), (256, WINDOW)).astype(BF16)
        even_ref[:, :WINDOW], odd_ref[:, :WINDOW] = even, lower(even)
        val_ref[:WINDOW] = jnp.zeros((WINDOW, 256), BF16)


def pool_kernel(groups, lists, where_ref, own_ref, *refs):
    sent = 2 * groups - 1
    ins, (key_ref, val_ref, ceven_ref, codd_ref, cval_ref, folded) = refs[:sent], refs[sent:]
    shard = where_ref[1]
    parity = lax.rem(shard, 2)
    base = shard - parity
    rows = lists * KBLK
    folds = (ins[0].shape[0] - lists * BROWS) // 3
    folded[...] = jnp.zeros_like(folded)
    cval_ref[...] = jnp.zeros_like(cval_ref)

    def fill(place, owner, ref, step, fold_at):
        keys, values = unpack(ref, 0, lists, step)
        at = slice(place * rows, place * rows + rows)
        key_ref[at] = keys
        val_ref[at] = values
        low = ref[fold_at : fold_at + folds]
        high = ref[fold_at + folds : fold_at + 2 * folds]
        owned = pl.ds(pl.multiple_of(owner * folds, 32), folds)
        folded[owned] = jnp.concatenate([low, high], axis=1)
        cval_ref[owned] = with_ones(ref[fold_at + 2 * folds : fold_at + 3 * folds])

    fill(0, shard, own_ref, QBLK // KBLK, own_ref.shape[0] - 3 * folds)
    fill(1, base + 1 - parity, ins[0], 1, lists * BROWS)
    for distance in range(1, groups):

        @pl.when(base >= 2 * distance)
        def _():
            for side in range(2):
                owner = base - 2 * distance + (parity if side == 0 else 1 - parity)
                fill(2 * distance + side, owner, ins[2 * distance - 1 + side], 1, lists * BROWS)

    ceven_ref[...], codd_ref[...] = turned(folded[...])


def iota(rows, cols, axis):
    return lax.broadcasted_iota(jnp.int32, (rows, cols), axis)


def scores_of(q, keys, mask):
    scores = jnp.dot(q, keys, preferred_element_type=F32)
    return scores if mask is None else mask(scores)


def in_range(total):
    good = jnp.where((total >= LOW_TOTAL) & (total <= HIGH_TOTAL), 1.0, 0.0)
    return jnp.min(good.reshape(-1, 8, DV), axis=0)


def over_heads(pairs, load, branches, finish):
    def sums(weights, values):
        out = jnp.dot(weights, values(), preferred_element_type=F32)
        return out[:, :DV], out[:, DV:]

    at_once = 2 if pairs % 2 == 0 else 1
    units = [(pair, side) for pair in range(0, pairs, at_once) for side in range(2)]
    worst, held = [], None
    for now, unit in zip([None] + units, units + [None]):
        q = None if unit is None else load(*unit, at_once)
        fresh, parts = [], []
        for at, (tiles, values) in enumerate(branches):
            weights, ahead = [], []
            for place, (keys, mask) in enumerate(tiles):
                if q is not None:
                    ahead.append(scores_of(q, keys(unit[1]), mask))
                if held is not None:
                    weights.append(jnp.exp2(held[at][place] * SCALE).astype(BF16))
            fresh.append(ahead)
            parts.append((weights, values))
        if held is not None:
            parts = [sums(jnp.concatenate(w, axis=1), values) for w, values in parts]
            worst += [in_range(x) for x in finish(*now, at_once, parts)]
        held = fresh

    @pl.when(jnp.min(functools.reduce(jnp.minimum, worst)) < 0.5)
    def _():
        def exact(pair, _):
            for side in range(2):
                q = load(pair, side, 1)
                parts = []
                for tiles, values in branches:
                    scores = [scores_of(q, keys(side), mask) for keys, mask in tiles]
                    scores = jnp.concatenate(scores, axis=1)
                    top = jnp.max(scores, axis=1, keepdims=True)
                    shifted = (scores - jnp.maximum(top, -1e28)) * SCALE
                    parts.append(sums(jnp.exp2(shifted).astype(BF16), values))
                finish(pair, side, 1, parts)
            return 0

        lax.fori_loop(0, pairs, exact, 0)


def aligned(at):
    return at if isinstance(at, int) else pl.multiple_of(at, 128)


def query_loader(q_ref):
    def load(pair, side, n):
        at = [aligned((pair + p) * PAIR + side * 128) for p in range(n)]
        return jnp.concatenate([q_ref[:, pl.ds(x, 256)] for x in at], axis=0)

    return load


def head_columns(pair, side):
    return pl.ds(aligned(pair * 2 * DV + side * DV), DV)


def gate_loader(gate_ref, first, heads):
    turned = pltpu.roll(gate_ref[...], lax.rem(128 - first, 128), 1)

    def load(pair, side, n, branch):
        if isinstance(pair, int):
            local, at = turned, branch * heads + side + 2 * pair
        else:
            local, at = pltpu.roll(turned, lax.rem(128 - 2 * pair, 128), 1), branch * heads + side
        columns = [local[:, at + 2 * p : at + 2 * p + 1] for p in range(n)]
        shape = (turned.shape[0], DV)
        return jnp.concatenate([jnp.broadcast_to(x, shape) for x in columns], axis=0)

    return load


def stacked(x, times):
    return jnp.concatenate([x] * times, axis=0) if times > 1 else x


def repeated(keep, rows):
    return stacked(keep, rows // keep.shape[0])


def near_kernel(heads, rim, where_ref, q_ref, gate_ref, *refs):
    keys = refs[:3]
    if rim:
        out_ref, ext = refs[6], refs[7:]

        @pl.when((pl.program_id(0) == 0) & (pl.program_id(1) == 0))
        def _():
            fill_rim(where_ref[1], refs[3], refs[4], keys, ext)

        keys = ext
    else:
        out_ref = refs[3]
    count = q_ref.shape[1] // QK
    gate = gate_loader(gate_ref, pl.program_id(1) * count, heads)
    base = pl.multiple_of(pl.program_id(0) * QBLK, QBLK)
    row, col = iota(QBLK, QBLK, 0), iota(QBLK, QBLK, 1)

    def tile(place, mask):
        return (lambda side: keys[side][:, pl.ds(base + place * QBLK, QBLK)]), mask

    def finish(pair, side, n, parts):
        ((num, den),) = parts
        total = gate(pair, side, n, 2) * (num / den)
        for p in range(n):
            part = total[p * QBLK : (p + 1) * QBLK]
            out_ref[:, head_columns(pair + p, side)] = part.astype(BF16)
        return [den]

    tiles = [
        tile(0, lambda x: jnp.where(repeated(col >= row, x.shape[0]), x, NEG)),
        tile(1, None),
        tile(2, lambda x: jnp.where(repeated(col <= row, x.shape[0]), x, NEG)),
    ]
    values = lambda: keys[2][pl.ds(base, WINDOW + QBLK)]
    over_heads(count // 2, query_loader(q_ref), [(tiles, values)], finish)


def near_branch(first_block, block_count, where, queries, gates, keys, rims, prior):
    tokens, width = queries.shape
    heads = width // QK
    at_once = 8 if heads % 8 == 0 else 2
    row_block = lambda i, p, *_: (i + first_block, p)
    whole = lambda x: pl.BlockSpec(x.shape, lambda i, p, *_: (0,) * x.ndim)
    operands = [queries, gates, *keys]
    specs = [
        pl.BlockSpec((QBLK, at_once * QK), row_block),
        pl.BlockSpec((QBLK, 128), lambda i, p, *_: (i + first_block, 0)),
    ]
    specs += [VMEM_SPEC] * len(keys)
    alias, scratch = {}, []
    if rims is not None:
        other, far = rims
        rim_rows = far.shape[0]
        last_rim = tokens // KBLK * BROWS // rim_rows - 1
        operands += [other, far, prior]
        specs += [
            pl.BlockSpec(far.shape, lambda i, p, *_: (last_rim, 0)),
            whole(far),
            pl.BlockSpec(memory_space=pl.ANY),
        ]
        alias = {len(operands): 0}
        scratch = [pltpu.VMEM((256, 2 * WINDOW), BF16)] * 2 + [pltpu.VMEM((2 * WINDOW, 256), BF16)]
    rows = block_count * QBLK * heads
    return pl.pallas_call(
        functools.partial(near_kernel, heads, rims is not None),
        grid_spec=pltpu.PrefetchScalarGridSpec(
            num_scalar_prefetch=1,
            grid=(block_count, heads // at_once),
            in_specs=specs,
            out_specs=pl.BlockSpec((QBLK, at_once * DV), row_block),
            scratch_shapes=scratch,
        ),
        out_shape=jax.ShapeDtypeStruct((tokens, heads * DV), BF16),
        input_output_aliases=alias,
        compiler_params=pltpu.CompilerParams(vmem_limit_bytes=VMEM_LIMIT),
        cost_estimate=pl.CostEstimate(
            flops=rows * (WINDOW + QBLK) * 64,
            bytes_accessed=rows * (2 * QK + 4 * DV),
            transcendentals=0,
        ),
        name="near_branch",
    )(where, *operands)


def chosen_kernel(heads, span, *refs):
    first_chunk, widths = span
    out_count = sum(len(w) for w in widths)
    meta_ref, slots_ref, dead_ref, q_ref, gate_ref, near_ref = refs[:6]
    (key_pool, val_pool), cfold, weight_ref = refs[6:8], refs[8:11], refs[11]
    outs = list(refs[12 : 12 + out_count])
    gathered, even, odd, val, attended, weight, weight_sem = refs[12 + out_count :]
    keys = (even, odd)
    turn, step = pl.program_id(0), pl.program_id(1)
    last = pl.num_programs(1) - 1
    rows = q_ref.shape[0]
    count = q_ref.shape[1] // QK
    chunk_start = meta_ref[2 + first_chunk + turn] * rows
    list_at = lax.div(chunk_start, QBLK)
    first_row = lax.rem(chunk_start, QBLK)
    position = meta_ref[2] + chunk_start
    copy = pltpu.make_async_copy(weight_ref, weight, weight_sem)

    @pl.when(step == 0)
    def _():
        for slot in range(PICKS):
            source = pl.multiple_of(slots_ref[list_at, slot] * KBLK, KBLK)
            gathered[slot * KBLK : (slot + 1) * KBLK] = key_pool[pl.ds(source, KBLK)]
            val[slot * KBLK : (slot + 1) * KBLK] = with_ones(val_pool[pl.ds(source, KBLK)])
        for slot in range(1, PICKS):

            @pl.when(dead_ref[list_at, slot] == 1)
            def _():
                at = slice(slot * KBLK, (slot + 1) * KBLK)
                gathered[at] = jnp.broadcast_to(gathered[:1], (KBLK, 256))
                val[at] = jnp.zeros((KBLK, 256), BF16)

        even[...], odd[...] = turned(gathered[...])

    @pl.when((turn == 0) & (step == 0))
    def _():
        copy.start()

    gate = gate_loader(gate_ref, step * count, heads)
    row = iota(rows, TILE, 0)
    col = iota(rows, TILE, 1)
    own_keep = (col >= KBLK) | (col <= row + first_row)

    def own_mask(scores):
        own = jnp.where(repeated(own_keep[:, :128], scores.shape[0]), scores[:, :128], NEG)
        return jnp.concatenate([own, scores[:, 128:]], axis=1)

    def comp_mask(place):
        ends = (col + place * TILE + 1) * CBLK - 1
        return lambda x: jnp.where(repeated(ends <= row + position, x.shape[0]), x, NEG)

    def tile(refs, place, mask):
        return (lambda side: refs[side][:, place * TILE : (place + 1) * TILE]), mask

    chosen = [tile(keys, p, own_mask if p == 0 else None) for p in range(PICKS * KBLK // TILE)]
    folded = [tile(cfold, p, comp_mask(p)) for p in range(cfold[2].shape[0] // TILE)]
    empty = row[:, :DV] + position < CBLK - 1

    def finish(pair, side, n, parts):
        (num, den), (folded_num, folded_den) = parts
        folded_den = jnp.where(stacked(empty, n), 1.0, folded_den)
        total = gate(pair, side, n, 1) * (num / den)
        total = total + gate(pair, side, n, 0) * (folded_num / folded_den)
        for p in range(n):
            cols = head_columns(pair + p, side)
            mixed = near_ref[:, cols].astype(F32) + total[p * rows : (p + 1) * rows]
            attended[step, :, cols] = mixed.astype(BF16)
        return [den, folded_den]

    branches = [(chosen, lambda: val[...]), (folded, lambda: cfold[2][...])]
    over_heads(count // 2, query_loader(q_ref), branches, finish)

    @pl.when((turn == 0) & (step == last))
    def _():
        copy.wait()

    for place, parts in enumerate(widths):
        chunk_outs = [outs.pop(0) for _ in parts]

        @pl.when((turn == place) & (step == last))
        def _():
            rows_in = jnp.concatenate([attended[s] for s in range(attended.shape[0])], axis=1)
            first_col = 0
            for out_ref in chunk_outs:
                for at in range(0, out_ref.shape[1], 256):
                    cols = weight[:, first_col + at : first_col + at + 256]
                    part = jnp.dot(rows_in, cols, preferred_element_type=F32)
                    out_ref[:, at : at + 256] = part.astype(out_ref.dtype)
                first_col += out_ref.shape[1]


def chosen_and_project(first_chunk, widths, rows, meta, slots, dead, queries, gates, near, pools, out_weight):
    tokens, width = queries.shape
    heads = width // QK
    at_once = 8 if heads % 8 == 0 else 2
    steps = heads // at_once
    whole = lambda x: pl.BlockSpec(x.shape, lambda i, p, *_: (0,) * x.ndim)
    outs = [jax.ShapeDtypeStruct((rows, width), BF16) for chunk in widths for width in chunk]
    return pl.pallas_call(
        functools.partial(chosen_kernel, heads, (first_chunk, widths)),
        grid_spec=pltpu.PrefetchScalarGridSpec(
            num_scalar_prefetch=3,
            grid=(len(widths), steps),
            in_specs=[
                pl.BlockSpec((rows, at_once * QK), lambda i, p, m, *_: (m[2 + first_chunk + i], p)),
                pl.BlockSpec((rows, 128), lambda i, p, m, *_: (m[2 + first_chunk + i], 0)),
                pl.BlockSpec((rows, at_once * DV), lambda i, p, m, *_: (m[2 + first_chunk + i], p)),
            ]
            + [VMEM_SPEC] * len(pools)
            + [pl.BlockSpec(memory_space=pl.ANY)],
            out_specs=[whole(out) for out in outs],
            scratch_shapes=[
                pltpu.VMEM((PICKS * KBLK, 256), BF16),
                pltpu.VMEM((256, PICKS * KBLK), BF16),
                pltpu.VMEM((256, PICKS * KBLK), BF16),
                pltpu.VMEM((PICKS * KBLK, 256), BF16),
                pltpu.VMEM((steps, rows, at_once * DV), BF16),
                pltpu.VMEM(out_weight.shape, BF16),
                pltpu.SemaphoreType.DMA,
            ],
        ),
        out_shape=outs,
        compiler_params=pltpu.CompilerParams(vmem_limit_bytes=VMEM_LIMIT),
        cost_estimate=pl.CostEstimate(
            flops=rows * heads * PICKS * KBLK * 64,
            bytes_accessed=out_weight.size,
            transcendentals=0,
        ),
        name="chosen_and_project",
    )(meta, slots, dead, queries, gates, near, *pools, out_weight)


VMEM_SPEC = pl.BlockSpec(memory_space=pltpu.VMEM)


def single_step(kernel, name, scalars, arrays, outs, scratch=(), in_spec=None, out_spec=None):
    whole = lambda x: pl.BlockSpec(x.shape, lambda i, *_: (0,) * len(x.shape))
    return pl.pallas_call(
        kernel,
        grid_spec=pltpu.PrefetchScalarGridSpec(
            num_scalar_prefetch=len(scalars),
            grid=(1,),
            in_specs=[in_spec or whole(x) for x in arrays],
            out_specs=[out_spec or whole(x) for x in outs],
            scratch_shapes=list(scratch),
        ),
        out_shape=outs,
        compiler_params=pltpu.CompilerParams(vmem_limit_bytes=VMEM_LIMIT),
        name=name,
    )(*scalars, *arrays)


def local(
    queries,
    key_rows,
    value_rows,
    comp_key_weight,
    comp_value_weight,
    block_picks,
    gate_logits,
    out_weight,
):
    tokens = queries.shape[0]
    heads = queries.shape[1] // QK
    n_ctx, n_head = lax.axis_size("ctx"), lax.axis_size("head")
    shard, head_at = lax.axis_index("ctx"), lax.axis_index("head")
    group = head_at * heads // (HEADS // GROUPS)
    per_owner = tokens // KBLK
    lists = tokens // QBLK
    folds = tokens // CBLK
    groups = n_ctx // 2
    rim_blocks = WINDOW // KBLK
    packed_rows = per_owner * BROWS
    bf16 = lambda *shape: jax.ShapeDtypeStruct(shape, BF16)

    chips = n_head // 2
    chip, core = head_at // 2, lax.rem(head_at, 2)
    order = []
    for step in list(range(1, chips)) + [0]:
        target = lax.rem(chip + step, chips) * 2
        order += [target + 1 - core, target + core]
    where = jnp.stack([group, shard, shard * tokens] + order).astype(jnp.int32)
    rim_rows = rim_blocks * BROWS
    int32 = lambda *shape: jax.ShapeDtypeStruct(shape, jnp.int32)
    prep_out = [bf16(packed_rows + 3 * folds, 128), bf16(rim_rows, 128)]
    prep_out += [int32(1, n_ctx * lists), int32(lists, 2 * PICKS), int32(lists, 2 * PICKS)]
    prep_out += [bf16(256, tokens)] * 2 + [bf16(tokens, 256)]
    packed, rim, named, slots, dead, even, odd, val = pl.pallas_call(
        prep_kernel,
        grid_spec=pltpu.PrefetchScalarGridSpec(
            num_scalar_prefetch=1,
            grid=(1,),
            in_specs=[
                pl.BlockSpec(block_picks.shape, lambda i, g: (0, 0, 0)),
                pl.BlockSpec((tokens, PAIR), lambda i, g: (0, g[0] // 2)),
                pl.BlockSpec((tokens, DV), lambda i, g: (0, g[0])),
                pl.BlockSpec((CBLK, PAIR), lambda i, g: (0, g[0] // 2)),
                pl.BlockSpec((CBLK, DV), lambda i, g: (0, g[0])),
            ],
            out_specs=[pl.BlockSpec(x.shape, lambda i, g: (0, 0)) for x in prep_out[:5]]
            + [VMEM_SPEC] * 3,
        ),
        out_shape=prep_out,
        compiler_params=pltpu.CompilerParams(vmem_limit_bytes=VMEM_LIMIT),
        name="prep",
    )(where, block_picks, key_rows, value_rows, comp_key_weight, comp_value_weight)
    other = lax.ppermute(packed, "ctx", [(i, i ^ 1) for i in range(n_ctx)])
    named = [named] + [
        lax.ppermute(named, "ctx", [(i, i - 2 * d) for i in range(2 * d, n_ctx)])
        for d in range(1, groups)
    ]
    far_rim = lax.ppermute(rim, "ctx", [(i, i + 1) for i in range(1, n_ctx - 1, 2)])

    gates = jax.nn.sigmoid(gate_logits).reshape(tokens, 3 * heads)
    gates = jnp.pad(gates, ((0, 0), (0, 128 - 3 * heads)))
    sent = bf16(lists * BROWS + 3 * folds, 128)

    def pack(beside, lists_in, rows):
        return single_step(
            functools.partial(pack_kernel, lists, beside),
            "pack",
            [where, *lists_in],
            [rows],
            [sent] * len(lists_in),
            [pltpu.SemaphoreType.DMA((len(lists_in) * (lists + 1),))],
            pl.BlockSpec(memory_space=pl.ANY),
        )

    def ahead(send, distance):
        return lax.ppermute(send, "ctx", [(i, i + 2 * distance) for i in range(n_ctx - 2 * distance)])

    own_sends = pack(False, named[1:], packed)
    own_sends, even = lax.optimization_barrier((own_sends, even))
    from_same = [ahead(send, d) for d, send in enumerate(own_sends, 1)]

    reach = WINDOW // QBLK
    near = functools.partial(near_branch, where=where, queries=queries, gates=gates)
    mixed = near(reach, lists - reach, keys=(even, odd, val), rims=None, prior=None)

    other, mixed = lax.optimization_barrier((other, mixed))
    beside, *other_sends = pack(True, named, other)
    from_other = [ahead(send, d) for d, send in enumerate(other_sends, 1)]

    mixed = near(0, reach, keys=(even, odd, val), rims=(other, far_rim), prior=mixed)

    received = [beside] + [x for both in zip(from_same, from_other) for x in both]
    pools = single_step(
        functools.partial(pool_kernel, groups, lists),
        "pool",
        [where],
        [packed] + received,
        [bf16(n_ctx * lists * KBLK, 256), bf16(n_ctx * lists * KBLK, DV)]
        + [bf16(256, n_ctx * folds)] * 2
        + [bf16(n_ctx * folds, 256)],
        [pltpu.VMEM((n_ctx * folds, 256), BF16)],
        out_spec=VMEM_SPEC,
    )
    rows = tokens // n_head
    across = [(i, i ^ 1) for i in range(n_head)]

    model = out_weight.shape[1]

    def project(first_chunk, widths):
        return chosen_and_project(
            first_chunk, widths, rows, where, slots, dead, queries, gates, mixed, pools, out_weight
        )

    sums = []
    for step in range(chips - 1):
        other = lax.ppermute(project(1 + 2 * step, [[model]])[0], "head", across)
        mine = project(2 + 2 * step, [[model]])[0]
        summed = (mine.astype(F32) + other.astype(F32)).astype(BF16)
        summed, where = lax.optimization_barrier((summed, where))
        sums.append(summed)
    *passed, kept = project(n_head - 1, [[model // 2] * 2, [model]])
    arrived = [jnp.concatenate([lax.ppermute(x, "head", across) for x in passed], axis=1)]
    for step, summed in enumerate(sums, 1):
        route = [(i, (i + 2 * step) % n_head) for i in range(n_head)]
        arrived.append(lax.ppermute(summed, "head", route))
    total = kept.astype(F32)
    for part in arrived:
        total = total + part.astype(F32)
    return total.astype(BF16)


def solution(mesh):
    placed = (
        P("ctx", "head"),
        P("ctx", None),
        P("ctx", None),
        P(),
        P(),
        P("ctx", None, None),
        P("ctx", None, "head"),
        P("head", None),
    )
    return jax.shard_map(
        local, mesh=mesh, in_specs=placed, out_specs=P(("ctx", "head"), None), check_vma=False
    )
```

```python
import functools

import jax
import jax.numpy as jnp
from jax import lax
from jax.experimental import pallas as pl
from jax.experimental.pallas import tpu as pltpu
from jax.sharding import PartitionSpec as P

HEADS = 64
GROUPS = 4
QK = 192
DV = 128
CBLK = 32
KBLK = 64
PICKS = 16
WINDOW = 512
QBLK = 256
PAIR = 2 * QK
BROWS = KBLK + KBLK // 2 + KBLK
VMEM_LIMIT = 50 * 1024 * 1024
NEG = -1e30
SCALE = QK ** (-0.5) * 1.4426950408889634
LOW_TOTAL, HIGH_TOTAL = 2.0**-60, 2.0**100
TILE = 256
NT = (((1,), (1,)), ((), ()))
F32 = jnp.float32
BF16 = jnp.bfloat16


def half_lanes(rows):
    return lax.broadcasted_iota(jnp.int32, (rows, 128), 1) < 64


def swap_halves(x):
    return pltpu.roll(x, 64, 1)


def turned(keys):
    row, col = iota(256, 256, 0), iota(256, 256, 1)
    unit = (row == col).astype(BF16)
    even = lax.dot_general(unit, keys, NT, preferred_element_type=F32).astype(BF16)
    return even, lower(even)


def lower(even):
    return jnp.concatenate([jnp.zeros((64, even.shape[1]), BF16), even[:QK]], axis=0)


def with_ones(values):
    return jnp.concatenate([values, jnp.ones_like(values)], axis=1)


def plan(group, shard, per_owner, picks_ref, lists_ref, slots_ref, dead_ref):
    lists = picks_ref.shape[0]
    total = lists_ref.shape[1] // lists * per_owner
    width = slots_ref.shape[1]
    picks = jnp.zeros((lists, PICKS), jnp.int32)
    for each in range(picks_ref.shape[1]):
        picks = jnp.where(group == each, picks_ref[:, each, :], picks)
    block = iota(lists, total, 1)
    hits = [block == picks[:, entry : entry + 1] for entry in range(PICKS)]
    named = functools.reduce(jnp.logical_or, hits).astype(F32)
    named = jnp.broadcast_to(jnp.max(named, axis=0, keepdims=True), (8, total))
    row, col = iota(total, total, 0), iota(total, total, 1)
    before = (lax.div(row, per_owner) == lax.div(col, per_owner)) & (row < col)
    rank = jnp.dot(named, before.astype(F32), preferred_element_type=F32)
    rank = jnp.minimum(rank, float(lists - 1))
    inside = lax.rem(iota(8, total, 1), per_owner).astype(F32)
    found = jnp.zeros((8, lists_ref.shape[1]), F32)
    row, col = iota(total, lists_ref.shape[1], 0), iota(total, lists_ref.shape[1], 1)
    for place in range(lists):
        to = (col == lax.div(row, per_owner) * lists + place).astype(F32)
        value = jnp.where(rank == float(place), named * inside, 0.0)
        found = found + jnp.dot(value, to, preferred_element_type=F32)
    lists_ref[...] = found[:1].astype(jnp.int32)

    owner = lax.div(block, per_owner)
    turn = (lax.div(shard, 2) - lax.div(owner, 2)) * 2 + ((owner ^ shard) & 1)
    slot = jnp.clip(turn * lists + rank[:lists].astype(jnp.int32), 0, lists_ref.shape[1] - 1)
    slot = slot.astype(F32)
    first = shard * per_owner + iota(lists, 1, 0) * (QBLK // KBLK)
    own = block == first

    def pick_out(hit, values):
        return jnp.sum(jnp.where(hit, values, 0.0), axis=1, keepdims=True)

    lane = iota(lists, width, 1)
    slots = jnp.where(lane == 0, pick_out(own, slot), 0.0)
    dead = jnp.zeros((lists, width), F32)
    seen = own.astype(F32)
    at = jnp.ones((lists, 1), jnp.int32)
    met = jnp.zeros((lists, 1), jnp.int32)
    for entry, hit in enumerate(hits):
        pick = picks[:, entry : entry + 1]
        is_own = (pick == first).astype(jnp.int32)
        gone = jnp.maximum(pick_out(hit, seen), (pick > first).astype(F32))
        slots = jnp.where(lane == at, pick_out(hit, slot), slots)
        dead = jnp.where(lane == at, gone, dead)
        seen = jnp.maximum(seen, hit.astype(F32))
        at = at + 1 - is_own * (1 - met)
        met = jnp.maximum(met, is_own)
    slots_ref[...] = slots.astype(jnp.int32)
    dead_ref[...] = dead.astype(jnp.int32)


def prep_kernel(
    where_ref,
    picks_in,
    keys_in,
    values_in,
    kw_in,
    vw_in,
    packed_ref,
    rim_ref,
    lists_ref,
    slots_ref,
    dead_ref,
    even_ref,
    odd_ref,
    val_ref,
    picks_ref,
    keys_ref,
    values_ref,
    kw_ref,
    vw_ref,
    sems,
):
    group, shard = where_ref[0], where_ref[1]
    pair = pl.ds(pl.multiple_of(lax.div(group, 2) * PAIR, 128), PAIR)
    single = pl.ds(pl.multiple_of(group * DV, 128), DV)
    copies = [
        pltpu.make_async_copy(source, target, sems.at[i])
        for i, (source, target) in enumerate(
            [
                (picks_in, picks_ref),
                (keys_in.at[:, pair], keys_ref),
                (values_in.at[:, single], values_ref),
                (kw_in.at[:, pair], kw_ref),
                (vw_in.at[:, single], vw_ref),
            ]
        )
    ]
    for copy in copies:
        copy.start()
    copies[0].wait()
    plan(group, shard, keys_ref.shape[0] // KBLK, picks_ref, lists_ref, slots_ref, dead_ref)
    for copy in copies[1:]:
        copy.wait()
    odd = lax.rem(group, 2) == 1

    def own_columns(ref):
        t0 = ref[:, :128].astype(F32)
        t1 = ref[:, 128:256].astype(F32)
        t2 = ref[:, 256:].astype(F32)
        r1, r2 = swap_halves(t1), swap_halves(t2)
        left = half_lanes(t0.shape[0])
        low = jnp.where(odd, jnp.where(left, r1, r2), t0)
        high = jnp.where(left, jnp.where(odd, r2, t1), 0.0)
        return low, high

    low, high = own_columns(keys_ref)
    values = values_ref[...]
    rows = low.shape[0]
    count = rows // KBLK
    high3 = high.reshape(count, KBLK, 128)
    packed_high = high3[:, : KBLK // 2] + swap_halves(
        high3[:, KBLK // 2 :].reshape(count * KBLK // 2, 128)
    ).reshape(count, KBLK // 2, 128)
    even = jnp.concatenate([low.astype(BF16), high.astype(BF16)], axis=1)
    even_ref[...], odd_ref[...] = turned(even)
    val_ref[...] = with_ones(values)
    for block in range(count):
        at = block * BROWS
        token = slice(block * KBLK, block * KBLK + KBLK)
        packed_ref[at : at + KBLK] = low[token].astype(BF16)
        packed_ref[at + KBLK : at + KBLK + KBLK // 2] = packed_high[block].astype(BF16)
        packed_ref[at + KBLK + KBLK // 2 : at + BROWS] = values[token]
    rim_rows = rim_ref.shape[0]
    rim_ref[...] = packed_ref[count * BROWS - rim_rows : count * BROWS]

    wlow, whigh = own_columns(kw_ref)
    folds = rows // CBLK

    def fold(x, w):
        return jnp.sum(x.reshape(folds, CBLK, 128) * w[None], axis=1).astype(BF16)

    at = count * BROWS
    packed_ref[at : at + folds] = fold(low, wlow)
    packed_ref[at + folds : at + 2 * folds] = fold(high, whigh)
    packed_ref[at + 2 * folds :] = fold(values.astype(F32), vw_ref[...])


def pack_kernel(lists, beside, where_ref, *refs):
    count = len(refs) // 2
    named, ref, outs = refs[:count], refs[count], refs[count + 1 :]
    shard = where_ref[1]
    owner = shard + 1 - 2 * lax.rem(shard, 2) if beside else shard
    data = ref.shape[0] - (outs[0].shape[0] - lists * BROWS)
    for blocks, out in zip(named, outs):
        for place in range(lists):
            at = pl.multiple_of(blocks[0, owner * lists + place] * BROWS, 16)
            out[place * BROWS : (place + 1) * BROWS] = ref[pl.ds(at, BROWS)]
        out[lists * BROWS :] = ref[data:]


def unpack(ref, at, count, step=1):
    lows, packed, values = [], [], []
    for block in range(count):
        first = at + block * step * BROWS
        lows.append(ref[first : first + KBLK])
        packed.append(ref[first + KBLK : first + KBLK + KBLK // 2])
        values.append(ref[first + KBLK + KBLK // 2 : first + BROWS])
    packed = jnp.concatenate(packed, axis=0)
    row, col = iota(128, 256, 0), iota(128, 256, 1)
    take = (row == jnp.where(col < 128, col, col - 64)) & (lax.rem(col, 128) < 64)
    both = jnp.dot(packed, take.astype(BF16), preferred_element_type=F32).astype(BF16)
    half = KBLK // 2
    highs = []
    for block in range(count):
        rows = slice(block * half, block * half + half)
        highs += [both[rows, :128], both[rows, 128:]]
    even = jnp.concatenate(
        [jnp.concatenate(lows, axis=0), jnp.concatenate(highs, axis=0)], axis=1
    )
    return even, jnp.concatenate(values, axis=0)


def fill_rim(shard, near_ref, far_ref, own, ext):
    rim_blocks = WINDOW // KBLK
    even_in, odd_in, val_in = own
    even_ref, odd_ref, val_ref = ext
    even_ref[:, WINDOW:] = even_in[:, :WINDOW]
    odd_ref[:, WINDOW:] = odd_in[:, :WINDOW]
    val_ref[WINDOW:] = val_in[:WINDOW]
    use_near = lax.rem(shard, 2) == 1
    rim_end = near_ref.shape[0] // BROWS * BROWS
    near_rim = near_ref[rim_end - far_ref.shape[0] : rim_end]

    @pl.when(shard > 0)
    def _():
        keys, values = unpack(jnp.where(use_near, near_rim, far_ref[...]), 0, rim_blocks)
        even_ref[:, :WINDOW], odd_ref[:, :WINDOW] = turned(keys)
        val_ref[:WINDOW] = with_ones(values)

    @pl.when(shard == 0)
    def _():
        even = jnp.broadcast_to(even_in[:, :1].astype(F32), (256, WINDOW)).astype(BF16)
        even_ref[:, :WINDOW], odd_ref[:, :WINDOW] = even, lower(even)
        val_ref[:WINDOW] = jnp.zeros((WINDOW, 256), BF16)


def pool_kernel(groups, lists, where_ref, own_ref, *refs):
    sent = 2 * groups - 1
    ins, (key_ref, val_ref, ceven_ref, codd_ref, cval_ref, folded) = refs[:sent], refs[sent:]
    shard = where_ref[1]
    parity = lax.rem(shard, 2)
    base = shard - parity
    rows = lists * KBLK
    folds = (ins[0].shape[0] - lists * BROWS) // 3
    folded[...] = jnp.zeros_like(folded)
    cval_ref[...] = jnp.zeros_like(cval_ref)

    def fill(place, owner, ref, step, fold_at):
        keys, values = unpack(ref, 0, lists, step)
        at = slice(place * rows, place * rows + rows)
        key_ref[at] = keys
        val_ref[at] = values
        low = ref[fold_at : fold_at + folds]
        high = ref[fold_at + folds : fold_at + 2 * folds]
        owned = pl.ds(pl.multiple_of(owner * folds, 32), folds)
        folded[owned] = jnp.concatenate([low, high], axis=1)
        cval_ref[owned] = with_ones(ref[fold_at + 2 * folds : fold_at + 3 * folds])

    fill(0, shard, own_ref, QBLK // KBLK, own_ref.shape[0] - 3 * folds)
    fill(1, base + 1 - parity, ins[0], 1, lists * BROWS)
    for distance in range(1, groups):

        @pl.when(base >= 2 * distance)
        def _():
            for side in range(2):
                owner = base - 2 * distance + (parity if side == 0 else 1 - parity)
                fill(2 * distance + side, owner, ins[2 * distance - 1 + side], 1, lists * BROWS)

    ceven_ref[...], codd_ref[...] = turned(folded[...])


def iota(rows, cols, axis):
    return lax.broadcasted_iota(jnp.int32, (rows, cols), axis)


def scores_of(q, keys, mask):
    scores = jnp.dot(q, keys, preferred_element_type=F32)
    return scores if mask is None else mask(scores)


def in_range(total):
    good = jnp.where((total >= LOW_TOTAL) & (total <= HIGH_TOTAL), 1.0, 0.0)
    return jnp.min(good.reshape(-1, 8, DV), axis=0)


def over_heads(pairs, load, branches, finish):
    def sums(weights, values):
        out = jnp.dot(weights, values(), preferred_element_type=F32)
        return out[:, :DV], out[:, DV:]

    at_once = 2 if pairs % 2 == 0 else 1
    units = [(pair, side) for pair in range(0, pairs, at_once) for side in range(2)]
    worst, held = [], None
    for now, unit in zip([None] + units, units + [None]):
        q = None if unit is None else load(*unit, at_once)
        fresh, parts = [], []
        for at, (tiles, values) in enumerate(branches):
            weights, ahead = [], []
            for place, (keys, mask) in enumerate(tiles):
                if q is not None:
                    ahead.append(scores_of(q, keys(unit[1]), mask))
                if held is not None:
                    weights.append(jnp.exp2(held[at][place] * SCALE).astype(BF16))
            fresh.append(ahead)
            parts.append((weights, values))
        if held is not None:
            parts = [sums(jnp.concatenate(w, axis=1), values) for w, values in parts]
            worst += [in_range(x) for x in finish(*now, at_once, parts)]
        held = fresh

    @pl.when(jnp.min(functools.reduce(jnp.minimum, worst)) < 0.5)
    def _():
        def exact(pair, _):
            for side in range(2):
                q = load(pair, side, 1)
                parts = []
                for tiles, values in branches:
                    scores = [scores_of(q, keys(side), mask) for keys, mask in tiles]
                    scores = jnp.concatenate(scores, axis=1)
                    top = jnp.max(scores, axis=1, keepdims=True)
                    shifted = (scores - jnp.maximum(top, -1e28)) * SCALE
                    parts.append(sums(jnp.exp2(shifted).astype(BF16), values))
                finish(pair, side, 1, parts)
            return 0

        lax.fori_loop(0, pairs, exact, 0)


def aligned(at):
    return at if isinstance(at, int) else pl.multiple_of(at, 128)


def query_loader(q_ref):
    def load(pair, side, n):
        at = [aligned((pair + p) * PAIR + side * 128) for p in range(n)]
        return jnp.concatenate([q_ref[:, pl.ds(x, 256)] for x in at], axis=0)

    return load


def head_columns(pair, side):
    return pl.ds(aligned(pair * 2 * DV + side * DV), DV)


def gate_loader(gate_ref, first, heads):
    turned = pltpu.roll(gate_ref[...], lax.rem(128 - first, 128), 1)

    def load(pair, side, n, branch):
        if isinstance(pair, int):
            local, at = turned, branch * heads + side + 2 * pair
        else:
            local, at = pltpu.roll(turned, lax.rem(128 - 2 * pair, 128), 1), branch * heads + side
        columns = [local[:, at + 2 * p : at + 2 * p + 1] for p in range(n)]
        shape = (turned.shape[0], DV)
        return jnp.concatenate([jnp.broadcast_to(x, shape) for x in columns], axis=0)

    return load


def stacked(x, times):
    return jnp.concatenate([x] * times, axis=0) if times > 1 else x


def repeated(keep, rows):
    return stacked(keep, rows // keep.shape[0])


def near_kernel(heads, rim, where_ref, q_ref, gate_ref, *refs):
    keys = refs[:3]
    if rim:
        out_ref, ext = refs[6], refs[7:]

        @pl.when((pl.program_id(0) == 0) & (pl.program_id(1) == 0))
        def _():
            fill_rim(where_ref[1], refs[3], refs[4], keys, ext)

        keys = ext
    else:
        out_ref = refs[3]
    count = q_ref.shape[1] // QK
    gate = gate_loader(gate_ref, pl.program_id(1) * count, heads)
    base = pl.multiple_of(pl.program_id(0) * QBLK, QBLK)
    row, col = iota(QBLK, QBLK, 0), iota(QBLK, QBLK, 1)

    def tile(place, mask):
        return (lambda side: keys[side][:, pl.ds(base + place * QBLK, QBLK)]), mask

    def finish(pair, side, n, parts):
        ((num, den),) = parts
        total = gate(pair, side, n, 2) * (num / den)
        for p in range(n):
            part = total[p * QBLK : (p + 1) * QBLK]
            out_ref[:, head_columns(pair + p, side)] = part.astype(BF16)
        return [den]

    tiles = [
        tile(0, lambda x: jnp.where(repeated(col >= row, x.shape[0]), x, NEG)),
        tile(1, None),
        tile(2, lambda x: jnp.where(repeated(col <= row, x.shape[0]), x, NEG)),
    ]
    values = lambda: keys[2][pl.ds(base, WINDOW + QBLK)]
    over_heads(count // 2, query_loader(q_ref), [(tiles, values)], finish)


def near_branch(first_block, block_count, where, queries, gates, keys, rims, prior):
    tokens, width = queries.shape
    heads = width // QK
    at_once = 8 if heads % 8 == 0 else 2
    row_block = lambda i, p, *_: (i + first_block, p)
    operands = [queries, gates, *keys]
    specs = [
        pl.BlockSpec((QBLK, at_once * QK), row_block),
        pl.BlockSpec((QBLK, 128), lambda i, p, *_: (i + first_block, 0)),
    ]
    specs += [VMEM_SPEC] * len(keys)
    alias, scratch = {}, []
    if rims is not None:
        other, far = rims
        operands += [other, far, prior]
        specs += [VMEM_SPEC, VMEM_SPEC, pl.BlockSpec(memory_space=pl.ANY)]
        alias = {len(operands): 0}
        scratch = [pltpu.VMEM((256, 2 * WINDOW), BF16)] * 2 + [pltpu.VMEM((2 * WINDOW, 256), BF16)]
    rows = block_count * QBLK * heads
    return pl.pallas_call(
        functools.partial(near_kernel, heads, rims is not None),
        grid_spec=pltpu.PrefetchScalarGridSpec(
            num_scalar_prefetch=1,
            grid=(block_count, heads // at_once),
            in_specs=specs,
            out_specs=pl.BlockSpec((QBLK, at_once * DV), row_block),
            scratch_shapes=scratch,
        ),
        out_shape=jax.ShapeDtypeStruct((tokens, heads * DV), BF16),
        input_output_aliases=alias,
        compiler_params=pltpu.CompilerParams(vmem_limit_bytes=VMEM_LIMIT),
        cost_estimate=pl.CostEstimate(
            flops=rows * (WINDOW + QBLK) * 64,
            bytes_accessed=rows * (2 * QK + 4 * DV),
            transcendentals=0,
        ),
        name="near_branch",
    )(where, *operands)


def chosen_kernel(heads, span, *refs):
    first_chunk, widths = span
    out_count = sum(len(w) for w in widths)
    meta_ref, slots_ref, dead_ref, q_ref, gate_ref, near_ref = refs[:6]
    (key_pool, val_pool), cfold, weight_ref = refs[6:8], refs[8:11], refs[11]
    outs = list(refs[12 : 12 + out_count])
    gathered, even, odd, val, attended, weight, weight_sem = refs[12 + out_count :]
    keys = (even, odd)
    turn, step = pl.program_id(0), pl.program_id(1)
    last = pl.num_programs(1) - 1
    rows = q_ref.shape[0]
    count = q_ref.shape[1] // QK
    chunk_start = meta_ref[2 + first_chunk + turn] * rows
    list_at = lax.div(chunk_start, QBLK)
    first_row = lax.rem(chunk_start, QBLK)
    position = meta_ref[2] + chunk_start
    copy = pltpu.make_async_copy(weight_ref, weight, weight_sem)

    @pl.when(step == 0)
    def _():
        for slot in range(PICKS):
            source = pl.multiple_of(slots_ref[list_at, slot] * KBLK, KBLK)
            gathered[slot * KBLK : (slot + 1) * KBLK] = key_pool[pl.ds(source, KBLK)]
            val[slot * KBLK : (slot + 1) * KBLK] = with_ones(val_pool[pl.ds(source, KBLK)])
        for slot in range(1, PICKS):

            @pl.when(dead_ref[list_at, slot] == 1)
            def _():
                at = slice(slot * KBLK, (slot + 1) * KBLK)
                gathered[at] = jnp.broadcast_to(gathered[:1], (KBLK, 256))
                val[at] = jnp.zeros((KBLK, 256), BF16)

        even[...], odd[...] = turned(gathered[...])

    @pl.when((turn == 0) & (step == 0))
    def _():
        copy.start()

    gate = gate_loader(gate_ref, step * count, heads)
    row = iota(rows, TILE, 0)
    col = iota(rows, TILE, 1)
    own_keep = (col >= KBLK) | (col <= row + first_row)

    def own_mask(scores):
        own = jnp.where(repeated(own_keep[:, :128], scores.shape[0]), scores[:, :128], NEG)
        return jnp.concatenate([own, scores[:, 128:]], axis=1)

    def comp_mask(place):
        ends = (col + place * TILE + 1) * CBLK - 1
        return lambda x: jnp.where(repeated(ends <= row + position, x.shape[0]), x, NEG)

    def tile(refs, place, mask):
        return (lambda side: refs[side][:, place * TILE : (place + 1) * TILE]), mask

    chosen = [tile(keys, p, own_mask if p == 0 else None) for p in range(PICKS * KBLK // TILE)]
    folded = [tile(cfold, p, comp_mask(p)) for p in range(cfold[2].shape[0] // TILE)]
    empty = row[:, :DV] + position < CBLK - 1

    def finish(pair, side, n, parts):
        (num, den), (folded_num, folded_den) = parts
        folded_den = jnp.where(stacked(empty, n), 1.0, folded_den)
        total = gate(pair, side, n, 1) * (num / den)
        total = total + gate(pair, side, n, 0) * (folded_num / folded_den)
        for p in range(n):
            cols = head_columns(pair + p, side)
            mixed = near_ref[:, cols].astype(F32) + total[p * rows : (p + 1) * rows]
            attended[step, :, cols] = mixed.astype(BF16)
        return [den, folded_den]

    branches = [(chosen, lambda: val[...]), (folded, lambda: cfold[2][...])]
    over_heads(count // 2, query_loader(q_ref), branches, finish)

    @pl.when((turn == 0) & (step == last))
    def _():
        copy.wait()

    for place, parts in enumerate(widths):
        chunk_outs = [outs.pop(0) for _ in parts]

        @pl.when((turn == place) & (step == last))
        def _():
            rows_in = jnp.concatenate([attended[s] for s in range(attended.shape[0])], axis=1)
            first_col = 0
            for out_ref in chunk_outs:
                for at in range(0, out_ref.shape[1], 256):
                    cols = weight[:, first_col + at : first_col + at + 256]
                    part = jnp.dot(rows_in, cols, preferred_element_type=F32)
                    out_ref[:, at : at + 256] = part.astype(out_ref.dtype)
                first_col += out_ref.shape[1]


def chosen_and_project(first_chunk, widths, rows, meta, slots, dead, queries, gates, near, pools, out_weight):
    tokens, width = queries.shape
    heads = width // QK
    at_once = 8 if heads % 8 == 0 else 2
    steps = heads // at_once
    whole = lambda x: pl.BlockSpec(x.shape, lambda i, p, *_: (0,) * x.ndim)
    outs = [jax.ShapeDtypeStruct((rows, width), BF16) for chunk in widths for width in chunk]
    return pl.pallas_call(
        functools.partial(chosen_kernel, heads, (first_chunk, widths)),
        grid_spec=pltpu.PrefetchScalarGridSpec(
            num_scalar_prefetch=3,
            grid=(len(widths), steps),
            in_specs=[
                pl.BlockSpec((rows, at_once * QK), lambda i, p, m, *_: (m[2 + first_chunk + i], p)),
                pl.BlockSpec((rows, 128), lambda i, p, m, *_: (m[2 + first_chunk + i], 0)),
                pl.BlockSpec((rows, at_once * DV), lambda i, p, m, *_: (m[2 + first_chunk + i], p)),
            ]
            + [VMEM_SPEC] * len(pools)
            + [pl.BlockSpec(memory_space=pl.ANY)],
            out_specs=[whole(out) for out in outs],
            scratch_shapes=[
                pltpu.VMEM((PICKS * KBLK, 256), BF16),
                pltpu.VMEM((256, PICKS * KBLK), BF16),
                pltpu.VMEM((256, PICKS * KBLK), BF16),
                pltpu.VMEM((PICKS * KBLK, 256), BF16),
                pltpu.VMEM((steps, rows, at_once * DV), BF16),
                pltpu.VMEM(out_weight.shape, BF16),
                pltpu.SemaphoreType.DMA,
            ],
        ),
        out_shape=outs,
        compiler_params=pltpu.CompilerParams(vmem_limit_bytes=VMEM_LIMIT),
        cost_estimate=pl.CostEstimate(
            flops=rows * heads * PICKS * KBLK * 64,
            bytes_accessed=out_weight.size,
            transcendentals=0,
        ),
        name="chosen_and_project",
    )(meta, slots, dead, queries, gates, near, *pools, out_weight)


VMEM_SPEC = pl.BlockSpec(memory_space=pltpu.VMEM)


def single_step(kernel, name, scalars, arrays, outs, scratch=(), in_spec=None, out_spec=None):
    whole = lambda x: pl.BlockSpec(x.shape, lambda i, *_: (0,) * len(x.shape))
    return pl.pallas_call(
        kernel,
        grid_spec=pltpu.PrefetchScalarGridSpec(
            num_scalar_prefetch=len(scalars),
            grid=(1,),
            in_specs=[in_spec or whole(x) for x in arrays],
            out_specs=[out_spec or whole(x) for x in outs],
            scratch_shapes=list(scratch),
        ),
        out_shape=outs,
        compiler_params=pltpu.CompilerParams(vmem_limit_bytes=VMEM_LIMIT),
        name=name,
    )(*scalars, *arrays)


def local(
    queries,
    key_rows,
    value_rows,
    comp_key_weight,
    comp_value_weight,
    block_picks,
    gate_logits,
    out_weight,
):
    tokens = queries.shape[0]
    heads = queries.shape[1] // QK
    n_ctx, n_head = lax.axis_size("ctx"), lax.axis_size("head")
    shard, head_at = lax.axis_index("ctx"), lax.axis_index("head")
    group = head_at * heads // (HEADS // GROUPS)
    per_owner = tokens // KBLK
    lists = tokens // QBLK
    folds = tokens // CBLK
    groups = n_ctx // 2
    rim_blocks = WINDOW // KBLK
    packed_rows = per_owner * BROWS
    bf16 = lambda *shape: jax.ShapeDtypeStruct(shape, BF16)

    chips = n_head // 2
    chip, core = head_at // 2, lax.rem(head_at, 2)
    order = []
    for step in list(range(1, chips)) + [0]:
        target = lax.rem(chip + step, chips) * 2
        order += [target + 1 - core, target + core]
    where = jnp.stack([group, shard, shard * tokens] + order).astype(jnp.int32)
    rim_rows = rim_blocks * BROWS
    int32 = lambda *shape: jax.ShapeDtypeStruct(shape, jnp.int32)
    prep_out = [bf16(packed_rows + 3 * folds, 128), bf16(rim_rows, 128)]
    prep_out += [int32(1, n_ctx * lists), int32(lists, 2 * PICKS), int32(lists, 2 * PICKS)]
    prep_out += [bf16(256, tokens)] * 2 + [bf16(tokens, 256)]
    packed, rim, named, slots, dead, even, odd, val = pl.pallas_call(
        prep_kernel,
        grid_spec=pltpu.PrefetchScalarGridSpec(
            num_scalar_prefetch=1,
            grid=(1,),
            in_specs=[pl.BlockSpec(memory_space=pltpu.HBM)] * 5,
            out_specs=[VMEM_SPEC] * 2
            + [pl.BlockSpec(x.shape, lambda i, g: (0, 0)) for x in prep_out[2:5]]
            + [VMEM_SPEC] * 3,
            scratch_shapes=[
                pltpu.VMEM(block_picks.shape, jnp.int32),
                pltpu.VMEM((tokens, PAIR), BF16),
                pltpu.VMEM((tokens, DV), BF16),
                pltpu.VMEM((CBLK, PAIR), F32),
                pltpu.VMEM((CBLK, DV), F32),
                pltpu.SemaphoreType.DMA((5,)),
            ],
        ),
        out_shape=prep_out,
        compiler_params=pltpu.CompilerParams(vmem_limit_bytes=51 * 1024 * 1024),
        name="prep",
    )(where, block_picks, key_rows, value_rows, comp_key_weight, comp_value_weight)
    other = lax.ppermute(packed, "ctx", [(i, i ^ 1) for i in range(n_ctx)])
    named = [named] + [
        lax.ppermute(named, "ctx", [(i, i - 2 * d) for i in range(2 * d, n_ctx)])
        for d in range(1, groups)
    ]
    far_rim = lax.ppermute(rim, "ctx", [(i, i + 1) for i in range(1, n_ctx - 1, 2)])

    gates = jax.nn.sigmoid(gate_logits).reshape(tokens, 3 * heads)
    gates = jnp.pad(gates, ((0, 0), (0, 128 - 3 * heads)))
    sent = bf16(lists * BROWS + 3 * folds, 128)

    def pack(beside, lists_in, rows):
        return single_step(
            functools.partial(pack_kernel, lists, beside),
            "pack",
            [where, *lists_in],
            [rows],
            [sent] * len(lists_in),
            in_spec=VMEM_SPEC,
            out_spec=VMEM_SPEC,
        )

    def ahead(send, distance):
        return lax.ppermute(send, "ctx", [(i, i + 2 * distance) for i in range(n_ctx - 2 * distance)])

    own_sends = pack(False, named[1:], packed)
    from_same = [ahead(send, d) for d, send in enumerate(own_sends, 1)]
    other, own_sends = lax.optimization_barrier((other, own_sends))
    beside, *other_sends = pack(True, named, other)
    other_sends, even = lax.optimization_barrier((other_sends, even))
    from_other = [ahead(send, d) for d, send in enumerate(other_sends, 1)]

    reach = WINDOW // QBLK
    near = functools.partial(near_branch, where=where, queries=queries, gates=gates)
    mixed = near(reach, lists - reach, keys=(even, odd, val), rims=None, prior=None)
    mixed = near(0, reach, keys=(even, odd, val), rims=(other, far_rim), prior=mixed)

    received = [beside] + [x for both in zip(from_same, from_other) for x in both]
    pools = single_step(
        functools.partial(pool_kernel, groups, lists),
        "pool",
        [where],
        [packed] + received,
        [bf16(n_ctx * lists * KBLK, 256), bf16(n_ctx * lists * KBLK, DV)]
        + [bf16(256, n_ctx * folds)] * 2
        + [bf16(n_ctx * folds, 256)],
        [pltpu.VMEM((n_ctx * folds, 256), BF16)],
        in_spec=VMEM_SPEC,
        out_spec=VMEM_SPEC,
    )
    rows = tokens // n_head
    across = [(i, i ^ 1) for i in range(n_head)]

    model = out_weight.shape[1]

    def project(first_chunk, widths):
        return chosen_and_project(
            first_chunk, widths, rows, where, slots, dead, queries, gates, mixed, pools, out_weight
        )

    sums = []
    for step in range(chips - 1):
        other = lax.ppermute(project(1 + 2 * step, [[model]])[0], "head", across)
        mine = project(2 + 2 * step, [[model]])[0]
        summed = (mine.astype(F32) + other.astype(F32)).astype(BF16)
        summed, where = lax.optimization_barrier((summed, where))
        sums.append(summed)
    *passed, kept = project(n_head - 1, [[model // 2] * 2, [model]])
    arrived = [jnp.concatenate([lax.ppermute(x, "head", across) for x in passed], axis=1)]
    for step, summed in enumerate(sums, 1):
        route = [(i, (i + 2 * step) % n_head) for i in range(n_head)]
        arrived.append(lax.ppermute(summed, "head", route))
    total = kept.astype(F32)
    for part in arrived:
        total = total + part.astype(F32)
    return total.astype(BF16)


def solution(mesh):
    placed = (
        P("ctx", "head"),
        P("ctx", None),
        P("ctx", None),
        P(),
        P(),
        P("ctx", None, None),
        P("ctx", None, "head"),
        P("head", None),
    )
    return jax.shard_map(
        local, mesh=mesh, in_specs=placed, out_specs=P(("ctx", "head"), None), check_vma=False
    )
```

```python
import functools

import jax
import jax.numpy as jnp
from jax import lax
from jax.experimental import pallas as pl
from jax.experimental.pallas import tpu as pltpu
from jax.sharding import PartitionSpec as P

HEADS = 64
GROUPS = 4
QK = 192
DV = 128
CBLK = 32
KBLK = 64
PICKS = 16
WINDOW = 512
QBLK = 256
PAIR = 2 * QK
BROWS = KBLK + KBLK // 2 + KBLK
VMEM_LIMIT = 50 * 1024 * 1024
NEG = -1e30
SCALE = QK ** (-0.5) * 1.4426950408889634
LOW_TOTAL, HIGH_TOTAL = 2.0**-60, 2.0**100
TILE = 256
NT = (((1,), (1,)), ((), ()))
F32 = jnp.float32
BF16 = jnp.bfloat16


def half_lanes(rows):
    return lax.broadcasted_iota(jnp.int32, (rows, 128), 1) < 64


def swap_halves(x):
    return pltpu.roll(x, 64, 1)


def turned(keys):
    row, col = iota(256, 256, 0), iota(256, 256, 1)
    unit = (row == col).astype(BF16)
    even = lax.dot_general(unit, keys, NT, preferred_element_type=F32).astype(BF16)
    return even, lower(even)


def lower(even):
    return jnp.concatenate([jnp.zeros((64, even.shape[1]), BF16), even[:QK]], axis=0)


def with_ones(values):
    return jnp.concatenate([values, jnp.ones_like(values)], axis=1)


def plan(group, shard, per_owner, picks_ref, lists_ref, slots_ref, dead_ref):
    lists = picks_ref.shape[0]
    total = lists_ref.shape[1] // lists * per_owner
    width = slots_ref.shape[1]
    picks = jnp.zeros((lists, PICKS), jnp.int32)
    for each in range(picks_ref.shape[1]):
        picks = jnp.where(group == each, picks_ref[:, each, :], picks)
    block = iota(lists, total, 1)
    hits = [block == picks[:, entry : entry + 1] for entry in range(PICKS)]
    named = functools.reduce(jnp.logical_or, hits).astype(F32)
    named = jnp.broadcast_to(jnp.max(named, axis=0, keepdims=True), (8, total))
    row, col = iota(total, total, 0), iota(total, total, 1)
    before = (lax.div(row, per_owner) == lax.div(col, per_owner)) & (row < col)
    rank = jnp.dot(named, before.astype(F32), preferred_element_type=F32)
    rank = jnp.minimum(rank, float(lists - 1))
    inside = lax.rem(iota(8, total, 1), per_owner).astype(F32)
    found = jnp.zeros((8, lists_ref.shape[1]), F32)
    row, col = iota(total, lists_ref.shape[1], 0), iota(total, lists_ref.shape[1], 1)
    for place in range(lists):
        to = (col == lax.div(row, per_owner) * lists + place).astype(F32)
        value = jnp.where(rank == float(place), named * inside, 0.0)
        found = found + jnp.dot(value, to, preferred_element_type=F32)
    lists_ref[...] = found[:1].astype(jnp.int32)

    owner = lax.div(block, per_owner)
    turn = (lax.div(shard, 2) - lax.div(owner, 2)) * 2 + ((owner ^ shard) & 1)
    slot = jnp.clip(turn * lists + rank[:lists].astype(jnp.int32), 0, lists_ref.shape[1] - 1)
    slot = slot.astype(F32)
    first = shard * per_owner + iota(lists, 1, 0) * (QBLK // KBLK)
    own = block == first

    def pick_out(hit, values):
        return jnp.sum(jnp.where(hit, values, 0.0), axis=1, keepdims=True)

    lane = iota(lists, width, 1)
    slots = jnp.where(lane == 0, pick_out(own, slot), 0.0)
    dead = jnp.zeros((lists, width), F32)
    seen = own.astype(F32)
    at = jnp.ones((lists, 1), jnp.int32)
    met = jnp.zeros((lists, 1), jnp.int32)
    for entry, hit in enumerate(hits):
        pick = picks[:, entry : entry + 1]
        is_own = (pick == first).astype(jnp.int32)
        gone = jnp.maximum(pick_out(hit, seen), (pick > first).astype(F32))
        slots = jnp.where(lane == at, pick_out(hit, slot), slots)
        dead = jnp.where(lane == at, gone, dead)
        seen = jnp.maximum(seen, hit.astype(F32))
        at = at + 1 - is_own * (1 - met)
        met = jnp.maximum(met, is_own)
    slots_ref[...] = slots.astype(jnp.int32)
    dead_ref[...] = dead.astype(jnp.int32)


def prep_kernel(
    where_ref,
    picks_in,
    keys_in,
    values_in,
    fold_in,
    packed_ref,
    rim_ref,
    lists_ref,
    slots_ref,
    dead_ref,
    even_ref,
    odd_ref,
    val_ref,
    picks_ref,
    keys_ref,
    values_ref,
    kw_ref,
    vw_ref,
    sems,
):
    group, shard = where_ref[0], where_ref[1]
    pair = pl.ds(pl.multiple_of(lax.div(group, 2) * PAIR, 128), PAIR)
    single = pl.ds(pl.multiple_of(group * DV, 128), DV)
    folded_value = pl.ds(pl.multiple_of(GROUPS * QK + group * DV, 128), DV)
    copies = [
        pltpu.make_async_copy(source, target, sems.at[i])
        for i, (source, target) in enumerate(
            [
                (picks_in, picks_ref),
                (keys_in.at[:, pair], keys_ref),
                (values_in.at[:, single], values_ref),
                (fold_in.at[:, pair], kw_ref),
                (fold_in.at[:, folded_value], vw_ref),
            ]
        )
    ]
    for copy in copies:
        copy.start()
    copies[0].wait()
    plan(group, shard, keys_ref.shape[0] // KBLK, picks_ref, lists_ref, slots_ref, dead_ref)
    for copy in copies[1:]:
        copy.wait()
    odd = lax.rem(group, 2) == 1

    def own_columns(ref):
        t0 = ref[:, :128].astype(F32)
        t1 = ref[:, 128:256].astype(F32)
        t2 = ref[:, 256:].astype(F32)
        r1, r2 = swap_halves(t1), swap_halves(t2)
        left = half_lanes(t0.shape[0])
        low = jnp.where(odd, jnp.where(left, r1, r2), t0)
        high = jnp.where(left, jnp.where(odd, r2, t1), 0.0)
        return low, high

    low, high = own_columns(keys_ref)
    values = values_ref[...]
    rows = low.shape[0]
    count = rows // KBLK
    high3 = high.reshape(count, KBLK, 128)
    packed_high = high3[:, : KBLK // 2] + swap_halves(
        high3[:, KBLK // 2 :].reshape(count * KBLK // 2, 128)
    ).reshape(count, KBLK // 2, 128)
    even = jnp.concatenate([low.astype(BF16), high.astype(BF16)], axis=1)
    even_ref[...], odd_ref[...] = turned(even)
    val_ref[...] = with_ones(values)
    for block in range(count):
        at = block * BROWS
        token = slice(block * KBLK, block * KBLK + KBLK)
        packed_ref[at : at + KBLK] = low[token].astype(BF16)
        packed_ref[at + KBLK : at + KBLK + KBLK // 2] = packed_high[block].astype(BF16)
        packed_ref[at + KBLK + KBLK // 2 : at + BROWS] = values[token]
    rim_rows = rim_ref.shape[0]
    rim_ref[...] = packed_ref[count * BROWS - rim_rows : count * BROWS]

    wlow, whigh = own_columns(kw_ref)
    folds = rows // CBLK

    def fold(x, w):
        return jnp.sum(x.reshape(folds, CBLK, 128) * w[None], axis=1).astype(BF16)

    at = count * BROWS
    packed_ref[at : at + folds] = fold(low, wlow)
    packed_ref[at + folds : at + 2 * folds] = fold(high, whigh)
    packed_ref[at + 2 * folds :] = fold(values.astype(F32), vw_ref[...])


def pack_kernel(lists, beside, where_ref, *refs):
    count = len(refs) // 2
    named, ref, outs = refs[:count], refs[count], refs[count + 1 :]
    shard = where_ref[1]
    owner = shard + 1 - 2 * lax.rem(shard, 2) if beside else shard
    data = ref.shape[0] - (outs[0].shape[0] - lists * BROWS)
    for blocks, out in zip(named, outs):
        for place in range(lists):
            at = pl.multiple_of(blocks[0, owner * lists + place] * BROWS, 16)
            out[place * BROWS : (place + 1) * BROWS] = ref[pl.ds(at, BROWS)]
        out[lists * BROWS :] = ref[data:]


def unpack(ref, at, count, step=1):
    lows, packed, values = [], [], []
    for block in range(count):
        first = at + block * step * BROWS
        lows.append(ref[first : first + KBLK])
        packed.append(ref[first + KBLK : first + KBLK + KBLK // 2])
        values.append(ref[first + KBLK + KBLK // 2 : first + BROWS])
    packed = jnp.concatenate(packed, axis=0)
    row, col = iota(128, 256, 0), iota(128, 256, 1)
    take = (row == jnp.where(col < 128, col, col - 64)) & (lax.rem(col, 128) < 64)
    both = jnp.dot(packed, take.astype(BF16), preferred_element_type=F32).astype(BF16)
    half = KBLK // 2
    highs = []
    for block in range(count):
        rows = slice(block * half, block * half + half)
        highs += [both[rows, :128], both[rows, 128:]]
    even = jnp.concatenate(
        [jnp.concatenate(lows, axis=0), jnp.concatenate(highs, axis=0)], axis=1
    )
    return even, jnp.concatenate(values, axis=0)


def fill_rim(shard, near_ref, far_ref, own, ext):
    rim_blocks = WINDOW // KBLK
    even_in, odd_in, val_in = own
    even_ref, odd_ref, val_ref = ext
    even_ref[:, WINDOW:] = even_in[:, :WINDOW]
    odd_ref[:, WINDOW:] = odd_in[:, :WINDOW]
    val_ref[WINDOW:] = val_in[:WINDOW]
    use_near = lax.rem(shard, 2) == 1
    rim_end = near_ref.shape[0] // BROWS * BROWS
    near_rim = near_ref[rim_end - far_ref.shape[0] : rim_end]

    @pl.when(shard > 0)
    def _():
        keys, values = unpack(jnp.where(use_near, near_rim, far_ref[...]), 0, rim_blocks)
        even_ref[:, :WINDOW], odd_ref[:, :WINDOW] = turned(keys)
        val_ref[:WINDOW] = with_ones(values)

    @pl.when(shard == 0)
    def _():
        even = jnp.broadcast_to(even_in[:, :1].astype(F32), (256, WINDOW)).astype(BF16)
        even_ref[:, :WINDOW], odd_ref[:, :WINDOW] = even, lower(even)
        val_ref[:WINDOW] = jnp.zeros((WINDOW, 256), BF16)


def pool_kernel(groups, lists, where_ref, own_ref, *refs):
    sent = 2 * groups - 1
    ins, (key_ref, val_ref, ceven_ref, codd_ref, cval_ref, folded) = refs[:sent], refs[sent:]
    shard = where_ref[1]
    parity = lax.rem(shard, 2)
    base = shard - parity
    rows = lists * KBLK
    folds = (ins[0].shape[0] - lists * BROWS) // 3
    folded[...] = jnp.zeros_like(folded)
    cval_ref[...] = jnp.zeros_like(cval_ref)

    def fill(place, owner, ref, step, fold_at):
        keys, values = unpack(ref, 0, lists, step)
        at = slice(place * rows, place * rows + rows)
        key_ref[at] = keys
        val_ref[at] = values
        low = ref[fold_at : fold_at + folds]
        high = ref[fold_at + folds : fold_at + 2 * folds]
        owned = pl.ds(pl.multiple_of(owner * folds, 32), folds)
        folded[owned] = jnp.concatenate([low, high], axis=1)
        cval_ref[owned] = with_ones(ref[fold_at + 2 * folds : fold_at + 3 * folds])

    fill(0, shard, own_ref, QBLK // KBLK, own_ref.shape[0] - 3 * folds)
    fill(1, base + 1 - parity, ins[0], 1, lists * BROWS)
    for distance in range(1, groups):

        @pl.when(base >= 2 * distance)
        def _():
            for side in range(2):
                owner = base - 2 * distance + (parity if side == 0 else 1 - parity)
                fill(2 * distance + side, owner, ins[2 * distance - 1 + side], 1, lists * BROWS)

    ceven_ref[...], codd_ref[...] = turned(folded[...])


def iota(rows, cols, axis):
    return lax.broadcasted_iota(jnp.int32, (rows, cols), axis)


def scores_of(q, keys, mask):
    scores = jnp.dot(q, keys, preferred_element_type=F32)
    return scores if mask is None else mask(scores)


def in_range(total):
    good = jnp.where((total >= LOW_TOTAL) & (total <= HIGH_TOTAL), 1.0, 0.0)
    return jnp.min(good.reshape(-1, 8, DV), axis=0)


def over_heads(pairs, load, branches, finish):
    def sums(weights, values):
        out = jnp.dot(weights, values(), preferred_element_type=F32)
        return out[:, :DV], out[:, DV:]

    at_once = 2 if pairs % 2 == 0 else 1
    units = [(pair, side) for pair in range(0, pairs, at_once) for side in range(2)]
    worst, held = [], None
    for now, unit in zip([None] + units, units + [None]):
        q = None if unit is None else load(*unit, at_once)
        fresh, parts = [], []
        for at, (tiles, values) in enumerate(branches):
            weights, ahead = [], []
            for place, (keys, mask) in enumerate(tiles):
                if q is not None:
                    ahead.append(scores_of(q, keys(unit[1]), mask))
                if held is not None:
                    weights.append(jnp.exp2(held[at][place] * SCALE).astype(BF16))
            fresh.append(ahead)
            parts.append((weights, values))
        if held is not None:
            parts = [sums(jnp.concatenate(w, axis=1), values) for w, values in parts]
            worst += [in_range(x) for x in finish(*now, at_once, parts)]
        held = fresh

    @pl.when(jnp.min(functools.reduce(jnp.minimum, worst)) < 0.5)
    def _():
        def exact(pair, _):
            for side in range(2):
                q = load(pair, side, 1)
                parts = []
                for tiles, values in branches:
                    scores = [scores_of(q, keys(side), mask) for keys, mask in tiles]
                    scores = jnp.concatenate(scores, axis=1)
                    top = jnp.max(scores, axis=1, keepdims=True)
                    shifted = (scores - jnp.maximum(top, -1e28)) * SCALE
                    parts.append(sums(jnp.exp2(shifted).astype(BF16), values))
                finish(pair, side, 1, parts)
            return 0

        lax.fori_loop(0, pairs, exact, 0)


def aligned(at):
    return at if isinstance(at, int) else pl.multiple_of(at, 128)


def query_loader(q_ref):
    def load(pair, side, n):
        at = [aligned((pair + p) * PAIR + side * 128) for p in range(n)]
        return jnp.concatenate([q_ref[:, pl.ds(x, 256)] for x in at], axis=0)

    return load


def head_columns(pair, side):
    return pl.ds(aligned(pair * 2 * DV + side * DV), DV)


def gate_loader(gate_ref, first, heads):
    turned = pltpu.roll(gate_ref[...], lax.rem(128 - first, 128), 1)

    def load(pair, side, n, branch):
        if isinstance(pair, int):
            local, at = turned, branch * heads + side + 2 * pair
        else:
            local, at = pltpu.roll(turned, lax.rem(128 - 2 * pair, 128), 1), branch * heads + side
        columns = [local[:, at + 2 * p : at + 2 * p + 1] for p in range(n)]
        shape = (turned.shape[0], DV)
        return jnp.concatenate([jnp.broadcast_to(x, shape) for x in columns], axis=0)

    return load


def stacked(x, times):
    return jnp.concatenate([x] * times, axis=0) if times > 1 else x


def repeated(keep, rows):
    return stacked(keep, rows // keep.shape[0])


def near_kernel(heads, rim, where_ref, q_ref, gate_ref, *refs):
    keys = refs[:3]
    if rim:
        out_ref, ext = refs[6], refs[7:]

        @pl.when((pl.program_id(0) == 0) & (pl.program_id(1) == 0))
        def _():
            fill_rim(where_ref[1], refs[3], refs[4], keys, ext)

        keys = ext
    else:
        out_ref = refs[3]
    count = q_ref.shape[1] // QK
    gate = gate_loader(gate_ref, pl.program_id(1) * count, heads)
    base = pl.multiple_of(pl.program_id(0) * QBLK, QBLK)
    row, col = iota(QBLK, QBLK, 0), iota(QBLK, QBLK, 1)

    def tile(place, mask):
        return (lambda side: keys[side][:, pl.ds(base + place * QBLK, QBLK)]), mask

    def finish(pair, side, n, parts):
        ((num, den),) = parts
        total = gate(pair, side, n, 2) * (num / den)
        for p in range(n):
            part = total[p * QBLK : (p + 1) * QBLK]
            out_ref[:, head_columns(pair + p, side)] = part.astype(BF16)
        return [den]

    tiles = [
        tile(0, lambda x: jnp.where(repeated(col >= row, x.shape[0]), x, NEG)),
        tile(1, None),
        tile(2, lambda x: jnp.where(repeated(col <= row, x.shape[0]), x, NEG)),
    ]
    values = lambda: keys[2][pl.ds(base, WINDOW + QBLK)]
    over_heads(count // 2, query_loader(q_ref), [(tiles, values)], finish)


def near_branch(first_block, block_count, where, queries, gates, keys, rims, prior):
    tokens, width = queries.shape
    heads = width // QK
    at_once = 8 if heads % 8 == 0 else 2
    row_block = lambda i, p, *_: (i + first_block, p)
    operands = [queries, gates, *keys]
    specs = [
        pl.BlockSpec((QBLK, at_once * QK), row_block),
        pl.BlockSpec((QBLK, 128), lambda i, p, *_: (i + first_block, 0)),
    ]
    specs += [VMEM_SPEC] * len(keys)
    alias, scratch = {}, []
    if rims is not None:
        other, far = rims
        operands += [other, far, prior]
        specs += [VMEM_SPEC, VMEM_SPEC, pl.BlockSpec(memory_space=pl.ANY)]
        alias = {len(operands): 0}
        scratch = [pltpu.VMEM((256, 2 * WINDOW), BF16)] * 2 + [pltpu.VMEM((2 * WINDOW, 256), BF16)]
    rows = block_count * QBLK * heads
    return pl.pallas_call(
        functools.partial(near_kernel, heads, rims is not None),
        grid_spec=pltpu.PrefetchScalarGridSpec(
            num_scalar_prefetch=1,
            grid=(block_count, heads // at_once),
            in_specs=specs,
            out_specs=pl.BlockSpec((QBLK, at_once * DV), row_block),
            scratch_shapes=scratch,
        ),
        out_shape=jax.ShapeDtypeStruct((tokens, heads * DV), BF16),
        input_output_aliases=alias,
        compiler_params=pltpu.CompilerParams(vmem_limit_bytes=VMEM_LIMIT),
        cost_estimate=pl.CostEstimate(
            flops=rows * (WINDOW + QBLK) * 64,
            bytes_accessed=rows * (2 * QK + 4 * DV),
            transcendentals=0,
        ),
        name="near_branch",
    )(where, *operands)


def chosen_kernel(heads, span, *refs):
    first_chunk, widths = span
    out_count = sum(len(w) for w in widths)
    meta_ref, slots_ref, dead_ref, q_ref, gate_ref, near_ref = refs[:6]
    (key_pool, val_pool), cfold, weight_ref = refs[6:8], refs[8:11], refs[11]
    outs = list(refs[12 : 12 + out_count])
    gathered, even, odd, val, attended, weight, weight_sem = refs[12 + out_count :]
    keys = (even, odd)
    turn, step = pl.program_id(0), pl.program_id(1)
    last = pl.num_programs(1) - 1
    rows = q_ref.shape[0]
    count = q_ref.shape[1] // QK
    chunk_start = meta_ref[2 + first_chunk + turn] * rows
    list_at = lax.div(chunk_start, QBLK)
    first_row = lax.rem(chunk_start, QBLK)
    position = meta_ref[2] + chunk_start
    copy = pltpu.make_async_copy(weight_ref, weight, weight_sem)

    @pl.when(step == 0)
    def _():
        for slot in range(PICKS):
            source = pl.multiple_of(slots_ref[list_at, slot] * KBLK, KBLK)
            gathered[slot * KBLK : (slot + 1) * KBLK] = key_pool[pl.ds(source, KBLK)]
            val[slot * KBLK : (slot + 1) * KBLK] = with_ones(val_pool[pl.ds(source, KBLK)])
        for slot in range(1, PICKS):

            @pl.when(dead_ref[list_at, slot] == 1)
            def _():
                at = slice(slot * KBLK, (slot + 1) * KBLK)
                gathered[at] = jnp.broadcast_to(gathered[:1], (KBLK, 256))
                val[at] = jnp.zeros((KBLK, 256), BF16)

        even[...], odd[...] = turned(gathered[...])

    @pl.when((turn == 0) & (step == 0))
    def _():
        copy.start()

    gate = gate_loader(gate_ref, step * count, heads)
    row = iota(rows, TILE, 0)
    col = iota(rows, TILE, 1)
    own_keep = (col >= KBLK) | (col <= row + first_row)

    def own_mask(scores):
        own = jnp.where(repeated(own_keep[:, :128], scores.shape[0]), scores[:, :128], NEG)
        return jnp.concatenate([own, scores[:, 128:]], axis=1)

    def comp_mask(place):
        ends = (col + place * TILE + 1) * CBLK - 1
        return lambda x: jnp.where(repeated(ends <= row + position, x.shape[0]), x, NEG)

    def tile(refs, place, mask):
        return (lambda side: refs[side][:, place * TILE : (place + 1) * TILE]), mask

    chosen = [tile(keys, p, own_mask if p == 0 else None) for p in range(PICKS * KBLK // TILE)]
    folded = [tile(cfold, p, comp_mask(p)) for p in range(cfold[2].shape[0] // TILE)]
    empty = row[:, :DV] + position < CBLK - 1

    def finish(pair, side, n, parts):
        (num, den), (folded_num, folded_den) = parts
        folded_den = jnp.where(stacked(empty, n), 1.0, folded_den)
        total = gate(pair, side, n, 1) * (num / den)
        total = total + gate(pair, side, n, 0) * (folded_num / folded_den)
        for p in range(n):
            cols = head_columns(pair + p, side)
            mixed = near_ref[:, cols].astype(F32) + total[p * rows : (p + 1) * rows]
            attended[step, :, cols] = mixed.astype(BF16)
        return [den, folded_den]

    branches = [(chosen, lambda: val[...]), (folded, lambda: cfold[2][...])]
    over_heads(count // 2, query_loader(q_ref), branches, finish)

    @pl.when((turn == 0) & (step == last))
    def _():
        copy.wait()

    for place, parts in enumerate(widths):
        chunk_outs = [outs.pop(0) for _ in parts]

        @pl.when((turn == place) & (step == last))
        def _():
            rows_in = jnp.concatenate([attended[s] for s in range(attended.shape[0])], axis=1)
            first_col = 0
            for out_ref in chunk_outs:
                for at in range(0, out_ref.shape[1], 256):
                    cols = weight[:, first_col + at : first_col + at + 256]
                    part = jnp.dot(rows_in, cols, preferred_element_type=F32)
                    out_ref[:, at : at + 256] = part.astype(out_ref.dtype)
                first_col += out_ref.shape[1]


def chosen_and_project(first_chunk, widths, rows, meta, slots, dead, queries, gates, near, pools, out_weight):
    tokens, width = queries.shape
    heads = width // QK
    at_once = 8 if heads % 8 == 0 else 2
    steps = heads // at_once
    whole = lambda x: pl.BlockSpec(x.shape, lambda i, p, *_: (0,) * x.ndim)
    outs = [jax.ShapeDtypeStruct((rows, width), BF16) for chunk in widths for width in chunk]
    return pl.pallas_call(
        functools.partial(chosen_kernel, heads, (first_chunk, widths)),
        grid_spec=pltpu.PrefetchScalarGridSpec(
            num_scalar_prefetch=3,
            grid=(len(widths), steps),
            in_specs=[
                pl.BlockSpec((rows, at_once * QK), lambda i, p, m, *_: (m[2 + first_chunk + i], p)),
                pl.BlockSpec((rows, 128), lambda i, p, m, *_: (m[2 + first_chunk + i], 0)),
                pl.BlockSpec((rows, at_once * DV), lambda i, p, m, *_: (m[2 + first_chunk + i], p)),
            ]
            + [VMEM_SPEC] * len(pools)
            + [pl.BlockSpec(memory_space=pl.ANY)],
            out_specs=[whole(out) for out in outs],
            scratch_shapes=[
                pltpu.VMEM((PICKS * KBLK, 256), BF16),
                pltpu.VMEM((256, PICKS * KBLK), BF16),
                pltpu.VMEM((256, PICKS * KBLK), BF16),
                pltpu.VMEM((PICKS * KBLK, 256), BF16),
                pltpu.VMEM((steps, rows, at_once * DV), BF16),
                pltpu.VMEM(out_weight.shape, BF16),
                pltpu.SemaphoreType.DMA,
            ],
        ),
        out_shape=outs,
        compiler_params=pltpu.CompilerParams(vmem_limit_bytes=VMEM_LIMIT),
        cost_estimate=pl.CostEstimate(
            flops=rows * heads * PICKS * KBLK * 64,
            bytes_accessed=out_weight.size,
            transcendentals=0,
        ),
        name="chosen_and_project",
    )(meta, slots, dead, queries, gates, near, *pools, out_weight)


VMEM_SPEC = pl.BlockSpec(memory_space=pltpu.VMEM)


def single_step(kernel, name, scalars, arrays, outs, scratch=(), in_spec=None, out_spec=None):
    whole = lambda x: pl.BlockSpec(x.shape, lambda i, *_: (0,) * len(x.shape))
    return pl.pallas_call(
        kernel,
        grid_spec=pltpu.PrefetchScalarGridSpec(
            num_scalar_prefetch=len(scalars),
            grid=(1,),
            in_specs=[in_spec or whole(x) for x in arrays],
            out_specs=[out_spec or whole(x) for x in outs],
            scratch_shapes=list(scratch),
        ),
        out_shape=outs,
        compiler_params=pltpu.CompilerParams(vmem_limit_bytes=VMEM_LIMIT),
        name=name,
    )(*scalars, *arrays)


def local(
    queries,
    key_rows,
    value_rows,
    comp_key_weight,
    comp_value_weight,
    block_picks,
    gate_logits,
    out_weight,
):
    tokens = queries.shape[0]
    heads = queries.shape[1] // QK
    n_ctx, n_head = lax.axis_size("ctx"), lax.axis_size("head")
    shard, head_at = lax.axis_index("ctx"), lax.axis_index("head")
    group = head_at * heads // (HEADS // GROUPS)
    per_owner = tokens // KBLK
    lists = tokens // QBLK
    folds = tokens // CBLK
    groups = n_ctx // 2
    rim_blocks = WINDOW // KBLK
    packed_rows = per_owner * BROWS
    bf16 = lambda *shape: jax.ShapeDtypeStruct(shape, BF16)

    chips = n_head // 2
    chip, core = head_at // 2, lax.rem(head_at, 2)
    order = []
    for step in list(range(1, chips)) + [0]:
        target = lax.rem(chip + step, chips) * 2
        order += [target + 1 - core, target + core]
    where = jnp.stack([group, shard, shard * tokens] + order).astype(jnp.int32)
    rim_rows = rim_blocks * BROWS
    fold_weights = jnp.concatenate([comp_key_weight, comp_value_weight], axis=1)
    int32 = lambda *shape: jax.ShapeDtypeStruct(shape, jnp.int32)
    prep_out = [bf16(packed_rows + 3 * folds, 128), bf16(rim_rows, 128)]
    prep_out += [int32(1, n_ctx * lists), int32(lists, 2 * PICKS), int32(lists, 2 * PICKS)]
    prep_out += [bf16(256, tokens)] * 2 + [bf16(tokens, 256)]
    packed, rim, named, slots, dead, even, odd, val = pl.pallas_call(
        prep_kernel,
        grid_spec=pltpu.PrefetchScalarGridSpec(
            num_scalar_prefetch=1,
            grid=(1,),
            in_specs=[pl.BlockSpec(memory_space=pl.ANY)] * 4,
            out_specs=[VMEM_SPEC] * 2
            + [pl.BlockSpec(x.shape, lambda i, g: (0, 0)) for x in prep_out[2:5]]
            + [VMEM_SPEC] * 3,
            scratch_shapes=[
                pltpu.VMEM(block_picks.shape, jnp.int32),
                pltpu.VMEM((tokens, PAIR), BF16),
                pltpu.VMEM((tokens, DV), BF16),
                pltpu.VMEM((CBLK, PAIR), F32),
                pltpu.VMEM((CBLK, DV), F32),
                pltpu.SemaphoreType.DMA((5,)),
            ],
        ),
        out_shape=prep_out,
        compiler_params=pltpu.CompilerParams(vmem_limit_bytes=51 * 1024 * 1024),
        name="prep",
    )(where, block_picks, key_rows, value_rows, fold_weights)
    other = lax.ppermute(packed, "ctx", [(i, i ^ 1) for i in range(n_ctx)])
    named = [named] + [
        lax.ppermute(named, "ctx", [(i, i - 2 * d) for i in range(2 * d, n_ctx)])
        for d in range(1, groups)
    ]
    far_rim = lax.ppermute(rim, "ctx", [(i, i + 1) for i in range(1, n_ctx - 1, 2)])

    gates = jax.nn.sigmoid(gate_logits).reshape(tokens, 3 * heads)
    gates = jnp.pad(gates, ((0, 0), (0, 128 - 3 * heads)))
    sent = bf16(lists * BROWS + 3 * folds, 128)

    def pack(beside, lists_in, rows):
        return single_step(
            functools.partial(pack_kernel, lists, beside),
            "pack",
            [where, *lists_in],
            [rows],
            [sent] * len(lists_in),
            in_spec=VMEM_SPEC,
            out_spec=VMEM_SPEC,
        )

    def ahead(send, distance):
        return lax.ppermute(send, "ctx", [(i, i + 2 * distance) for i in range(n_ctx - 2 * distance)])

    named, gates = lax.optimization_barrier((named, gates))
    own_sends = pack(False, named[1:], packed)
    own_sends, even = lax.optimization_barrier((own_sends, even))
    from_same = [ahead(send, d) for d, send in enumerate(own_sends, 1)]

    reach = WINDOW // QBLK
    near = functools.partial(near_branch, where=where, queries=queries, gates=gates)
    mixed = near(reach, lists - reach, keys=(even, odd, val), rims=None, prior=None)

    other, mixed = lax.optimization_barrier((other, mixed))
    beside, *other_sends = pack(True, named, other)
    from_other = [ahead(send, d) for d, send in enumerate(other_sends, 1)]
    mixed = near(0, reach, keys=(even, odd, val), rims=(other, far_rim), prior=mixed)

    received = [beside] + [x for both in zip(from_same, from_other) for x in both]
    pools = single_step(
        functools.partial(pool_kernel, groups, lists),
        "pool",
        [where],
        [packed] + received,
        [bf16(n_ctx * lists * KBLK, 256), bf16(n_ctx * lists * KBLK, DV)]
        + [bf16(256, n_ctx * folds)] * 2
        + [bf16(n_ctx * folds, 256)],
        [pltpu.VMEM((n_ctx * folds, 256), BF16)],
        in_spec=VMEM_SPEC,
        out_spec=VMEM_SPEC,
    )
    rows = tokens // n_head
    across = [(i, i ^ 1) for i in range(n_head)]

    model = out_weight.shape[1]

    def project(first_chunk, widths):
        return chosen_and_project(
            first_chunk, widths, rows, where, slots, dead, queries, gates, mixed, pools, out_weight
        )

    sums = []
    for step in range(chips - 1):
        other = lax.ppermute(project(1 + 2 * step, [[model]])[0], "head", across)
        mine = project(2 + 2 * step, [[model]])[0]
        summed = (mine.astype(F32) + other.astype(F32)).astype(BF16)
        summed, where = lax.optimization_barrier((summed, where))
        sums.append(summed)
    *passed, kept = project(n_head - 1, [[model // 2] * 2, [model]])
    arrived = [jnp.concatenate([lax.ppermute(x, "head", across) for x in passed], axis=1)]
    for step, summed in enumerate(sums, 1):
        route = [(i, (i + 2 * step) % n_head) for i in range(n_head)]
        arrived.append(lax.ppermute(summed, "head", route))
    total = kept.astype(F32)
    for part in arrived:
        total = total + part.astype(F32)
    return total.astype(BF16)


def solution(mesh):
    placed = (
        P("ctx", "head"),
        P("ctx", None),
        P("ctx", None),
        P(),
        P(),
        P("ctx", None, None),
        P("ctx", None, "head"),
        P("head", None),
    )
    return jax.shard_map(
        local, mesh=mesh, in_specs=placed, out_specs=P(("ctx", "head"), None), check_vma=False
    )
```

```python
import functools

import jax
import jax.numpy as jnp
from jax import lax
from jax.experimental import pallas as pl
from jax.experimental.pallas import tpu as pltpu
from jax.sharding import PartitionSpec as P

HEADS = 64
GROUPS = 4
QK = 192
DV = 128
CBLK = 32
KBLK = 64
PICKS = 16
WINDOW = 512
QBLK = 256
PAIR = 2 * QK
BROWS = KBLK + KBLK // 2 + KBLK
VMEM_LIMIT = 50 * 1024 * 1024
NEG = -1e30
SCALE = QK ** (-0.5) * 1.4426950408889634
LOW_TOTAL, HIGH_TOTAL = 2.0**-60, 2.0**100
TILE = 256
NT = (((1,), (1,)), ((), ()))
F32 = jnp.float32
BF16 = jnp.bfloat16


def half_lanes(rows):
    return lax.broadcasted_iota(jnp.int32, (rows, 128), 1) < 64


def swap_halves(x):
    return pltpu.roll(x, 64, 1)


def turned(keys):
    row, col = iota(256, 256, 0), iota(256, 256, 1)
    unit = (row == col).astype(BF16)
    even = lax.dot_general(unit, keys, NT, preferred_element_type=F32).astype(BF16)
    return even, lower(even)


def lower(even):
    return jnp.concatenate([jnp.zeros((64, even.shape[1]), BF16), even[:QK]], axis=0)


def with_ones(values):
    return jnp.concatenate([values, jnp.ones_like(values)], axis=1)


def plan(group, shard, per_owner, picks_ref, lists_ref, slots_ref, dead_ref):
    lists = picks_ref.shape[0]
    total = lists_ref.shape[1] // lists * per_owner
    width = slots_ref.shape[1]
    picks = jnp.zeros((lists, PICKS), jnp.int32)
    for each in range(picks_ref.shape[1]):
        picks = jnp.where(group == each, picks_ref[:, each, :], picks)
    block = iota(lists, total, 1)
    hits = [block == picks[:, entry : entry + 1] for entry in range(PICKS)]
    named = functools.reduce(jnp.logical_or, hits).astype(F32)
    named = jnp.broadcast_to(jnp.max(named, axis=0, keepdims=True), (8, total))
    row, col = iota(total, total, 0), iota(total, total, 1)
    before = (lax.div(row, per_owner) == lax.div(col, per_owner)) & (row < col)
    rank = jnp.dot(named, before.astype(F32), preferred_element_type=F32)
    rank = jnp.minimum(rank, float(lists - 1))
    inside = lax.rem(iota(8, total, 1), per_owner).astype(F32)
    found = jnp.zeros((8, lists_ref.shape[1]), F32)
    row, col = iota(total, lists_ref.shape[1], 0), iota(total, lists_ref.shape[1], 1)
    for place in range(lists):
        to = (col == lax.div(row, per_owner) * lists + place).astype(F32)
        value = jnp.where(rank == float(place), named * inside, 0.0)
        found = found + jnp.dot(value, to, preferred_element_type=F32)
    lists_ref[...] = found[:1].astype(jnp.int32)

    owner = lax.div(block, per_owner)
    turn = (lax.div(shard, 2) - lax.div(owner, 2)) * 2 + ((owner ^ shard) & 1)
    slot = jnp.clip(turn * lists + rank[:lists].astype(jnp.int32), 0, lists_ref.shape[1] - 1)
    slot = slot.astype(F32)
    first = shard * per_owner + iota(lists, 1, 0) * (QBLK // KBLK)
    own = block == first

    def pick_out(hit, values):
        return jnp.sum(jnp.where(hit, values, 0.0), axis=1, keepdims=True)

    lane = iota(lists, width, 1)
    slots = jnp.where(lane == 0, pick_out(own, slot), 0.0)
    dead = jnp.zeros((lists, width), F32)
    seen = own.astype(F32)
    at = jnp.ones((lists, 1), jnp.int32)
    met = jnp.zeros((lists, 1), jnp.int32)
    for entry, hit in enumerate(hits):
        pick = picks[:, entry : entry + 1]
        is_own = (pick == first).astype(jnp.int32)
        gone = jnp.maximum(pick_out(hit, seen), (pick > first).astype(F32))
        slots = jnp.where(lane == at, pick_out(hit, slot), slots)
        dead = jnp.where(lane == at, gone, dead)
        seen = jnp.maximum(seen, hit.astype(F32))
        at = at + 1 - is_own * (1 - met)
        met = jnp.maximum(met, is_own)
    slots_ref[...] = slots.astype(jnp.int32)
    dead_ref[...] = dead.astype(jnp.int32)


def prep_kernel(
    where_ref,
    picks_in,
    keys_in,
    values_in,
    fold_in,
    packed_ref,
    rim_ref,
    lists_ref,
    slots_ref,
    dead_ref,
    even_ref,
    odd_ref,
    val_ref,
    picks_ref,
    keys_ref,
    values_ref,
    kw_ref,
    vw_ref,
    sems,
):
    group, shard = where_ref[0], where_ref[1]
    pair = pl.ds(pl.multiple_of(lax.div(group, 2) * PAIR, 128), PAIR)
    single = pl.ds(pl.multiple_of(group * DV, 128), DV)
    folded_value = pl.ds(pl.multiple_of(GROUPS * QK + group * DV, 128), DV)
    copies = [
        pltpu.make_async_copy(source, target, sems.at[i])
        for i, (source, target) in enumerate(
            [
                (picks_in, picks_ref),
                (keys_in.at[:, pair], keys_ref),
                (values_in.at[:, single], values_ref),
                (fold_in.at[:, pair], kw_ref),
                (fold_in.at[:, folded_value], vw_ref),
            ]
        )
    ]
    for copy in copies:
        copy.start()
    copies[0].wait()
    plan(group, shard, keys_ref.shape[0] // KBLK, picks_ref, lists_ref, slots_ref, dead_ref)
    for copy in copies[1:]:
        copy.wait()
    odd = lax.rem(group, 2) == 1

    def own_columns(ref):
        t0 = ref[:, :128].astype(F32)
        t1 = ref[:, 128:256].astype(F32)
        t2 = ref[:, 256:].astype(F32)
        r1, r2 = swap_halves(t1), swap_halves(t2)
        left = half_lanes(t0.shape[0])
        low = jnp.where(odd, jnp.where(left, r1, r2), t0)
        high = jnp.where(left, jnp.where(odd, r2, t1), 0.0)
        return low, high

    low, high = own_columns(keys_ref)
    values = values_ref[...]
    rows = low.shape[0]
    count = rows // KBLK
    high3 = high.reshape(count, KBLK, 128)
    packed_high = high3[:, : KBLK // 2] + swap_halves(
        high3[:, KBLK // 2 :].reshape(count * KBLK // 2, 128)
    ).reshape(count, KBLK // 2, 128)
    even = jnp.concatenate([low.astype(BF16), high.astype(BF16)], axis=1)
    even_ref[...], odd_ref[...] = turned(even)
    val_ref[...] = with_ones(values)
    for block in range(count):
        at = block * BROWS
        token = slice(block * KBLK, block * KBLK + KBLK)
        packed_ref[at : at + KBLK] = low[token].astype(BF16)
        packed_ref[at + KBLK : at + KBLK + KBLK // 2] = packed_high[block].astype(BF16)
        packed_ref[at + KBLK + KBLK // 2 : at + BROWS] = values[token]
    rim_rows = rim_ref.shape[0]
    rim_ref[...] = packed_ref[count * BROWS - rim_rows : count * BROWS]

    wlow, whigh = own_columns(kw_ref)
    folds = rows // CBLK

    def fold(x, w):
        return jnp.sum(x.reshape(folds, CBLK, 128) * w[None], axis=1).astype(BF16)

    at = count * BROWS
    packed_ref[at : at + folds] = fold(low, wlow)
    packed_ref[at + folds : at + 2 * folds] = fold(high, whigh)
    packed_ref[at + 2 * folds :] = fold(values.astype(F32), vw_ref[...])


def pack_kernel(lists, beside, where_ref, *refs):
    count = len(refs) // 2
    named, ref, outs = refs[:count], refs[count], refs[count + 1 :]
    shard = where_ref[1]
    owner = shard + 1 - 2 * lax.rem(shard, 2) if beside else shard
    data = ref.shape[0] - (outs[0].shape[0] - lists * BROWS)
    for blocks, out in zip(named, outs):
        for place in range(lists):
            at = pl.multiple_of(blocks[0, owner * lists + place] * BROWS, 16)
            out[place * BROWS : (place + 1) * BROWS] = ref[pl.ds(at, BROWS)]
        out[lists * BROWS :] = ref[data:]


def unpack(ref, at, count, step=1):
    lows, packed, values = [], [], []
    for block in range(count):
        first = at + block * step * BROWS
        lows.append(ref[first : first + KBLK])
        packed.append(ref[first + KBLK : first + KBLK + KBLK // 2])
        values.append(ref[first + KBLK + KBLK // 2 : first + BROWS])
    packed = jnp.concatenate(packed, axis=0)
    row, col = iota(128, 256, 0), iota(128, 256, 1)
    take = (row == jnp.where(col < 128, col, col - 64)) & (lax.rem(col, 128) < 64)
    both = jnp.dot(packed, take.astype(BF16), preferred_element_type=F32).astype(BF16)
    half = KBLK // 2
    highs = []
    for block in range(count):
        rows = slice(block * half, block * half + half)
        highs += [both[rows, :128], both[rows, 128:]]
    even = jnp.concatenate(
        [jnp.concatenate(lows, axis=0), jnp.concatenate(highs, axis=0)], axis=1
    )
    return even, jnp.concatenate(values, axis=0)


def fill_rim(shard, near_ref, far_ref, own, ext):
    rim_blocks = WINDOW // KBLK
    even_in, odd_in, val_in = own
    even_ref, odd_ref, val_ref = ext
    even_ref[:, WINDOW:] = even_in[:, :WINDOW]
    odd_ref[:, WINDOW:] = odd_in[:, :WINDOW]
    val_ref[WINDOW:] = val_in[:WINDOW]
    use_near = lax.rem(shard, 2) == 1
    rim_end = near_ref.shape[0] // BROWS * BROWS
    near_rim = near_ref[rim_end - far_ref.shape[0] : rim_end]

    @pl.when(shard > 0)
    def _():
        keys, values = unpack(jnp.where(use_near, near_rim, far_ref[...]), 0, rim_blocks)
        even_ref[:, :WINDOW], odd_ref[:, :WINDOW] = turned(keys)
        val_ref[:WINDOW] = with_ones(values)

    @pl.when(shard == 0)
    def _():
        even = jnp.broadcast_to(even_in[:, :1].astype(F32), (256, WINDOW)).astype(BF16)
        even_ref[:, :WINDOW], odd_ref[:, :WINDOW] = even, lower(even)
        val_ref[:WINDOW] = jnp.zeros((WINDOW, 256), BF16)


def pool_kernel(groups, lists, where_ref, own_ref, *refs):
    sent = 2 * groups - 1
    ins, (key_ref, val_ref, ceven_ref, codd_ref, cval_ref, folded) = refs[:sent], refs[sent:]
    shard = where_ref[1]
    parity = lax.rem(shard, 2)
    base = shard - parity
    rows = lists * KBLK
    folds = (ins[0].shape[0] - lists * BROWS) // 3
    folded[...] = jnp.zeros_like(folded)
    cval_ref[...] = jnp.zeros_like(cval_ref)

    def fill(place, owner, ref, step, fold_at):
        keys, values = unpack(ref, 0, lists, step)
        at = slice(place * rows, place * rows + rows)
        key_ref[at] = keys
        val_ref[at] = values
        low = ref[fold_at : fold_at + folds]
        high = ref[fold_at + folds : fold_at + 2 * folds]
        owned = pl.ds(pl.multiple_of(owner * folds, 32), folds)
        folded[owned] = jnp.concatenate([low, high], axis=1)
        cval_ref[owned] = with_ones(ref[fold_at + 2 * folds : fold_at + 3 * folds])

    fill(0, shard, own_ref, QBLK // KBLK, own_ref.shape[0] - 3 * folds)
    fill(1, base + 1 - parity, ins[0], 1, lists * BROWS)
    for distance in range(1, groups):

        @pl.when(base >= 2 * distance)
        def _():
            for side in range(2):
                owner = base - 2 * distance + (parity if side == 0 else 1 - parity)
                fill(2 * distance + side, owner, ins[2 * distance - 1 + side], 1, lists * BROWS)

    ceven_ref[...], codd_ref[...] = turned(folded[...])


def iota(rows, cols, axis):
    return lax.broadcasted_iota(jnp.int32, (rows, cols), axis)


def scores_of(q, keys, mask):
    scores = jnp.dot(q, keys, preferred_element_type=F32)
    return scores if mask is None else mask(scores)


def in_range(total):
    good = jnp.where((total >= LOW_TOTAL) & (total <= HIGH_TOTAL), 1.0, 0.0)
    return jnp.min(good.reshape(-1, 8, DV), axis=0)


def over_heads(pairs, load, branches, finish):
    def sums(weights, values):
        out = jnp.dot(weights, values(), preferred_element_type=F32)
        return out[:, :DV], out[:, DV:]

    at_once = 2 if pairs % 2 == 0 else 1
    units = [(pair, side) for pair in range(0, pairs, at_once) for side in range(2)]
    worst, held = [], None
    for now, unit in zip([None] + units, units + [None]):
        q = None if unit is None else load(*unit, at_once)
        fresh, parts = [], []
        for at, (tiles, values) in enumerate(branches):
            weights, ahead = [], []
            for place, (keys, mask) in enumerate(tiles):
                if q is not None:
                    ahead.append(scores_of(q, keys(unit[1]), mask))
                if held is not None:
                    weights.append(jnp.exp2(held[at][place] * SCALE).astype(BF16))
            fresh.append(ahead)
            parts.append((weights, values))
        if held is not None:
            parts = [sums(jnp.concatenate(w, axis=1), values) for w, values in parts]
            worst += [in_range(x) for x in finish(*now, at_once, parts)]
        held = fresh

    @pl.when(jnp.min(functools.reduce(jnp.minimum, worst)) < 0.5)
    def _():
        def exact(pair, _):
            for side in range(2):
                q = load(pair, side, 1)
                parts = []
                for tiles, values in branches:
                    scores = [scores_of(q, keys(side), mask) for keys, mask in tiles]
                    scores = jnp.concatenate(scores, axis=1)
                    top = jnp.max(scores, axis=1, keepdims=True)
                    shifted = (scores - jnp.maximum(top, -1e28)) * SCALE
                    parts.append(sums(jnp.exp2(shifted).astype(BF16), values))
                finish(pair, side, 1, parts)
            return 0

        lax.fori_loop(0, pairs, exact, 0)


def aligned(at):
    return at if isinstance(at, int) else pl.multiple_of(at, 128)


def query_loader(q_ref):
    def load(pair, side, n):
        at = [aligned((pair + p) * PAIR + side * 128) for p in range(n)]
        return jnp.concatenate([q_ref[:, pl.ds(x, 256)] for x in at], axis=0)

    return load


def head_columns(pair, side):
    return pl.ds(aligned(pair * 2 * DV + side * DV), DV)


def gate_loader(gate_ref, first, heads):
    turned = pltpu.roll(gate_ref[...], lax.rem(128 - first, 128), 1)

    def load(pair, side, n, branch):
        if isinstance(pair, int):
            local, at = turned, branch * heads + side + 2 * pair
        else:
            local, at = pltpu.roll(turned, lax.rem(128 - 2 * pair, 128), 1), branch * heads + side
        columns = [local[:, at + 2 * p : at + 2 * p + 1] for p in range(n)]
        shape = (turned.shape[0], DV)
        return jnp.concatenate([jnp.broadcast_to(x, shape) for x in columns], axis=0)

    return load


def stacked(x, times):
    return jnp.concatenate([x] * times, axis=0) if times > 1 else x


def repeated(keep, rows):
    return stacked(keep, rows // keep.shape[0])


def near_kernel(heads, first_block, rim, where_ref, q_ref, gate_ref, *refs):
    keys = refs[:3]
    if rim:
        out_ref, ext = refs[-4], refs[-3:]

        @pl.when((pl.program_id(0) == 0) & (pl.program_id(1) == 0))
        def _():
            fill_rim(where_ref[1], refs[3], refs[4], keys, ext)

        keys, reach = ext, 0
    else:
        out_ref, reach = refs[-1], WINDOW
    count = q_ref.shape[1] // QK
    gate = gate_loader(gate_ref, pl.program_id(1) * count, heads)
    base = pl.multiple_of((first_block + pl.program_id(0)) * QBLK - reach, QBLK)
    row, col = iota(QBLK, QBLK, 0), iota(QBLK, QBLK, 1)

    def tile(place, mask):
        return (lambda side: keys[side][:, pl.ds(base + place * QBLK, QBLK)]), mask

    def finish(pair, side, n, parts):
        ((num, den),) = parts
        total = gate(pair, side, n, 2) * (num / den)
        for p in range(n):
            part = total[p * QBLK : (p + 1) * QBLK]
            out_ref[:, head_columns(pair + p, side)] = part.astype(BF16)
        return [den]

    tiles = [
        tile(0, lambda x: jnp.where(repeated(col >= row, x.shape[0]), x, NEG)),
        tile(1, None),
        tile(2, lambda x: jnp.where(repeated(col <= row, x.shape[0]), x, NEG)),
    ]
    values = lambda: keys[2][pl.ds(base, WINDOW + QBLK)]
    over_heads(count // 2, query_loader(q_ref), [(tiles, values)], finish)


def near_branch(first_block, block_count, where, queries, gates, keys, rims, prior):
    tokens, width = queries.shape
    heads = width // QK
    at_once = 8 if heads % 8 == 0 else 2
    row_block = lambda i, p, *_: (i + first_block, p)
    operands = [queries, gates, *keys]
    specs = [
        pl.BlockSpec((QBLK, at_once * QK), row_block),
        pl.BlockSpec((QBLK, 128), lambda i, p, *_: (i + first_block, 0)),
    ]
    specs += [VMEM_SPEC] * len(keys)
    alias, scratch = {}, []
    if rims is not None:
        other, far = rims
        operands += [other, far]
        specs += [VMEM_SPEC, VMEM_SPEC]
        scratch = [pltpu.VMEM((256, 2 * WINDOW), BF16)] * 2 + [pltpu.VMEM((2 * WINDOW, 256), BF16)]
    if prior is not None:
        operands.append(prior)
        specs.append(pl.BlockSpec(memory_space=pl.ANY))
        alias = {len(operands): 0}
    rows = block_count * QBLK * heads
    return pl.pallas_call(
        functools.partial(near_kernel, heads, first_block, rims is not None),
        grid_spec=pltpu.PrefetchScalarGridSpec(
            num_scalar_prefetch=1,
            grid=(block_count, heads // at_once),
            in_specs=specs,
            out_specs=pl.BlockSpec((QBLK, at_once * DV), row_block),
            scratch_shapes=scratch,
        ),
        out_shape=jax.ShapeDtypeStruct((tokens, heads * DV), BF16),
        input_output_aliases=alias,
        compiler_params=pltpu.CompilerParams(vmem_limit_bytes=VMEM_LIMIT),
        cost_estimate=pl.CostEstimate(
            flops=rows * (WINDOW + QBLK) * 64,
            bytes_accessed=rows * (2 * QK + 4 * DV),
            transcendentals=0,
        ),
        name="near_branch",
    )(where, *operands)


def chosen_kernel(heads, span, *refs):
    first_chunk, widths = span
    out_count = sum(len(w) for w in widths)
    meta_ref, slots_ref, dead_ref, q_ref, gate_ref, near_ref = refs[:6]
    (key_pool, val_pool), cfold, weight_ref = refs[6:8], refs[8:11], refs[11]
    outs = list(refs[12 : 12 + out_count])
    gathered, even, odd, val, attended, weight, weight_sem = refs[12 + out_count :]
    keys = (even, odd)
    turn, step = pl.program_id(0), pl.program_id(1)
    last = pl.num_programs(1) - 1
    rows = q_ref.shape[0]
    count = q_ref.shape[1] // QK
    chunk_start = meta_ref[2 + first_chunk + turn] * rows
    list_at = lax.div(chunk_start, QBLK)
    first_row = lax.rem(chunk_start, QBLK)
    position = meta_ref[2] + chunk_start
    copy = pltpu.make_async_copy(weight_ref, weight, weight_sem)

    @pl.when(step == 0)
    def _():
        for slot in range(PICKS):
            source = pl.multiple_of(slots_ref[list_at, slot] * KBLK, KBLK)
            gathered[slot * KBLK : (slot + 1) * KBLK] = key_pool[pl.ds(source, KBLK)]
            val[slot * KBLK : (slot + 1) * KBLK] = with_ones(val_pool[pl.ds(source, KBLK)])
        for slot in range(1, PICKS):

            @pl.when(dead_ref[list_at, slot] == 1)
            def _():
                at = slice(slot * KBLK, (slot + 1) * KBLK)
                gathered[at] = jnp.broadcast_to(gathered[:1], (KBLK, 256))
                val[at] = jnp.zeros((KBLK, 256), BF16)

        even[...], odd[...] = turned(gathered[...])

    @pl.when((turn == 0) & (step == 0))
    def _():
        copy.start()

    gate = gate_loader(gate_ref, step * count, heads)
    row = iota(rows, TILE, 0)
    col = iota(rows, TILE, 1)
    own_keep = (col >= KBLK) | (col <= row + first_row)

    def own_mask(scores):
        own = jnp.where(repeated(own_keep[:, :128], scores.shape[0]), scores[:, :128], NEG)
        return jnp.concatenate([own, scores[:, 128:]], axis=1)

    def comp_mask(place):
        ends = (col + place * TILE + 1) * CBLK - 1
        return lambda x: jnp.where(repeated(ends <= row + position, x.shape[0]), x, NEG)

    def tile(refs, place, mask):
        return (lambda side: refs[side][:, place * TILE : (place + 1) * TILE]), mask

    chosen = [tile(keys, p, own_mask if p == 0 else None) for p in range(PICKS * KBLK // TILE)]
    folded = [tile(cfold, p, comp_mask(p)) for p in range(cfold[2].shape[0] // TILE)]
    empty = row[:, :DV] + position < CBLK - 1

    def finish(pair, side, n, parts):
        (num, den), (folded_num, folded_den) = parts
        folded_den = jnp.where(stacked(empty, n), 1.0, folded_den)
        total = gate(pair, side, n, 1) * (num / den)
        total = total + gate(pair, side, n, 0) * (folded_num / folded_den)
        for p in range(n):
            cols = head_columns(pair + p, side)
            mixed = near_ref[:, cols].astype(F32) + total[p * rows : (p + 1) * rows]
            attended[step, :, cols] = mixed.astype(BF16)
        return [den, folded_den]

    branches = [(chosen, lambda: val[...]), (folded, lambda: cfold[2][...])]
    over_heads(count // 2, query_loader(q_ref), branches, finish)

    @pl.when((turn == 0) & (step == last))
    def _():
        copy.wait()

    for place, parts in enumerate(widths):
        chunk_outs = [outs.pop(0) for _ in parts]

        @pl.when((turn == place) & (step == last))
        def _():
            rows_in = jnp.concatenate([attended[s] for s in range(attended.shape[0])], axis=1)
            first_col = 0
            for out_ref in chunk_outs:
                for at in range(0, out_ref.shape[1], 256):
                    cols = weight[:, first_col + at : first_col + at + 256]
                    part = jnp.dot(rows_in, cols, preferred_element_type=F32)
                    out_ref[:, at : at + 256] = part.astype(out_ref.dtype)
                first_col += out_ref.shape[1]


def chosen_and_project(first_chunk, widths, rows, meta, slots, dead, queries, gates, near, pools, out_weight):
    tokens, width = queries.shape
    heads = width // QK
    at_once = 8 if heads % 8 == 0 else 2
    steps = heads // at_once
    whole = lambda x: pl.BlockSpec(x.shape, lambda i, p, *_: (0,) * x.ndim)
    outs = [jax.ShapeDtypeStruct((rows, width), BF16) for chunk in widths for width in chunk]
    return pl.pallas_call(
        functools.partial(chosen_kernel, heads, (first_chunk, widths)),
        grid_spec=pltpu.PrefetchScalarGridSpec(
            num_scalar_prefetch=3,
            grid=(len(widths), steps),
            in_specs=[
                pl.BlockSpec((rows, at_once * QK), lambda i, p, m, *_: (m[2 + first_chunk + i], p)),
                pl.BlockSpec((rows, 128), lambda i, p, m, *_: (m[2 + first_chunk + i], 0)),
                pl.BlockSpec((rows, at_once * DV), lambda i, p, m, *_: (m[2 + first_chunk + i], p)),
            ]
            + [VMEM_SPEC] * len(pools)
            + [pl.BlockSpec(memory_space=pl.ANY)],
            out_specs=[VMEM_SPEC] * len(outs),
            scratch_shapes=[
                pltpu.VMEM((PICKS * KBLK, 256), BF16),
                pltpu.VMEM((256, PICKS * KBLK), BF16),
                pltpu.VMEM((256, PICKS * KBLK), BF16),
                pltpu.VMEM((PICKS * KBLK, 256), BF16),
                pltpu.VMEM((steps, rows, at_once * DV), BF16),
                pltpu.VMEM(out_weight.shape, BF16),
                pltpu.SemaphoreType.DMA,
            ],
        ),
        out_shape=outs,
        compiler_params=pltpu.CompilerParams(vmem_limit_bytes=VMEM_LIMIT),
        cost_estimate=pl.CostEstimate(
            flops=rows * heads * PICKS * KBLK * 64,
            bytes_accessed=out_weight.size,
            transcendentals=0,
        ),
        name="chosen_and_project",
    )(meta, slots, dead, queries, gates, near, *pools, out_weight)


VMEM_SPEC = pl.BlockSpec(memory_space=pltpu.VMEM)


def single_step(kernel, name, scalars, arrays, outs, scratch=(), in_spec=None, out_spec=None):
    whole = lambda x: pl.BlockSpec(x.shape, lambda i, *_: (0,) * len(x.shape))
    return pl.pallas_call(
        kernel,
        grid_spec=pltpu.PrefetchScalarGridSpec(
            num_scalar_prefetch=len(scalars),
            grid=(1,),
            in_specs=[in_spec or whole(x) for x in arrays],
            out_specs=[out_spec or whole(x) for x in outs],
            scratch_shapes=list(scratch),
        ),
        out_shape=outs,
        compiler_params=pltpu.CompilerParams(vmem_limit_bytes=VMEM_LIMIT),
        name=name,
    )(*scalars, *arrays)


def last_sum(halves, rows, kept_ref, *refs):
    halves, others, out_ref = refs[:halves], refs[halves:-1], refs[-1]
    at = pl.ds(pl.multiple_of(pl.program_id(0) * rows, rows), rows)
    first = 0
    for half in halves:
        cols = slice(first, first + half.shape[1])
        total = kept_ref[:, cols].astype(F32) + half[at].astype(F32)
        for other in others:
            total = total + other[at, cols].astype(F32)
        out_ref[:, cols] = total.astype(BF16)
        first += half.shape[1]


def local(
    queries,
    key_rows,
    value_rows,
    comp_key_weight,
    comp_value_weight,
    block_picks,
    gate_logits,
    out_weight,
):
    tokens = queries.shape[0]
    heads = queries.shape[1] // QK
    n_ctx, n_head = lax.axis_size("ctx"), lax.axis_size("head")
    shard, head_at = lax.axis_index("ctx"), lax.axis_index("head")
    group = head_at * heads // (HEADS // GROUPS)
    per_owner = tokens // KBLK
    lists = tokens // QBLK
    folds = tokens // CBLK
    groups = n_ctx // 2
    rim_blocks = WINDOW // KBLK
    packed_rows = per_owner * BROWS
    bf16 = lambda *shape: jax.ShapeDtypeStruct(shape, BF16)

    chips = n_head // 2
    chip, core = head_at // 2, lax.rem(head_at, 2)
    order = []
    for step in list(range(1, chips)) + [0]:
        target = lax.rem(chip + step, chips) * 2
        order += [target + 1 - core, target + core]
    where = jnp.stack([group, shard, shard * tokens] + order).astype(jnp.int32)
    rim_rows = rim_blocks * BROWS
    fold_weights = jnp.concatenate([comp_key_weight, comp_value_weight], axis=1)
    int32 = lambda *shape: jax.ShapeDtypeStruct(shape, jnp.int32)
    prep_out = [bf16(packed_rows + 3 * folds, 128), bf16(rim_rows, 128)]
    prep_out += [int32(1, n_ctx * lists), int32(lists, 2 * PICKS), int32(lists, 2 * PICKS)]
    prep_out += [bf16(256, tokens)] * 2 + [bf16(tokens, 256)]
    packed, rim, named, slots, dead, even, odd, val = pl.pallas_call(
        prep_kernel,
        grid_spec=pltpu.PrefetchScalarGridSpec(
            num_scalar_prefetch=1,
            grid=(1,),
            in_specs=[pl.BlockSpec(memory_space=pl.ANY)] * 4,
            out_specs=[VMEM_SPEC] * 2
            + [pl.BlockSpec(x.shape, lambda i, g: (0, 0)) for x in prep_out[2:5]]
            + [VMEM_SPEC] * 3,
            scratch_shapes=[
                pltpu.VMEM(block_picks.shape, jnp.int32),
                pltpu.VMEM((tokens, PAIR), BF16),
                pltpu.VMEM((tokens, DV), BF16),
                pltpu.VMEM((CBLK, PAIR), F32),
                pltpu.VMEM((CBLK, DV), F32),
                pltpu.SemaphoreType.DMA((5,)),
            ],
        ),
        out_shape=prep_out,
        compiler_params=pltpu.CompilerParams(vmem_limit_bytes=51 * 1024 * 1024),
        name="prep",
    )(where, block_picks, key_rows, value_rows, fold_weights)
    other = lax.ppermute(packed, "ctx", [(i, i ^ 1) for i in range(n_ctx)])
    named = [named] + [
        lax.ppermute(named, "ctx", [(i, i - 2 * d) for i in range(2 * d, n_ctx)])
        for d in range(1, groups)
    ]
    far_rim = lax.ppermute(rim, "ctx", [(i, i + 1) for i in range(1, n_ctx - 1, 2)])

    gates = jax.nn.sigmoid(gate_logits).reshape(tokens, 3 * heads)
    gates = jnp.pad(gates, ((0, 0), (0, 128 - 3 * heads)))
    sent = bf16(lists * BROWS + 3 * folds, 128)

    def pack(beside, lists_in, rows):
        return single_step(
            functools.partial(pack_kernel, lists, beside),
            "pack",
            [where, *lists_in],
            [rows],
            [sent] * len(lists_in),
            in_spec=VMEM_SPEC,
            out_spec=VMEM_SPEC,
        )

    def ahead(send, distance):
        return lax.ppermute(send, "ctx", [(i, i + 2 * distance) for i in range(n_ctx - 2 * distance)])

    named, gates = lax.optimization_barrier((named, gates))
    own_sends = pack(False, named[1:], packed)
    own_sends, even = lax.optimization_barrier((own_sends, even))
    from_same = [ahead(send, d) for d, send in enumerate(own_sends, 1)]

    reach = WINDOW // QBLK
    near = functools.partial(near_branch, where=where, queries=queries, gates=gates)
    near = functools.partial(near, keys=(even, odd, val))
    mixed = near(lists - 1, 1, rims=None, prior=None)

    other, mixed = lax.optimization_barrier((other, mixed))
    beside, *other_sends = pack(True, named, other)
    other_sends, mixed = lax.optimization_barrier((other_sends, mixed))
    from_other = [ahead(send, d) for d, send in enumerate(other_sends, 1)]
    if lists - reach > 1:
        mixed = near(reach, lists - reach - 1, rims=None, prior=mixed)
    mixed = near(0, reach, rims=(other, far_rim), prior=mixed)

    received = [beside] + [x for both in zip(from_same, from_other) for x in both]
    pools = single_step(
        functools.partial(pool_kernel, groups, lists),
        "pool",
        [where],
        [packed] + received,
        [bf16(n_ctx * lists * KBLK, 256), bf16(n_ctx * lists * KBLK, DV)]
        + [bf16(256, n_ctx * folds)] * 2
        + [bf16(n_ctx * folds, 256)],
        [pltpu.VMEM((n_ctx * folds, 256), BF16)],
        in_spec=VMEM_SPEC,
        out_spec=VMEM_SPEC,
    )
    rows = tokens // n_head
    across = [(i, i ^ 1) for i in range(n_head)]

    model = out_weight.shape[1]

    def project(first_chunk, widths):
        return chosen_and_project(
            first_chunk, widths, rows, where, slots, dead, queries, gates, mixed, pools, out_weight
        )

    sums = []
    for step in range(chips - 1):
        other = lax.ppermute(project(1 + 2 * step, [[model]])[0], "head", across)
        mine = project(2 + 2 * step, [[model]])[0]
        summed = (mine.astype(F32) + other.astype(F32)).astype(BF16)
        summed, where = lax.optimization_barrier((summed, where))
        sums.append(summed)
    *passed, kept = project(n_head - 1, [[model // 2] * 2, [model]])
    near_parts = [lax.ppermute(x, "head", across) for x in passed]
    arrived = []
    for step, summed in enumerate(sums, 1):
        route = [(i, (i + 2 * step) % n_head) for i in range(n_head)]
        arrived.append(lax.ppermute(summed, "head", route))
    steps = 4 if rows % 64 == 0 else 1
    row_block = pl.BlockSpec((rows // steps, model), lambda i: (i, 0))
    return pl.pallas_call(
        functools.partial(last_sum, len(near_parts), rows // steps),
        grid=(steps,),
        in_specs=[row_block] + [VMEM_SPEC] * (len(near_parts) + len(arrived)),
        out_specs=row_block,
        out_shape=bf16(rows, model),
        compiler_params=pltpu.CompilerParams(vmem_limit_bytes=VMEM_LIMIT),
        name="last_sum",
    )(kept, *near_parts, *arrived)


def solution(mesh):
    placed = (
        P("ctx", "head"),
        P("ctx", None),
        P("ctx", None),
        P(),
        P(),
        P("ctx", None, None),
        P("ctx", None, "head"),
        P("head", None),
    )
    return jax.shard_map(
        local, mesh=mesh, in_specs=placed, out_specs=P(("ctx", "head"), None), check_vma=False
    )
```

```python
import functools

import jax
import jax.numpy as jnp
from jax import lax
from jax.experimental import pallas as pl
from jax.experimental.pallas import tpu as pltpu
from jax.sharding import PartitionSpec as P

HEADS = 64
GROUPS = 4
QK = 192
DV = 128
CBLK = 32
KBLK = 64
PICKS = 16
WINDOW = 512
QBLK = 256
PAIR = 2 * QK
BROWS = KBLK + KBLK // 2 + KBLK
VMEM_LIMIT = 50 * 1024 * 1024
CHOSEN_LIMIT = 48 * 1024 * 1024
NEG = -1e30
SCALE = QK ** (-0.5) * 1.4426950408889634
LOW_TOTAL, HIGH_TOTAL = 2.0**-60, 2.0**100
TILE = 256
NT = (((1,), (1,)), ((), ()))
F32 = jnp.float32
BF16 = jnp.bfloat16


def half_lanes(rows):
    return lax.broadcasted_iota(jnp.int32, (rows, 128), 1) < 64


def swap_halves(x):
    return pltpu.roll(x, 64, 1)


def turned(keys):
    row, col = iota(256, 256, 0), iota(256, 256, 1)
    unit = (row == col).astype(BF16)
    even = lax.dot_general(unit, keys, NT, preferred_element_type=F32).astype(BF16)
    return even, lower(even)


def lower(even):
    return jnp.concatenate([jnp.zeros((64, even.shape[1]), BF16), even[:QK]], axis=0)


def with_ones(values):
    return jnp.concatenate([values, jnp.ones_like(values)], axis=1)


def plan(group, shard, per_owner, picks_ref, lists_ref, slots_ref, dead_ref):
    lists = picks_ref.shape[0]
    total = lists_ref.shape[1] // lists * per_owner
    width = slots_ref.shape[1]
    picks = jnp.zeros((lists, PICKS), jnp.int32)
    for each in range(picks_ref.shape[1]):
        picks = jnp.where(group == each, picks_ref[:, each, :], picks)
    block = iota(lists, total, 1)
    hits = [block == picks[:, entry : entry + 1] for entry in range(PICKS)]
    named = functools.reduce(jnp.logical_or, hits).astype(F32)
    named = jnp.broadcast_to(jnp.max(named, axis=0, keepdims=True), (8, total))
    row, col = iota(total, total, 0), iota(total, total, 1)
    before = (lax.div(row, per_owner) == lax.div(col, per_owner)) & (row < col)
    rank = jnp.dot(named, before.astype(F32), preferred_element_type=F32)
    rank = jnp.minimum(rank, float(lists - 1))
    inside = lax.rem(iota(8, total, 1), per_owner).astype(F32)
    found = jnp.zeros((8, lists_ref.shape[1]), F32)
    row, col = iota(total, lists_ref.shape[1], 0), iota(total, lists_ref.shape[1], 1)
    for place in range(lists):
        to = (col == lax.div(row, per_owner) * lists + place).astype(F32)
        value = jnp.where(rank == float(place), named * inside, 0.0)
        found = found + jnp.dot(value, to, preferred_element_type=F32)
    lists_ref[...] = found[:1].astype(jnp.int32)

    owner = lax.div(block, per_owner)
    turn = (lax.div(shard, 2) - lax.div(owner, 2)) * 2 + ((owner ^ shard) & 1)
    slot = jnp.clip(turn * lists + rank[:lists].astype(jnp.int32), 0, lists_ref.shape[1] - 1)
    slot = slot.astype(F32)
    first = shard * per_owner + iota(lists, 1, 0) * (QBLK // KBLK)
    own = block == first

    def pick_out(hit, values):
        return jnp.sum(jnp.where(hit, values, 0.0), axis=1, keepdims=True)

    lane = iota(lists, width, 1)
    slots = jnp.where(lane == 0, pick_out(own, slot), 0.0)
    dead = jnp.zeros((lists, width), F32)
    seen = own.astype(F32)
    at = jnp.ones((lists, 1), jnp.int32)
    met = jnp.zeros((lists, 1), jnp.int32)
    for entry, hit in enumerate(hits):
        pick = picks[:, entry : entry + 1]
        is_own = (pick == first).astype(jnp.int32)
        gone = jnp.maximum(pick_out(hit, seen), (pick > first).astype(F32))
        slots = jnp.where(lane == at, pick_out(hit, slot), slots)
        dead = jnp.where(lane == at, gone, dead)
        seen = jnp.maximum(seen, hit.astype(F32))
        at = at + 1 - is_own * (1 - met)
        met = jnp.maximum(met, is_own)
    slots_ref[...] = slots.astype(jnp.int32)
    dead_ref[...] = dead.astype(jnp.int32)


def prep_kernel(
    where_ref,
    picks_in,
    keys_in,
    values_in,
    fold_in,
    packed_ref,
    rim_ref,
    lists_ref,
    slots_ref,
    dead_ref,
    even_ref,
    odd_ref,
    val_ref,
    picks_ref,
    keys_ref,
    values_ref,
    kw_ref,
    vw_ref,
    sems,
):
    group, shard = where_ref[0], where_ref[1]
    pair = pl.ds(pl.multiple_of(lax.div(group, 2) * PAIR, 128), PAIR)
    single = pl.ds(pl.multiple_of(group * DV, 128), DV)
    folded_value = pl.ds(pl.multiple_of(GROUPS * QK + group * DV, 128), DV)
    copies = [
        pltpu.make_async_copy(source, target, sems.at[i])
        for i, (source, target) in enumerate(
            [
                (picks_in, picks_ref),
                (keys_in.at[:, pair], keys_ref),
                (values_in.at[:, single], values_ref),
                (fold_in.at[:, pair], kw_ref),
                (fold_in.at[:, folded_value], vw_ref),
            ]
        )
    ]
    for copy in copies:
        copy.start()
    copies[0].wait()
    plan(group, shard, keys_ref.shape[0] // KBLK, picks_ref, lists_ref, slots_ref, dead_ref)
    for copy in copies[1:]:
        copy.wait()
    odd = lax.rem(group, 2) == 1

    def own_columns(ref):
        t0 = ref[:, :128].astype(F32)
        t1 = ref[:, 128:256].astype(F32)
        t2 = ref[:, 256:].astype(F32)
        r1, r2 = swap_halves(t1), swap_halves(t2)
        left = half_lanes(t0.shape[0])
        low = jnp.where(odd, jnp.where(left, r1, r2), t0)
        high = jnp.where(left, jnp.where(odd, r2, t1), 0.0)
        return low, high

    low, high = own_columns(keys_ref)
    values = values_ref[...]
    rows = low.shape[0]
    count = rows // KBLK
    high3 = high.reshape(count, KBLK, 128)
    packed_high = high3[:, : KBLK // 2] + swap_halves(
        high3[:, KBLK // 2 :].reshape(count * KBLK // 2, 128)
    ).reshape(count, KBLK // 2, 128)
    even = jnp.concatenate([low.astype(BF16), high.astype(BF16)], axis=1)
    even_ref[...], odd_ref[...] = turned(even)
    val_ref[...] = with_ones(values)
    for block in range(count):
        at = block * BROWS
        token = slice(block * KBLK, block * KBLK + KBLK)
        packed_ref[at : at + KBLK] = low[token].astype(BF16)
        packed_ref[at + KBLK : at + KBLK + KBLK // 2] = packed_high[block].astype(BF16)
        packed_ref[at + KBLK + KBLK // 2 : at + BROWS] = values[token]
    rim_rows = rim_ref.shape[0]
    rim_ref[...] = packed_ref[count * BROWS - rim_rows : count * BROWS]

    wlow, whigh = own_columns(kw_ref)
    folds = rows // CBLK

    def fold(x, w):
        return jnp.sum(x.reshape(folds, CBLK, 128) * w[None], axis=1).astype(BF16)

    at = count * BROWS
    packed_ref[at : at + folds] = fold(low, wlow)
    packed_ref[at + folds : at + 2 * folds] = fold(high, whigh)
    packed_ref[at + 2 * folds :] = fold(values.astype(F32), vw_ref[...])


def pack_kernel(lists, beside, where_ref, *refs):
    count = len(refs) // 2
    named, ref, outs = refs[:count], refs[count], refs[count + 1 :]
    shard = where_ref[1]
    owner = shard + 1 - 2 * lax.rem(shard, 2) if beside else shard
    data = ref.shape[0] - (outs[0].shape[0] - lists * BROWS)
    for blocks, out in zip(named, outs):
        for place in range(lists):
            at = pl.multiple_of(blocks[0, owner * lists + place] * BROWS, 16)
            out[place * BROWS : (place + 1) * BROWS] = ref[pl.ds(at, BROWS)]
        out[lists * BROWS :] = ref[data:]


def unpack(ref, at, count, step=1):
    lows, packed, values = [], [], []
    for block in range(count):
        first = at + block * step * BROWS
        lows.append(ref[first : first + KBLK])
        packed.append(ref[first + KBLK : first + KBLK + KBLK // 2])
        values.append(ref[first + KBLK + KBLK // 2 : first + BROWS])
    packed = jnp.concatenate(packed, axis=0)
    row, col = iota(128, 256, 0), iota(128, 256, 1)
    take = (row == jnp.where(col < 128, col, col - 64)) & (lax.rem(col, 128) < 64)
    both = jnp.dot(packed, take.astype(BF16), preferred_element_type=F32).astype(BF16)
    half = KBLK // 2
    highs = []
    for block in range(count):
        rows = slice(block * half, block * half + half)
        highs += [both[rows, :128], both[rows, 128:]]
    even = jnp.concatenate(
        [jnp.concatenate(lows, axis=0), jnp.concatenate(highs, axis=0)], axis=1
    )
    return even, jnp.concatenate(values, axis=0)


def fill_rim(shard, near_ref, far_ref, own, ext):
    rim_blocks = WINDOW // KBLK
    even_in, odd_in, val_in = own
    even_ref, odd_ref, val_ref = ext
    even_ref[:, WINDOW:] = even_in[:, :WINDOW]
    odd_ref[:, WINDOW:] = odd_in[:, :WINDOW]
    val_ref[WINDOW:] = val_in[:WINDOW]
    use_near = lax.rem(shard, 2) == 1
    rim_end = near_ref.shape[0] // BROWS * BROWS
    near_rim = near_ref[rim_end - far_ref.shape[0] : rim_end]

    @pl.when(shard > 0)
    def _():
        keys, values = unpack(jnp.where(use_near, near_rim, far_ref[...]), 0, rim_blocks)
        even_ref[:, :WINDOW], odd_ref[:, :WINDOW] = turned(keys)
        val_ref[:WINDOW] = with_ones(values)

    @pl.when(shard == 0)
    def _():
        even = jnp.broadcast_to(even_in[:, :1].astype(F32), (256, WINDOW)).astype(BF16)
        even_ref[:, :WINDOW], odd_ref[:, :WINDOW] = even, lower(even)
        val_ref[:WINDOW] = jnp.zeros((WINDOW, 256), BF16)


def pool_kernel(groups, lists, where_ref, own_ref, *refs):
    sent = 2 * groups - 1
    ins, (key_ref, val_ref, ceven_ref, codd_ref, cval_ref, folded) = refs[:sent], refs[sent:]
    shard = where_ref[1]
    parity = lax.rem(shard, 2)
    base = shard - parity
    rows = lists * KBLK
    folds = (ins[0].shape[0] - lists * BROWS) // 3
    folded[...] = jnp.zeros_like(folded)
    cval_ref[...] = jnp.zeros_like(cval_ref)

    def fill(place, owner, ref, step, fold_at):
        keys, values = unpack(ref, 0, lists, step)
        at = slice(place * rows, place * rows + rows)
        key_ref[at] = keys
        val_ref[at] = values
        low = ref[fold_at : fold_at + folds]
        high = ref[fold_at + folds : fold_at + 2 * folds]
        owned = pl.ds(pl.multiple_of(owner * folds, 32), folds)
        folded[owned] = jnp.concatenate([low, high], axis=1)
        cval_ref[owned] = with_ones(ref[fold_at + 2 * folds : fold_at + 3 * folds])

    fill(0, shard, own_ref, QBLK // KBLK, own_ref.shape[0] - 3 * folds)
    fill(1, base + 1 - parity, ins[0], 1, lists * BROWS)
    for distance in range(1, groups):

        @pl.when(base >= 2 * distance)
        def _():
            for side in range(2):
                owner = base - 2 * distance + (parity if side == 0 else 1 - parity)
                fill(2 * distance + side, owner, ins[2 * distance - 1 + side], 1, lists * BROWS)

    ceven_ref[...], codd_ref[...] = turned(folded[...])


def iota(rows, cols, axis):
    return lax.broadcasted_iota(jnp.int32, (rows, cols), axis)


def scores_of(q, keys, mask):
    scores = jnp.dot(q, keys, preferred_element_type=F32)
    return scores if mask is None else mask(scores)


def in_range(total):
    good = jnp.where((total >= LOW_TOTAL) & (total <= HIGH_TOTAL), 1.0, 0.0)
    return jnp.min(good.reshape(-1, 8, DV), axis=0)


def over_heads(pairs, load, branches, finish):
    def sums(weights, values):
        out = jnp.dot(weights, values(), preferred_element_type=F32)
        return out[:, :DV], out[:, DV:]

    at_once = 2 if pairs % 2 == 0 else 1
    units = [(pair, side) for pair in range(0, pairs, at_once) for side in range(2)]
    worst, held = [], None
    for now, unit in zip([None] + units, units + [None]):
        q = None if unit is None else load(*unit, at_once)
        fresh, parts = [], []
        for at, (tiles, values) in enumerate(branches):
            weights, ahead = [], []
            for place, (keys, mask) in enumerate(tiles):
                if q is not None:
                    ahead.append(scores_of(q, keys(unit[1]), mask))
                if held is not None:
                    weights.append(jnp.exp2(held[at][place] * SCALE).astype(BF16))
            fresh.append(ahead)
            parts.append((weights, values))
        if held is not None:
            parts = [sums(jnp.concatenate(w, axis=1), values) for w, values in parts]
            worst += [in_range(x) for x in finish(*now, at_once, parts)]
        held = fresh

    @pl.when(jnp.min(functools.reduce(jnp.minimum, worst)) < 0.5)
    def _():
        def exact(pair, _):
            for side in range(2):
                q = load(pair, side, 1)
                parts = []
                for tiles, values in branches:
                    scores = [scores_of(q, keys(side), mask) for keys, mask in tiles]
                    scores = jnp.concatenate(scores, axis=1)
                    top = jnp.max(scores, axis=1, keepdims=True)
                    shifted = (scores - jnp.maximum(top, -1e28)) * SCALE
                    parts.append(sums(jnp.exp2(shifted).astype(BF16), values))
                finish(pair, side, 1, parts)
            return 0

        lax.fori_loop(0, pairs, exact, 0)


def aligned(at):
    return at if isinstance(at, int) else pl.multiple_of(at, 128)


def query_loader(q_ref):
    def load(pair, side, n):
        at = [aligned((pair + p) * PAIR + side * 128) for p in range(n)]
        return jnp.concatenate([q_ref[:, pl.ds(x, 256)] for x in at], axis=0)

    return load


def head_columns(pair, side):
    return pl.ds(aligned(pair * 2 * DV + side * DV), DV)


def gate_loader(gate_ref, first, heads):
    turned = pltpu.roll(gate_ref[...], lax.rem(128 - first, 128), 1)

    def load(pair, side, n, branch):
        if isinstance(pair, int):
            local, at = turned, branch * heads + side + 2 * pair
        else:
            local, at = pltpu.roll(turned, lax.rem(128 - 2 * pair, 128), 1), branch * heads + side
        columns = [local[:, at + 2 * p : at + 2 * p + 1] for p in range(n)]
        shape = (turned.shape[0], DV)
        return jnp.concatenate([jnp.broadcast_to(x, shape) for x in columns], axis=0)

    return load


def stacked(x, times):
    return jnp.concatenate([x] * times, axis=0) if times > 1 else x


def repeated(keep, rows):
    return stacked(keep, rows // keep.shape[0])


def near_kernel(heads, first_block, rim, where_ref, q_ref, gate_ref, *refs):
    keys = refs[:3]
    if rim:
        out_ref, ext = refs[-4], refs[-3:]

        @pl.when((pl.program_id(0) == 0) & (pl.program_id(1) == 0))
        def _():
            fill_rim(where_ref[1], refs[3], refs[4], keys, ext)

        keys, reach = ext, 0
    else:
        out_ref, reach = refs[-1], WINDOW
    count = q_ref.shape[1] // QK
    gate = gate_loader(gate_ref, pl.program_id(1) * count, heads)
    base = pl.multiple_of((first_block + pl.program_id(0)) * QBLK - reach, QBLK)
    row, col = iota(QBLK, QBLK, 0), iota(QBLK, QBLK, 1)

    def tile(place, mask):
        return (lambda side: keys[side][:, pl.ds(base + place * QBLK, QBLK)]), mask

    def finish(pair, side, n, parts):
        ((num, den),) = parts
        total = gate(pair, side, n, 2) * (num / den)
        for p in range(n):
            part = total[p * QBLK : (p + 1) * QBLK]
            out_ref[:, head_columns(pair + p, side)] = part.astype(BF16)
        return [den]

    tiles = [
        tile(0, lambda x: jnp.where(repeated(col >= row, x.shape[0]), x, NEG)),
        tile(1, None),
        tile(2, lambda x: jnp.where(repeated(col <= row, x.shape[0]), x, NEG)),
    ]
    values = lambda: keys[2][pl.ds(base, WINDOW + QBLK)]
    over_heads(count // 2, query_loader(q_ref), [(tiles, values)], finish)


def near_branch(first_block, block_count, where, queries, gates, keys, rims, prior):
    tokens, width = queries.shape
    heads = width // QK
    at_once = next(n for n in (16, 8, 4, 2) if heads % n == 0)
    row_block = lambda i, p, *_: (i + first_block, p)
    operands = [queries, gates, *keys]
    specs = [
        pl.BlockSpec((QBLK, at_once * QK), row_block),
        pl.BlockSpec((QBLK, 128), lambda i, p, *_: (i + first_block, 0)),
    ]
    specs += [VMEM_SPEC] * len(keys)
    alias, scratch = {}, []
    if rims is not None:
        other, far = rims
        operands += [other, far]
        specs += [VMEM_SPEC, VMEM_SPEC]
        scratch = [pltpu.VMEM((256, 2 * WINDOW), BF16)] * 2 + [pltpu.VMEM((2 * WINDOW, 256), BF16)]
    if prior is not None:
        operands.append(prior)
        specs.append(pl.BlockSpec(memory_space=pl.ANY))
        alias = {len(operands): 0}
    rows = block_count * QBLK * heads
    return pl.pallas_call(
        functools.partial(near_kernel, heads, first_block, rims is not None),
        grid_spec=pltpu.PrefetchScalarGridSpec(
            num_scalar_prefetch=1,
            grid=(block_count, heads // at_once),
            in_specs=specs,
            out_specs=pl.BlockSpec((QBLK, at_once * DV), row_block),
            scratch_shapes=scratch,
        ),
        out_shape=jax.ShapeDtypeStruct((tokens, heads * DV), BF16),
        input_output_aliases=alias,
        compiler_params=pltpu.CompilerParams(vmem_limit_bytes=VMEM_LIMIT),
        cost_estimate=pl.CostEstimate(
            flops=rows * (WINDOW + QBLK) * 64,
            bytes_accessed=rows * (2 * QK + 4 * DV),
            transcendentals=0,
        ),
        name="near_branch",
    )(where, *operands)


def chosen_kernel(heads, span, *refs):
    first_chunk, widths = span
    out_count = sum(len(w) for w in widths)
    meta_ref, slots_ref, dead_ref, q_ref, gate_ref, near_ref = refs[:6]
    (key_pool, val_pool), cfold, weight_ref = refs[6:8], refs[8:11], refs[11]
    outs = list(refs[12 : 12 + out_count])
    gathered, even, odd, val, attended, weight, weight_sem = refs[12 + out_count :]
    keys = (even, odd)
    turn, step = pl.program_id(0), pl.program_id(1)
    last = pl.num_programs(1) - 1
    rows = q_ref.shape[0]
    count = q_ref.shape[1] // QK
    chunk_start = meta_ref[2 + first_chunk + turn] * rows
    list_at = lax.div(chunk_start, QBLK)
    first_row = lax.rem(chunk_start, QBLK)
    position = meta_ref[2] + chunk_start
    copy = pltpu.make_async_copy(weight_ref, weight, weight_sem)

    @pl.when(step == 0)
    def _():
        for slot in range(PICKS):
            source = pl.multiple_of(slots_ref[list_at, slot] * KBLK, KBLK)
            gathered[slot * KBLK : (slot + 1) * KBLK] = key_pool[pl.ds(source, KBLK)]
            val[slot * KBLK : (slot + 1) * KBLK] = with_ones(val_pool[pl.ds(source, KBLK)])
        for slot in range(1, PICKS):

            @pl.when(dead_ref[list_at, slot] == 1)
            def _():
                at = slice(slot * KBLK, (slot + 1) * KBLK)
                gathered[at] = jnp.broadcast_to(gathered[:1], (KBLK, 256))
                val[at] = jnp.zeros((KBLK, 256), BF16)

        even[...], odd[...] = turned(gathered[...])

    @pl.when((turn == 0) & (step == 0))
    def _():
        copy.start()

    gate = gate_loader(gate_ref, step * count, heads)
    row = iota(rows, TILE, 0)
    col = iota(rows, TILE, 1)
    own_keep = (col >= KBLK) | (col <= row + first_row)

    def own_mask(scores):
        own = jnp.where(repeated(own_keep[:, :128], scores.shape[0]), scores[:, :128], NEG)
        return jnp.concatenate([own, scores[:, 128:]], axis=1)

    def comp_mask(place):
        ends = (col + place * TILE + 1) * CBLK - 1
        return lambda x: jnp.where(repeated(ends <= row + position, x.shape[0]), x, NEG)

    def tile(refs, place, mask):
        return (lambda side: refs[side][:, place * TILE : (place + 1) * TILE]), mask

    chosen = [tile(keys, p, own_mask if p == 0 else None) for p in range(PICKS * KBLK // TILE)]
    folded = [tile(cfold, p, comp_mask(p)) for p in range(cfold[2].shape[0] // TILE)]
    empty = row[:, :DV] + position < CBLK - 1

    def finish(pair, side, n, parts):
        (num, den), (folded_num, folded_den) = parts
        folded_den = jnp.where(stacked(empty, n), 1.0, folded_den)
        total = gate(pair, side, n, 1) * (num / den)
        total = total + gate(pair, side, n, 0) * (folded_num / folded_den)
        for p in range(n):
            cols = head_columns(pair + p, side)
            mixed = near_ref[:, cols].astype(F32) + total[p * rows : (p + 1) * rows]
            attended[step, :, cols] = mixed.astype(BF16)
        return [den, folded_den]

    branches = [(chosen, lambda: val[...]), (folded, lambda: cfold[2][...])]
    over_heads(count // 2, query_loader(q_ref), branches, finish)

    @pl.when((turn == 0) & (step == last))
    def _():
        copy.wait()

    for place, parts in enumerate(widths):
        chunk_outs = [outs.pop(0) for _ in parts]

        @pl.when((turn == place) & (step == last))
        def _():
            rows_in = jnp.concatenate([attended[s] for s in range(attended.shape[0])], axis=1)
            first_col = 0
            for out_ref in chunk_outs:
                for at in range(0, out_ref.shape[1], 256):
                    cols = weight[:, first_col + at : first_col + at + 256]
                    part = jnp.dot(rows_in, cols, preferred_element_type=F32)
                    out_ref[:, at : at + 256] = part.astype(out_ref.dtype)
                first_col += out_ref.shape[1]


def chosen_and_project(first_chunk, widths, rows, meta, slots, dead, queries, gates, near, pools, out_weight):
    tokens, width = queries.shape
    heads = width // QK
    at_once = next(n for n in (16, 8, 4, 2) if heads % n == 0)
    steps = heads // at_once
    whole = lambda x: pl.BlockSpec(x.shape, lambda i, p, *_: (0,) * x.ndim)
    outs = [jax.ShapeDtypeStruct((rows, width), BF16) for chunk in widths for width in chunk]
    return pl.pallas_call(
        functools.partial(chosen_kernel, heads, (first_chunk, widths)),
        grid_spec=pltpu.PrefetchScalarGridSpec(
            num_scalar_prefetch=3,
            grid=(len(widths), steps),
            in_specs=[
                pl.BlockSpec((rows, at_once * QK), lambda i, p, m, *_: (m[2 + first_chunk + i], p)),
                pl.BlockSpec((rows, 128), lambda i, p, m, *_: (m[2 + first_chunk + i], 0)),
                pl.BlockSpec((rows, at_once * DV), lambda i, p, m, *_: (m[2 + first_chunk + i], p)),
            ]
            + [VMEM_SPEC] * len(pools)
            + [pl.BlockSpec(memory_space=pl.ANY)],
            out_specs=[VMEM_SPEC] * len(outs),
            scratch_shapes=[
                pltpu.VMEM((PICKS * KBLK, 256), BF16),
                pltpu.VMEM((256, PICKS * KBLK), BF16),
                pltpu.VMEM((256, PICKS * KBLK), BF16),
                pltpu.VMEM((PICKS * KBLK, 256), BF16),
                pltpu.VMEM((steps, rows, at_once * DV), BF16),
                pltpu.VMEM(out_weight.shape, BF16),
                pltpu.SemaphoreType.DMA,
            ],
        ),
        out_shape=outs,
        compiler_params=pltpu.CompilerParams(vmem_limit_bytes=CHOSEN_LIMIT),
        cost_estimate=pl.CostEstimate(
            flops=rows * heads * PICKS * KBLK * 64,
            bytes_accessed=out_weight.size,
            transcendentals=0,
        ),
        name="chosen_and_project",
    )(meta, slots, dead, queries, gates, near, *pools, out_weight)


VMEM_SPEC = pl.BlockSpec(memory_space=pltpu.VMEM)


def single_step(kernel, name, scalars, arrays, outs, scratch=(), in_spec=None, out_spec=None):
    whole = lambda x: pl.BlockSpec(x.shape, lambda i, *_: (0,) * len(x.shape))
    return pl.pallas_call(
        kernel,
        grid_spec=pltpu.PrefetchScalarGridSpec(
            num_scalar_prefetch=len(scalars),
            grid=(1,),
            in_specs=[in_spec or whole(x) for x in arrays],
            out_specs=[out_spec or whole(x) for x in outs],
            scratch_shapes=list(scratch),
        ),
        out_shape=outs,
        compiler_params=pltpu.CompilerParams(vmem_limit_bytes=VMEM_LIMIT),
        name=name,
    )(*scalars, *arrays)


def last_sum(halves, rows, kept_ref, *refs):
    halves, others, out_ref = refs[:halves], refs[halves:-1], refs[-1]
    at = pl.ds(pl.multiple_of(pl.program_id(0) * rows, rows), rows)
    first = 0
    for half in halves:
        cols = slice(first, first + half.shape[1])
        total = kept_ref[at, cols].astype(F32) + half[at].astype(F32)
        for other in others:
            total = total + other[at, cols].astype(F32)
        out_ref[:, cols] = total.astype(BF16)
        first += half.shape[1]


def local(
    queries,
    key_rows,
    value_rows,
    comp_key_weight,
    comp_value_weight,
    block_picks,
    gate_logits,
    out_weight,
):
    tokens = queries.shape[0]
    heads = queries.shape[1] // QK
    n_ctx, n_head = lax.axis_size("ctx"), lax.axis_size("head")
    shard, head_at = lax.axis_index("ctx"), lax.axis_index("head")
    group = head_at * heads // (HEADS // GROUPS)
    per_owner = tokens // KBLK
    lists = tokens // QBLK
    folds = tokens // CBLK
    groups = n_ctx // 2
    rim_blocks = WINDOW // KBLK
    packed_rows = per_owner * BROWS
    bf16 = lambda *shape: jax.ShapeDtypeStruct(shape, BF16)

    chips = n_head // 2
    chip, core = head_at // 2, lax.rem(head_at, 2)
    order = []
    for step in list(range(1, chips)) + [0]:
        target = lax.rem(chip + step, chips) * 2
        order += [target + 1 - core, target + core]
    where = jnp.stack([group, shard, shard * tokens] + order).astype(jnp.int32)
    rim_rows = rim_blocks * BROWS
    fold_weights = jnp.concatenate([comp_key_weight, comp_value_weight], axis=1)
    int32 = lambda *shape: jax.ShapeDtypeStruct(shape, jnp.int32)
    prep_out = [bf16(packed_rows + 3 * folds, 128), bf16(rim_rows, 128)]
    prep_out += [int32(1, n_ctx * lists), int32(lists, 2 * PICKS), int32(lists, 2 * PICKS)]
    prep_out += [bf16(256, tokens)] * 2 + [bf16(tokens, 256)]
    packed, rim, named, slots, dead, even, odd, val = pl.pallas_call(
        prep_kernel,
        grid_spec=pltpu.PrefetchScalarGridSpec(
            num_scalar_prefetch=1,
            grid=(1,),
            in_specs=[pl.BlockSpec(memory_space=pl.ANY)] * 4,
            out_specs=[VMEM_SPEC] * 2
            + [pl.BlockSpec(x.shape, lambda i, g: (0, 0)) for x in prep_out[2:5]]
            + [VMEM_SPEC] * 3,
            scratch_shapes=[
                pltpu.VMEM(block_picks.shape, jnp.int32),
                pltpu.VMEM((tokens, PAIR), BF16),
                pltpu.VMEM((tokens, DV), BF16),
                pltpu.VMEM((CBLK, PAIR), F32),
                pltpu.VMEM((CBLK, DV), F32),
                pltpu.SemaphoreType.DMA((5,)),
            ],
        ),
        out_shape=prep_out,
        compiler_params=pltpu.CompilerParams(vmem_limit_bytes=51 * 1024 * 1024),
        name="prep",
    )(where, block_picks, key_rows, value_rows, fold_weights)
    other = lax.ppermute(packed, "ctx", [(i, i ^ 1) for i in range(n_ctx)])
    named = [named] + [
        lax.ppermute(named, "ctx", [(i, i - 2 * d) for i in range(2 * d, n_ctx)])
        for d in range(1, groups)
    ]
    far_rim = lax.ppermute(rim, "ctx", [(i, i + 1) for i in range(1, n_ctx - 1, 2)])

    gates = jax.nn.sigmoid(gate_logits).reshape(tokens, 3 * heads)
    gates = jnp.pad(gates, ((0, 0), (0, 128 - 3 * heads)))
    sent = bf16(lists * BROWS + 3 * folds, 128)

    def pack(beside, lists_in, rows):
        return single_step(
            functools.partial(pack_kernel, lists, beside),
            "pack",
            [where, *lists_in],
            [rows],
            [sent] * len(lists_in),
            in_spec=VMEM_SPEC,
            out_spec=VMEM_SPEC,
        )

    def ahead(send, distance):
        return lax.ppermute(send, "ctx", [(i, i + 2 * distance) for i in range(n_ctx - 2 * distance)])

    named, gates = lax.optimization_barrier((named, gates))
    own_sends = pack(False, named[1:], packed)
    own_sends, even = lax.optimization_barrier((own_sends, even))
    from_same = [ahead(send, d) for d, send in enumerate(own_sends, 1)]

    reach = WINDOW // QBLK
    near = functools.partial(near_branch, where=where, queries=queries, gates=gates)
    near = functools.partial(near, keys=(even, odd, val))
    mixed = near(reach, lists - reach, rims=None, prior=None)

    other, mixed = lax.optimization_barrier((other, mixed))
    beside, *other_sends = pack(True, named, other)
    from_other = [ahead(send, d) for d, send in enumerate(other_sends, 1)]
    mixed = near(0, reach, rims=(other, far_rim), prior=mixed)

    received = [beside] + [x for both in zip(from_same, from_other) for x in both]
    pools = single_step(
        functools.partial(pool_kernel, groups, lists),
        "pool",
        [where],
        [packed] + received,
        [bf16(n_ctx * lists * KBLK, 256), bf16(n_ctx * lists * KBLK, DV)]
        + [bf16(256, n_ctx * folds)] * 2
        + [bf16(n_ctx * folds, 256)],
        [pltpu.VMEM((n_ctx * folds, 256), BF16)],
        in_spec=VMEM_SPEC,
        out_spec=VMEM_SPEC,
    )
    rows = tokens // n_head
    across = [(i, i ^ 1) for i in range(n_head)]

    model = out_weight.shape[1]

    def project(first_chunk, widths):
        return chosen_and_project(
            first_chunk, widths, rows, where, slots, dead, queries, gates, mixed, pools, out_weight
        )

    sums = []
    for step in range(chips - 1):
        other = lax.ppermute(project(1 + 2 * step, [[model]])[0], "head", across)
        mine = project(2 + 2 * step, [[model]])[0]
        summed = (mine.astype(F32) + other.astype(F32)).astype(BF16)
        summed, where = lax.optimization_barrier((summed, where))
        sums.append(summed)
    *passed, kept = project(n_head - 1, [[model // 2] * 2, [model]])
    near_parts = [lax.ppermute(x, "head", across) for x in passed]
    arrived = []
    for step, summed in enumerate(sums, 1):
        route = [(i, (i + 2 * step) % n_head) for i in range(n_head)]
        arrived.append(lax.ppermute(summed, "head", route))
    steps = 4 if rows % 64 == 0 else 1
    row_block = pl.BlockSpec((rows // steps, model), lambda i: (i, 0))
    return pl.pallas_call(
        functools.partial(last_sum, len(near_parts), rows // steps),
        grid=(steps,),
        in_specs=[VMEM_SPEC] * (1 + len(near_parts) + len(arrived)),
        out_specs=row_block,
        out_shape=bf16(rows, model),
        compiler_params=pltpu.CompilerParams(vmem_limit_bytes=VMEM_LIMIT),
        name="last_sum",
    )(kept, *near_parts, *arrived)


def solution(mesh):
    placed = (
        P("ctx", "head"),
        P("ctx", None),
        P("ctx", None),
        P(),
        P(),
        P("ctx", None, None),
        P("ctx", None, "head"),
        P("head", None),
    )
    return jax.shard_map(
        local, mesh=mesh, in_specs=placed, out_specs=P(("ctx", "head"), None), check_vma=False
    )
```

```python
import functools

import jax
import jax.numpy as jnp
from jax import lax
from jax.experimental import pallas as pl
from jax.experimental.pallas import tpu as pltpu
from jax.sharding import PartitionSpec as P

HEADS = 64
GROUPS = 4
QK = 192
DV = 128
CBLK = 32
KBLK = 64
PICKS = 16
WINDOW = 512
QBLK = 256
PAIR = 2 * QK
BROWS = KBLK + KBLK // 2 + KBLK
VMEM_LIMIT = 50 * 1024 * 1024
CHOSEN_LIMIT = 48 * 1024 * 1024
NEG = -1e30
SCALE = QK ** (-0.5) * 1.4426950408889634
LOW_TOTAL, HIGH_TOTAL = 2.0**-60, 2.0**100
TILE = 256
NT = (((1,), (1,)), ((), ()))
F32 = jnp.float32
BF16 = jnp.bfloat16


def half_lanes(rows):
    return lax.broadcasted_iota(jnp.int32, (rows, 128), 1) < 64


def swap_halves(x):
    return pltpu.roll(x, 64, 1)


def turned(keys):
    row, col = iota(256, 256, 0), iota(256, 256, 1)
    unit = (row == col).astype(BF16)
    even = lax.dot_general(unit, keys, NT, preferred_element_type=F32).astype(BF16)
    return even, lower(even)


def lower(even):
    return jnp.concatenate([jnp.zeros((64, even.shape[1]), BF16), even[:QK]], axis=0)


def with_ones(values):
    return jnp.concatenate([values, jnp.ones_like(values)], axis=1)


def plan(group, shard, per_owner, picks_ref, lists_ref, slots_ref, dead_ref):
    lists = picks_ref.shape[0]
    total = lists_ref.shape[1] // lists * per_owner
    width = slots_ref.shape[1]
    picks = jnp.zeros((lists, PICKS), jnp.int32)
    for each in range(picks_ref.shape[1]):
        picks = jnp.where(group == each, picks_ref[:, each, :], picks)
    block = iota(lists, total, 1)
    hits = [block == picks[:, entry : entry + 1] for entry in range(PICKS)]
    named = functools.reduce(jnp.logical_or, hits).astype(F32)
    named = jnp.broadcast_to(jnp.max(named, axis=0, keepdims=True), (8, total))
    row, col = iota(total, total, 0), iota(total, total, 1)
    before = (lax.div(row, per_owner) == lax.div(col, per_owner)) & (row < col)
    rank = jnp.dot(named, before.astype(F32), preferred_element_type=F32)
    rank = jnp.minimum(rank, float(lists - 1))
    inside = lax.rem(iota(8, total, 1), per_owner).astype(F32)
    found = jnp.zeros((8, lists_ref.shape[1]), F32)
    row, col = iota(total, lists_ref.shape[1], 0), iota(total, lists_ref.shape[1], 1)
    for place in range(lists):
        to = (col == lax.div(row, per_owner) * lists + place).astype(F32)
        value = jnp.where(rank == float(place), named * inside, 0.0)
        found = found + jnp.dot(value, to, preferred_element_type=F32)
    lists_ref[...] = found[:1].astype(jnp.int32)

    owner = lax.div(block, per_owner)
    turn = (lax.div(shard, 2) - lax.div(owner, 2)) * 2 + ((owner ^ shard) & 1)
    slot = jnp.clip(turn * lists + rank[:lists].astype(jnp.int32), 0, lists_ref.shape[1] - 1)
    slot = slot.astype(F32)
    first = shard * per_owner + iota(lists, 1, 0) * (QBLK // KBLK)
    own = block == first

    def pick_out(hit, values):
        return jnp.sum(jnp.where(hit, values, 0.0), axis=1, keepdims=True)

    lane = iota(lists, width, 1)
    slots = jnp.where(lane == 0, pick_out(own, slot), 0.0)
    dead = jnp.zeros((lists, width), F32)
    seen = own.astype(F32)
    at = jnp.ones((lists, 1), jnp.int32)
    met = jnp.zeros((lists, 1), jnp.int32)
    for entry, hit in enumerate(hits):
        pick = picks[:, entry : entry + 1]
        is_own = (pick == first).astype(jnp.int32)
        gone = jnp.maximum(pick_out(hit, seen), (pick > first).astype(F32))
        slots = jnp.where(lane == at, pick_out(hit, slot), slots)
        dead = jnp.where(lane == at, gone, dead)
        seen = jnp.maximum(seen, hit.astype(F32))
        at = at + 1 - is_own * (1 - met)
        met = jnp.maximum(met, is_own)
    slots_ref[...] = slots.astype(jnp.int32)
    dead_ref[...] = dead.astype(jnp.int32)


def prep_kernel(
    where_ref,
    picks_in,
    keys_in,
    values_in,
    fold_in,
    packed_ref,
    rim_ref,
    lists_ref,
    slots_ref,
    dead_ref,
    even_ref,
    odd_ref,
    val_ref,
    picks_ref,
    keys_ref,
    values_ref,
    kw_ref,
    vw_ref,
    sems,
):
    group, shard = where_ref[0], where_ref[1]
    pair = pl.ds(pl.multiple_of(lax.div(group, 2) * PAIR, 128), PAIR)
    single = pl.ds(pl.multiple_of(group * DV, 128), DV)
    folded_value = pl.ds(pl.multiple_of(GROUPS * QK + group * DV, 128), DV)
    copies = [
        pltpu.make_async_copy(source, target, sems.at[i])
        for i, (source, target) in enumerate(
            [
                (picks_in, picks_ref),
                (keys_in.at[:, pair], keys_ref),
                (values_in.at[:, single], values_ref),
                (fold_in.at[:, pair], kw_ref),
                (fold_in.at[:, folded_value], vw_ref),
            ]
        )
    ]
    for copy in copies:
        copy.start()
    copies[0].wait()
    plan(group, shard, keys_ref.shape[0] // KBLK, picks_ref, lists_ref, slots_ref, dead_ref)
    for copy in copies[1:]:
        copy.wait()
    odd = lax.rem(group, 2) == 1

    def own_columns(ref):
        t0 = ref[:, :128].astype(F32)
        t1 = ref[:, 128:256].astype(F32)
        t2 = ref[:, 256:].astype(F32)
        r1, r2 = swap_halves(t1), swap_halves(t2)
        left = half_lanes(t0.shape[0])
        low = jnp.where(odd, jnp.where(left, r1, r2), t0)
        high = jnp.where(left, jnp.where(odd, r2, t1), 0.0)
        return low, high

    low, high = own_columns(keys_ref)
    values = values_ref[...]
    rows = low.shape[0]
    count = rows // KBLK
    high3 = high.reshape(count, KBLK, 128)
    packed_high = high3[:, : KBLK // 2] + swap_halves(
        high3[:, KBLK // 2 :].reshape(count * KBLK // 2, 128)
    ).reshape(count, KBLK // 2, 128)
    even = jnp.concatenate([low.astype(BF16), high.astype(BF16)], axis=1)
    even_ref[...], odd_ref[...] = turned(even)
    val_ref[...] = with_ones(values)
    for block in range(count):
        at = block * BROWS
        token = slice(block * KBLK, block * KBLK + KBLK)
        packed_ref[at : at + KBLK] = low[token].astype(BF16)
        packed_ref[at + KBLK : at + KBLK + KBLK // 2] = packed_high[block].astype(BF16)
        packed_ref[at + KBLK + KBLK // 2 : at + BROWS] = values[token]
    rim_rows = rim_ref.shape[0]
    rim_ref[...] = packed_ref[count * BROWS - rim_rows : count * BROWS]

    wlow, whigh = own_columns(kw_ref)
    folds = rows // CBLK

    def fold(x, w):
        return jnp.sum(x.reshape(folds, CBLK, 128) * w[None], axis=1).astype(BF16)

    at = count * BROWS
    packed_ref[at : at + folds] = fold(low, wlow)
    packed_ref[at + folds : at + 2 * folds] = fold(high, whigh)
    packed_ref[at + 2 * folds :] = fold(values.astype(F32), vw_ref[...])


def pack_kernel(lists, beside, where_ref, *refs):
    count = len(refs) // 2
    named, ref, outs = refs[:count], refs[count], refs[count + 1 :]
    shard = where_ref[1]
    owner = shard + 1 - 2 * lax.rem(shard, 2) if beside else shard
    data = ref.shape[0] - (outs[0].shape[0] - lists * BROWS)
    for blocks, out in zip(named, outs):
        for place in range(lists):
            at = pl.multiple_of(blocks[0, owner * lists + place] * BROWS, 16)
            out[place * BROWS : (place + 1) * BROWS] = ref[pl.ds(at, BROWS)]
        out[lists * BROWS :] = ref[data:]


def unpack(ref, at, count, step=1):
    lows, packed, values = [], [], []
    for block in range(count):
        first = at + block * step * BROWS
        lows.append(ref[first : first + KBLK])
        packed.append(ref[first + KBLK : first + KBLK + KBLK // 2])
        values.append(ref[first + KBLK + KBLK // 2 : first + BROWS])
    packed = jnp.concatenate(packed, axis=0)
    row, col = iota(128, 256, 0), iota(128, 256, 1)
    take = (row == jnp.where(col < 128, col, col - 64)) & (lax.rem(col, 128) < 64)
    both = jnp.dot(packed, take.astype(BF16), preferred_element_type=F32).astype(BF16)
    half = KBLK // 2
    highs = []
    for block in range(count):
        rows = slice(block * half, block * half + half)
        highs += [both[rows, :128], both[rows, 128:]]
    even = jnp.concatenate(
        [jnp.concatenate(lows, axis=0), jnp.concatenate(highs, axis=0)], axis=1
    )
    return even, jnp.concatenate(values, axis=0)


def fill_rim(shard, near_ref, far_ref, own, ext):
    rim_blocks = WINDOW // KBLK
    even_in, odd_in, val_in = own
    even_ref, odd_ref, val_ref = ext
    even_ref[:, WINDOW:] = even_in[:, :WINDOW]
    odd_ref[:, WINDOW:] = odd_in[:, :WINDOW]
    val_ref[WINDOW:] = val_in[:WINDOW]
    use_near = lax.rem(shard, 2) == 1
    rim_end = near_ref.shape[0] // BROWS * BROWS
    near_rim = near_ref[rim_end - far_ref.shape[0] : rim_end]

    @pl.when(shard > 0)
    def _():
        keys, values = unpack(jnp.where(use_near, near_rim, far_ref[...]), 0, rim_blocks)
        even_ref[:, :WINDOW], odd_ref[:, :WINDOW] = turned(keys)
        val_ref[:WINDOW] = with_ones(values)

    @pl.when(shard == 0)
    def _():
        even = jnp.broadcast_to(even_in[:, :1].astype(F32), (256, WINDOW)).astype(BF16)
        even_ref[:, :WINDOW], odd_ref[:, :WINDOW] = even, lower(even)
        val_ref[:WINDOW] = jnp.zeros((WINDOW, 256), BF16)


def pool_kernel(groups, lists, where_ref, own_ref, *refs):
    sent = 2 * groups - 1
    ins, (key_ref, val_ref, ceven_ref, codd_ref, cval_ref, folded) = refs[:sent], refs[sent:]
    shard = where_ref[1]
    parity = lax.rem(shard, 2)
    base = shard - parity
    rows = lists * KBLK
    folds = (ins[0].shape[0] - lists * BROWS) // 3
    folded[...] = jnp.zeros_like(folded)
    cval_ref[...] = jnp.zeros_like(cval_ref)

    def fill(place, owner, ref, step, fold_at):
        keys, values = unpack(ref, 0, lists, step)
        at = slice(place * rows, place * rows + rows)
        key_ref[at] = keys
        val_ref[at] = values
        low = ref[fold_at : fold_at + folds]
        high = ref[fold_at + folds : fold_at + 2 * folds]
        owned = pl.ds(pl.multiple_of(owner * folds, 32), folds)
        folded[owned] = jnp.concatenate([low, high], axis=1)
        cval_ref[owned] = with_ones(ref[fold_at + 2 * folds : fold_at + 3 * folds])

    fill(0, shard, own_ref, QBLK // KBLK, own_ref.shape[0] - 3 * folds)
    fill(1, base + 1 - parity, ins[0], 1, lists * BROWS)
    for distance in range(1, groups):

        @pl.when(base >= 2 * distance)
        def _():
            for side in range(2):
                owner = base - 2 * distance + (parity if side == 0 else 1 - parity)
                fill(2 * distance + side, owner, ins[2 * (groups - distance) - 1 + side], 1, lists * BROWS)

    ceven_ref[...], codd_ref[...] = turned(folded[...])


def iota(rows, cols, axis):
    return lax.broadcasted_iota(jnp.int32, (rows, cols), axis)


def scores_of(q, keys, mask):
    scores = jnp.dot(q, keys, preferred_element_type=F32)
    return scores if mask is None else mask(scores)


def in_range(total):
    good = jnp.where((total >= LOW_TOTAL) & (total <= HIGH_TOTAL), 1.0, 0.0)
    return jnp.min(good.reshape(-1, 8, DV), axis=0)


def over_heads(pairs, load, branches, finish):
    def sums(weights, values):
        out = jnp.dot(weights, values(), preferred_element_type=F32)
        return out[:, :DV], out[:, DV:]

    at_once = 2 if pairs % 2 == 0 else 1
    units = [(pair, side) for pair in range(0, pairs, at_once) for side in range(2)]
    worst, held = [], None
    for now, unit in zip([None] + units, units + [None]):
        q = None if unit is None else load(*unit, at_once)
        fresh, parts = [], []
        for at, (tiles, values) in enumerate(branches):
            weights, ahead = [], []
            for place, (keys, mask) in enumerate(tiles):
                if q is not None:
                    ahead.append(scores_of(q, keys(unit[1]), mask))
                if held is not None:
                    weights.append(jnp.exp2(held[at][place] * SCALE).astype(BF16))
            fresh.append(ahead)
            parts.append((weights, values))
        if held is not None:
            parts = [sums(jnp.concatenate(w, axis=1), values) for w, values in parts]
            worst += [in_range(x) for x in finish(*now, at_once, parts)]
        held = fresh

    @pl.when(jnp.min(functools.reduce(jnp.minimum, worst)) < 0.5)
    def _():
        def exact(pair, _):
            for side in range(2):
                q = load(pair, side, 1)
                parts = []
                for tiles, values in branches:
                    scores = [scores_of(q, keys(side), mask) for keys, mask in tiles]
                    scores = jnp.concatenate(scores, axis=1)
                    top = jnp.max(scores, axis=1, keepdims=True)
                    shifted = (scores - jnp.maximum(top, -1e28)) * SCALE
                    parts.append(sums(jnp.exp2(shifted).astype(BF16), values))
                finish(pair, side, 1, parts)
            return 0

        lax.fori_loop(0, pairs, exact, 0)


def aligned(at):
    return at if isinstance(at, int) else pl.multiple_of(at, 128)


def query_loader(q_ref):
    def load(pair, side, n):
        at = [aligned((pair + p) * PAIR + side * 128) for p in range(n)]
        return jnp.concatenate([q_ref[:, pl.ds(x, 256)] for x in at], axis=0)

    return load


def head_columns(pair, side):
    return pl.ds(aligned(pair * 2 * DV + side * DV), DV)


def gate_loader(gate_ref, first, heads):
    turned = pltpu.roll(gate_ref[...], lax.rem(128 - first, 128), 1)

    def load(pair, side, n, branch):
        if isinstance(pair, int):
            local, at = turned, branch * heads + side + 2 * pair
        else:
            local, at = pltpu.roll(turned, lax.rem(128 - 2 * pair, 128), 1), branch * heads + side
        columns = [local[:, at + 2 * p : at + 2 * p + 1] for p in range(n)]
        shape = (turned.shape[0], DV)
        return jnp.concatenate([jnp.broadcast_to(x, shape) for x in columns], axis=0)

    return load


def stacked(x, times):
    return jnp.concatenate([x] * times, axis=0) if times > 1 else x


def repeated(keep, rows):
    return stacked(keep, rows // keep.shape[0])


def near_kernel(heads, first_block, rim, where_ref, q_ref, gate_ref, *refs):
    keys = refs[:3]
    if rim:
        out_ref, ext = refs[-4], refs[-3:]

        @pl.when((pl.program_id(0) == 0) & (pl.program_id(1) == 0))
        def _():
            fill_rim(where_ref[1], refs[3], refs[4], keys, ext)

        keys, reach = ext, 0
    else:
        out_ref, reach = refs[-1], WINDOW
    count = q_ref.shape[1] // QK
    gate = gate_loader(gate_ref, pl.program_id(1) * count, heads)
    base = pl.multiple_of((first_block + pl.program_id(0)) * QBLK - reach, QBLK)
    row, col = iota(QBLK, QBLK, 0), iota(QBLK, QBLK, 1)

    def tile(place, mask):
        return (lambda side: keys[side][:, pl.ds(base + place * QBLK, QBLK)]), mask

    def finish(pair, side, n, parts):
        ((num, den),) = parts
        total = gate(pair, side, n, 2) * (num / den)
        for p in range(n):
            part = total[p * QBLK : (p + 1) * QBLK]
            out_ref[:, head_columns(pair + p, side)] = part.astype(BF16)
        return [den]

    tiles = [
        tile(0, lambda x: jnp.where(repeated(col >= row, x.shape[0]), x, NEG)),
        tile(1, None),
        tile(2, lambda x: jnp.where(repeated(col <= row, x.shape[0]), x, NEG)),
    ]
    values = lambda: keys[2][pl.ds(base, WINDOW + QBLK)]
    over_heads(count // 2, query_loader(q_ref), [(tiles, values)], finish)


def near_branch(first_block, block_count, where, queries, gates, keys, rims, prior):
    tokens, width = queries.shape
    heads = width // QK
    at_once = next(n for n in (8, 4, 2) if heads % n == 0)
    row_block = lambda i, p, *_: (i + first_block, p)
    operands = [queries, gates, *keys]
    specs = [
        pl.BlockSpec((QBLK, at_once * QK), row_block),
        pl.BlockSpec((QBLK, 128), lambda i, p, *_: (i + first_block, 0)),
    ]
    specs += [VMEM_SPEC] * len(keys)
    alias, scratch = {}, []
    if rims is not None:
        other, far = rims
        operands += [other, far]
        specs += [VMEM_SPEC, VMEM_SPEC]
        scratch = [pltpu.VMEM((256, 2 * WINDOW), BF16)] * 2 + [pltpu.VMEM((2 * WINDOW, 256), BF16)]
    if prior is not None:
        operands.append(prior)
        specs.append(pl.BlockSpec(memory_space=pl.ANY))
        alias = {len(operands): 0}
    rows = block_count * QBLK * heads
    return pl.pallas_call(
        functools.partial(near_kernel, heads, first_block, rims is not None),
        grid_spec=pltpu.PrefetchScalarGridSpec(
            num_scalar_prefetch=1,
            grid=(block_count, heads // at_once),
            in_specs=specs,
            out_specs=pl.BlockSpec((QBLK, at_once * DV), row_block),
            scratch_shapes=scratch,
        ),
        out_shape=jax.ShapeDtypeStruct((tokens, heads * DV), BF16),
        input_output_aliases=alias,
        compiler_params=pltpu.CompilerParams(vmem_limit_bytes=VMEM_LIMIT),
        cost_estimate=pl.CostEstimate(
            flops=rows * (WINDOW + QBLK) * 64,
            bytes_accessed=rows * (2 * QK + 4 * DV),
            transcendentals=0,
        ),
        name="near_branch",
    )(where, *operands)


def chosen_kernel(heads, span, *refs):
    first_chunk, widths = span
    out_count = sum(len(w) for w in widths)
    meta_ref, slots_ref, dead_ref, q_ref, gate_ref, near_ref = refs[:6]
    (key_pool, val_pool), cfold, weight_ref = refs[6:8], refs[8:11], refs[11]
    outs = list(refs[12 : 12 + out_count])
    gathered, even, odd, val, attended, weight, weight_sem = refs[12 + out_count :]
    keys = (even, odd)
    turn, step = pl.program_id(0), pl.program_id(1)
    last = pl.num_programs(1) - 1
    rows = q_ref.shape[0]
    count = q_ref.shape[1] // QK
    chunk_start = meta_ref[2 + first_chunk + turn] * rows
    list_at = lax.div(chunk_start, QBLK)
    first_row = lax.rem(chunk_start, QBLK)
    position = meta_ref[2] + chunk_start
    copy = pltpu.make_async_copy(weight_ref, weight, weight_sem)

    @pl.when(step == 0)
    def _():
        for slot in range(PICKS):
            source = pl.multiple_of(slots_ref[list_at, slot] * KBLK, KBLK)
            gathered[slot * KBLK : (slot + 1) * KBLK] = key_pool[pl.ds(source, KBLK)]
            val[slot * KBLK : (slot + 1) * KBLK] = with_ones(val_pool[pl.ds(source, KBLK)])
        for slot in range(1, PICKS):

            @pl.when(dead_ref[list_at, slot] == 1)
            def _():
                at = slice(slot * KBLK, (slot + 1) * KBLK)
                gathered[at] = jnp.broadcast_to(gathered[:1], (KBLK, 256))
                val[at] = jnp.zeros((KBLK, 256), BF16)

        even[...], odd[...] = turned(gathered[...])

    @pl.when((turn == 0) & (step == 0))
    def _():
        copy.start()

    gate = gate_loader(gate_ref, step * count, heads)
    row = iota(rows, TILE, 0)
    col = iota(rows, TILE, 1)
    own_keep = (col >= KBLK) | (col <= row + first_row)

    def own_mask(scores):
        own = jnp.where(repeated(own_keep[:, :128], scores.shape[0]), scores[:, :128], NEG)
        return jnp.concatenate([own, scores[:, 128:]], axis=1)

    def comp_mask(place):
        ends = (col + place * TILE + 1) * CBLK - 1
        return lambda x: jnp.where(repeated(ends <= row + position, x.shape[0]), x, NEG)

    def tile(refs, place, mask):
        return (lambda side: refs[side][:, place * TILE : (place + 1) * TILE]), mask

    chosen = [tile(keys, p, own_mask if p == 0 else None) for p in range(PICKS * KBLK // TILE)]
    folded = [tile(cfold, p, comp_mask(p)) for p in range(cfold[2].shape[0] // TILE)]
    empty = row[:, :DV] + position < CBLK - 1

    def finish(pair, side, n, parts):
        (num, den), (folded_num, folded_den) = parts
        folded_den = jnp.where(stacked(empty, n), 1.0, folded_den)
        total = gate(pair, side, n, 1) * (num / den)
        total = total + gate(pair, side, n, 0) * (folded_num / folded_den)
        for p in range(n):
            cols = head_columns(pair + p, side)
            mixed = near_ref[:, cols].astype(F32) + total[p * rows : (p + 1) * rows]
            attended[step, :, cols] = mixed.astype(BF16)
        return [den, folded_den]

    branches = [(chosen, lambda: val[...]), (folded, lambda: cfold[2][...])]
    over_heads(count // 2, query_loader(q_ref), branches, finish)

    @pl.when((turn == 0) & (step == last))
    def _():
        copy.wait()

    for place, parts in enumerate(widths):
        chunk_outs = [outs.pop(0) for _ in parts]

        @pl.when((turn == place) & (step == last))
        def _():
            rows_in = jnp.concatenate([attended[s] for s in range(attended.shape[0])], axis=1)
            first_col = 0
            for out_ref in chunk_outs:
                for at in range(0, out_ref.shape[1], 256):
                    cols = weight[:, first_col + at : first_col + at + 256]
                    part = jnp.dot(rows_in, cols, preferred_element_type=F32)
                    out_ref[:, at : at + 256] = part.astype(out_ref.dtype)
                first_col += out_ref.shape[1]


def chosen_and_project(first_chunk, widths, rows, meta, slots, dead, queries, gates, near, pools, out_weight):
    tokens, width = queries.shape
    heads = width // QK
    at_once = next(n for n in (8, 4, 2) if heads % n == 0)
    steps = heads // at_once
    whole = lambda x: pl.BlockSpec(x.shape, lambda i, p, *_: (0,) * x.ndim)
    outs = [jax.ShapeDtypeStruct((rows, width), BF16) for chunk in widths for width in chunk]
    return pl.pallas_call(
        functools.partial(chosen_kernel, heads, (first_chunk, widths)),
        grid_spec=pltpu.PrefetchScalarGridSpec(
            num_scalar_prefetch=3,
            grid=(len(widths), steps),
            in_specs=[
                pl.BlockSpec((rows, at_once * QK), lambda i, p, m, *_: (m[2 + first_chunk + i], p)),
                pl.BlockSpec((rows, 128), lambda i, p, m, *_: (m[2 + first_chunk + i], 0)),
                pl.BlockSpec((rows, at_once * DV), lambda i, p, m, *_: (m[2 + first_chunk + i], p)),
            ]
            + [VMEM_SPEC] * len(pools)
            + [pl.BlockSpec(memory_space=pl.ANY)],
            out_specs=[VMEM_SPEC] * len(outs),
            scratch_shapes=[
                pltpu.VMEM((PICKS * KBLK, 256), BF16),
                pltpu.VMEM((256, PICKS * KBLK), BF16),
                pltpu.VMEM((256, PICKS * KBLK), BF16),
                pltpu.VMEM((PICKS * KBLK, 256), BF16),
                pltpu.VMEM((steps, rows, at_once * DV), BF16),
                pltpu.VMEM(out_weight.shape, BF16),
                pltpu.SemaphoreType.DMA,
            ],
        ),
        out_shape=outs,
        compiler_params=pltpu.CompilerParams(vmem_limit_bytes=CHOSEN_LIMIT),
        cost_estimate=pl.CostEstimate(
            flops=rows * heads * PICKS * KBLK * 64,
            bytes_accessed=out_weight.size,
            transcendentals=0,
        ),
        name="chosen_and_project",
    )(meta, slots, dead, queries, gates, near, *pools, out_weight)


VMEM_SPEC = pl.BlockSpec(memory_space=pltpu.VMEM)


def single_step(kernel, name, scalars, arrays, outs, scratch=(), in_spec=None, out_spec=None):
    whole = lambda x: pl.BlockSpec(x.shape, lambda i, *_: (0,) * len(x.shape))
    return pl.pallas_call(
        kernel,
        grid_spec=pltpu.PrefetchScalarGridSpec(
            num_scalar_prefetch=len(scalars),
            grid=(1,),
            in_specs=[in_spec or whole(x) for x in arrays],
            out_specs=[out_spec or whole(x) for x in outs],
            scratch_shapes=list(scratch),
        ),
        out_shape=outs,
        compiler_params=pltpu.CompilerParams(vmem_limit_bytes=VMEM_LIMIT),
        name=name,
    )(*scalars, *arrays)


def last_sum(halves, rows, kept_ref, *refs):
    halves, others, out_ref = refs[:halves], refs[halves:-1], refs[-1]
    at = pl.ds(pl.multiple_of(pl.program_id(0) * rows, rows), rows)
    first = 0
    for half in halves:
        cols = slice(first, first + half.shape[1])
        total = kept_ref[at, cols].astype(F32) + half[at].astype(F32)
        for other in others:
            total = total + other[at, cols].astype(F32)
        out_ref[:, cols] = total.astype(BF16)
        first += half.shape[1]


def local(
    queries,
    key_rows,
    value_rows,
    comp_key_weight,
    comp_value_weight,
    block_picks,
    gate_logits,
    out_weight,
):
    tokens = queries.shape[0]
    heads = queries.shape[1] // QK
    n_ctx, n_head = lax.axis_size("ctx"), lax.axis_size("head")
    shard, head_at = lax.axis_index("ctx"), lax.axis_index("head")
    group = head_at * heads // (HEADS // GROUPS)
    per_owner = tokens // KBLK
    lists = tokens // QBLK
    folds = tokens // CBLK
    groups = n_ctx // 2
    rim_blocks = WINDOW // KBLK
    packed_rows = per_owner * BROWS
    bf16 = lambda *shape: jax.ShapeDtypeStruct(shape, BF16)

    chips = n_head // 2
    chip, core = head_at // 2, lax.rem(head_at, 2)
    order = []
    for step in list(range(1, chips)) + [0]:
        target = lax.rem(chip + step, chips) * 2
        order += [target + 1 - core, target + core]
    where = jnp.stack([group, shard, shard * tokens] + order).astype(jnp.int32)
    rim_rows = rim_blocks * BROWS
    fold_weights = jnp.concatenate([comp_key_weight, comp_value_weight], axis=1)
    int32 = lambda *shape: jax.ShapeDtypeStruct(shape, jnp.int32)
    prep_out = [bf16(packed_rows + 3 * folds, 128), bf16(rim_rows, 128)]
    prep_out += [int32(1, n_ctx * lists), int32(lists, 2 * PICKS), int32(lists, 2 * PICKS)]
    prep_out += [bf16(256, tokens)] * 2 + [bf16(tokens, 256)]
    packed, rim, named, slots, dead, even, odd, val = pl.pallas_call(
        prep_kernel,
        grid_spec=pltpu.PrefetchScalarGridSpec(
            num_scalar_prefetch=1,
            grid=(1,),
            in_specs=[pl.BlockSpec(memory_space=pl.ANY)] * 4,
            out_specs=[VMEM_SPEC] * 2
            + [pl.BlockSpec(x.shape, lambda i, g: (0, 0)) for x in prep_out[2:5]]
            + [VMEM_SPEC] * 3,
            scratch_shapes=[
                pltpu.VMEM(block_picks.shape, jnp.int32),
                pltpu.VMEM((tokens, PAIR), BF16),
                pltpu.VMEM((tokens, DV), BF16),
                pltpu.VMEM((CBLK, PAIR), F32),
                pltpu.VMEM((CBLK, DV), F32),
                pltpu.SemaphoreType.DMA((5,)),
            ],
        ),
        out_shape=prep_out,
        compiler_params=pltpu.CompilerParams(vmem_limit_bytes=51 * 1024 * 1024),
        name="prep",
    )(where, block_picks, key_rows, value_rows, fold_weights)
    other = lax.ppermute(packed, "ctx", [(i, i ^ 1) for i in range(n_ctx)])
    named = [named] + [
        lax.ppermute(named, "ctx", [(i, i - 2 * d) for i in range(2 * d, n_ctx)])
        for d in range(1, groups)
    ]
    far_rim = lax.ppermute(rim, "ctx", [(i, i + 1) for i in range(1, n_ctx - 1, 2)])

    gates = jax.nn.sigmoid(gate_logits).reshape(tokens, 3 * heads)
    gates = jnp.pad(gates, ((0, 0), (0, 128 - 3 * heads)))
    sent = bf16(lists * BROWS + 3 * folds, 128)

    def pack(beside, lists_in, rows):
        return single_step(
            functools.partial(pack_kernel, lists, beside),
            "pack",
            [where, *lists_in],
            [rows],
            [sent] * len(lists_in),
            in_spec=VMEM_SPEC,
            out_spec=VMEM_SPEC,
        )

    def all_ahead(sends):
        moved = []
        for distance, send in reversed(list(enumerate(sends, 1))):
            route = [(i, i + 2 * distance) for i in range(n_ctx - 2 * distance)]
            moved.append(lax.ppermute(send, "ctx", route))
        return moved[::-1]

    named, gates = lax.optimization_barrier((named, gates))
    own_sends = pack(False, named[1:], packed)
    own_sends, even = lax.optimization_barrier((own_sends, even))
    from_same = all_ahead(own_sends)

    reach = WINDOW // QBLK
    near = functools.partial(near_branch, where=where, queries=queries, gates=gates)
    near = functools.partial(near, keys=(even, odd, val))
    mixed = near(reach, lists - reach, rims=None, prior=None)

    other, mixed = lax.optimization_barrier((other, mixed))
    beside, *other_sends = pack(True, named, other)
    from_other = all_ahead(other_sends)
    mixed = near(0, reach, rims=(other, far_rim), prior=mixed)

    farthest_first = reversed(list(zip(from_same, from_other)))
    received = [beside] + [x for both in farthest_first for x in both]
    pools = single_step(
        functools.partial(pool_kernel, groups, lists),
        "pool",
        [where],
        [packed] + received,
        [bf16(n_ctx * lists * KBLK, 256), bf16(n_ctx * lists * KBLK, DV)]
        + [bf16(256, n_ctx * folds)] * 2
        + [bf16(n_ctx * folds, 256)],
        [pltpu.VMEM((n_ctx * folds, 256), BF16)],
        in_spec=VMEM_SPEC,
        out_spec=VMEM_SPEC,
    )
    rows = tokens // n_head
    across = [(i, i ^ 1) for i in range(n_head)]

    model = out_weight.shape[1]

    def project(first_chunk, widths):
        return chosen_and_project(
            first_chunk, widths, rows, where, slots, dead, queries, gates, mixed, pools, out_weight
        )

    sums = []
    for step in range(chips - 1):
        other = lax.ppermute(project(1 + 2 * step, [[model]])[0], "head", across)
        mine = project(2 + 2 * step, [[model]])[0]
        summed = (mine.astype(F32) + other.astype(F32)).astype(BF16)
        summed, where = lax.optimization_barrier((summed, where))
        sums.append(summed)
    *passed, kept = project(n_head - 1, [[model // 2] * 2, [model]])
    near_parts = [lax.ppermute(x, "head", across) for x in passed]
    arrived = []
    for step, summed in enumerate(sums, 1):
        route = [(i, (i + 2 * step) % n_head) for i in range(n_head)]
        arrived.append(lax.ppermute(summed, "head", route))
    steps = 4 if rows % 64 == 0 else 1
    row_block = pl.BlockSpec((rows // steps, model), lambda i: (i, 0))
    return pl.pallas_call(
        functools.partial(last_sum, len(near_parts), rows // steps),
        grid=(steps,),
        in_specs=[VMEM_SPEC] * (1 + len(near_parts) + len(arrived)),
        out_specs=row_block,
        out_shape=bf16(rows, model),
        compiler_params=pltpu.CompilerParams(vmem_limit_bytes=VMEM_LIMIT),
        name="last_sum",
    )(kept, *near_parts, *arrived)


def solution(mesh):
    placed = (
        P("ctx", "head"),
        P("ctx", None),
        P("ctx", None),
        P(),
        P(),
        P("ctx", None, None),
        P("ctx", None, "head"),
        P("head", None),
    )
    return jax.shard_map(
        local, mesh=mesh, in_specs=placed, out_specs=P(("ctx", "head"), None), check_vma=False
    )
```

```python
import functools

import jax
import jax.numpy as jnp
from jax import lax
from jax.experimental import pallas as pl
from jax.experimental.pallas import tpu as pltpu
from jax.sharding import PartitionSpec as P

HEADS = 64
GROUPS = 4
QK = 192
DV = 128
CBLK = 32
KBLK = 64
PICKS = 16
WINDOW = 512
QBLK = 256
PAIR = 2 * QK
BROWS = KBLK + KBLK // 2 + KBLK
VMEM_LIMIT = 50 * 1024 * 1024
CHOSEN_LIMIT = 48 * 1024 * 1024
NEG = -1e30
SCALE = QK ** (-0.5) * 1.4426950408889634
LOW_TOTAL, HIGH_TOTAL = 2.0**-60, 2.0**100
TILE = 256
NT = (((1,), (1,)), ((), ()))
F32 = jnp.float32
BF16 = jnp.bfloat16


def half_lanes(rows):
    return lax.broadcasted_iota(jnp.int32, (rows, 128), 1) < 64


def swap_halves(x):
    return pltpu.roll(x, 64, 1)


def turned(keys):
    row, col = iota(256, 256, 0), iota(256, 256, 1)
    unit = (row == col).astype(BF16)
    even = lax.dot_general(unit, keys, NT, preferred_element_type=F32).astype(BF16)
    return even, lower(even)


def lower(even):
    return jnp.concatenate([jnp.zeros((64, even.shape[1]), BF16), even[:QK]], axis=0)


def with_ones(values):
    return jnp.concatenate([values, jnp.ones_like(values)], axis=1)


def plan(group, shard, per_owner, picks_ref, lists_ref, slots_ref, dead_ref):
    lists = picks_ref.shape[0]
    total = lists_ref.shape[1] // lists * per_owner
    width = slots_ref.shape[1]
    picks = jnp.zeros((lists, PICKS), jnp.int32)
    for each in range(picks_ref.shape[1]):
        picks = jnp.where(group == each, picks_ref[:, each, :], picks)
    block = iota(lists, total, 1)
    hits = [block == picks[:, entry : entry + 1] for entry in range(PICKS)]
    named = functools.reduce(jnp.logical_or, hits).astype(F32)
    named = jnp.broadcast_to(jnp.max(named, axis=0, keepdims=True), (8, total))
    row, col = iota(total, total, 0), iota(total, total, 1)
    before = (lax.div(row, per_owner) == lax.div(col, per_owner)) & (row < col)
    rank = jnp.dot(named, before.astype(F32), preferred_element_type=F32)
    rank = jnp.minimum(rank, float(lists - 1))
    inside = lax.rem(iota(8, total, 1), per_owner).astype(F32)
    found = jnp.zeros((8, lists_ref.shape[1]), F32)
    row, col = iota(total, lists_ref.shape[1], 0), iota(total, lists_ref.shape[1], 1)
    for place in range(lists):
        to = (col == lax.div(row, per_owner) * lists + place).astype(F32)
        value = jnp.where(rank == float(place), named * inside, 0.0)
        found = found + jnp.dot(value, to, preferred_element_type=F32)
    lists_ref[...] = found[:1].astype(jnp.int32)

    owner = lax.div(block, per_owner)
    turn = (lax.div(shard, 2) - lax.div(owner, 2)) * 2 + ((owner ^ shard) & 1)
    slot = jnp.clip(turn * lists + rank[:lists].astype(jnp.int32), 0, lists_ref.shape[1] - 1)
    slot = slot.astype(F32)
    first = shard * per_owner + iota(lists, 1, 0) * (QBLK // KBLK)
    own = block == first

    def pick_out(hit, values):
        return jnp.sum(jnp.where(hit, values, 0.0), axis=1, keepdims=True)

    lane = iota(lists, width, 1)
    slots = jnp.where(lane == 0, pick_out(own, slot), 0.0)
    dead = jnp.zeros((lists, width), F32)
    seen = own.astype(F32)
    at = jnp.ones((lists, 1), jnp.int32)
    met = jnp.zeros((lists, 1), jnp.int32)
    for entry, hit in enumerate(hits):
        pick = picks[:, entry : entry + 1]
        is_own = (pick == first).astype(jnp.int32)
        gone = jnp.maximum(pick_out(hit, seen), (pick > first).astype(F32))
        slots = jnp.where(lane == at, pick_out(hit, slot), slots)
        dead = jnp.where(lane == at, gone, dead)
        seen = jnp.maximum(seen, hit.astype(F32))
        at = at + 1 - is_own * (1 - met)
        met = jnp.maximum(met, is_own)
    slots_ref[...] = slots.astype(jnp.int32)
    dead_ref[...] = dead.astype(jnp.int32)


def prep_kernel(
    where_ref,
    picks_in,
    keys_in,
    values_in,
    fold_in,
    packed_ref,
    rim_ref,
    lists_ref,
    slots_ref,
    dead_ref,
    even_ref,
    odd_ref,
    val_ref,
    picks_ref,
    keys_ref,
    values_ref,
    kw_ref,
    vw_ref,
    sems,
):
    group, shard = where_ref[0], where_ref[1]
    pair = pl.ds(pl.multiple_of(lax.div(group, 2) * PAIR, 128), PAIR)
    single = pl.ds(pl.multiple_of(group * DV, 128), DV)
    folded_value = pl.ds(pl.multiple_of(GROUPS * QK + group * DV, 128), DV)
    copies = [
        pltpu.make_async_copy(source, target, sems.at[i])
        for i, (source, target) in enumerate(
            [
                (picks_in, picks_ref),
                (keys_in.at[:, pair], keys_ref),
                (values_in.at[:, single], values_ref),
                (fold_in.at[:, pair], kw_ref),
                (fold_in.at[:, folded_value], vw_ref),
            ]
        )
    ]
    for copy in copies:
        copy.start()
    copies[0].wait()
    plan(group, shard, keys_ref.shape[0] // KBLK, picks_ref, lists_ref, slots_ref, dead_ref)
    for copy in copies[1:]:
        copy.wait()
    odd = lax.rem(group, 2) == 1

    def own_columns(ref):
        t0 = ref[:, :128].astype(F32)
        t1 = ref[:, 128:256].astype(F32)
        t2 = ref[:, 256:].astype(F32)
        r1, r2 = swap_halves(t1), swap_halves(t2)
        left = half_lanes(t0.shape[0])
        low = jnp.where(odd, jnp.where(left, r1, r2), t0)
        high = jnp.where(left, jnp.where(odd, r2, t1), 0.0)
        return low, high

    low, high = own_columns(keys_ref)
    values = values_ref[...]
    rows = low.shape[0]
    count = rows // KBLK
    high3 = high.reshape(count, KBLK, 128)
    packed_high = high3[:, : KBLK // 2] + swap_halves(
        high3[:, KBLK // 2 :].reshape(count * KBLK // 2, 128)
    ).reshape(count, KBLK // 2, 128)
    even = jnp.concatenate([low.astype(BF16), high.astype(BF16)], axis=1)
    even_ref[...], odd_ref[...] = turned(even)
    val_ref[...] = with_ones(values)
    for block in range(count):
        at = block * BROWS
        token = slice(block * KBLK, block * KBLK + KBLK)
        packed_ref[at : at + KBLK] = low[token].astype(BF16)
        packed_ref[at + KBLK : at + KBLK + KBLK // 2] = packed_high[block].astype(BF16)
        packed_ref[at + KBLK + KBLK // 2 : at + BROWS] = values[token]
    rim_rows = rim_ref.shape[0]
    rim_ref[...] = packed_ref[count * BROWS - rim_rows : count * BROWS]

    wlow, whigh = own_columns(kw_ref)
    folds = rows // CBLK

    def fold(x, w):
        return jnp.sum(x.reshape(folds, CBLK, 128) * w[None], axis=1).astype(BF16)

    at = count * BROWS
    packed_ref[at : at + folds] = fold(low, wlow)
    packed_ref[at + folds : at + 2 * folds] = fold(high, whigh)
    packed_ref[at + 2 * folds :] = fold(values.astype(F32), vw_ref[...])


def pack_kernel(lists, beside, where_ref, *refs):
    count = len(refs) // 2
    named, ref, outs = refs[:count], refs[count], refs[count + 1 :]
    shard = where_ref[1]
    owner = shard + 1 - 2 * lax.rem(shard, 2) if beside else shard
    data = ref.shape[0] - (outs[0].shape[0] - lists * BROWS)
    for blocks, out in zip(named, outs):
        for place in range(lists):
            at = pl.multiple_of(blocks[0, owner * lists + place] * BROWS, 16)
            out[place * BROWS : (place + 1) * BROWS] = ref[pl.ds(at, BROWS)]
        out[lists * BROWS :] = ref[data:]


def unpack(ref, at, count, step=1):
    lows, packed, values = [], [], []
    for block in range(count):
        first = at + block * step * BROWS
        lows.append(ref[first : first + KBLK])
        packed.append(ref[first + KBLK : first + KBLK + KBLK // 2])
        values.append(ref[first + KBLK + KBLK // 2 : first + BROWS])
    packed = jnp.concatenate(packed, axis=0)
    row, col = iota(128, 256, 0), iota(128, 256, 1)
    take = (row == jnp.where(col < 128, col, col - 64)) & (lax.rem(col, 128) < 64)
    both = jnp.dot(packed, take.astype(BF16), preferred_element_type=F32).astype(BF16)
    half = KBLK // 2
    highs = []
    for block in range(count):
        rows = slice(block * half, block * half + half)
        highs += [both[rows, :128], both[rows, 128:]]
    even = jnp.concatenate(
        [jnp.concatenate(lows, axis=0), jnp.concatenate(highs, axis=0)], axis=1
    )
    return even, jnp.concatenate(values, axis=0)


def fill_rim(shard, near_ref, far_ref, own, ext):
    rim_blocks = WINDOW // KBLK
    even_in, odd_in, val_in = own
    even_ref, odd_ref, val_ref = ext
    even_ref[:, WINDOW:] = even_in[:, :WINDOW]
    odd_ref[:, WINDOW:] = odd_in[:, :WINDOW]
    val_ref[WINDOW:] = val_in[:WINDOW]
    use_near = lax.rem(shard, 2) == 1
    rim_end = near_ref.shape[0] // BROWS * BROWS
    near_rim = near_ref[rim_end - far_ref.shape[0] : rim_end]

    @pl.when(shard > 0)
    def _():
        keys, values = unpack(jnp.where(use_near, near_rim, far_ref[...]), 0, rim_blocks)
        even_ref[:, :WINDOW], odd_ref[:, :WINDOW] = turned(keys)
        val_ref[:WINDOW] = with_ones(values)

    @pl.when(shard == 0)
    def _():
        even = jnp.broadcast_to(even_in[:, :1].astype(F32), (256, WINDOW)).astype(BF16)
        even_ref[:, :WINDOW], odd_ref[:, :WINDOW] = even, lower(even)
        val_ref[:WINDOW] = jnp.zeros((WINDOW, 256), BF16)


def pool_kernel(groups, lists, where_ref, own_ref, *refs):
    sent = 2 * groups - 1
    ins, (key_ref, val_ref, ceven_ref, codd_ref, cval_ref, folded) = refs[:sent], refs[sent:]
    shard = where_ref[1]
    parity = lax.rem(shard, 2)
    base = shard - parity
    rows = lists * KBLK
    folds = (ins[0].shape[0] - lists * BROWS) // 3
    folded[...] = jnp.zeros_like(folded)
    cval_ref[...] = jnp.zeros_like(cval_ref)

    def fill(place, owner, ref, step, fold_at):
        keys, values = unpack(ref, 0, lists, step)
        at = slice(place * rows, place * rows + rows)
        key_ref[at] = keys
        val_ref[at] = values
        low = ref[fold_at : fold_at + folds]
        high = ref[fold_at + folds : fold_at + 2 * folds]
        owned = pl.ds(pl.multiple_of(owner * folds, 32), folds)
        folded[owned] = jnp.concatenate([low, high], axis=1)
        cval_ref[owned] = with_ones(ref[fold_at + 2 * folds : fold_at + 3 * folds])

    fill(0, shard, own_ref, QBLK // KBLK, own_ref.shape[0] - 3 * folds)
    fill(1, base + 1 - parity, ins[0], 1, lists * BROWS)
    for distance in range(1, groups):

        @pl.when(base >= 2 * distance)
        def _():
            for side in range(2):
                owner = base - 2 * distance + (parity if side == 0 else 1 - parity)
                fill(2 * distance + side, owner, ins[2 * (groups - distance) - 1 + side], 1, lists * BROWS)

    ceven_ref[...], codd_ref[...] = turned(folded[...])


def iota(rows, cols, axis):
    return lax.broadcasted_iota(jnp.int32, (rows, cols), axis)


def scores_of(q, keys, mask):
    scores = jnp.dot(q, keys, preferred_element_type=F32)
    return scores if mask is None else mask(scores)


def plain_weights(scores):
    return jnp.exp2(scores * SCALE).astype(BF16)


def corner_weights(scores, later):
    half = QBLK // 2
    row, col = iota(half, half, 0), iota(half, half, 1)
    keep = col >= row if later else col <= row
    none = jnp.zeros((half, half), BF16)
    pieces = []
    for first in range(0, scores.shape[0], QBLK):
        for lower_half in range(2):
            rows = scores[first + lower_half * half : first + (lower_half + 1) * half]
            parts = [rows[:, :half], rows[:, half:]]
            parts[lower_half] = plain_weights(jnp.where(keep, parts[lower_half], NEG))
            other = 1 - lower_half
            full = (lower_half == 0) == later
            parts[other] = plain_weights(parts[other]) if full else none
            pieces.append(jnp.concatenate(parts, axis=1))
    return jnp.concatenate(pieces, axis=0)


def in_range(total):
    good = jnp.where((total >= LOW_TOTAL) & (total <= HIGH_TOTAL), 1.0, 0.0)
    return jnp.min(good.reshape(-1, 8, DV), axis=0)


def over_heads(pairs, load, branches, finish):
    def sums(weights, values):
        out = jnp.dot(weights, values(), preferred_element_type=F32)
        return out[:, :DV], out[:, DV:]

    at_once = 2 if pairs % 2 == 0 else 1
    units = [(pair, side) for pair in range(0, pairs, at_once) for side in range(2)]
    worst, held = [], None
    for now, unit in zip([None] + units, units + [None]):
        q = None if unit is None else load(*unit, at_once)
        fresh, parts = [], []
        for at, (tiles, values) in enumerate(branches):
            weights, ahead = [], []
            for place, (keys, mask, weigh) in enumerate(tiles):
                if q is not None:
                    ahead.append(scores_of(q, keys(unit[1]), mask if weigh is None else None))
                if held is not None:
                    weights.append((weigh or plain_weights)(held[at][place]))
            fresh.append(ahead)
            parts.append((weights, values))
        if held is not None:
            parts = [sums(jnp.concatenate(w, axis=1), values) for w, values in parts]
            worst += [in_range(x) for x in finish(*now, at_once, parts)]
        held = fresh

    @pl.when(jnp.min(functools.reduce(jnp.minimum, worst)) < 0.5)
    def _():
        def exact(pair, _):
            for side in range(2):
                q = load(pair, side, 1)
                parts = []
                for tiles, values in branches:
                    scores = [scores_of(q, keys(side), mask) for keys, mask, _ in tiles]
                    scores = jnp.concatenate(scores, axis=1)
                    top = jnp.max(scores, axis=1, keepdims=True)
                    shifted = (scores - jnp.maximum(top, -1e28)) * SCALE
                    parts.append(sums(jnp.exp2(shifted).astype(BF16), values))
                finish(pair, side, 1, parts)
            return 0

        lax.fori_loop(0, pairs, exact, 0)


def aligned(at):
    return at if isinstance(at, int) else pl.multiple_of(at, 128)


def query_loader(q_ref):
    def load(pair, side, n):
        at = [aligned((pair + p) * PAIR + side * 128) for p in range(n)]
        return jnp.concatenate([q_ref[:, pl.ds(x, 256)] for x in at], axis=0)

    return load


def head_columns(pair, side):
    return pl.ds(aligned(pair * 2 * DV + side * DV), DV)


def gate_loader(gate_ref, wide, first, heads):
    wide[:, : gate_ref.shape[1]] = jax.nn.sigmoid(gate_ref[...])
    turned = pltpu.roll(wide[...], lax.rem(128 - first, 128), 1)

    def load(pair, side, n, branch):
        if isinstance(pair, int):
            local, at = turned, branch * heads + side + 2 * pair
        else:
            local, at = pltpu.roll(turned, lax.rem(128 - 2 * pair, 128), 1), branch * heads + side
        columns = [local[:, at + 2 * p : at + 2 * p + 1] for p in range(n)]
        shape = (turned.shape[0], DV)
        return jnp.concatenate([jnp.broadcast_to(x, shape) for x in columns], axis=0)

    return load


def stacked(x, times):
    return jnp.concatenate([x] * times, axis=0) if times > 1 else x


def repeated(keep, rows):
    return stacked(keep, rows // keep.shape[0])


def near_kernel(heads, first_block, rim, where_ref, q_ref, gate_ref, *refs):
    *refs, wide = refs
    keys = refs[:3]
    if rim:
        out_ref, ext = refs[-4], refs[-3:]

        @pl.when((pl.program_id(0) == 0) & (pl.program_id(1) == 0))
        def _():
            fill_rim(where_ref[1], refs[3], refs[4], keys, ext)

        keys, reach = ext, 0
    else:
        out_ref, reach = refs[-1], WINDOW
    count = q_ref.shape[1] // QK
    gate = gate_loader(gate_ref, wide, pl.program_id(1) * count, heads)
    base = pl.multiple_of((first_block + pl.program_id(0)) * QBLK - reach, QBLK)
    row, col = iota(QBLK, QBLK, 0), iota(QBLK, QBLK, 1)

    def tile(place, mask, weigh):
        return (lambda side: keys[side][:, pl.ds(base + place * QBLK, QBLK)]), mask, weigh

    def finish(pair, side, n, parts):
        ((num, den),) = parts
        total = gate(pair, side, n, 2) * (num / den)
        for p in range(n):
            part = total[p * QBLK : (p + 1) * QBLK]
            out_ref[:, head_columns(pair + p, side)] = part.astype(BF16)
        return [den]

    tiles = [
        tile(
            0,
            lambda x: jnp.where(repeated(col >= row, x.shape[0]), x, NEG),
            lambda x: corner_weights(x, True),
        ),
        tile(1, None, None),
        tile(
            2,
            lambda x: jnp.where(repeated(col <= row, x.shape[0]), x, NEG),
            lambda x: corner_weights(x, False),
        ),
    ]
    values = lambda: keys[2][pl.ds(base, WINDOW + QBLK)]
    over_heads(count // 2, query_loader(q_ref), [(tiles, values)], finish)


def near_branch(first_block, block_count, where, queries, gates, keys, rims, prior):
    tokens, width = queries.shape
    heads = width // QK
    at_once = next(n for n in (8, 4, 2) if heads % n == 0)
    row_block = lambda i, p, *_: (i + first_block, p)
    operands = [queries, gates, *keys]
    specs = [
        pl.BlockSpec((QBLK, at_once * QK), row_block),
        pl.BlockSpec((QBLK, 3 * heads), lambda i, p, *_: (i + first_block, 0)),
    ]
    specs += [VMEM_SPEC] * len(keys)
    alias, scratch = {}, []
    if rims is not None:
        other, far = rims
        operands += [other, far]
        specs += [VMEM_SPEC, VMEM_SPEC]
        scratch = [pltpu.VMEM((256, 2 * WINDOW), BF16)] * 2 + [pltpu.VMEM((2 * WINDOW, 256), BF16)]
    if prior is not None:
        operands.append(prior)
        specs.append(pl.BlockSpec(memory_space=pl.ANY))
        alias = {len(operands): 0}
    rows = block_count * QBLK * heads
    return pl.pallas_call(
        functools.partial(near_kernel, heads, first_block, rims is not None),
        grid_spec=pltpu.PrefetchScalarGridSpec(
            num_scalar_prefetch=1,
            grid=(block_count, heads // at_once),
            in_specs=specs,
            out_specs=pl.BlockSpec((QBLK, at_once * DV), row_block),
            scratch_shapes=scratch + [pltpu.VMEM((QBLK, 128), F32)],
        ),
        out_shape=jax.ShapeDtypeStruct((tokens, heads * DV), BF16),
        input_output_aliases=alias,
        compiler_params=pltpu.CompilerParams(vmem_limit_bytes=VMEM_LIMIT),
        cost_estimate=pl.CostEstimate(
            flops=rows * (WINDOW + QBLK) * 64,
            bytes_accessed=rows * (2 * QK + 4 * DV),
            transcendentals=0,
        ),
        name="near_branch",
    )(where, *operands)


def chosen_kernel(heads, span, *refs):
    first_chunk, widths = span
    out_count = sum(len(w) for w in widths)
    meta_ref, slots_ref, dead_ref, q_ref, gate_ref, near_ref = refs[:6]
    (key_pool, val_pool), cfold, weight_ref = refs[6:8], refs[8:11], refs[11]
    outs = list(refs[12 : 12 + out_count])
    gathered, even, odd, val, attended, weight, weight_sem, wide = refs[12 + out_count :]
    keys = (even, odd)
    turn, step = pl.program_id(0), pl.program_id(1)
    last = pl.num_programs(1) - 1
    rows = q_ref.shape[0]
    count = q_ref.shape[1] // QK
    chunk_start = meta_ref[2 + first_chunk + turn] * rows
    list_at = lax.div(chunk_start, QBLK)
    first_row = lax.rem(chunk_start, QBLK)
    position = meta_ref[2] + chunk_start
    copy = pltpu.make_async_copy(weight_ref, weight, weight_sem)

    @pl.when(step == 0)
    def _():
        for slot in range(PICKS):
            source = pl.multiple_of(slots_ref[list_at, slot] * KBLK, KBLK)
            gathered[slot * KBLK : (slot + 1) * KBLK] = key_pool[pl.ds(source, KBLK)]
            val[slot * KBLK : (slot + 1) * KBLK] = with_ones(val_pool[pl.ds(source, KBLK)])
        for slot in range(1, PICKS):

            @pl.when(dead_ref[list_at, slot] == 1)
            def _():
                at = slice(slot * KBLK, (slot + 1) * KBLK)
                gathered[at] = jnp.broadcast_to(gathered[:1], (KBLK, 256))
                val[at] = jnp.zeros((KBLK, 256), BF16)

        even[...], odd[...] = turned(gathered[...])

    @pl.when((turn == 0) & (step == 0))
    def _():
        copy.start()

    gate = gate_loader(gate_ref, wide, step * count, heads)
    row = iota(rows, TILE, 0)
    col = iota(rows, TILE, 1)
    own_keep = (col >= KBLK) | (col <= row + first_row)

    def own_mask(scores):
        own = jnp.where(repeated(own_keep[:, :128], scores.shape[0]), scores[:, :128], NEG)
        return jnp.concatenate([own, scores[:, 128:]], axis=1)

    def comp_mask(place):
        ends = (col + place * TILE + 1) * CBLK - 1
        return lambda x: jnp.where(repeated(ends <= row + position, x.shape[0]), x, NEG)

    def tile(refs, place, mask):
        return (lambda side: refs[side][:, place * TILE : (place + 1) * TILE]), mask, None

    chosen = [tile(keys, p, own_mask if p == 0 else None) for p in range(PICKS * KBLK // TILE)]
    folded = [tile(cfold, p, comp_mask(p)) for p in range(cfold[2].shape[0] // TILE)]
    empty = row[:, :DV] + position < CBLK - 1

    def finish(pair, side, n, parts):
        (num, den), (folded_num, folded_den) = parts
        folded_den = jnp.where(stacked(empty, n), 1.0, folded_den)
        total = gate(pair, side, n, 1) * (num / den)
        total = total + gate(pair, side, n, 0) * (folded_num / folded_den)
        for p in range(n):
            cols = head_columns(pair + p, side)
            mixed = near_ref[:, cols].astype(F32) + total[p * rows : (p + 1) * rows]
            attended[step, :, cols] = mixed.astype(BF16)
        return [den, folded_den]

    branches = [(chosen, lambda: val[...]), (folded, lambda: cfold[2][...])]
    over_heads(count // 2, query_loader(q_ref), branches, finish)

    @pl.when((turn == 0) & (step == last))
    def _():
        copy.wait()

    for place, parts in enumerate(widths):
        chunk_outs = [outs.pop(0) for _ in parts]

        @pl.when((turn == place) & (step == last))
        def _():
            rows_in = jnp.concatenate([attended[s] for s in range(attended.shape[0])], axis=1)
            first_col = 0
            for out_ref in chunk_outs:
                for at in range(0, out_ref.shape[1], 256):
                    cols = weight[:, first_col + at : first_col + at + 256]
                    part = jnp.dot(rows_in, cols, preferred_element_type=F32)
                    out_ref[:, at : at + 256] = part.astype(out_ref.dtype)
                first_col += out_ref.shape[1]


def chosen_and_project(first_chunk, widths, rows, meta, slots, dead, queries, gates, near, pools, out_weight):
    tokens, width = queries.shape
    heads = width // QK
    at_once = next(n for n in (8, 4, 2) if heads % n == 0)
    steps = heads // at_once
    whole = lambda x: pl.BlockSpec(x.shape, lambda i, p, *_: (0,) * x.ndim)
    outs = [jax.ShapeDtypeStruct((rows, width), BF16) for chunk in widths for width in chunk]
    return pl.pallas_call(
        functools.partial(chosen_kernel, heads, (first_chunk, widths)),
        grid_spec=pltpu.PrefetchScalarGridSpec(
            num_scalar_prefetch=3,
            grid=(len(widths), steps),
            in_specs=[
                pl.BlockSpec((rows, at_once * QK), lambda i, p, m, *_: (m[2 + first_chunk + i], p)),
                pl.BlockSpec((rows, 3 * heads), lambda i, p, m, *_: (m[2 + first_chunk + i], 0)),
                pl.BlockSpec((rows, at_once * DV), lambda i, p, m, *_: (m[2 + first_chunk + i], p)),
            ]
            + [VMEM_SPEC] * len(pools)
            + [pl.BlockSpec(memory_space=pl.ANY)],
            out_specs=[VMEM_SPEC] * len(outs),
            scratch_shapes=[
                pltpu.VMEM((PICKS * KBLK, 256), BF16),
                pltpu.VMEM((256, PICKS * KBLK), BF16),
                pltpu.VMEM((256, PICKS * KBLK), BF16),
                pltpu.VMEM((PICKS * KBLK, 256), BF16),
                pltpu.VMEM((steps, rows, at_once * DV), BF16),
                pltpu.VMEM(out_weight.shape, BF16),
                pltpu.SemaphoreType.DMA,
                pltpu.VMEM((rows, 128), F32),
            ],
        ),
        out_shape=outs,
        compiler_params=pltpu.CompilerParams(vmem_limit_bytes=CHOSEN_LIMIT),
        cost_estimate=pl.CostEstimate(
            flops=rows * heads * PICKS * KBLK * 64,
            bytes_accessed=out_weight.size,
            transcendentals=0,
        ),
        name="chosen_and_project",
    )(meta, slots, dead, queries, gates, near, *pools, out_weight)


VMEM_SPEC = pl.BlockSpec(memory_space=pltpu.VMEM)


def single_step(kernel, name, scalars, arrays, outs, scratch=(), in_spec=None, out_spec=None):
    whole = lambda x: pl.BlockSpec(x.shape, lambda i, *_: (0,) * len(x.shape))
    return pl.pallas_call(
        kernel,
        grid_spec=pltpu.PrefetchScalarGridSpec(
            num_scalar_prefetch=len(scalars),
            grid=(1,),
            in_specs=[in_spec or whole(x) for x in arrays],
            out_specs=[out_spec or whole(x) for x in outs],
            scratch_shapes=list(scratch),
        ),
        out_shape=outs,
        compiler_params=pltpu.CompilerParams(vmem_limit_bytes=VMEM_LIMIT),
        name=name,
    )(*scalars, *arrays)


def last_sum(halves, rows, kept_ref, *refs):
    halves, others, out_ref = refs[:halves], refs[halves:-1], refs[-1]
    at = pl.ds(pl.multiple_of(pl.program_id(0) * rows, rows), rows)
    first = 0
    for half in halves:
        cols = slice(first, first + half.shape[1])
        total = kept_ref[at, cols].astype(F32) + half[at].astype(F32)
        for other in others:
            total = total + other[at, cols].astype(F32)
        out_ref[:, cols] = total.astype(BF16)
        first += half.shape[1]


def local(
    queries,
    key_rows,
    value_rows,
    comp_key_weight,
    comp_value_weight,
    block_picks,
    gate_logits,
    out_weight,
):
    tokens = queries.shape[0]
    heads = queries.shape[1] // QK
    n_ctx, n_head = lax.axis_size("ctx"), lax.axis_size("head")
    shard, head_at = lax.axis_index("ctx"), lax.axis_index("head")
    group = head_at * heads // (HEADS // GROUPS)
    per_owner = tokens // KBLK
    lists = tokens // QBLK
    folds = tokens // CBLK
    groups = n_ctx // 2
    rim_blocks = WINDOW // KBLK
    packed_rows = per_owner * BROWS
    bf16 = lambda *shape: jax.ShapeDtypeStruct(shape, BF16)

    chips = n_head // 2
    chip, core = head_at // 2, lax.rem(head_at, 2)
    order = []
    for step in list(range(1, chips)) + [0]:
        target = lax.rem(chip + step, chips) * 2
        order += [target + 1 - core, target + core]
    where = jnp.stack([group, shard, shard * tokens] + order).astype(jnp.int32)
    rim_rows = rim_blocks * BROWS
    fold_weights = jnp.concatenate([comp_key_weight, comp_value_weight], axis=1)
    int32 = lambda *shape: jax.ShapeDtypeStruct(shape, jnp.int32)
    prep_out = [bf16(packed_rows + 3 * folds, 128), bf16(rim_rows, 128)]
    prep_out += [int32(1, n_ctx * lists), int32(lists, 2 * PICKS), int32(lists, 2 * PICKS)]
    prep_out += [bf16(256, tokens)] * 2 + [bf16(tokens, 256)]
    packed, rim, named, slots, dead, even, odd, val = pl.pallas_call(
        prep_kernel,
        grid_spec=pltpu.PrefetchScalarGridSpec(
            num_scalar_prefetch=1,
            grid=(1,),
            in_specs=[pl.BlockSpec(memory_space=pl.ANY)] * 4,
            out_specs=[VMEM_SPEC] * 2
            + [pl.BlockSpec(x.shape, lambda i, g: (0, 0)) for x in prep_out[2:5]]
            + [VMEM_SPEC] * 3,
            scratch_shapes=[
                pltpu.VMEM(block_picks.shape, jnp.int32),
                pltpu.VMEM((tokens, PAIR), BF16),
                pltpu.VMEM((tokens, DV), BF16),
                pltpu.VMEM((CBLK, PAIR), F32),
                pltpu.VMEM((CBLK, DV), F32),
                pltpu.SemaphoreType.DMA((5,)),
            ],
        ),
        out_shape=prep_out,
        compiler_params=pltpu.CompilerParams(vmem_limit_bytes=51 * 1024 * 1024),
        name="prep",
    )(where, block_picks, key_rows, value_rows, fold_weights)
    other = lax.ppermute(packed, "ctx", [(i, i ^ 1) for i in range(n_ctx)])
    named = [named] + [
        lax.ppermute(named, "ctx", [(i, i - 2 * d) for i in range(2 * d, n_ctx)])
        for d in range(1, groups)
    ]

    gates = gate_logits.reshape(tokens, 3 * heads)
    sent = bf16(lists * BROWS + 3 * folds, 128)

    def pack(beside, lists_in, rows):
        return single_step(
            functools.partial(pack_kernel, lists, beside),
            "pack",
            [where, *lists_in],
            [rows],
            [sent] * len(lists_in),
            in_spec=VMEM_SPEC,
            out_spec=VMEM_SPEC,
        )

    def all_ahead(sends):
        moved = []
        for distance, send in reversed(list(enumerate(sends, 1))):
            route = [(i, i + 2 * distance) for i in range(n_ctx - 2 * distance)]
            moved.append(lax.ppermute(send, "ctx", route))
        return moved[::-1]

    named, gates, rim = lax.optimization_barrier((named, gates, rim))
    far_rim = lax.ppermute(rim, "ctx", [(i, i + 1) for i in range(1, n_ctx - 1, 2)])
    own_sends = pack(False, named[1:], packed)
    own_sends, even = lax.optimization_barrier((own_sends, even))
    from_same = all_ahead(own_sends)

    reach = WINDOW // QBLK
    near = functools.partial(near_branch, where=where, queries=queries, gates=gates)
    near = functools.partial(near, keys=(even, odd, val))
    mixed = near(reach, lists - reach, rims=None, prior=None)

    other, mixed = lax.optimization_barrier((other, mixed))
    beside, *other_sends = pack(True, named, other)
    from_other = all_ahead(other_sends)
    mixed = near(0, reach, rims=(other, far_rim), prior=mixed)

    farthest_first = reversed(list(zip(from_same, from_other)))
    received = [beside] + [x for both in farthest_first for x in both]
    pools = single_step(
        functools.partial(pool_kernel, groups, lists),
        "pool",
        [where],
        [packed] + received,
        [bf16(n_ctx * lists * KBLK, 256), bf16(n_ctx * lists * KBLK, DV)]
        + [bf16(256, n_ctx * folds)] * 2
        + [bf16(n_ctx * folds, 256)],
        [pltpu.VMEM((n_ctx * folds, 256), BF16)],
        in_spec=VMEM_SPEC,
        out_spec=VMEM_SPEC,
    )
    rows = tokens // n_head
    across = [(i, i ^ 1) for i in range(n_head)]

    model = out_weight.shape[1]

    def project(first_chunk, widths):
        return chosen_and_project(
            first_chunk, widths, rows, where, slots, dead, queries, gates, mixed, pools, out_weight
        )

    sums = []
    for step in range(chips - 1):
        other = lax.ppermute(project(1 + 2 * step, [[model]])[0], "head", across)
        mine = project(2 + 2 * step, [[model]])[0]
        summed = (mine.astype(F32) + other.astype(F32)).astype(BF16)
        summed, where = lax.optimization_barrier((summed, where))
        sums.append(summed)
    *passed, kept = project(n_head - 1, [[model // 2] * 2, [model]])
    near_parts = [lax.ppermute(x, "head", across) for x in passed]
    arrived = []
    for step, summed in enumerate(sums, 1):
        route = [(i, (i + 2 * step) % n_head) for i in range(n_head)]
        arrived.append(lax.ppermute(summed, "head", route))
    steps = 2 if rows % 32 == 0 else 1
    row_block = pl.BlockSpec((rows // steps, model), lambda i: (i, 0))
    return pl.pallas_call(
        functools.partial(last_sum, len(near_parts), rows // steps),
        grid=(steps,),
        in_specs=[VMEM_SPEC] * (1 + len(near_parts) + len(arrived)),
        out_specs=row_block,
        out_shape=bf16(rows, model),
        compiler_params=pltpu.CompilerParams(vmem_limit_bytes=VMEM_LIMIT),
        name="last_sum",
    )(kept, *near_parts, *arrived)


def solution(mesh):
    placed = (
        P("ctx", "head"),
        P("ctx", None),
        P("ctx", None),
        P(),
        P(),
        P("ctx", None, None),
        P("ctx", None, "head"),
        P("head", None),
    )
    return jax.shard_map(
        local, mesh=mesh, in_specs=placed, out_specs=P(("ctx", "head"), None), check_vma=False
    )
```

```python
import functools

import jax
import jax.numpy as jnp
from jax import lax
from jax.experimental import pallas as pl
from jax.experimental.pallas import tpu as pltpu
from jax.sharding import PartitionSpec as P

HEADS = 64
GROUPS = 4
QK = 192
DV = 128
CBLK = 32
KBLK = 64
PICKS = 16
WINDOW = 512
QBLK = 256
PAIR = 2 * QK
BROWS = KBLK + KBLK // 2 + KBLK
VMEM_LIMIT = 50 * 1024 * 1024
CHOSEN_LIMIT = 48 * 1024 * 1024
NEG = -1e30
SCALE = QK ** (-0.5) * 1.4426950408889634
LOW_TOTAL, HIGH_TOTAL = 2.0**-60, 2.0**100
TILE = 256
NT = (((1,), (1,)), ((), ()))
F32 = jnp.float32
BF16 = jnp.bfloat16


def half_lanes(rows):
    return lax.broadcasted_iota(jnp.int32, (rows, 128), 1) < 64


def swap_halves(x):
    return pltpu.roll(x, 64, 1)


def turned(keys):
    row, col = iota(256, 256, 0), iota(256, 256, 1)
    unit = (row == col).astype(BF16)
    even = lax.dot_general(unit, keys, NT, preferred_element_type=F32).astype(BF16)
    return even, lower(even)


def lower(even):
    return jnp.concatenate([jnp.zeros((64, even.shape[1]), BF16), even[:QK]], axis=0)


def with_ones(values):
    return jnp.concatenate([values, jnp.ones_like(values)], axis=1)


def plan(group, shard, per_owner, picks_ref, lists_ref, slots_ref, dead_ref):
    lists = picks_ref.shape[0]
    total = lists_ref.shape[1] // lists * per_owner
    width = slots_ref.shape[1]
    picks = jnp.zeros((lists, PICKS), jnp.int32)
    for each in range(picks_ref.shape[1]):
        picks = jnp.where(group == each, picks_ref[:, each, :], picks)
    block = iota(lists, total, 1)
    hits = [block == picks[:, entry : entry + 1] for entry in range(PICKS)]
    named = functools.reduce(jnp.logical_or, hits).astype(F32)
    named = jnp.broadcast_to(jnp.max(named, axis=0, keepdims=True), (8, total))
    row, col = iota(total, total, 0), iota(total, total, 1)
    before = (lax.div(row, per_owner) == lax.div(col, per_owner)) & (row < col)
    rank = jnp.dot(named, before.astype(F32), preferred_element_type=F32)
    rank = jnp.minimum(rank, float(lists - 1))
    inside = lax.rem(iota(8, total, 1), per_owner).astype(F32)
    found = jnp.zeros((8, lists_ref.shape[1]), F32)
    row, col = iota(total, lists_ref.shape[1], 0), iota(total, lists_ref.shape[1], 1)
    for place in range(lists):
        to = (col == lax.div(row, per_owner) * lists + place).astype(F32)
        value = jnp.where(rank == float(place), named * inside, 0.0)
        found = found + jnp.dot(value, to, preferred_element_type=F32)
    lists_ref[...] = found[:1].astype(jnp.int32)

    owner = lax.div(block, per_owner)
    turn = (lax.div(shard, 2) - lax.div(owner, 2)) * 2 + ((owner ^ shard) & 1)
    slot = jnp.clip(turn * lists + rank[:lists].astype(jnp.int32), 0, lists_ref.shape[1] - 1)
    slot = slot.astype(F32)
    first = shard * per_owner + iota(lists, 1, 0) * (QBLK // KBLK)
    own = block == first

    def pick_out(hit, values):
        return jnp.sum(jnp.where(hit, values, 0.0), axis=1, keepdims=True)

    lane = iota(lists, width, 1)
    slots = jnp.where(lane == 0, pick_out(own, slot), 0.0)
    dead = jnp.zeros((lists, width), F32)
    seen = own.astype(F32)
    at = jnp.ones((lists, 1), jnp.int32)
    met = jnp.zeros((lists, 1), jnp.int32)
    for entry, hit in enumerate(hits):
        pick = picks[:, entry : entry + 1]
        is_own = (pick == first).astype(jnp.int32)
        gone = jnp.maximum(pick_out(hit, seen), (pick > first).astype(F32))
        slots = jnp.where(lane == at, pick_out(hit, slot), slots)
        dead = jnp.where(lane == at, gone, dead)
        seen = jnp.maximum(seen, hit.astype(F32))
        at = at + 1 - is_own * (1 - met)
        met = jnp.maximum(met, is_own)
    slots_ref[...] = slots.astype(jnp.int32)
    dead_ref[...] = dead.astype(jnp.int32)


def prep_kernel(
    where_ref,
    picks_in,
    keys_in,
    values_in,
    fold_in,
    packed_ref,
    rim_ref,
    lists_ref,
    slots_ref,
    dead_ref,
    even_ref,
    odd_ref,
    val_ref,
    picks_ref,
    keys_ref,
    values_ref,
    kw_ref,
    vw_ref,
    sems,
):
    group, shard = where_ref[0], where_ref[1]
    pair = pl.ds(pl.multiple_of(lax.div(group, 2) * PAIR, 128), PAIR)
    single = pl.ds(pl.multiple_of(group * DV, 128), DV)
    folded_value = pl.ds(pl.multiple_of(GROUPS * QK + group * DV, 128), DV)
    copies = [
        pltpu.make_async_copy(source, target, sems.at[i])
        for i, (source, target) in enumerate(
            [
                (picks_in, picks_ref),
                (keys_in.at[:, pair], keys_ref),
                (values_in.at[:, single], values_ref),
                (fold_in.at[:, pair], kw_ref),
                (fold_in.at[:, folded_value], vw_ref),
            ]
        )
    ]
    for copy in copies:
        copy.start()
    copies[0].wait()
    plan(group, shard, keys_ref.shape[0] // KBLK, picks_ref, lists_ref, slots_ref, dead_ref)
    for copy in copies[1:]:
        copy.wait()
    odd = lax.rem(group, 2) == 1

    def own_columns(ref):
        t0 = ref[:, :128].astype(F32)
        t1 = ref[:, 128:256].astype(F32)
        t2 = ref[:, 256:].astype(F32)
        r1, r2 = swap_halves(t1), swap_halves(t2)
        left = half_lanes(t0.shape[0])
        low = jnp.where(odd, jnp.where(left, r1, r2), t0)
        high = jnp.where(left, jnp.where(odd, r2, t1), 0.0)
        return low, high

    low, high = own_columns(keys_ref)
    values = values_ref[...]
    rows = low.shape[0]
    count = rows // KBLK
    high3 = high.reshape(count, KBLK, 128)
    packed_high = high3[:, : KBLK // 2] + swap_halves(
        high3[:, KBLK // 2 :].reshape(count * KBLK // 2, 128)
    ).reshape(count, KBLK // 2, 128)
    even = jnp.concatenate([low.astype(BF16), high.astype(BF16)], axis=1)
    even_ref[...], odd_ref[...] = turned(even)
    val_ref[...] = with_ones(values)
    for block in range(count):
        at = block * BROWS
        token = slice(block * KBLK, block * KBLK + KBLK)
        packed_ref[at : at + KBLK] = low[token].astype(BF16)
        packed_ref[at + KBLK : at + KBLK + KBLK // 2] = packed_high[block].astype(BF16)
        packed_ref[at + KBLK + KBLK // 2 : at + BROWS] = values[token]
    rim_rows = rim_ref.shape[0]
    rim_ref[...] = packed_ref[count * BROWS - rim_rows : count * BROWS]

    wlow, whigh = own_columns(kw_ref)
    folds = rows // CBLK

    def fold(x, w):
        return jnp.sum(x.reshape(folds, CBLK, 128) * w[None], axis=1)

    at = count * BROWS
    half = folds // 2
    high_fold = fold(high, whigh)
    high_fold = high_fold[:half] + swap_halves(high_fold[half:])
    packed_ref[at : at + folds] = fold(low, wlow).astype(BF16)
    packed_ref[at + folds : at + folds + half] = high_fold.astype(BF16)
    packed_ref[at + folds + half :] = fold(values.astype(F32), vw_ref[...]).astype(BF16)


def pack_kernel(lists, beside, where_ref, *refs):
    count = len(refs) // 2
    named, ref, outs = refs[:count], refs[count], refs[count + 1 :]
    shard = where_ref[1]
    owner = shard + 1 - 2 * lax.rem(shard, 2) if beside else shard
    data = ref.shape[0] - (outs[0].shape[0] - lists * BROWS)
    for blocks, out in zip(named, outs):
        for place in range(lists):
            at = pl.multiple_of(blocks[0, owner * lists + place] * BROWS, 16)
            out[place * BROWS : (place + 1) * BROWS] = ref[pl.ds(at, BROWS)]
        out[lists * BROWS :] = ref[data:]


def unpack(ref, at, count, step=1):
    lows, packed, values = [], [], []
    for block in range(count):
        first = at + block * step * BROWS
        lows.append(ref[first : first + KBLK])
        packed.append(ref[first + KBLK : first + KBLK + KBLK // 2])
        values.append(ref[first + KBLK + KBLK // 2 : first + BROWS])
    packed = jnp.concatenate(packed, axis=0)
    row, col = iota(128, 256, 0), iota(128, 256, 1)
    take = (row == jnp.where(col < 128, col, col - 64)) & (lax.rem(col, 128) < 64)
    both = jnp.dot(packed, take.astype(BF16), preferred_element_type=F32).astype(BF16)
    half = KBLK // 2
    highs = []
    for block in range(count):
        rows = slice(block * half, block * half + half)
        highs += [both[rows, :128], both[rows, 128:]]
    even = jnp.concatenate(
        [jnp.concatenate(lows, axis=0), jnp.concatenate(highs, axis=0)], axis=1
    )
    return even, jnp.concatenate(values, axis=0)


def fill_rim(shard, near_ref, far_ref, own, ext):
    rim_blocks = WINDOW // KBLK
    even_in, odd_in, val_in = own
    even_ref, odd_ref, val_ref = ext
    even_ref[:, WINDOW:] = even_in[:, :WINDOW]
    odd_ref[:, WINDOW:] = odd_in[:, :WINDOW]
    val_ref[WINDOW:] = val_in[:WINDOW]
    use_near = lax.rem(shard, 2) == 1
    rim_end = near_ref.shape[0] // BROWS * BROWS
    near_rim = near_ref[rim_end - far_ref.shape[0] : rim_end]

    @pl.when(shard > 0)
    def _():
        keys, values = unpack(jnp.where(use_near, near_rim, far_ref[...]), 0, rim_blocks)
        even_ref[:, :WINDOW], odd_ref[:, :WINDOW] = turned(keys)
        val_ref[:WINDOW] = with_ones(values)

    @pl.when(shard == 0)
    def _():
        even = jnp.broadcast_to(even_in[:, :1].astype(F32), (256, WINDOW)).astype(BF16)
        even_ref[:, :WINDOW], odd_ref[:, :WINDOW] = even, lower(even)
        val_ref[:WINDOW] = jnp.zeros((WINDOW, 256), BF16)


def pool_kernel(groups, lists, where_ref, own_ref, *refs):
    sent = 2 * groups - 1
    ins, (key_ref, val_ref, ceven_ref, codd_ref, cval_ref, folded) = refs[:sent], refs[sent:]
    shard = where_ref[1]
    parity = lax.rem(shard, 2)
    base = shard - parity
    rows = lists * KBLK
    folds = (ins[0].shape[0] - lists * BROWS) * 2 // 5
    half = folds // 2
    folded[...] = jnp.zeros_like(folded)
    cval_ref[...] = jnp.zeros_like(cval_ref)

    def fill(place, owner, ref, step, fold_at):
        keys, values = unpack(ref, 0, lists, step)
        at = slice(place * rows, place * rows + rows)
        key_ref[at] = keys
        val_ref[at] = values
        low = ref[fold_at : fold_at + folds]
        high = ref[fold_at + folds : fold_at + folds + half].astype(F32)
        left = half_lanes(half)
        high = [jnp.where(left, x, 0.0) for x in (high, swap_halves(high))]
        high = jnp.concatenate(high, axis=0).astype(BF16)
        owned = pl.ds(pl.multiple_of(owner * folds, 32), folds)
        folded[owned] = jnp.concatenate([low, high], axis=1)
        cval_ref[owned] = with_ones(ref[fold_at + folds + half : fold_at + 2 * folds + half])

    fill(0, shard, own_ref, QBLK // KBLK, own_ref.shape[0] - 2 * folds - half)
    fill(1, base + 1 - parity, ins[0], 1, lists * BROWS)
    for distance in range(1, groups):

        @pl.when(base >= 2 * distance)
        def _():
            for side in range(2):
                owner = base - 2 * distance + (parity if side == 0 else 1 - parity)
                fill(2 * distance + side, owner, ins[2 * (groups - distance) - 1 + side], 1, lists * BROWS)

    ceven_ref[...], codd_ref[...] = turned(folded[...])


def iota(rows, cols, axis):
    return lax.broadcasted_iota(jnp.int32, (rows, cols), axis)


def scores_of(q, keys, mask):
    scores = jnp.dot(q, keys, preferred_element_type=F32)
    return scores if mask is None else mask(scores)


def in_range(total):
    good = jnp.where((total >= LOW_TOTAL) & (total <= HIGH_TOTAL), 1.0, 0.0)
    return jnp.min(good.reshape(-1, 8, DV), axis=0)


def over_heads(pairs, load, branches, finish):
    def sums(weights, values):
        out = jnp.dot(weights, values(), preferred_element_type=F32)
        return out[:, :DV], out[:, DV:]

    at_once = 2 if pairs % 2 == 0 else 1
    units = [(pair, side) for pair in range(0, pairs, at_once) for side in range(2)]
    worst, held = [], None
    for now, unit in zip([None] + units, units + [None]):
        q = None if unit is None else load(*unit, at_once)
        fresh, parts = [], []
        for at, (tiles, values) in enumerate(branches):
            weights, ahead = [], []
            for place, (keys, mask) in enumerate(tiles):
                if q is not None:
                    ahead.append(scores_of(q, keys(unit[1]), mask))
                if held is not None:
                    weights.append(jnp.exp2(held[at][place] * SCALE).astype(BF16))
            fresh.append(ahead)
            parts.append((weights, values))
        if held is not None:
            parts = [sums(jnp.concatenate(w, axis=1), values) for w, values in parts]
            worst += [in_range(x) for x in finish(*now, at_once, parts)]
        held = fresh

    @pl.when(jnp.min(functools.reduce(jnp.minimum, worst)) < 0.5)
    def _():
        def exact(pair, _):
            for side in range(2):
                q = load(pair, side, 1)
                parts = []
                for tiles, values in branches:
                    scores = [scores_of(q, keys(side), mask) for keys, mask in tiles]
                    scores = jnp.concatenate(scores, axis=1)
                    top = jnp.max(scores, axis=1, keepdims=True)
                    shifted = (scores - jnp.maximum(top, -1e28)) * SCALE
                    parts.append(sums(jnp.exp2(shifted).astype(BF16), values))
                finish(pair, side, 1, parts)
            return 0

        lax.fori_loop(0, pairs, exact, 0)


def aligned(at):
    return at if isinstance(at, int) else pl.multiple_of(at, 128)


def query_loader(q_ref):
    def load(pair, side, n):
        at = [aligned((pair + p) * PAIR + side * 128) for p in range(n)]
        return jnp.concatenate([q_ref[:, pl.ds(x, 256)] for x in at], axis=0)

    return load


def head_columns(pair, side):
    return pl.ds(aligned(pair * 2 * DV + side * DV), DV)


def gate_loader(gate_ref, first, heads):
    turned = pltpu.roll(gate_ref[...], lax.rem(128 - first, 128), 1)

    def load(pair, side, n, branch):
        if isinstance(pair, int):
            local, at = turned, branch * heads + side + 2 * pair
        else:
            local, at = pltpu.roll(turned, lax.rem(128 - 2 * pair, 128), 1), branch * heads + side
        columns = [local[:, at + 2 * p : at + 2 * p + 1] for p in range(n)]
        shape = (turned.shape[0], DV)
        return jnp.concatenate([jnp.broadcast_to(x, shape) for x in columns], axis=0)

    return load


def stacked(x, times):
    return jnp.concatenate([x] * times, axis=0) if times > 1 else x


def repeated(keep, rows):
    return stacked(keep, rows // keep.shape[0])


def near_kernel(heads, first_block, rim, where_ref, q_ref, gate_ref, *refs):
    keys = refs[:3]
    if rim:
        out_ref, ext = refs[-4], refs[-3:]

        @pl.when((pl.program_id(0) == 0) & (pl.program_id(1) == 0))
        def _():
            fill_rim(where_ref[1], refs[3], refs[4], keys, ext)

        keys, reach = ext, 0
    else:
        out_ref, reach = refs[-1], WINDOW
    count = q_ref.shape[1] // QK
    gate = gate_loader(gate_ref, pl.program_id(1) * count, heads)
    base = pl.multiple_of((first_block + pl.program_id(0)) * QBLK - reach, QBLK)
    row, col = iota(QBLK, QBLK, 0), iota(QBLK, QBLK, 1)

    def tile(place, mask):
        return (lambda side: keys[side][:, pl.ds(base + place * QBLK, QBLK)]), mask

    def finish(pair, side, n, parts):
        ((num, den),) = parts
        total = gate(pair, side, n, 2) * (num / den)
        for p in range(n):
            part = total[p * QBLK : (p + 1) * QBLK]
            out_ref[:, head_columns(pair + p, side)] = part.astype(BF16)
        return [den]

    tiles = [
        tile(0, lambda x: jnp.where(repeated(col >= row, x.shape[0]), x, NEG)),
        tile(1, None),
        tile(2, lambda x: jnp.where(repeated(col <= row, x.shape[0]), x, NEG)),
    ]
    values = lambda: keys[2][pl.ds(base, WINDOW + QBLK)]
    over_heads(count // 2, query_loader(q_ref), [(tiles, values)], finish)


def near_branch(first_block, block_count, where, queries, gates, keys, rims, prior):
    tokens, width = queries.shape
    heads = width // QK
    at_once = next(n for n in (8, 4, 2) if heads % n == 0)
    row_block = lambda i, p, *_: (i + first_block, p)
    operands = [queries, gates, *keys]
    specs = [
        pl.BlockSpec((QBLK, at_once * QK), row_block),
        pl.BlockSpec((QBLK, 128), lambda i, p, *_: (i + first_block, 0)),
    ]
    specs += [VMEM_SPEC] * len(keys)
    alias, scratch = {}, []
    if rims is not None:
        other, far = rims
        operands += [other, far]
        specs += [VMEM_SPEC, VMEM_SPEC]
        scratch = [pltpu.VMEM((256, 2 * WINDOW), BF16)] * 2 + [pltpu.VMEM((2 * WINDOW, 256), BF16)]
    if prior is not None:
        operands.append(prior)
        specs.append(pl.BlockSpec(memory_space=pl.ANY))
        alias = {len(operands): 0}
    rows = block_count * QBLK * heads
    return pl.pallas_call(
        functools.partial(near_kernel, heads, first_block, rims is not None),
        grid_spec=pltpu.PrefetchScalarGridSpec(
            num_scalar_prefetch=1,
            grid=(block_count, heads // at_once),
            in_specs=specs,
            out_specs=pl.BlockSpec((QBLK, at_once * DV), row_block),
            scratch_shapes=scratch,
        ),
        out_shape=jax.ShapeDtypeStruct((tokens, heads * DV), BF16),
        input_output_aliases=alias,
        compiler_params=pltpu.CompilerParams(vmem_limit_bytes=VMEM_LIMIT),
        cost_estimate=pl.CostEstimate(
            flops=rows * (WINDOW + QBLK) * 64,
            bytes_accessed=rows * (2 * QK + 4 * DV),
            transcendentals=0,
        ),
        name="near_branch",
    )(where, *operands)


def chosen_kernel(heads, span, *refs):
    first_chunk, widths = span
    out_count = sum(len(w) for w in widths)
    meta_ref, slots_ref, dead_ref, q_ref, gate_ref, near_ref = refs[:6]
    (key_pool, val_pool), cfold, weight_ref = refs[6:8], refs[8:11], refs[11]
    outs = list(refs[12 : 12 + out_count])
    gathered, even, odd, val, attended, weight, weight_sem = refs[12 + out_count :]
    keys = (even, odd)
    turn, step = pl.program_id(0), pl.program_id(1)
    last = pl.num_programs(1) - 1
    rows = q_ref.shape[0]
    count = q_ref.shape[1] // QK
    chunk_start = meta_ref[2 + first_chunk + turn] * rows
    list_at = lax.div(chunk_start, QBLK)
    first_row = lax.rem(chunk_start, QBLK)
    position = meta_ref[2] + chunk_start
    copy = pltpu.make_async_copy(weight_ref, weight, weight_sem)

    @pl.when(step == 0)
    def _():
        for slot in range(PICKS):
            source = pl.multiple_of(slots_ref[list_at, slot] * KBLK, KBLK)
            gathered[slot * KBLK : (slot + 1) * KBLK] = key_pool[pl.ds(source, KBLK)]
            val[slot * KBLK : (slot + 1) * KBLK] = with_ones(val_pool[pl.ds(source, KBLK)])
        for slot in range(1, PICKS):

            @pl.when(dead_ref[list_at, slot] == 1)
            def _():
                at = slice(slot * KBLK, (slot + 1) * KBLK)
                gathered[at] = jnp.broadcast_to(gathered[:1], (KBLK, 256))
                val[at] = jnp.zeros((KBLK, 256), BF16)

        even[...], odd[...] = turned(gathered[...])

    @pl.when((turn == 0) & (step == 0))
    def _():
        copy.start()

    gate = gate_loader(gate_ref, step * count, heads)
    row = iota(rows, TILE, 0)
    col = iota(rows, TILE, 1)
    own_keep = (col >= KBLK) | (col <= row + first_row)

    def own_mask(scores):
        own = jnp.where(repeated(own_keep[:, :128], scores.shape[0]), scores[:, :128], NEG)
        return jnp.concatenate([own, scores[:, 128:]], axis=1)

    def comp_mask(place):
        ends = (col + place * TILE + 1) * CBLK - 1
        return lambda x: jnp.where(repeated(ends <= row + position, x.shape[0]), x, NEG)

    def tile(refs, place, mask):
        return (lambda side: refs[side][:, place * TILE : (place + 1) * TILE]), mask

    chosen = [tile(keys, p, own_mask if p == 0 else None) for p in range(PICKS * KBLK // TILE)]
    folded = [tile(cfold, p, comp_mask(p)) for p in range(cfold[2].shape[0] // TILE)]
    empty = row[:, :DV] + position < CBLK - 1

    def finish(pair, side, n, parts):
        (num, den), (folded_num, folded_den) = parts
        folded_den = jnp.where(stacked(empty, n), 1.0, folded_den)
        total = gate(pair, side, n, 1) * (num / den)
        total = total + gate(pair, side, n, 0) * (folded_num / folded_den)
        for p in range(n):
            cols = head_columns(pair + p, side)
            mixed = near_ref[:, cols].astype(F32) + total[p * rows : (p + 1) * rows]
            attended[step, :, cols] = mixed.astype(BF16)
        return [den, folded_den]

    branches = [(chosen, lambda: val[...]), (folded, lambda: cfold[2][...])]
    over_heads(count // 2, query_loader(q_ref), branches, finish)

    @pl.when((turn == 0) & (step == last))
    def _():
        copy.wait()

    for place, parts in enumerate(widths):
        chunk_outs = [outs.pop(0) for _ in parts]

        @pl.when((turn == place) & (step == last))
        def _():
            rows_in = jnp.concatenate([attended[s] for s in range(attended.shape[0])], axis=1)
            first_col = 0
            for out_ref in chunk_outs:
                for at in range(0, out_ref.shape[1], 256):
                    cols = weight[:, first_col + at : first_col + at + 256]
                    part = jnp.dot(rows_in, cols, preferred_element_type=F32)
                    out_ref[:, at : at + 256] = part.astype(out_ref.dtype)
                first_col += out_ref.shape[1]


def chosen_and_project(first_chunk, widths, rows, meta, slots, dead, queries, gates, near, pools, out_weight):
    tokens, width = queries.shape
    heads = width // QK
    at_once = next(n for n in (8, 4, 2) if heads % n == 0)
    steps = heads // at_once
    whole = lambda x: pl.BlockSpec(x.shape, lambda i, p, *_: (0,) * x.ndim)
    outs = [jax.ShapeDtypeStruct((rows, width), BF16) for chunk in widths for width in chunk]
    return pl.pallas_call(
        functools.partial(chosen_kernel, heads, (first_chunk, widths)),
        grid_spec=pltpu.PrefetchScalarGridSpec(
            num_scalar_prefetch=3,
            grid=(len(widths), steps),
            in_specs=[
                pl.BlockSpec((rows, at_once * QK), lambda i, p, m, *_: (m[2 + first_chunk + i], p)),
                pl.BlockSpec((rows, 128), lambda i, p, m, *_: (m[2 + first_chunk + i], 0)),
                pl.BlockSpec((rows, at_once * DV), lambda i, p, m, *_: (m[2 + first_chunk + i], p)),
            ]
            + [VMEM_SPEC] * len(pools)
            + [pl.BlockSpec(memory_space=pl.ANY)],
            out_specs=[VMEM_SPEC] * len(outs),
            scratch_shapes=[
                pltpu.VMEM((PICKS * KBLK, 256), BF16),
                pltpu.VMEM((256, PICKS * KBLK), BF16),
                pltpu.VMEM((256, PICKS * KBLK), BF16),
                pltpu.VMEM((PICKS * KBLK, 256), BF16),
                pltpu.VMEM((steps, rows, at_once * DV), BF16),
                pltpu.VMEM(out_weight.shape, BF16),
                pltpu.SemaphoreType.DMA,
            ],
        ),
        out_shape=outs,
        compiler_params=pltpu.CompilerParams(vmem_limit_bytes=CHOSEN_LIMIT),
        cost_estimate=pl.CostEstimate(
            flops=rows * heads * PICKS * KBLK * 64,
            bytes_accessed=out_weight.size,
            transcendentals=0,
        ),
        name="chosen_and_project",
    )(meta, slots, dead, queries, gates, near, *pools, out_weight)


VMEM_SPEC = pl.BlockSpec(memory_space=pltpu.VMEM)


def single_step(kernel, name, scalars, arrays, outs, scratch=(), in_spec=None, out_spec=None):
    whole = lambda x: pl.BlockSpec(x.shape, lambda i, *_: (0,) * len(x.shape))
    return pl.pallas_call(
        kernel,
        grid_spec=pltpu.PrefetchScalarGridSpec(
            num_scalar_prefetch=len(scalars),
            grid=(1,),
            in_specs=[in_spec or whole(x) for x in arrays],
            out_specs=[out_spec or whole(x) for x in outs],
            scratch_shapes=list(scratch),
        ),
        out_shape=outs,
        compiler_params=pltpu.CompilerParams(vmem_limit_bytes=VMEM_LIMIT),
        name=name,
    )(*scalars, *arrays)


def last_sum(halves, rows, kept_ref, *refs):
    halves, others, out_ref = refs[:halves], refs[halves:-1], refs[-1]
    at = pl.ds(pl.multiple_of(pl.program_id(0) * rows, rows), rows)
    first = 0
    for half in halves:
        cols = slice(first, first + half.shape[1])
        total = kept_ref[at, cols].astype(F32) + half[at].astype(F32)
        for other in others:
            total = total + other[at, cols].astype(F32)
        out_ref[:, cols] = total.astype(BF16)
        first += half.shape[1]


def local(
    queries,
    key_rows,
    value_rows,
    comp_key_weight,
    comp_value_weight,
    block_picks,
    gate_logits,
    out_weight,
):
    tokens = queries.shape[0]
    heads = queries.shape[1] // QK
    n_ctx, n_head = lax.axis_size("ctx"), lax.axis_size("head")
    shard, head_at = lax.axis_index("ctx"), lax.axis_index("head")
    group = head_at * heads // (HEADS // GROUPS)
    per_owner = tokens // KBLK
    lists = tokens // QBLK
    folds = tokens // CBLK
    groups = n_ctx // 2
    rim_blocks = WINDOW // KBLK
    packed_rows = per_owner * BROWS
    bf16 = lambda *shape: jax.ShapeDtypeStruct(shape, BF16)

    chips = n_head // 2
    chip, core = head_at // 2, lax.rem(head_at, 2)
    order = []
    for step in list(range(1, chips)) + [0]:
        target = lax.rem(chip + step, chips) * 2
        order += [target + 1 - core, target + core]
    where = jnp.stack([group, shard, shard * tokens] + order).astype(jnp.int32)
    rim_rows = rim_blocks * BROWS
    fold_weights = jnp.concatenate([comp_key_weight, comp_value_weight], axis=1)
    int32 = lambda *shape: jax.ShapeDtypeStruct(shape, jnp.int32)
    prep_out = [bf16(packed_rows + folds * 5 // 2, 128), bf16(rim_rows, 128)]
    prep_out += [int32(1, n_ctx * lists), int32(lists, 2 * PICKS), int32(lists, 2 * PICKS)]
    prep_out += [bf16(256, tokens)] * 2 + [bf16(tokens, 256)]
    packed, rim, named, slots, dead, even, odd, val = pl.pallas_call(
        prep_kernel,
        grid_spec=pltpu.PrefetchScalarGridSpec(
            num_scalar_prefetch=1,
            grid=(1,),
            in_specs=[pl.BlockSpec(memory_space=pl.ANY)] * 4,
            out_specs=[VMEM_SPEC] * 2
            + [pl.BlockSpec(x.shape, lambda i, g: (0, 0)) for x in prep_out[2:5]]
            + [VMEM_SPEC] * 3,
            scratch_shapes=[
                pltpu.VMEM(block_picks.shape, jnp.int32),
                pltpu.VMEM((tokens, PAIR), BF16),
                pltpu.VMEM((tokens, DV), BF16),
                pltpu.VMEM((CBLK, PAIR), F32),
                pltpu.VMEM((CBLK, DV), F32),
                pltpu.SemaphoreType.DMA((5,)),
            ],
        ),
        out_shape=prep_out,
        compiler_params=pltpu.CompilerParams(vmem_limit_bytes=51 * 1024 * 1024),
        name="prep",
    )(where, block_picks, key_rows, value_rows, fold_weights)
    other = lax.ppermute(packed, "ctx", [(i, i ^ 1) for i in range(n_ctx)])
    named = [named] + [
        lax.ppermute(named, "ctx", [(i, i - 2 * d) for i in range(2 * d, n_ctx)])
        for d in range(1, groups)
    ]
    far_rim = lax.ppermute(rim, "ctx", [(i, i + 1) for i in range(1, n_ctx - 1, 2)])

    gates = jax.nn.sigmoid(gate_logits).reshape(tokens, 3 * heads)
    gates = jnp.pad(gates, ((0, 0), (0, 128 - 3 * heads)))
    sent = bf16(lists * BROWS + folds * 5 // 2, 128)

    def pack(beside, lists_in, rows):
        return single_step(
            functools.partial(pack_kernel, lists, beside),
            "pack",
            [where, *lists_in],
            [rows],
            [sent] * len(lists_in),
            in_spec=VMEM_SPEC,
            out_spec=VMEM_SPEC,
        )

    def all_ahead(sends):
        moved = []
        for distance, send in reversed(list(enumerate(sends, 1))):
            route = [(i, i + 2 * distance) for i in range(n_ctx - 2 * distance)]
            moved.append(lax.ppermute(send, "ctx", route))
        return moved[::-1]

    named, gates = lax.optimization_barrier((named, gates))
    own_sends = pack(False, named[1:], packed)
    own_sends, even = lax.optimization_barrier((own_sends, even))
    from_same = all_ahead(own_sends)

    reach = WINDOW // QBLK
    near = functools.partial(near_branch, where=where, queries=queries, gates=gates)
    near = functools.partial(near, keys=(even, odd, val))
    mixed = near(reach, lists - reach, rims=None, prior=None)

    other, mixed = lax.optimization_barrier((other, mixed))
    beside, *other_sends = pack(True, named, other)
    from_other = all_ahead(other_sends)
    mixed = near(0, reach, rims=(other, far_rim), prior=mixed)

    farthest_first = reversed(list(zip(from_same, from_other)))
    received = [beside] + [x for both in farthest_first for x in both]
    pools = single_step(
        functools.partial(pool_kernel, groups, lists),
        "pool",
        [where],
        [packed] + received,
        [bf16(n_ctx * lists * KBLK, 256), bf16(n_ctx * lists * KBLK, DV)]
        + [bf16(256, n_ctx * folds)] * 2
        + [bf16(n_ctx * folds, 256)],
        [pltpu.VMEM((n_ctx * folds, 256), BF16)],
        in_spec=VMEM_SPEC,
        out_spec=VMEM_SPEC,
    )
    rows = tokens // n_head
    across = [(i, i ^ 1) for i in range(n_head)]

    model = out_weight.shape[1]

    def project(first_chunk, widths):
        return chosen_and_project(
            first_chunk, widths, rows, where, slots, dead, queries, gates, mixed, pools, out_weight
        )

    sums = []
    for step in range(chips - 1):
        other = lax.ppermute(project(1 + 2 * step, [[model]])[0], "head", across)
        mine = project(2 + 2 * step, [[model]])[0]
        summed = (mine.astype(F32) + other.astype(F32)).astype(BF16)
        summed, where = lax.optimization_barrier((summed, where))
        sums.append(summed)
    *passed, kept = project(n_head - 1, [[model // 2] * 2, [model]])
    near_parts = [lax.ppermute(x, "head", across) for x in passed]
    arrived = []
    for step, summed in enumerate(sums, 1):
        route = [(i, (i + 2 * step) % n_head) for i in range(n_head)]
        arrived.append(lax.ppermute(summed, "head", route))
    steps = 2 if rows % 32 == 0 else 1
    row_block = pl.BlockSpec((rows // steps, model), lambda i: (i, 0))
    return pl.pallas_call(
        functools.partial(last_sum, len(near_parts), rows // steps),
        grid=(steps,),
        in_specs=[VMEM_SPEC] * (1 + len(near_parts) + len(arrived)),
        out_specs=row_block,
        out_shape=bf16(rows, model),
        compiler_params=pltpu.CompilerParams(vmem_limit_bytes=VMEM_LIMIT),
        name="last_sum",
    )(kept, *near_parts, *arrived)


def solution(mesh):
    placed = (
        P("ctx", "head"),
        P("ctx", None),
        P("ctx", None),
        P(),
        P(),
        P("ctx", None, None),
        P("ctx", None, "head"),
        P("head", None),
    )
    return jax.shard_map(
        local, mesh=mesh, in_specs=placed, out_specs=P(("ctx", "head"), None), check_vma=False
    )
```

```python
import functools

import jax
import jax.numpy as jnp
from jax import lax
from jax.experimental import pallas as pl
from jax.experimental.pallas import tpu as pltpu
from jax.sharding import PartitionSpec as P

HEADS = 64
GROUPS = 4
QK = 192
DV = 128
CBLK = 32
KBLK = 64
PICKS = 16
WINDOW = 512
QBLK = 256
PAIR = 2 * QK
BROWS = KBLK + KBLK // 2 + KBLK
VMEM_LIMIT = 50 * 1024 * 1024
CHOSEN_LIMIT = 48 * 1024 * 1024
NEG = -1e30
SCALE = QK ** (-0.5) * 1.4426950408889634
LOW_TOTAL, HIGH_TOTAL = 2.0**-60, 2.0**100
TILE = 256
NT = (((1,), (1,)), ((), ()))
F32 = jnp.float32
BF16 = jnp.bfloat16


def half_lanes(rows):
    return lax.broadcasted_iota(jnp.int32, (rows, 128), 1) < 64


def swap_halves(x):
    return pltpu.roll(x, 64, 1)


def turned(keys):
    row, col = iota(256, 256, 0), iota(256, 256, 1)
    unit = (row == col).astype(BF16)
    even = lax.dot_general(unit, keys, NT, preferred_element_type=F32).astype(BF16)
    return even, lower(even)


def lower(even):
    return jnp.concatenate([jnp.zeros((64, even.shape[1]), BF16), even[:QK]], axis=0)


def with_ones(values):
    return jnp.concatenate([values, jnp.ones_like(values)], axis=1)


def plan(group, shard, per_owner, picks_ref, lists_ref, slots_ref, dead_ref):
    lists = picks_ref.shape[0]
    total = lists_ref.shape[1] // lists * per_owner
    width = slots_ref.shape[1]
    picks = jnp.zeros((lists, PICKS), jnp.int32)
    for each in range(picks_ref.shape[1]):
        picks = jnp.where(group == each, picks_ref[:, each, :], picks)
    block = iota(lists, total, 1)
    hits = [block == picks[:, entry : entry + 1] for entry in range(PICKS)]
    named = functools.reduce(jnp.logical_or, hits).astype(F32)
    named = jnp.broadcast_to(jnp.max(named, axis=0, keepdims=True), (8, total))
    row, col = iota(total, total, 0), iota(total, total, 1)
    before = (lax.div(row, per_owner) == lax.div(col, per_owner)) & (row < col)
    rank = jnp.dot(named, before.astype(F32), preferred_element_type=F32)
    rank = jnp.minimum(rank, float(lists - 1))
    inside = lax.rem(iota(8, total, 1), per_owner).astype(F32)
    found = jnp.zeros((8, lists_ref.shape[1]), F32)
    row, col = iota(total, lists_ref.shape[1], 0), iota(total, lists_ref.shape[1], 1)
    for place in range(lists):
        to = (col == lax.div(row, per_owner) * lists + place).astype(F32)
        value = jnp.where(rank == float(place), named * inside, 0.0)
        found = found + jnp.dot(value, to, preferred_element_type=F32)
    lists_ref[...] = found[:1].astype(jnp.int32)

    owner = lax.div(block, per_owner)
    turn = (lax.div(shard, 2) - lax.div(owner, 2)) * 2 + ((owner ^ shard) & 1)
    slot = jnp.clip(turn * lists + rank[:lists].astype(jnp.int32), 0, lists_ref.shape[1] - 1)
    slot = slot.astype(F32)
    first = shard * per_owner + iota(lists, 1, 0) * (QBLK // KBLK)
    own = block == first

    def pick_out(hit, values):
        return jnp.sum(jnp.where(hit, values, 0.0), axis=1, keepdims=True)

    lane = iota(lists, width, 1)
    slots = jnp.where(lane == 0, pick_out(own, slot), 0.0)
    dead = jnp.zeros((lists, width), F32)
    seen = own.astype(F32)
    at = jnp.ones((lists, 1), jnp.int32)
    met = jnp.zeros((lists, 1), jnp.int32)
    for entry, hit in enumerate(hits):
        pick = picks[:, entry : entry + 1]
        is_own = (pick == first).astype(jnp.int32)
        gone = jnp.maximum(pick_out(hit, seen), (pick > first).astype(F32))
        slots = jnp.where(lane == at, pick_out(hit, slot), slots)
        dead = jnp.where(lane == at, gone, dead)
        seen = jnp.maximum(seen, hit.astype(F32))
        at = at + 1 - is_own * (1 - met)
        met = jnp.maximum(met, is_own)
    slots_ref[...] = slots.astype(jnp.int32)
    dead_ref[...] = dead.astype(jnp.int32)


def prep_kernel(
    where_ref,
    picks_in,
    keys_in,
    values_in,
    fold_in,
    packed_ref,
    rim_ref,
    lists_ref,
    slots_ref,
    dead_ref,
    even_ref,
    odd_ref,
    val_ref,
    picks_ref,
    keys_ref,
    values_ref,
    kw_ref,
    vw_ref,
    sems,
):
    group, shard = where_ref[0], where_ref[1]
    pair = pl.ds(pl.multiple_of(lax.div(group, 2) * PAIR, 128), PAIR)
    single = pl.ds(pl.multiple_of(group * DV, 128), DV)
    folded_value = pl.ds(pl.multiple_of(GROUPS * QK + group * DV, 128), DV)
    copies = [
        pltpu.make_async_copy(source, target, sems.at[i])
        for i, (source, target) in enumerate(
            [
                (picks_in, picks_ref),
                (keys_in.at[:, pair], keys_ref),
                (values_in.at[:, single], values_ref),
                (fold_in.at[:, pair], kw_ref),
                (fold_in.at[:, folded_value], vw_ref),
            ]
        )
    ]
    for copy in copies:
        copy.start()
    copies[0].wait()
    plan(group, shard, keys_ref.shape[0] // KBLK, picks_ref, lists_ref, slots_ref, dead_ref)
    for copy in copies[1:]:
        copy.wait()
    odd = lax.rem(group, 2) == 1

    def own_columns(ref):
        t0 = ref[:, :128].astype(F32)
        t1 = ref[:, 128:256].astype(F32)
        t2 = ref[:, 256:].astype(F32)
        r1, r2 = swap_halves(t1), swap_halves(t2)
        left = half_lanes(t0.shape[0])
        low = jnp.where(odd, jnp.where(left, r1, r2), t0)
        high = jnp.where(left, jnp.where(odd, r2, t1), 0.0)
        return low, high

    low, high = own_columns(keys_ref)
    values = values_ref[...]
    rows = low.shape[0]
    count = rows // KBLK
    high3 = high.reshape(count, KBLK, 128)
    packed_high = high3[:, : KBLK // 2] + swap_halves(
        high3[:, KBLK // 2 :].reshape(count * KBLK // 2, 128)
    ).reshape(count, KBLK // 2, 128)
    even = jnp.concatenate([low.astype(BF16), high.astype(BF16)], axis=1)
    even_ref[...], odd_ref[...] = turned(even)
    val_ref[...] = with_ones(values)
    for block in range(count):
        at = block * BROWS
        token = slice(block * KBLK, block * KBLK + KBLK)
        packed_ref[at : at + KBLK] = low[token].astype(BF16)
        packed_ref[at + KBLK : at + KBLK + KBLK // 2] = packed_high[block].astype(BF16)
        packed_ref[at + KBLK + KBLK // 2 : at + BROWS] = values[token]
    rim_rows = rim_ref.shape[0]
    rim_ref[...] = packed_ref[count * BROWS - rim_rows : count * BROWS]

    wlow, whigh = own_columns(kw_ref)
    folds = rows // CBLK

    def fold(x, w):
        return jnp.sum(x.reshape(folds, CBLK, 128) * w[None], axis=1)

    at = count * BROWS
    half = folds // 2
    high_fold = fold(high, whigh)
    high_fold = high_fold[:half] + swap_halves(high_fold[half:])
    packed_ref[at : at + folds] = fold(low, wlow).astype(BF16)
    packed_ref[at + folds : at + folds + half] = high_fold.astype(BF16)
    packed_ref[at + folds + half :] = fold(values.astype(F32), vw_ref[...]).astype(BF16)


def pack_kernel(lists, beside, where_ref, *refs):
    count = len(refs) // 2
    named, ref, outs = refs[:count], refs[count], refs[count + 1 :]
    shard = where_ref[1]
    owner = shard + 1 - 2 * lax.rem(shard, 2) if beside else shard
    data = ref.shape[0] - (outs[0].shape[0] - lists * BROWS)
    for blocks, out in zip(named, outs):
        for place in range(lists):
            at = pl.multiple_of(blocks[0, owner * lists + place] * BROWS, 16)
            out[place * BROWS : (place + 1) * BROWS] = ref[pl.ds(at, BROWS)]
        out[lists * BROWS :] = ref[data:]


def unpack(ref, at, count, step=1):
    lows, packed, values = [], [], []
    for block in range(count):
        first = at + block * step * BROWS
        lows.append(ref[first : first + KBLK])
        packed.append(ref[first + KBLK : first + KBLK + KBLK // 2])
        values.append(ref[first + KBLK + KBLK // 2 : first + BROWS])
    packed = jnp.concatenate(packed, axis=0)
    row, col = iota(128, 256, 0), iota(128, 256, 1)
    take = (row == jnp.where(col < 128, col, col - 64)) & (lax.rem(col, 128) < 64)
    both = jnp.dot(packed, take.astype(BF16), preferred_element_type=F32).astype(BF16)
    half = KBLK // 2
    highs = []
    for block in range(count):
        rows = slice(block * half, block * half + half)
        highs += [both[rows, :128], both[rows, 128:]]
    even = jnp.concatenate(
        [jnp.concatenate(lows, axis=0), jnp.concatenate(highs, axis=0)], axis=1
    )
    return even, jnp.concatenate(values, axis=0)


def fill_rim(shard, near_ref, far_ref, own, ext):
    rim_blocks = WINDOW // KBLK
    even_in, odd_in, val_in = own
    even_ref, odd_ref, val_ref = ext
    even_ref[:, WINDOW:] = even_in[:, :WINDOW]
    odd_ref[:, WINDOW:] = odd_in[:, :WINDOW]
    val_ref[WINDOW:] = val_in[:WINDOW]
    use_near = lax.rem(shard, 2) == 1
    rim_end = near_ref.shape[0] // BROWS * BROWS
    near_rim = near_ref[rim_end - far_ref.shape[0] : rim_end]

    @pl.when(shard > 0)
    def _():
        keys, values = unpack(jnp.where(use_near, near_rim, far_ref[...]), 0, rim_blocks)
        even_ref[:, :WINDOW], odd_ref[:, :WINDOW] = turned(keys)
        val_ref[:WINDOW] = with_ones(values)

    @pl.when(shard == 0)
    def _():
        even = jnp.broadcast_to(even_in[:, :1].astype(F32), (256, WINDOW)).astype(BF16)
        even_ref[:, :WINDOW], odd_ref[:, :WINDOW] = even, lower(even)
        val_ref[:WINDOW] = jnp.zeros((WINDOW, 256), BF16)


def pool_kernel(groups, lists, where_ref, own_ref, *refs):
    sent = 2 * groups - 1
    ins, (key_ref, val_ref, ceven_ref, codd_ref, cval_ref, folded) = refs[:sent], refs[sent:]
    shard = where_ref[1]
    parity = lax.rem(shard, 2)
    base = shard - parity
    rows = lists * KBLK
    folds = (ins[0].shape[0] - lists * BROWS) * 2 // 5
    half = folds // 2
    folded[...] = jnp.zeros_like(folded)
    cval_ref[...] = jnp.zeros_like(cval_ref)

    def fill(place, owner, ref, step, fold_at):
        keys, values = unpack(ref, 0, lists, step)
        at = slice(place * rows, place * rows + rows)
        key_ref[at] = keys
        val_ref[at] = values
        low = ref[fold_at : fold_at + folds]
        high = ref[fold_at + folds : fold_at + folds + half].astype(F32)
        left = half_lanes(half)
        high = [jnp.where(left, x, 0.0) for x in (high, swap_halves(high))]
        high = jnp.concatenate(high, axis=0).astype(BF16)
        owned = pl.ds(pl.multiple_of(owner * folds, 32), folds)
        folded[owned] = jnp.concatenate([low, high], axis=1)
        cval_ref[owned] = with_ones(ref[fold_at + folds + half : fold_at + 2 * folds + half])

    fill(0, shard, own_ref, QBLK // KBLK, own_ref.shape[0] - 2 * folds - half)
    fill(1, base + 1 - parity, ins[0], 1, lists * BROWS)
    for distance in range(1, groups):

        @pl.when(base >= 2 * distance)
        def _():
            for side in range(2):
                owner = base - 2 * distance + (parity if side == 0 else 1 - parity)
                fill(2 * distance + side, owner, ins[2 * (groups - distance) - 1 + side], 1, lists * BROWS)

    ceven_ref[...], codd_ref[...] = turned(folded[...])


def iota(rows, cols, axis):
    return lax.broadcasted_iota(jnp.int32, (rows, cols), axis)


def scores_of(q, keys, mask):
    scores = jnp.dot(q, keys, preferred_element_type=F32)
    return scores if mask is None else mask(scores)


def in_range(total):
    good = jnp.where((total >= LOW_TOTAL) & (total <= HIGH_TOTAL), 1.0, 0.0)
    return jnp.min(good.reshape(-1, 8, DV), axis=0)


def over_heads(pairs, load, branches, finish):
    def sums(weights, values):
        out = jnp.dot(weights, values(), preferred_element_type=F32)
        return out[:, :DV], out[:, DV:]

    at_once = 2 if pairs % 2 == 0 else 1
    units = [(pair, side) for pair in range(0, pairs, at_once) for side in range(2)]
    worst, held = [], None
    for now, unit in zip([None] + units, units + [None]):
        q = None if unit is None else load(*unit, at_once)
        fresh, parts = [], []
        for at, (tiles, values) in enumerate(branches):
            weights, ahead = [], []
            for place, (keys, mask) in enumerate(tiles):
                if q is not None:
                    ahead.append(scores_of(q, keys(unit[1]), mask))
                if held is not None:
                    weights.append(jnp.exp2(held[at][place] * SCALE).astype(BF16))
            fresh.append(ahead)
            parts.append((weights, values))
        if held is not None:
            parts = [sums(jnp.concatenate(w, axis=1), values) for w, values in parts]
            worst += [in_range(x) for x in finish(*now, at_once, parts)]
        held = fresh

    @pl.when(jnp.min(functools.reduce(jnp.minimum, worst)) < 0.5)
    def _():
        def exact(pair, _):
            for side in range(2):
                q = load(pair, side, 1)
                parts = []
                for tiles, values in branches:
                    scores = [scores_of(q, keys(side), mask) for keys, mask in tiles]
                    scores = jnp.concatenate(scores, axis=1)
                    top = jnp.max(scores, axis=1, keepdims=True)
                    shifted = (scores - jnp.maximum(top, -1e28)) * SCALE
                    parts.append(sums(jnp.exp2(shifted).astype(BF16), values))
                finish(pair, side, 1, parts)
            return 0

        lax.fori_loop(0, pairs, exact, 0)


def aligned(at):
    return at if isinstance(at, int) else pl.multiple_of(at, 128)


def query_loader(q_ref):
    def load(pair, side, n):
        at = [aligned((pair + p) * PAIR + side * 128) for p in range(n)]
        return jnp.concatenate([q_ref[:, pl.ds(x, 256)] for x in at], axis=0)

    return load


def head_columns(pair, side):
    return pl.ds(aligned(pair * 2 * DV + side * DV), DV)


def gate_loader(gate_ref, first, heads):
    turned = pltpu.roll(gate_ref[...], lax.rem(128 - first, 128), 1)

    def load(pair, side, n, branch):
        if isinstance(pair, int):
            local, at = turned, branch * heads + side + 2 * pair
        else:
            local, at = pltpu.roll(turned, lax.rem(128 - 2 * pair, 128), 1), branch * heads + side
        columns = [local[:, at + 2 * p : at + 2 * p + 1] for p in range(n)]
        shape = (turned.shape[0], DV)
        return jnp.concatenate([jnp.broadcast_to(x, shape) for x in columns], axis=0)

    return load


def stacked(x, times):
    return jnp.concatenate([x] * times, axis=0) if times > 1 else x


def repeated(keep, rows):
    return stacked(keep, rows // keep.shape[0])


def near_kernel(heads, first_block, rim, where_ref, q_ref, gate_ref, *refs):
    keys = refs[:3]
    if rim:
        out_ref, ext = refs[-4], refs[-3:]

        @pl.when((pl.program_id(0) == 0) & (pl.program_id(1) == 0))
        def _():
            fill_rim(where_ref[1], refs[3], refs[4], keys, ext)

        keys, reach = ext, 0
    else:
        out_ref, reach = refs[-1], WINDOW
    count = q_ref.shape[1] // QK
    gate = gate_loader(gate_ref, pl.program_id(1) * count, heads)
    base = pl.multiple_of((first_block + pl.program_id(0)) * QBLK - reach, QBLK)
    row, col = iota(QBLK, QBLK, 0), iota(QBLK, QBLK, 1)

    def tile(place, mask):
        return (lambda side: keys[side][:, pl.ds(base + place * QBLK, QBLK)]), mask

    def finish(pair, side, n, parts):
        ((num, den),) = parts
        total = gate(pair, side, n, 2) * (num / den)
        for p in range(n):
            part = total[p * QBLK : (p + 1) * QBLK]
            out_ref[:, head_columns(pair + p, side)] = part.astype(BF16)
        return [den]

    tiles = [
        tile(0, lambda x: jnp.where(repeated(col >= row, x.shape[0]), x, NEG)),
        tile(1, None),
        tile(2, lambda x: jnp.where(repeated(col <= row, x.shape[0]), x, NEG)),
    ]
    values = lambda: keys[2][pl.ds(base, WINDOW + QBLK)]
    over_heads(count // 2, query_loader(q_ref), [(tiles, values)], finish)


def near_branch(first_block, block_count, where, queries, gates, keys, rims, prior):
    tokens, width = queries.shape
    heads = width // QK
    at_once = next(n for n in (8, 4, 2) if heads % n == 0)
    row_block = lambda i, p, *_: (i + first_block, p)
    operands = [queries, gates, *keys]
    specs = [
        pl.BlockSpec((QBLK, at_once * QK), row_block),
        pl.BlockSpec((QBLK, 128), lambda i, p, *_: (i + first_block, 0)),
    ]
    specs += [VMEM_SPEC] * len(keys)
    alias, scratch = {}, []
    if rims is not None:
        other, far = rims
        operands += [other, far]
        specs += [VMEM_SPEC, VMEM_SPEC]
        scratch = [pltpu.VMEM((256, 2 * WINDOW), BF16)] * 2 + [pltpu.VMEM((2 * WINDOW, 256), BF16)]
    if prior is not None:
        operands.append(prior)
        specs.append(pl.BlockSpec(memory_space=pl.ANY))
        alias = {len(operands): 0}
    rows = block_count * QBLK * heads
    return pl.pallas_call(
        functools.partial(near_kernel, heads, first_block, rims is not None),
        grid_spec=pltpu.PrefetchScalarGridSpec(
            num_scalar_prefetch=1,
            grid=(block_count, heads // at_once),
            in_specs=specs,
            out_specs=pl.BlockSpec((QBLK, at_once * DV), row_block),
            scratch_shapes=scratch,
        ),
        out_shape=jax.ShapeDtypeStruct((tokens, heads * DV), BF16),
        input_output_aliases=alias,
        compiler_params=pltpu.CompilerParams(vmem_limit_bytes=VMEM_LIMIT),
        cost_estimate=pl.CostEstimate(
            flops=rows * (WINDOW + QBLK) * 64,
            bytes_accessed=rows * (2 * QK + 4 * DV),
            transcendentals=0,
        ),
        name="near_branch",
    )(where, *operands)


def chosen_kernel(heads, span, *refs):
    first_chunk, widths = span
    out_count = sum(len(w) for w in widths)
    meta_ref, slots_ref, dead_ref, q_ref, gate_ref, near_ref = refs[:6]
    (key_pool, val_pool), cfold, weight_ref = refs[6:8], refs[8:11], refs[11]
    outs = list(refs[12 : 12 + out_count])
    gathered, even, odd, val, attended, weight, weight_sem = refs[12 + out_count :]
    keys = (even, odd)
    turn, step = pl.program_id(0), pl.program_id(1)
    last = pl.num_programs(1) - 1
    rows = q_ref.shape[0]
    count = q_ref.shape[1] // QK
    chunk_start = meta_ref[2 + first_chunk + turn] * rows
    list_at = lax.div(chunk_start, QBLK)
    first_row = lax.rem(chunk_start, QBLK)
    position = meta_ref[2] + chunk_start
    copy = pltpu.make_async_copy(weight_ref, weight, weight_sem)

    @pl.when(step == 0)
    def _():
        for slot in range(PICKS):
            source = pl.multiple_of(slots_ref[list_at, slot] * KBLK, KBLK)
            gathered[slot * KBLK : (slot + 1) * KBLK] = key_pool[pl.ds(source, KBLK)]
            val[slot * KBLK : (slot + 1) * KBLK] = with_ones(val_pool[pl.ds(source, KBLK)])
        for slot in range(1, PICKS):

            @pl.when(dead_ref[list_at, slot] == 1)
            def _():
                at = slice(slot * KBLK, (slot + 1) * KBLK)
                gathered[at] = jnp.broadcast_to(gathered[:1], (KBLK, 256))
                val[at] = jnp.zeros((KBLK, 256), BF16)

        even[...], odd[...] = turned(gathered[...])

    @pl.when((turn == 0) & (step == 0))
    def _():
        copy.start()

    gate = gate_loader(gate_ref, step * count, heads)
    row = iota(rows, TILE, 0)
    col = iota(rows, TILE, 1)
    own_keep = (col >= KBLK) | (col <= row + first_row)

    def own_mask(scores):
        own = jnp.where(repeated(own_keep[:, :128], scores.shape[0]), scores[:, :128], NEG)
        return jnp.concatenate([own, scores[:, 128:]], axis=1)

    def comp_mask(place):
        ends = (col + place * TILE + 1) * CBLK - 1
        return lambda x: jnp.where(repeated(ends <= row + position, x.shape[0]), x, NEG)

    def tile(refs, place, mask):
        return (lambda side: refs[side][:, place * TILE : (place + 1) * TILE]), mask

    chosen = [tile(keys, p, own_mask if p == 0 else None) for p in range(PICKS * KBLK // TILE)]
    folded = [tile(cfold, p, comp_mask(p)) for p in range(cfold[2].shape[0] // TILE)]
    empty = row[:, :DV] + position < CBLK - 1

    def finish(pair, side, n, parts):
        (num, den), (folded_num, folded_den) = parts
        folded_den = jnp.where(stacked(empty, n), 1.0, folded_den)
        total = gate(pair, side, n, 1) * (num / den)
        total = total + gate(pair, side, n, 0) * (folded_num / folded_den)
        for p in range(n):
            cols = head_columns(pair + p, side)
            mixed = near_ref[:, cols].astype(F32) + total[p * rows : (p + 1) * rows]
            attended[step, :, cols] = mixed.astype(BF16)
        return [den, folded_den]

    branches = [(chosen, lambda: val[...]), (folded, lambda: cfold[2][...])]
    over_heads(count // 2, query_loader(q_ref), branches, finish)

    @pl.when((turn == 0) & (step == last))
    def _():
        copy.wait()

    for place, parts in enumerate(widths):
        chunk_outs = [outs.pop(0) for _ in parts]

        @pl.when((turn == place) & (step == last))
        def _():
            rows_in = jnp.concatenate([attended[s] for s in range(attended.shape[0])], axis=1)
            first_col = 0
            for out_ref in chunk_outs:
                for at in range(0, out_ref.shape[1], 256):
                    cols = weight[:, first_col + at : first_col + at + 256]
                    part = jnp.dot(rows_in, cols, preferred_element_type=F32)
                    out_ref[:, at : at + 256] = part.astype(out_ref.dtype)
                first_col += out_ref.shape[1]


def chosen_and_project(first_chunk, widths, rows, meta, slots, dead, queries, gates, near, pools, out_weight):
    tokens, width = queries.shape
    heads = width // QK
    at_once = next(n for n in (8, 4, 2) if heads % n == 0)
    steps = heads // at_once
    whole = lambda x: pl.BlockSpec(x.shape, lambda i, p, *_: (0,) * x.ndim)
    outs = [jax.ShapeDtypeStruct((rows, width), BF16) for chunk in widths for width in chunk]
    return pl.pallas_call(
        functools.partial(chosen_kernel, heads, (first_chunk, widths)),
        grid_spec=pltpu.PrefetchScalarGridSpec(
            num_scalar_prefetch=3,
            grid=(len(widths), steps),
            in_specs=[
                pl.BlockSpec((rows, at_once * QK), lambda i, p, m, *_: (m[2 + first_chunk + i], p)),
                pl.BlockSpec((rows, 128), lambda i, p, m, *_: (m[2 + first_chunk + i], 0)),
                pl.BlockSpec((rows, at_once * DV), lambda i, p, m, *_: (m[2 + first_chunk + i], p)),
            ]
            + [VMEM_SPEC] * len(pools)
            + [pl.BlockSpec(memory_space=pl.ANY)],
            out_specs=[VMEM_SPEC] * len(outs),
            scratch_shapes=[
                pltpu.VMEM((PICKS * KBLK, 256), BF16),
                pltpu.VMEM((256, PICKS * KBLK), BF16),
                pltpu.VMEM((256, PICKS * KBLK), BF16),
                pltpu.VMEM((PICKS * KBLK, 256), BF16),
                pltpu.VMEM((steps, rows, at_once * DV), BF16),
                pltpu.VMEM(out_weight.shape, BF16),
                pltpu.SemaphoreType.DMA,
            ],
        ),
        out_shape=outs,
        compiler_params=pltpu.CompilerParams(vmem_limit_bytes=CHOSEN_LIMIT),
        cost_estimate=pl.CostEstimate(
            flops=rows * heads * PICKS * KBLK * 64,
            bytes_accessed=out_weight.size,
            transcendentals=0,
        ),
        name="chosen_and_project",
    )(meta, slots, dead, queries, gates, near, *pools, out_weight)


VMEM_SPEC = pl.BlockSpec(memory_space=pltpu.VMEM)


def single_step(kernel, name, scalars, arrays, outs, scratch=(), in_spec=None, out_spec=None):
    whole = lambda x: pl.BlockSpec(x.shape, lambda i, *_: (0,) * len(x.shape))
    return pl.pallas_call(
        kernel,
        grid_spec=pltpu.PrefetchScalarGridSpec(
            num_scalar_prefetch=len(scalars),
            grid=(1,),
            in_specs=[in_spec or whole(x) for x in arrays],
            out_specs=[out_spec or whole(x) for x in outs],
            scratch_shapes=list(scratch),
        ),
        out_shape=outs,
        compiler_params=pltpu.CompilerParams(vmem_limit_bytes=VMEM_LIMIT),
        name=name,
    )(*scalars, *arrays)


def last_sum(halves, rows, kept_ref, *refs):
    halves, others, out_ref = refs[:halves], refs[halves:-1], refs[-1]
    at = pl.ds(pl.multiple_of(pl.program_id(0) * rows, rows), rows)
    first = 0
    for half in halves:
        cols = slice(first, first + half.shape[1])
        total = kept_ref[at, cols].astype(F32) + half[at].astype(F32)
        for other in others:
            total = total + other[at, cols].astype(F32)
        out_ref[:, cols] = total.astype(BF16)
        first += half.shape[1]


def local(
    queries,
    key_rows,
    value_rows,
    comp_key_weight,
    comp_value_weight,
    block_picks,
    gate_logits,
    out_weight,
):
    tokens = queries.shape[0]
    heads = queries.shape[1] // QK
    n_ctx, n_head = lax.axis_size("ctx"), lax.axis_size("head")
    shard, head_at = lax.axis_index("ctx"), lax.axis_index("head")
    group = head_at * heads // (HEADS // GROUPS)
    per_owner = tokens // KBLK
    lists = tokens // QBLK
    folds = tokens // CBLK
    groups = n_ctx // 2
    rim_blocks = WINDOW // KBLK
    packed_rows = per_owner * BROWS
    bf16 = lambda *shape: jax.ShapeDtypeStruct(shape, BF16)

    chips = n_head // 2
    chip, core = head_at // 2, lax.rem(head_at, 2)
    order = []
    for step in list(range(1, chips)) + [0]:
        target = lax.rem(chip + step, chips) * 2
        order += [target + 1 - core, target + core]
    where = jnp.stack([group, shard, shard * tokens] + order).astype(jnp.int32)
    rim_rows = rim_blocks * BROWS
    fold_weights = jnp.concatenate([comp_key_weight, comp_value_weight], axis=1)
    int32 = lambda *shape: jax.ShapeDtypeStruct(shape, jnp.int32)
    prep_out = [bf16(packed_rows + folds * 5 // 2, 128), bf16(rim_rows, 128)]
    prep_out += [int32(1, n_ctx * lists), int32(lists, 2 * PICKS), int32(lists, 2 * PICKS)]
    prep_out += [bf16(256, tokens)] * 2 + [bf16(tokens, 256)]
    packed, rim, named, slots, dead, even, odd, val = pl.pallas_call(
        prep_kernel,
        grid_spec=pltpu.PrefetchScalarGridSpec(
            num_scalar_prefetch=1,
            grid=(1,),
            in_specs=[pl.BlockSpec(memory_space=pl.ANY)] * 4,
            out_specs=[VMEM_SPEC] * 2
            + [pl.BlockSpec(x.shape, lambda i, g: (0, 0)) for x in prep_out[2:5]]
            + [VMEM_SPEC] * 3,
            scratch_shapes=[
                pltpu.VMEM(block_picks.shape, jnp.int32),
                pltpu.VMEM((tokens, PAIR), BF16),
                pltpu.VMEM((tokens, DV), BF16),
                pltpu.VMEM((CBLK, PAIR), F32),
                pltpu.VMEM((CBLK, DV), F32),
                pltpu.SemaphoreType.DMA((5,)),
            ],
        ),
        out_shape=prep_out,
        compiler_params=pltpu.CompilerParams(vmem_limit_bytes=51 * 1024 * 1024),
        name="prep",
    )(where, block_picks, key_rows, value_rows, fold_weights)
    other = lax.ppermute(packed, "ctx", [(i, i ^ 1) for i in range(n_ctx)])
    named = [named] + [
        lax.ppermute(named, "ctx", [(i, i - 2 * d) for i in range(2 * d, n_ctx)])
        for d in range(1, groups)
    ]

    gates = jax.nn.sigmoid(gate_logits).reshape(tokens, 3 * heads)
    gates = jnp.pad(gates, ((0, 0), (0, 128 - 3 * heads)))
    sent = bf16(lists * BROWS + folds * 5 // 2, 128)

    def pack(beside, lists_in, rows):
        return single_step(
            functools.partial(pack_kernel, lists, beside),
            "pack",
            [where, *lists_in],
            [rows],
            [sent] * len(lists_in),
            in_spec=VMEM_SPEC,
            out_spec=VMEM_SPEC,
        )

    def all_ahead(sends):
        moved = []
        for distance, send in reversed(list(enumerate(sends, 1))):
            route = [(i, i + 2 * distance) for i in range(n_ctx - 2 * distance)]
            moved.append(lax.ppermute(send, "ctx", route))
        return moved[::-1]

    named, gates = lax.optimization_barrier((named, gates))
    own_sends = pack(False, named[1:], packed)
    own_sends, even, rim = lax.optimization_barrier((own_sends, even, rim))
    from_same = all_ahead(own_sends)
    far_rim = lax.ppermute(rim, "ctx", [(i, i + 1) for i in range(1, n_ctx - 1, 2)])

    reach = WINDOW // QBLK
    near = functools.partial(near_branch, where=where, queries=queries, gates=gates)
    near = functools.partial(near, keys=(even, odd, val))
    mixed = near(reach, lists - reach, rims=None, prior=None)

    other, mixed = lax.optimization_barrier((other, mixed))
    beside, *other_sends = pack(True, named, other)
    from_other = all_ahead(other_sends)
    mixed = near(0, reach, rims=(other, far_rim), prior=mixed)

    farthest_first = reversed(list(zip(from_same, from_other)))
    received = [beside] + [x for both in farthest_first for x in both]
    pools = single_step(
        functools.partial(pool_kernel, groups, lists),
        "pool",
        [where],
        [packed] + received,
        [bf16(n_ctx * lists * KBLK, 256), bf16(n_ctx * lists * KBLK, DV)]
        + [bf16(256, n_ctx * folds)] * 2
        + [bf16(n_ctx * folds, 256)],
        [pltpu.VMEM((n_ctx * folds, 256), BF16)],
        in_spec=VMEM_SPEC,
        out_spec=VMEM_SPEC,
    )
    rows = tokens // n_head
    across = [(i, i ^ 1) for i in range(n_head)]

    model = out_weight.shape[1]

    def project(first_chunk, widths):
        return chosen_and_project(
            first_chunk, widths, rows, where, slots, dead, queries, gates, mixed, pools, out_weight
        )

    sums = []
    for step in range(chips - 1):
        other = lax.ppermute(project(1 + 2 * step, [[model]])[0], "head", across)
        mine = project(2 + 2 * step, [[model]])[0]
        summed = (mine.astype(F32) + other.astype(F32)).astype(BF16)
        summed, where = lax.optimization_barrier((summed, where))
        sums.append(summed)
    *passed, kept = project(n_head - 1, [[model // 2] * 2, [model]])
    near_parts = [lax.ppermute(x, "head", across) for x in passed]
    arrived = []
    for step, summed in enumerate(sums, 1):
        route = [(i, (i + 2 * step) % n_head) for i in range(n_head)]
        arrived.append(lax.ppermute(summed, "head", route))
    steps = 2 if rows % 32 == 0 else 1
    row_block = pl.BlockSpec((rows // steps, model), lambda i: (i, 0))
    return pl.pallas_call(
        functools.partial(last_sum, len(near_parts), rows // steps),
        grid=(steps,),
        in_specs=[VMEM_SPEC] * (1 + len(near_parts) + len(arrived)),
        out_specs=row_block,
        out_shape=bf16(rows, model),
        compiler_params=pltpu.CompilerParams(vmem_limit_bytes=VMEM_LIMIT),
        name="last_sum",
    )(kept, *near_parts, *arrived)


def solution(mesh):
    placed = (
        P("ctx", "head"),
        P("ctx", None),
        P("ctx", None),
        P(),
        P(),
        P("ctx", None, None),
        P("ctx", None, "head"),
        P("head", None),
    )
    return jax.shard_map(
        local, mesh=mesh, in_specs=placed, out_specs=P(("ctx", "head"), None), check_vma=False
    )
```
